32 devices in a mesh: dp: 16 (over z, x, core), tensor: 2 (over y).
Axes of the slice: x: 2, y: 2, z: 4, core: 2. Of those that a mesh axis runs over, the one named last changes fastest.
Arguments:
- activations: bfloat16 [8192, 2048], P('dp'), may hold values from -6 to 6
- cotangent: bfloat16 [8192, 2048], P('dp'), may hold values from -12 to 12
- padding_mask: int32 [8192], P('dp'), may hold values from 0 to 1, as said below
- positions: int32 [8192], P('dp'), may hold values from 0 to 255, as said below
- norm_gains: float32 [2, 2048], replicated, may hold values from 0.1 to 1.9
- base_query: bfloat16 [2048, 2048], P('dp', 'tensor'), may hold values from -0.125 to 0.125
- base_key: bfloat16 [2048, 2048], P('dp', 'tensor'), may hold values from -0.125 to 0.125
- base_value: bfloat16 [2048, 2048], P('dp', 'tensor'), may hold values from -0.125 to 0.125
- base_gate: bfloat16 [2048, 5632], P('dp', 'tensor'), may hold values from -0.125 to 0.125
- base_widen: bfloat16 [2048, 5632], P('dp', 'tensor'), may hold values from -0.125 to 0.125
- base_mixer: bfloat16 [2048, 2048], P('tensor', 'dp'), may hold values from -0.125 to 0.125
- base_funnel: bfloat16 [5632, 2048], P('tensor', 'dp'), may hold values from -0.078125 to 0.078125
- entry_value: float32 [5, 2048, 16], replicated, may hold values from -0.125 to 0.125
- attend_value: float32 [3, 16, 2048], P(None, None, 'tensor'), may hold values from -0.75 to 0.75
- widen_value: float32 [2, 16, 5632], P(None, None, 'tensor'), may hold values from -0.75 to 0.75
- mixer_value: float32 [2048, 16], P('tensor'), may hold values from -0.125 to 0.125
- funnel_value: float32 [5632, 16], P('tensor'), may hold values from -0.078125 to 0.078125
- output_value: float32 [2, 16, 2048], replicated, may hold values from -0.75 to 0.75
- stature_value: float32 [3, 2048], P(None, 'tensor'), may hold values from 0.5 to 10
- amplitude_value: float32 [2, 5632], P(None, 'tensor'), may hold values from 0.5 to 10
- loudness_value: float32 [2, 2048], replicated, may hold values from 0.5 to 11.313708
- entry_first: float32 [5, 2048, 16], replicated, may hold values from -0.0008544922 to 0.0008544922
- attend_first: float32 [3, 16, 2048], P(None, None, 'tensor'), may hold values from -0.0008544922 to 0.0008544922
- widen_first: float32 [2, 16, 5632], P(None, None, 'tensor'), may hold values from -9.1552734e-05 to 9.1552734e-05
- mixer_first: float32 [2048, 16], P('tensor'), may hold values from -0.0008544922 to 0.0008544922
- funnel_first: float32 [5632, 16], P('tensor'), may hold values from -0.0008544922 to 0.0008544922
- output_first: float32 [2, 16, 2048], replicated, may hold values from -0.0008544922 to 0.0008544922
- stature_first: float32 [3, 2048], P(None, 'tensor'), may hold values from -0.00015258789 to 0.00015258789
- amplitude_first: float32 [2, 5632], P(None, 'tensor'), may hold values from -4.5776367e-05 to 4.5776367e-05
- loudness_first: float32 [2, 2048], replicated, may hold values from -3.8146973e-05 to 3.8146973e-05
- entry_second: float32 [5, 2048, 16], replicated, may hold values from 1.5330651e-09 to 6.1322605e-09
- attend_second: float32 [3, 16, 2048], P(None, None, 'tensor'), may hold values from 1.5330651e-09 to 6.1322605e-09
- widen_second: float32 [2, 16, 5632], P(None, None, 'tensor'), may hold values from 1.7421195e-11 to 6.968478e-11
- mixer_second: float32 [2048, 16], P('tensor'), may hold values from 1.5330651e-09 to 6.1322605e-09
- funnel_second: float32 [5632, 16], P('tensor'), may hold values from 1.5330651e-09 to 6.1322605e-09
- output_second: float32 [2, 16, 2048], replicated, may hold values from 1.5330651e-09 to 6.1322605e-09
- stature_second: float32 [3, 2048], P(None, 'tensor'), may hold values from 4.7908285e-11 to 1.9163314e-10
- amplitude_second: float32 [2, 5632], P(None, 'tensor'), may hold values from 4.3552987e-12 to 1.7421195e-11
- loudness_second: float32 [2, 2048], replicated, may hold values from 3.9923572e-12 to 1.5969429e-11
Outputs:
- block_output: bfloat16 [8192, 2048], P('dp')
- input_gradient: float32 [8192, 2048], P('dp')
- gradient_norm: float32 [], replicated
- entry_updated: float32 [5, 2048, 16], replicated
- attend_updated: float32 [3, 16, 2048], P(None, None, 'tensor')
- widen_updated: float32 [2, 16, 5632], P(None, None, 'tensor')
- mixer_updated: float32 [2048, 16], P('tensor')
- funnel_updated: float32 [5632, 16], P('tensor')
- output_updated: float32 [2, 16, 2048], replicated
- stature_updated: float32 [3, 2048], P(None, 'tensor')
- amplitude_updated: float32 [2, 5632], P(None, 'tensor')
- loudness_updated: float32 [2, 2048], replicated
- entry_momentum: float32 [5, 2048, 16], replicated
- attend_momentum: float32 [3, 16, 2048], P(None, None, 'tensor')
- widen_momentum: float32 [2, 16, 5632], P(None, None, 'tensor')
- mixer_momentum: float32 [2048, 16], P('tensor')
- funnel_momentum: float32 [5632, 16], P('tensor')
- output_momentum: float32 [2, 16, 2048], replicated
- stature_momentum: float32 [3, 2048], P(None, 'tensor')
- amplitude_momentum: float32 [2, 5632], P(None, 'tensor')
- loudness_momentum: float32 [2, 2048], replicated
- entry_variance: float32 [5, 2048, 16], replicated
- attend_variance: float32 [3, 16, 2048], P(None, None, 'tensor')
- widen_variance: float32 [2, 16, 5632], P(None, None, 'tensor')
- mixer_variance: float32 [2048, 16], P('tensor')
- funnel_variance: float32 [5632, 16], P('tensor')
- output_variance: float32 [2, 16, 2048], replicated
- stature_variance: float32 [3, 2048], P(None, 'tensor')
- amplitude_variance: float32 [2, 5632], P(None, 'tensor')
- loudness_variance: float32 [2, 2048], replicated
The draws below stay inside these ranges and needn't reach their ends.
Inputs may be any that keep to these rules, and one draw needn't show every extreme that they name: `padding_mask`: sequences are 256 consecutive rows, pairs are sequences 2i and 2i+1. In each pair one sequence has no padding and the other has 1 to 128 leading padded positions, marked 0. Positions count from 0 at a sequence's first unpadded token; padded positions hold 0.
All inputs are finite; a program needn't handle non-finite values.
Results may differ from the reference program's by a relative error of at most 0.013.
The reference program's roundings to bfloat16 on the way count: a program that leaves them out, or rounds other values in their place, can miss the bound.
Values may be sent and summed in bfloat16 or wider, within the bound.
A program may use at most 264 MiB of HBM per device.

```python
import math
import jax
import jax.numpy as jnp
from jax import lax

D = 2048
HEAD_DIM = 128
FF = 5632
RANK = 16
SEQ = 256
STEP = 5
TOK_DEV = 512
TOKENS = 8192
ADAPTED = 652288
N_DP = 16


def padding_layout(key):
    count = TOKENS // SEQ
    pairs = count // 2
    which = jax.random.randint(jax.random.fold_in(key, 11), (pairs,), 0, 2)
    depth = jax.random.randint(jax.random.fold_in(key, 12), (pairs,), 1, SEQ // 2 + 1)
    leading = jnp.stack([jnp.where(which == 0, 0, depth), jnp.where(which == 0, depth, 0)], axis=1).reshape(count)
    steps = jnp.arange(SEQ, dtype=jnp.int32)
    marks = (steps[None, :] >= leading[:, None]).astype(jnp.int32).reshape(TOKENS)
    places = jnp.maximum(steps[None, :] - leading[:, None], 0).astype(jnp.int32).reshape(TOKENS)
    return (marks, places)


def draw_padding_mask(key, part):
    return padding_layout(key)[0]


def draw_positions(key, part):
    return padding_layout(key)[1]


def draw_cotangent(key, part):
    key = jax.random.fold_in(key, 3)
    index = jnp.arange(TOKENS, dtype=jnp.float32) / (TOKENS - 1)
    drawn = jax.random.truncated_normal(key, -4.0, 4.0, (TOKENS, D), jnp.float32)
    ramp = 1.0 + 2.0 * index
    return (drawn * ramp[:, None]).astype(jnp.bfloat16)


def mixed_scales(key, steady, columns, top):
    drawn = jax.random.uniform(jax.random.fold_in(key, 21), (steady, columns), jnp.float32, 0.7, 1.4)
    spread = jnp.exp(jax.random.uniform(jax.random.fold_in(key, 22), (1, columns), jnp.float32, -0.6931, 0.6931))
    ramp = 1.0 + top * jnp.arange(columns, dtype=jnp.float32) / (columns - 1)
    return jnp.concatenate([drawn, spread * ramp[None, :]], axis=0)


def draw_stature_value(key, part):
    key = jax.random.fold_in(key, 5)
    return mixed_scales(key, 2, D, 2.0)


def draw_amplitude_value(key, part):
    key = jax.random.fold_in(key, 6)
    return mixed_scales(key, 1, FF, 2.0)


def draw_loudness_value(key, part):
    key = jax.random.fold_in(key, 7)
    lead = max(1.0, SEQ / 8.0) ** 0.5
    spread = jnp.exp(jax.random.uniform(key, (2, D), jnp.float32, -0.6931, 0.6931))
    return spread * jnp.array([[lead], [1.0]], jnp.float32)


def shard_levels(stream_key, shape, pieces, smallest, top_value):
    def one(position, blocks):
        heights = jax.random.uniform(jax.random.fold_in(jax.random.fold_in(stream_key, 6), position), (blocks,), jnp.float32, smallest / len(pieces), top_value / len(pieces))
        return jnp.repeat(jnp.exp(heights), shape[position] // blocks).reshape((-1,) + (1,) * (len(shape) - position - 1))

    level = one(*pieces[0])
    for cut in pieces[1:]:
        level = level * one(*cut)
    return level


def normal_values(own_key, shape, width, limit, cuts=(), kind=jnp.bfloat16):
    values = width * jax.random.normal(own_key, shape, jnp.float32)
    if cuts:
        values = values * shard_levels(own_key, shape, cuts, -0.22, 0.18)
    return jnp.clip(values, -limit, limit).astype(kind)


def setup_inputs(seed: int = 0) -> dict:
    streams_of = jax.random.split(jax.random.key(seed), 40)
    return {
        "activations": normal_values(streams_of[0], (TOKENS, D), 1.0, 6.0, ((0, 16),)),
        "cotangent": draw_cotangent(jax.random.fold_in(streams_of[39], 71), 0),
        "padding_mask": draw_padding_mask(jax.random.fold_in(streams_of[39], 71), 0),
        "positions": draw_positions(jax.random.fold_in(streams_of[39], 71), 0),
        "norm_gains": jnp.clip(1.0 + 0.18 * jax.random.normal(streams_of[4], (2, D), jnp.float32), 0.1, 1.9),
        "base_query": normal_values(streams_of[5], (D, D), D ** -0.5, 0.125, ((0, 16), (1, 2))),
        "base_key": normal_values(streams_of[6], (D, D), D ** -0.5, 0.125, ((0, 16), (1, 2))),
        "base_value": normal_values(streams_of[7], (D, D), D ** -0.5, 0.125, ((0, 16), (1, 2))),
        "base_gate": normal_values(streams_of[8], (D, FF), D ** -0.5, 0.125, ((0, 16), (1, 2))),
        "base_widen": normal_values(streams_of[9], (D, FF), D ** -0.5, 0.125, ((0, 16), (1, 2))),
        "base_mixer": normal_values(streams_of[10], (D, D), D ** -0.5, 0.125, ((0, 2), (1, 16))),
        "base_funnel": normal_values(streams_of[11], (FF, D), FF ** -0.5, 0.078125, ((0, 2), (1, 16))),
        "entry_value": normal_values(streams_of[12], (5, D, RANK), D ** -0.5, 0.125, (), jnp.float32),
        "attend_value": normal_values(streams_of[13], (3, RANK, D), (4 * RANK) ** -0.5, 0.75, ((2, 2),), jnp.float32),
        "widen_value": normal_values(streams_of[14], (2, RANK, FF), (4 * RANK) ** -0.5, 0.75, ((2, 2),), jnp.float32),
        "mixer_value": normal_values(streams_of[15], (D, RANK), D ** -0.5, 0.125, ((0, 2),), jnp.float32),
        "funnel_value": normal_values(streams_of[16], (FF, RANK), FF ** -0.5, 0.078125, ((0, 2),), jnp.float32),
        "output_value": normal_values(streams_of[17], (2, RANK, D), (4 * RANK) ** -0.5, 0.75, (), jnp.float32),
        "stature_value": draw_stature_value(jax.random.fold_in(streams_of[39], 71), 0),
        "amplitude_value": draw_amplitude_value(jax.random.fold_in(streams_of[39], 71), 0),
        "loudness_value": draw_loudness_value(jax.random.fold_in(streams_of[39], 71), 0),
        "entry_first": normal_values(streams_of[21], (5, D, RANK), (0.111 / ADAPTED ** 0.5), 0.0008544922, (), jnp.float32),
        "attend_first": normal_values(streams_of[22], (3, RANK, D), (0.111 / ADAPTED ** 0.5), 0.0008544922, ((2, 2),), jnp.float32),
        "widen_first": normal_values(streams_of[23], (2, RANK, FF), (0.111 * (4 * RANK / (FF * ADAPTED)) ** 0.5), 9.1552734375e-05, ((2, 2),), jnp.float32),
        "mixer_first": normal_values(streams_of[24], (D, RANK), (0.111 / ADAPTED ** 0.5), 0.0008544922, ((0, 2),), jnp.float32),
        "funnel_first": normal_values(streams_of[25], (FF, RANK), (0.111 / ADAPTED ** 0.5), 0.0008544922, ((0, 2),), jnp.float32),
        "output_first": normal_values(streams_of[26], (2, RANK, D), (0.111 / ADAPTED ** 0.5), 0.0008544922, (), jnp.float32),
        "stature_first": normal_values(streams_of[27], (3, D), (0.111 * (4 * RANK / (D * ADAPTED)) ** 0.5), 0.00015258789, ((1, 2),), jnp.float32),
        "amplitude_first": normal_values(streams_of[28], (2, FF), (0.111 * (RANK / (FF * ADAPTED)) ** 0.5), 4.57763671875e-05, ((1, 2),), jnp.float32),
        "loudness_first": normal_values(streams_of[29], (2, D), (0.111 * (RANK / (3 * D * ADAPTED)) ** 0.5), 3.814697265625e-05, (), jnp.float32),
        "entry_second": jnp.clip(jnp.exp(jax.random.uniform(streams_of[30], (5, D, RANK), jnp.float32, math.log(1.5330651192968503e-09), math.log(6.132260477187401e-09))), 1.5330651192968503e-09, 6.132260477187401e-09),
        "attend_second": jnp.clip(jnp.exp(math.log(6.132260477187401e-09) - 1.3862944 * jax.random.uniform(streams_of[31], (3, RANK, D), jnp.float32) ** shard_levels(streams_of[31], (3, RANK, D), ((2, 2),), -0.2, 0.2)), 1.5330651192968503e-09, 6.132260477187401e-09),
        "widen_second": jnp.clip(jnp.exp(math.log(6.968477878066537e-11) - 1.3862944 * jax.random.uniform(streams_of[32], (2, RANK, FF), jnp.float32) ** shard_levels(streams_of[32], (2, RANK, FF), ((2, 2),), -0.2, 0.2)), 1.7421194695166342e-11, 6.968477878066537e-11),
        "mixer_second": jnp.clip(jnp.exp(math.log(6.132260477187401e-09) - 1.3862944 * jax.random.uniform(streams_of[33], (D, RANK), jnp.float32) ** shard_levels(streams_of[33], (D, RANK), ((0, 2),), -0.2, 0.2)), 1.5330651192968503e-09, 6.132260477187401e-09),
        "funnel_second": jnp.clip(jnp.exp(math.log(6.132260477187401e-09) - 1.3862944 * jax.random.uniform(streams_of[34], (FF, RANK), jnp.float32) ** shard_levels(streams_of[34], (FF, RANK), ((0, 2),), -0.2, 0.2)), 1.5330651192968503e-09, 6.132260477187401e-09),
        "output_second": jnp.clip(jnp.exp(jax.random.uniform(streams_of[35], (2, RANK, D), jnp.float32, math.log(1.5330651192968503e-09), math.log(6.132260477187401e-09))), 1.5330651192968503e-09, 6.132260477187401e-09),
        "stature_second": jnp.clip(jnp.exp(math.log(1.916331399121063e-10) - 1.3862944 * jax.random.uniform(streams_of[36], (3, D), jnp.float32) ** shard_levels(streams_of[36], (3, D), ((1, 2),), -0.2, 0.2)), 4.790828497802657e-11, 1.916331399121063e-10),
        "amplitude_second": jnp.clip(jnp.exp(math.log(1.7421194695166342e-11) - 1.3862944 * jax.random.uniform(streams_of[37], (2, FF), jnp.float32) ** shard_levels(streams_of[37], (2, FF), ((1, 2),), -0.2, 0.2)), 4.3552986737915855e-12, 1.7421194695166342e-11),
        "loudness_second": jnp.clip(jnp.exp(jax.random.uniform(streams_of[38], (2, D), jnp.float32, math.log(3.992357226062504e-12), math.log(1.5969428904250016e-11))), 3.992357226062504e-12, 1.5969428904250016e-11),
    }


HIGH_PRECISION = lax.Precision.HIGHEST
ADAPTER_SCALE = 2.0
NORM_EPS = 1e-05
COLUMN_EPS = 1e-06
BETA_ONE = 0.9
BETA_TWO = 0.999
ADAM_EPS = 1e-08
DECAY = 0.01
CLIP = 1.0
RATE_FACTOR = 0.02
RATE_LIFT = 0.2
RATE_SCALE = 0.5
RATE_LOUD = 2.0
ROPE_BASE = 10000.0
MASKED = -1e+30

@jax.custom_vjp
def low(v):
    return lax.optimization_barrier(v.astype(jnp.bfloat16)).astype(jnp.float32)

@jax.custom_vjp
def low_back(v):
    return v

def low_keep(v):
    return (low(v), None)

def low_pass(kept, grad):
    return (grad,)

def back_keep(v):
    return (v, None)

def back_low(kept, grad):
    return (low(grad),)
low.defvjp(low_keep, low_pass)
low_back.defvjp(back_keep, back_low)

def root_norm(values, gain):
    return values * lax.rsqrt(lax.optimization_barrier(jnp.mean(values * values, axis=-1, keepdims=True)) + NORM_EPS) * gain

def rotate(values, places, sign):
    half = values.shape[-1] // 2
    steps = jnp.arange(half, dtype=jnp.float32)
    frequency = ROPE_BASE ** (-2.0 * steps / values.shape[-1])
    angles = places.astype(jnp.float32)[:, None] * frequency[None, :]
    cosine = jnp.cos(angles)[:, None, :]
    sine = sign * jnp.sin(angles)[:, None, :]
    first = values[..., :half]
    second = values[..., half:]
    return jnp.concatenate([first * cosine - second * sine, second * cosine + first * sine], axis=-1)

def allowed_of(padding, count):
    valid = padding.reshape(count, SEQ) > 0
    index = jnp.arange(SEQ)
    causal = index[:, None] >= index[None, :]
    itself = index[:, None] == index[None, :]
    return (causal[None] & valid[:, None, :] | itself[None])[:, None]

def merge_one(base_matrix, down_factor, up_factor, magnitude):
    unit_direction = base_matrix + ADAPTER_SCALE * jnp.dot(down_factor, up_factor, precision=HIGH_PRECISION)
    norms = jnp.sqrt(lax.optimization_barrier(jnp.sum(unit_direction * unit_direction, axis=0)) + COLUMN_EPS)
    return low(unit_direction * (magnitude / norms))

def merge_weights(bases, params):
    entry, attend, widen, mixer, funnel, output, stature, amplitude, loudness = params
    return (merge_one(bases[0], entry[0], attend[0], stature[0]), merge_one(bases[1], entry[1], attend[1], stature[1]), merge_one(bases[2], entry[2], attend[2], stature[2]), merge_one(bases[3], entry[3], widen[0], amplitude[0]), merge_one(bases[4], entry[4], widen[1], amplitude[1]), merge_one(bases[5], mixer, output[0], loudness[0]), merge_one(bases[6], funnel, output[1], loudness[1]))

def block(rows, padding, places, gains, merged):
    count = rows.shape[0] // SEQ
    heads = rows.shape[1] // HEAD_DIM
    scale = HEAD_DIM ** (-0.5)
    normed_one = low(root_norm(rows, gains[0]))
    queries = jnp.dot(normed_one, merged[0], precision=HIGH_PRECISION).reshape(-1, heads, HEAD_DIM)
    keys = jnp.dot(normed_one, merged[1], precision=HIGH_PRECISION).reshape(-1, heads, HEAD_DIM)
    values = jnp.dot(normed_one, merged[2], precision=HIGH_PRECISION)
    turned_queries = low(rotate(low_back(queries), places, 1.0)).reshape(count, SEQ, heads, HEAD_DIM)
    turned_keys = low(rotate(low_back(keys), places, 1.0)).reshape(count, SEQ, heads, HEAD_DIM)
    values_low = low(low_back(values)).reshape(count, SEQ, heads, HEAD_DIM)
    scores = low_back(jnp.einsum('bqhd,bkhd->bhqk', turned_queries, turned_keys, precision=HIGH_PRECISION) * scale)
    masked = jnp.where(allowed_of(padding, count), scores, MASKED)
    attention = jax.nn.softmax(masked, axis=-1)
    mixed = jnp.einsum('bhqk,bkhd->bqhd', low(attention), values_low, precision=HIGH_PRECISION).reshape(rows.shape[0], -1)
    mixed = low(low_back(mixed))
    residual = rows + low_back(jnp.dot(mixed, merged[5], precision=HIGH_PRECISION))
    normed_two = low(root_norm(residual, gains[1]))
    gate = low_back(jnp.dot(normed_two, merged[3], precision=HIGH_PRECISION))
    lifted = low_back(jnp.dot(normed_two, merged[4], precision=HIGH_PRECISION))
    hidden = low(jax.nn.silu(gate) * lifted)
    return residual + low_back(jnp.dot(hidden, merged[6], precision=HIGH_PRECISION))

def decoupled_update(value, gradient, first, second, rate):
    momentum = BETA_ONE * first + (1.0 - BETA_ONE) * gradient
    variance = BETA_TWO * second + (1.0 - BETA_TWO) * gradient * gradient
    corrected = momentum / (1.0 - BETA_ONE ** STEP)
    spread = jnp.sqrt(variance / (1.0 - BETA_TWO ** STEP))
    return (value - rate * (corrected / (spread + ADAM_EPS) + DECAY * value), momentum, variance)

def reference(activations, cotangent, padding_mask, positions, norm_gains, base_query, base_key, base_value, base_gate, base_widen, base_mixer, base_funnel, entry_value, attend_value, widen_value, mixer_value, funnel_value, output_value, stature_value, amplitude_value, loudness_value, entry_first, attend_first, widen_first, mixer_first, funnel_first, output_first, stature_first, amplitude_first, loudness_first, entry_second, attend_second, widen_second, mixer_second, funnel_second, output_second, stature_second, amplitude_second, loudness_second):
    gains = norm_gains.astype(jnp.float32)
    bases = tuple((weight.astype(jnp.float32) for weight in (base_query, base_key, base_value, base_gate, base_widen, base_mixer, base_funnel)))
    params = (entry_value, attend_value, widen_value, mixer_value, funnel_value, output_value, stature_value, amplitude_value, loudness_value)
    firsts = (entry_first, attend_first, widen_first, mixer_first, funnel_first, output_first, stature_first, amplitude_first, loudness_first)
    seconds = (entry_second, attend_second, widen_second, mixer_second, funnel_second, output_second, stature_second, amplitude_second, loudness_second)
    merged, build_back = jax.vjp(lambda values: merge_weights(bases, values), params)
    row_blocks = activations.astype(jnp.float32).reshape(N_DP, TOK_DEV, D)
    back_blocks = cotangent.astype(jnp.float32).reshape(N_DP, TOK_DEV, D)
    pad_blocks = padding_mask.reshape(N_DP, TOK_DEV)
    place_blocks = positions.reshape(N_DP, TOK_DEV)

    def step(total, inputs):
        rows, back, padding, places = inputs
        result, pull = jax.vjp(lambda r, m: block(r, padding, places, gains, m), rows, merged)
        d_rows, d_merged = pull(back)
        return (jax.tree.map(jnp.add, total, d_merged), (result.astype(jnp.bfloat16), d_rows))
    start = jax.tree.map(jnp.zeros_like, merged)
    total, (outputs, d_rows) = lax.scan(step, start, (row_blocks, back_blocks, pad_blocks, place_blocks))
    gradients = build_back(total)[0]
    squares = jnp.zeros((), jnp.float32)
    for gradient in gradients:
        squares = squares + jnp.sum(gradient * gradient)
    gradient_norm = jnp.sqrt(squares)
    down_factor = jnp.minimum(1.0, CLIP / (gradient_norm + 1e-06))
    rates = (RATE_FACTOR, RATE_LIFT, RATE_LIFT, RATE_FACTOR, RATE_FACTOR, RATE_LIFT, RATE_SCALE, RATE_SCALE, RATE_LOUD)
    updated = []
    momenta = []
    variances = []
    for value, gradient, first, second, rate in zip(params, gradients, firsts, seconds, rates):
        fresh, momentum, variance = decoupled_update(value, gradient * down_factor, first, second, rate)
        updated.append(fresh)
        momenta.append(momentum)
        variances.append(variance)
    return (outputs.reshape(TOKENS, D), d_rows.reshape(TOKENS, D), gradient_norm, updated[0], updated[1], updated[2], updated[3], updated[4], updated[5], updated[6], updated[7], updated[8], momenta[0], momenta[1], momenta[2], momenta[3], momenta[4], momenta[5], momenta[6], momenta[7], momenta[8], variances[0], variances[1], variances[2], variances[3], variances[4], variances[5], variances[6], variances[7], variances[8])
```

```python
import jax
import jax.numpy as jnp
from jax import lax
from jax.sharding import PartitionSpec as P

HEAD_DIM = 128
SEQ = 256
STEP = 5


HIGH_PRECISION = lax.Precision.HIGHEST
ADAPTER_SCALE = 2.0
NORM_EPS = 1e-05
COLUMN_EPS = 1e-06
BETA_ONE = 0.9
BETA_TWO = 0.999
ADAM_EPS = 1e-08
DECAY = 0.01
CLIP = 1.0
RATE_FACTOR = 0.02
RATE_LIFT = 0.2
RATE_SCALE = 0.5
RATE_LOUD = 2.0
ROPE_BASE = 10000.0
MASKED = -1e30


def root_norm(values, gain):
    return values * lax.rsqrt(jnp.mean(values * values, axis=-1, keepdims=True) + NORM_EPS) * gain


def rotate(values, places, sign):
    half = values.shape[-1] // 2
    steps = jnp.arange(half, dtype=jnp.float32)
    frequency = ROPE_BASE ** (-2.0 * steps / values.shape[-1])
    angles = places.astype(jnp.float32)[:, None] * frequency[None, :]
    cosine = jnp.cos(angles)[:, None, :]
    sine = sign * jnp.sin(angles)[:, None, :]
    first = values[..., :half]
    second = values[..., half:]
    return jnp.concatenate(
        [first * cosine - second * sine, second * cosine + first * sine], axis=-1
    )


def allowed_of(padding, count):
    valid = padding.reshape(count, SEQ) > 0
    index = jnp.arange(SEQ)
    causal = index[:, None] >= index[None, :]
    itself = index[:, None] == index[None, :]
    return (causal[None] & valid[:, None, :] | itself[None])[:, None]


def squares_of(items):
    total = jnp.zeros((), jnp.float32)
    for param_entry in items:
        total = total + jnp.sum(param_entry * param_entry)
    return total


def decoupled_update(value, gradient, first, second, rate):
    momentum = BETA_ONE * first + (1.0 - BETA_ONE) * gradient
    variance = BETA_TWO * second + (1.0 - BETA_TWO) * gradient * gradient
    corrected = momentum / (1.0 - BETA_ONE**STEP)
    spread = jnp.sqrt(variance / (1.0 - BETA_TWO**STEP))
    return (value - rate * (corrected / (spread + ADAM_EPS) + DECAY * value), momentum, variance)


def swap(partial):
    low = partial.astype(jnp.bfloat16)
    size = lax.axis_size("tensor")
    total = low.astype(jnp.float32)
    for step in range(1, size):
        other = lax.ppermute(low, "tensor", [(i, (i + step) % size) for i in range(size)])
        total = total + other.astype(jnp.float32)
    return total


def matmul(left, right):
    return jnp.dot(left, right, preferred_element_type=jnp.float32)


def matmul_nt(left, right):
    return jnp.einsum("ik,jk->ij", left, right, preferred_element_type=jnp.float32)


def matmul_tn(left, right):
    return jnp.einsum("ki,kj->ij", left, right, preferred_element_type=jnp.float32)


def low(values):
    return values.astype(jnp.bfloat16)


def body(
    activations,
    cotangent,
    padding_mask,
    positions,
    norm_gains,
    base_query,
    base_key,
    base_value,
    base_gate,
    base_widen,
    base_mixer,
    base_funnel,
    entry_value,
    attend_value,
    widen_value,
    mixer_value,
    funnel_value,
    output_value,
    stature_value,
    amplitude_value,
    loudness_value,
    entry_first,
    attend_first,
    widen_first,
    mixer_first,
    funnel_first,
    output_first,
    stature_first,
    amplitude_first,
    loudness_first,
    entry_second,
    attend_second,
    widen_second,
    mixer_second,
    funnel_second,
    output_second,
    stature_second,
    amplitude_second,
    loudness_second,
):
    params = (
        entry_value,
        attend_value,
        widen_value,
        mixer_value,
        funnel_value,
        output_value,
        stature_value,
        amplitude_value,
        loudness_value,
    )
    firsts = (
        entry_first,
        attend_first,
        widen_first,
        mixer_first,
        funnel_first,
        output_first,
        stature_first,
        amplitude_first,
        loudness_first,
    )
    seconds = (
        entry_second,
        attend_second,
        widen_second,
        mixer_second,
        funnel_second,
        output_second,
        stature_second,
        amplitude_second,
        loudness_second,
    )
    rows = base_query.shape[0]
    width = activations.shape[1]
    place = lax.axis_index("dp") * rows
    side = lax.axis_index("tensor")
    sides = lax.axis_size("tensor")
    cut = base_query.shape[1]
    wide = base_gate.shape[1]
    entry_rows = lax.dynamic_slice_in_dim(entry_value, place, rows, 1)
    output_columns = lax.dynamic_slice_in_dim(output_value, place, rows, 2)
    firsts_in = [base_query, base_key, base_value, base_gate, base_widen]
    lifts = [attend_value[0], attend_value[1], attend_value[2], widen_value[0], widen_value[1]]
    shards = [
        base.astype(jnp.float32)
        + ADAPTER_SCALE * jnp.dot(entry_rows[i], lifts[i], precision=HIGH_PRECISION)
        for i, base in enumerate(firsts_in)
    ]
    shards += [
        base.T.astype(jnp.float32)
        + ADAPTER_SCALE * jnp.dot(output_columns[i].T, down.T, precision=HIGH_PRECISION)
        for i, (base, down) in enumerate(((base_mixer, mixer_value), (base_funnel, funnel_value)))
    ]
    split_squares = jnp.concatenate([jnp.sum(v * v, axis=0) for v in shards[:5]])
    split_wide = split_squares.shape[0]
    shared_squares = jnp.stack([jnp.sum(v * v, axis=1) for v in shards[5:]])
    split_all = lax.dynamic_update_slice(
        jnp.zeros((sides, split_wide), jnp.float32), split_squares[None], (side, 0)
    )
    shared_all = lax.dynamic_update_slice(
        jnp.zeros((2, width), jnp.float32), shared_squares, (0, place)
    )
    packed = lax.psum(
        jnp.concatenate([split_all.reshape(-1), shared_all.reshape(-1)]), ("dp", "tensor")
    )
    split_squares = lax.dynamic_slice_in_dim(packed, side * split_wide, split_wide)
    shared_squares = packed[sides * split_wide :].reshape(2, width)
    split_norms = jnp.sqrt(split_squares + COLUMN_EPS)
    shared_norms = jnp.sqrt(shared_squares + COLUMN_EPS)
    split_magnitudes = jnp.concatenate([stature_value.reshape(-1), amplitude_value.reshape(-1)])
    split_ratio = split_magnitudes / split_norms
    shared_ratio = loudness_value / shared_norms
    own_ratio = lax.dynamic_slice_in_dim(shared_ratio, place, rows, 1)
    attend_shard = jnp.concatenate(
        [low(shards[i] * split_ratio[None, i * cut : (i + 1) * cut]) for i in range(3)]
        + [low(shards[5] * own_ratio[0][:, None])],
        axis=1,
    )
    feed_shard = jnp.concatenate(
        [
            low(shards[3 + i] * split_ratio[None, 3 * cut + i * wide : 3 * cut + (i + 1) * wide])
            for i in range(2)
        ]
        + [low(shards[6] * own_ratio[1][:, None])],
        axis=1,
    )
    attend_all = lax.all_gather(attend_shard, "dp", axis=0, tiled=True)
    feed_all = lax.all_gather(feed_shard, "dp", axis=0, tiled=True)
    merged_attend = attend_all[:, : 3 * cut]
    merged_mixer = attend_all[:, 3 * cut :]
    merged_gate = feed_all[:, :wide]
    merged_widen = feed_all[:, wide : 2 * wide]
    merged_funnel = feed_all[:, 2 * wide :]

    count = activations.shape[0] // SEQ
    heads = cut // HEAD_DIM
    scale = HEAD_DIM ** (-0.5)
    floats = activations.astype(jnp.float32)
    normed_one = low(root_norm(floats, norm_gains[0]))
    projected = matmul(normed_one, merged_attend)
    queries = projected[:, :cut]
    keys = projected[:, cut : 2 * cut]
    values = projected[:, 2 * cut :]
    values_low = low(values).reshape(count, SEQ, heads, HEAD_DIM)
    turned_queries = low(rotate(queries.reshape(-1, heads, HEAD_DIM), positions, 1.0))
    turned_queries = turned_queries.reshape(count, SEQ, heads, HEAD_DIM)
    turned_keys = low(rotate(keys.reshape(-1, heads, HEAD_DIM), positions, 1.0))
    turned_keys = turned_keys.reshape(count, SEQ, heads, HEAD_DIM)
    allowed = allowed_of(padding_mask, count)
    scores = (
        jnp.einsum(
            "bqhd,bkhd->bhqk", turned_queries, turned_keys, preferred_element_type=jnp.float32
        )
        * scale
    )
    masked = jnp.where(allowed, scores, MASKED)
    top = jnp.max(masked, axis=-1, keepdims=True)
    log_total = top + jnp.log(jnp.sum(jnp.exp(masked - top), axis=-1, keepdims=True))
    attention = jnp.exp(masked - log_total)
    attention_low = low(attention)
    mixed = jnp.einsum(
        "bhqk,bkhd->bqhd", attention_low, values_low, preferred_element_type=jnp.float32
    )
    mixed = low(mixed.reshape(activations.shape[0], cut))
    attended = swap(matmul_nt(mixed, merged_mixer))
    residual = floats + attended
    normed_two = low(root_norm(residual, norm_gains[1]))
    gate = matmul(normed_two, merged_gate)
    lifted = matmul(normed_two, merged_widen)
    hidden = low(jax.nn.silu(gate) * lifted)
    funneled = swap(matmul_nt(hidden, merged_funnel))
    block_output = low(residual + funneled)

    back = cotangent.astype(jnp.float32)
    d_hidden = matmul(cotangent, merged_funnel)
    unused, silu_pull = jax.vjp(lambda g, u: jax.nn.silu(g) * u, gate, lifted)
    d_gate, d_lifted = silu_pull(d_hidden)
    d_gate = low(d_gate)
    d_lifted = low(d_lifted)
    d_normed_two = swap(matmul_nt(d_gate, merged_gate) + matmul_nt(d_lifted, merged_widen))
    unused, second_pull = jax.vjp(lambda v: root_norm(v, norm_gains[1]), residual)
    d_residual = back + second_pull(d_normed_two)[0]
    d_residual_low = low(d_residual)
    d_mixed = low(matmul(d_residual_low, merged_mixer)).reshape(count, SEQ, heads, HEAD_DIM)
    d_attention = jnp.einsum(
        "bqhd,bkhd->bhqk", d_mixed, values_low, preferred_element_type=jnp.float32
    )
    d_values = jnp.einsum(
        "bhqk,bqhd->bkhd", attention_low, d_mixed, preferred_element_type=jnp.float32
    )
    d_values = low(d_values).reshape(-1, cut)
    d_scores = attention * (d_attention - jnp.sum(attention * d_attention, axis=-1, keepdims=True))
    d_scores = low(d_scores)
    d_turned_queries = (
        jnp.einsum("bhqk,bkhd->bqhd", d_scores, turned_keys, preferred_element_type=jnp.float32)
        * scale
    )
    d_turned_keys = (
        jnp.einsum("bhqk,bqhd->bkhd", d_scores, turned_queries, preferred_element_type=jnp.float32)
        * scale
    )
    d_queries = low(rotate(d_turned_queries.reshape(-1, heads, HEAD_DIM), positions, -1.0))
    d_keys = low(rotate(d_turned_keys.reshape(-1, heads, HEAD_DIM), positions, -1.0))
    d_queries = d_queries.reshape(-1, cut)
    d_keys = d_keys.reshape(-1, cut)
    d_projected = jnp.concatenate([d_queries, d_keys, d_values], axis=1)
    d_normed_one = swap(matmul_nt(d_projected, merged_attend))
    unused, first_pull = jax.vjp(lambda v: root_norm(v, norm_gains[0]), floats)
    input_gradient = d_residual + first_pull(d_normed_one)[0]

    d_parts = (d_queries, d_keys, d_values, d_gate, d_lifted)
    parts = (queries, keys, values, gate, lifted)
    split_dots = jnp.concatenate(
        [jnp.sum(d.astype(jnp.float32) * y, axis=0) for d, y in zip(d_parts, parts)]
    )
    shared_dots = jnp.stack(
        [
            jnp.sum(d_residual_low.astype(jnp.float32) * attended, axis=0),
            jnp.sum(back * funneled, axis=0),
        ]
    )
    split_pull = split_dots / (split_norms * split_magnitudes)
    shared_pull = shared_dots / (shared_norms * loudness_value)

    down_gradients = []
    up_gradients = []
    inputs = (normed_one, normed_one, normed_one, normed_two, normed_two)
    weights = (
        merged_attend[:, :cut],
        merged_attend[:, cut : 2 * cut],
        merged_attend[:, 2 * cut :],
        merged_gate,
        merged_widen,
    )
    offset = 0
    for i in range(5):
        out = weights[i].shape[1]
        ratio = split_ratio[offset : offset + out]
        pull = split_pull[offset : offset + out]
        offset += out
        low_lift = low(lifts[i] * ratio)
        pull_lift = low(lifts[i] * pull)
        lowered = low(matmul_nt(low_lift, d_parts[i]))
        down_gradients.append(
            ADAPTER_SCALE * (matmul(lowered, inputs[i]) - matmul_nt(pull_lift, weights[i]))
        )
        low_down = low(entry_value[i])
        reduced = low(matmul(inputs[i], low_down))
        up_gradients.append(
            ADAPTER_SCALE
            * (matmul_tn(reduced, d_parts[i]) * ratio - matmul_tn(low_down, weights[i]) * pull)
        )
    out_downs = []
    out_ups = []
    plan = (
        (mixed, d_residual_low, mixer_value, merged_mixer),
        (hidden, cotangent, funnel_value, merged_funnel),
    )
    for i, (source, d_out, down, weight) in enumerate(plan):
        low_lift = low(output_value[i] * shared_ratio[i])
        pull_lift = low(output_value[i] * shared_pull[i])
        lowered = low(matmul_nt(low_lift, d_out))
        out_downs.append(ADAPTER_SCALE * (matmul(lowered, source) - matmul(pull_lift, weight)))
        low_down = low(down)
        reduced = low(matmul(source, low_down))
        out_ups.append(
            ADAPTER_SCALE
            * (
                matmul_tn(reduced, d_out) * shared_ratio[i]
                - jnp.einsum("ir,ji->rj", low_down, weight, preferred_element_type=jnp.float32)
                * shared_pull[i]
            )
        )
    shared_terms = jnp.concatenate(down_gradients + out_ups, axis=1)
    split_terms = jnp.concatenate(up_gradients + out_downs, axis=1)
    shared_terms, split_terms, split_dots, shared_dots = lax.psum(
        (shared_terms, split_terms, split_dots, shared_dots), "dp"
    )
    split_scale = split_dots / split_magnitudes
    shared_scale = shared_dots / loudness_value
    split_total = jnp.sum(split_terms * split_terms) + jnp.sum(split_scale * split_scale)
    shared_terms, split_total = lax.psum((shared_terms, split_total), "tensor")
    totals = (
        jnp.stack([shared_terms[:, i * width : (i + 1) * width].T for i in range(5)]),
        jnp.stack([split_terms[:, i * cut : (i + 1) * cut] for i in range(3)]),
        jnp.stack([split_terms[:, 3 * cut + i * wide : 3 * cut + (i + 1) * wide] for i in range(2)]),
        split_terms[:, split_wide : split_wide + cut].T,
        split_terms[:, split_wide + cut :].T,
        jnp.stack([shared_terms[:, (5 + i) * width : (6 + i) * width] for i in range(2)]),
        split_scale[: 3 * cut].reshape(3, cut),
        split_scale[3 * cut :].reshape(2, wide),
        shared_scale,
    )
    gradient_norm = jnp.sqrt(split_total + squares_of((totals[0], totals[5], totals[8])))
    down_factor = jnp.minimum(1.0, CLIP / (gradient_norm + 1e-06))
    rates = (
        RATE_FACTOR,
        RATE_LIFT,
        RATE_LIFT,
        RATE_FACTOR,
        RATE_FACTOR,
        RATE_LIFT,
        RATE_SCALE,
        RATE_SCALE,
        RATE_LOUD,
    )
    updated = []
    momenta = []
    variances = []
    for value, gradient, first, second, rate in zip(params, totals, firsts, seconds, rates):
        fresh, momentum, variance = decoupled_update(
            value, gradient * down_factor, first, second, rate
        )
        updated.append(fresh)
        momenta.append(momentum)
        variances.append(variance)
    return (
        block_output,
        input_gradient,
        gradient_norm,
        updated[0],
        updated[1],
        updated[2],
        updated[3],
        updated[4],
        updated[5],
        updated[6],
        updated[7],
        updated[8],
        momenta[0],
        momenta[1],
        momenta[2],
        momenta[3],
        momenta[4],
        momenta[5],
        momenta[6],
        momenta[7],
        momenta[8],
        variances[0],
        variances[1],
        variances[2],
        variances[3],
        variances[4],
        variances[5],
        variances[6],
        variances[7],
        variances[8],
    )


def solution(mesh):
    return jax.shard_map(
        body,
        mesh=mesh,
        in_specs=(
            P("dp", None),
            P("dp", None),
            P("dp"),
            P("dp"),
            P(),
            P("dp", "tensor"),
            P("dp", "tensor"),
            P("dp", "tensor"),
            P("dp", "tensor"),
            P("dp", "tensor"),
            P("tensor", "dp"),
            P("tensor", "dp"),
            P(),
            P(None, None, "tensor"),
            P(None, None, "tensor"),
            P("tensor", None),
            P("tensor", None),
            P(),
            P(None, "tensor"),
            P(None, "tensor"),
            P(),
            P(),
            P(None, None, "tensor"),
            P(None, None, "tensor"),
            P("tensor", None),
            P("tensor", None),
            P(),
            P(None, "tensor"),
            P(None, "tensor"),
            P(),
            P(),
            P(None, None, "tensor"),
            P(None, None, "tensor"),
            P("tensor", None),
            P("tensor", None),
            P(),
            P(None, "tensor"),
            P(None, "tensor"),
            P(),
        ),
        out_specs=(
            P("dp", None),
            P("dp", None),
            P(),
            P(),
            P(None, None, "tensor"),
            P(None, None, "tensor"),
            P("tensor", None),
            P("tensor", None),
            P(),
            P(None, "tensor"),
            P(None, "tensor"),
            P(),
            P(),
            P(None, None, "tensor"),
            P(None, None, "tensor"),
            P("tensor", None),
            P("tensor", None),
            P(),
            P(None, "tensor"),
            P(None, "tensor"),
            P(),
            P(),
            P(None, None, "tensor"),
            P(None, None, "tensor"),
            P("tensor", None),
            P("tensor", None),
            P(),
            P(None, "tensor"),
            P(None, "tensor"),
            P(),
        ),
        check_vma=False,
    )
```

```python
import functools

import jax
import jax.numpy as jnp
from jax import lax
from jax.experimental import pallas as pl
from jax.experimental.pallas import tpu as pltpu
from jax.sharding import PartitionSpec as P

HEAD_DIM = 128
SEQ = 256
STEP = 5


HIGH_PRECISION = lax.Precision.HIGHEST
ADAPTER_SCALE = 2.0
NORM_EPS = 1e-05
COLUMN_EPS = 1e-06
BETA_ONE = 0.9
BETA_TWO = 0.999
ADAM_EPS = 1e-08
DECAY = 0.01
CLIP = 1.0
RATE_FACTOR = 0.02
RATE_LIFT = 0.2
RATE_SCALE = 0.5
RATE_LOUD = 2.0
ROPE_BASE = 10000.0
MASKED = -1e30


def root_norm(values, gain):
    return values * lax.rsqrt(jnp.mean(values * values, axis=-1, keepdims=True) + NORM_EPS) * gain


def rotate(values, places, sign):
    half = values.shape[-1] // 2
    steps = jnp.arange(half, dtype=jnp.float32)
    frequency = ROPE_BASE ** (-2.0 * steps / values.shape[-1])
    angles = places.astype(jnp.float32)[:, None] * frequency[None, :]
    cosine = jnp.cos(angles)[:, None, :]
    sine = sign * jnp.sin(angles)[:, None, :]
    first = values[..., :half]
    second = values[..., half:]
    return jnp.concatenate(
        [first * cosine - second * sine, second * cosine + first * sine], axis=-1
    )


def allowed_of(padding, count):
    valid = padding.reshape(count, SEQ) > 0
    index = jnp.arange(SEQ)
    causal = index[:, None] >= index[None, :]
    itself = index[:, None] == index[None, :]
    return (causal[None] & valid[:, None, :] | itself[None])[:, None]


def squares_of(items):
    total = jnp.zeros((), jnp.float32)
    for param_entry in items:
        total = total + jnp.sum(param_entry * param_entry)
    return total


def decoupled_update(value, gradient, first, second, rate):
    momentum = BETA_ONE * first + (1.0 - BETA_ONE) * gradient
    variance = BETA_TWO * second + (1.0 - BETA_TWO) * gradient * gradient
    corrected = momentum / (1.0 - BETA_ONE**STEP)
    spread = jnp.sqrt(variance / (1.0 - BETA_TWO**STEP))
    return (value - rate * (corrected / (spread + ADAM_EPS) + DECAY * value), momentum, variance)


def swap(partial):
    low = partial.astype(jnp.bfloat16)
    size = lax.axis_size("tensor")
    total = low.astype(jnp.float32)
    for step in range(1, size):
        other = lax.ppermute(low, "tensor", [(i, (i + step) % size) for i in range(size)])
        total = total + other.astype(jnp.float32)
    return total


def matmul(left, right):
    return jnp.dot(left, right, preferred_element_type=jnp.float32)


def matmul_nt(left, right):
    return jnp.einsum("ik,jk->ij", left, right, preferred_element_type=jnp.float32)


def matmul_tn(left, right):
    return jnp.einsum("ki,kj->ij", left, right, preferred_element_type=jnp.float32)


def low(values):
    return values.astype(jnp.bfloat16)


MESH = pl.DeviceIdType.MESH
LANES = 1024
CHUNK = 256


def partners_of(size):
    me = lax.axis_index("dp")
    found = []
    bit = 1
    while bit < size:
        down = lax.rem(lax.div(me, bit), 2)
        found.append(me + bit - 2 * bit * down)
        bit *= 2
    return found


def double_sum(total, inbox, sends, receives, size, sides, shared_rows):
    targets = [({"dp": p}, total.shape[0]) for p in partners_of(size)]
    side = lax.axis_index("tensor")
    targets += [
        ({"tensor": lax.rem(side + step, sides)}, shared_rows) for step in range(1, sides)
    ]
    for step, (target, count) in enumerate(targets):
        kept = pl.ds(0, count)
        copy = pltpu.make_async_remote_copy(
            src_ref=total,
            dst_ref=inbox.at[step],
            send_sem=sends.at[step],
            recv_sem=receives.at[step],
            device_id=target,
            device_id_type=MESH,
        )
        copy.start()
        copy.wait()
        total[kept] += inbox[step, kept]


def greet_sum(size, sides):
    barrier = pltpu.get_barrier_semaphore()
    side = lax.axis_index("tensor")
    targets = [{"dp": p} for p in partners_of(size)]
    targets += [{"tensor": lax.rem(side + step, sides)} for step in range(1, sides)]
    for target in targets:
        pl.semaphore_signal(barrier, inc=1, device_id=target, device_id_type=MESH)
    pl.semaphore_wait(barrier, len(targets))


def merge_kernel(
    size,
    sides,
    query_ref,
    key_ref,
    value_ref,
    gate_ref,
    widen_ref,
    mixer_ref,
    funnel_ref,
    entry_ref,
    attend_ref,
    lift_ref,
    mixer_down_ref,
    funnel_down_ref,
    output_ref,
    magnitude_ref,
    attend_out,
    feed_out,
    squares_out,
    total,
    inbox,
    direction_cut,
    direction_wide,
    direction_mixer,
    direction_funnel,
    sends,
    receives,
):
    greet_sum(size, sides)
    rows = query_ref.shape[0]
    wide = gate_ref.shape[1]
    me = lax.axis_index("dp")
    total[...] = jnp.zeros_like(total)

    def direction(base, down, up):
        return base.astype(jnp.float32) + ADAPTER_SCALE * jnp.dot(
            down, up, precision=HIGH_PRECISION, preferred_element_type=jnp.float32
        )

    group = LANES // rows
    lane_group = lax.broadcasted_iota(jnp.int32, (1, LANES), 1) // rows
    for i, (base, down) in enumerate(
        ((mixer_ref, mixer_down_ref), (funnel_ref, funnel_down_ref))
    ):
        held = (direction_mixer, direction_funnel)[i]
        sums = jnp.zeros((1, rows), jnp.float32)
        for start in range(0, base.shape[0], CHUNK):
            piece = pl.ds(start, CHUNK)
            part = direction(base[piece], down[piece], output_ref[i])
            held[piece] = part
            sums += jnp.sum(part * part, axis=0, keepdims=True)
        spread = jnp.concatenate([sums] * group, axis=1)
        for r in range(2):
            here = lane_group == me - r * group
            total[2 * i + r : 2 * i + r + 1, :] = jnp.where(here, spread, 0.0)
    for i, base in enumerate((query_ref, key_ref, value_ref)):
        for start in range(0, LANES, CHUNK):
            piece = pl.ds(start, CHUNK)
            part = direction(base[:, piece], entry_ref[i], attend_ref[i, :, piece])
            direction_cut[i, :, piece] = part
            total[4 + i : 5 + i, piece] = jnp.sum(part * part, axis=0, keepdims=True)
    for i, base in enumerate((gate_ref, widen_ref)):
        for start in range(0, wide, CHUNK):
            piece = pl.ds(start, CHUNK)
            part = direction(base[:, piece], entry_ref[3 + i], lift_ref[i, :, piece])
            direction_wide[i, :, piece] = part
            row = 7 + 3 * i + start // LANES
            total[row : row + 1, pl.ds(start % LANES, CHUNK)] = jnp.sum(
                part * part, axis=0, keepdims=True
            )
    double_sum(total, inbox, sends, receives, size, sides, 4)
    squares_out[...] = total[...]
    ratio = magnitude_ref[...] / jnp.sqrt(total[...] + COLUMN_EPS)
    for i in range(3):
        attend_out[i] = (direction_cut[i] * ratio[4 + i : 5 + i]).astype(jnp.bfloat16)
    for i in range(2):
        for start in range(0, wide, CHUNK):
            row = 7 + 3 * i + start // LANES
            feed_out[i, :, pl.ds(start, CHUNK)] = (
                direction_wide[i, :, pl.ds(start, CHUNK)]
                * ratio[row : row + 1, start % LANES : start % LANES + CHUNK]
            ).astype(jnp.bfloat16)
    for i, held in enumerate((direction_mixer, direction_funnel)):
        own = jnp.zeros((1, rows), jnp.float32)
        for r in range(2):
            for g in range(group):
                own += jnp.where(
                    me == r * group + g,
                    ratio[2 * i + r : 2 * i + r + 1, g * rows : (g + 1) * rows],
                    0.0,
                )
        for start in range(0, held.shape[0], CHUNK):
            part = (held[pl.ds(start, CHUNK)] * own).T.astype(jnp.bfloat16)
            if i == 0:
                attend_out[3, :, pl.ds(start, CHUNK)] = part
            else:
                feed_out[2, :, pl.ds(start, CHUNK)] = part


def merge(bases, entry_rows, attend, widen, mixer_down, funnel_down, output_columns, magnitudes):
    size = lax.axis_size("dp")
    sides = lax.axis_size("tensor")
    rows, cut = bases[0].shape
    wide = bases[3].shape[1]
    steps = len(bin(size)) - 3 + sides - 1
    lines = magnitudes.shape[0]
    return pl.pallas_call(
        functools.partial(merge_kernel, size, sides),
        name="merge",
        out_shape=(
            jax.ShapeDtypeStruct((4, rows, cut), jnp.bfloat16),
            jax.ShapeDtypeStruct((3, rows, wide), jnp.bfloat16),
            jax.ShapeDtypeStruct((lines, LANES), jnp.float32),
        ),
        in_specs=[pl.BlockSpec(memory_space=pltpu.VMEM)] * 14,
        out_specs=[pl.BlockSpec(memory_space=pltpu.VMEM)] * 3,
        scratch_shapes=[
            pltpu.VMEM((lines, LANES), jnp.float32),
            pltpu.VMEM((steps, lines, LANES), jnp.float32),
            pltpu.VMEM((3, rows, cut), jnp.float32),
            pltpu.VMEM((2, rows, wide), jnp.float32),
            pltpu.VMEM((cut, rows), jnp.float32),
            pltpu.VMEM((wide, rows), jnp.float32),
            pltpu.SemaphoreType.DMA((steps,)),
            pltpu.SemaphoreType.DMA((steps,)),
        ],
        compiler_params=pltpu.CompilerParams(
            collective_id=0, has_side_effects=True, vmem_limit_bytes=48 * 1024 * 1024
        ),
    )(*bases, entry_rows, attend, widen, mixer_down, funnel_down, output_columns, magnitudes)


def body(
    activations,
    cotangent,
    padding_mask,
    positions,
    norm_gains,
    base_query,
    base_key,
    base_value,
    base_gate,
    base_widen,
    base_mixer,
    base_funnel,
    entry_value,
    attend_value,
    widen_value,
    mixer_value,
    funnel_value,
    output_value,
    stature_value,
    amplitude_value,
    loudness_value,
    entry_first,
    attend_first,
    widen_first,
    mixer_first,
    funnel_first,
    output_first,
    stature_first,
    amplitude_first,
    loudness_first,
    entry_second,
    attend_second,
    widen_second,
    mixer_second,
    funnel_second,
    output_second,
    stature_second,
    amplitude_second,
    loudness_second,
):
    params = (
        entry_value,
        attend_value,
        widen_value,
        mixer_value,
        funnel_value,
        output_value,
        stature_value,
        amplitude_value,
        loudness_value,
    )
    firsts = (
        entry_first,
        attend_first,
        widen_first,
        mixer_first,
        funnel_first,
        output_first,
        stature_first,
        amplitude_first,
        loudness_first,
    )
    seconds = (
        entry_second,
        attend_second,
        widen_second,
        mixer_second,
        funnel_second,
        output_second,
        stature_second,
        amplitude_second,
        loudness_second,
    )
    rows = base_query.shape[0]
    width = activations.shape[1]
    place = lax.axis_index("dp") * rows
    cut = base_query.shape[1]
    wide = base_gate.shape[1]
    entry_rows = lax.dynamic_slice_in_dim(entry_value, place, rows, 1)
    output_columns = lax.dynamic_slice_in_dim(output_value, place, rows, 2)
    lifts = [attend_value[0], attend_value[1], attend_value[2], widen_value[0], widen_value[1]]
    pad = -wide % LANES
    magnitudes = jnp.concatenate(
        [
            loudness_value.reshape(-1, LANES),
            stature_value.reshape(-1, LANES),
            jnp.pad(amplitude_value, ((0, 0), (0, pad)), constant_values=1.0).reshape(-1, LANES),
        ]
    )
    magnitudes = jnp.pad(magnitudes, ((0, -magnitudes.shape[0] % 8), (0, 0)), constant_values=1.0)
    attend_shard, feed_shard, squares = merge(
        (base_query, base_key, base_value, base_gate, base_widen, base_mixer, base_funnel),
        entry_rows,
        attend_value,
        widen_value,
        mixer_value,
        funnel_value,
        output_columns,
        magnitudes,
    )
    lines = (wide + pad) // LANES
    shared_norms = jnp.sqrt(squares[:4].reshape(2, width) + COLUMN_EPS)
    split_norms = jnp.sqrt(
        jnp.concatenate(
            [squares[4:7].reshape(-1)]
            + [
                squares[7 + i * lines : 7 + (i + 1) * lines].reshape(-1)[:wide]
                for i in range(2)
            ]
        )
        + COLUMN_EPS
    )
    split_wide = split_norms.shape[0]
    split_magnitudes = jnp.concatenate([stature_value.reshape(-1), amplitude_value.reshape(-1)])
    split_ratio = split_magnitudes / split_norms
    shared_ratio = loudness_value / shared_norms
    attend_all = lax.all_gather(attend_shard, "dp", axis=1, tiled=True)
    feed_all = lax.all_gather(feed_shard, "dp", axis=1, tiled=True)
    merged_attend = jnp.concatenate([attend_all[0], attend_all[1], attend_all[2]], axis=1)
    merged_mixer = attend_all[3]
    merged_gate, merged_widen, merged_funnel = feed_all

    count = activations.shape[0] // SEQ
    heads = cut // HEAD_DIM
    scale = HEAD_DIM ** (-0.5)
    floats = activations.astype(jnp.float32)
    normed_one = low(root_norm(floats, norm_gains[0]))
    projected = matmul(normed_one, merged_attend)
    queries = projected[:, :cut]
    keys = projected[:, cut : 2 * cut]
    values = projected[:, 2 * cut :]
    values_low = low(values).reshape(count, SEQ, heads, HEAD_DIM)
    turned_queries = low(rotate(queries.reshape(-1, heads, HEAD_DIM), positions, 1.0))
    turned_queries = turned_queries.reshape(count, SEQ, heads, HEAD_DIM)
    turned_keys = low(rotate(keys.reshape(-1, heads, HEAD_DIM), positions, 1.0))
    turned_keys = turned_keys.reshape(count, SEQ, heads, HEAD_DIM)
    allowed = allowed_of(padding_mask, count)
    scores = (
        jnp.einsum(
            "bqhd,bkhd->bhqk", turned_queries, turned_keys, preferred_element_type=jnp.float32
        )
        * scale
    )
    masked = jnp.where(allowed, scores, MASKED)
    top = jnp.max(masked, axis=-1, keepdims=True)
    log_total = top + jnp.log(jnp.sum(jnp.exp(masked - top), axis=-1, keepdims=True))
    attention = jnp.exp(masked - log_total)
    attention_low = low(attention)
    mixed = jnp.einsum(
        "bhqk,bkhd->bqhd", attention_low, values_low, preferred_element_type=jnp.float32
    )
    mixed = low(mixed.reshape(activations.shape[0], cut))
    attended = swap(matmul_nt(mixed, merged_mixer))
    residual = floats + attended
    normed_two = low(root_norm(residual, norm_gains[1]))
    gate = matmul(normed_two, merged_gate)
    lifted = matmul(normed_two, merged_widen)
    hidden = low(jax.nn.silu(gate) * lifted)
    funneled = swap(matmul_nt(hidden, merged_funnel))
    block_output = low(residual + funneled)

    back = cotangent.astype(jnp.float32)
    d_hidden = matmul(cotangent, merged_funnel)
    unused, silu_pull = jax.vjp(lambda g, u: jax.nn.silu(g) * u, gate, lifted)
    d_gate, d_lifted = silu_pull(d_hidden)
    d_gate = low(d_gate)
    d_lifted = low(d_lifted)
    d_normed_two = swap(matmul_nt(d_gate, merged_gate) + matmul_nt(d_lifted, merged_widen))
    unused, second_pull = jax.vjp(lambda v: root_norm(v, norm_gains[1]), residual)
    d_residual = back + second_pull(d_normed_two)[0]
    d_residual_low = low(d_residual)
    d_mixed = low(matmul(d_residual_low, merged_mixer)).reshape(count, SEQ, heads, HEAD_DIM)
    d_attention = jnp.einsum(
        "bqhd,bkhd->bhqk", d_mixed, values_low, preferred_element_type=jnp.float32
    )
    d_values = jnp.einsum(
        "bhqk,bqhd->bkhd", attention_low, d_mixed, preferred_element_type=jnp.float32
    )
    d_values = low(d_values).reshape(-1, cut)
    d_scores = attention * (d_attention - jnp.sum(attention * d_attention, axis=-1, keepdims=True))
    d_scores = low(d_scores)
    d_turned_queries = (
        jnp.einsum("bhqk,bkhd->bqhd", d_scores, turned_keys, preferred_element_type=jnp.float32)
        * scale
    )
    d_turned_keys = (
        jnp.einsum("bhqk,bqhd->bkhd", d_scores, turned_queries, preferred_element_type=jnp.float32)
        * scale
    )
    d_queries = low(rotate(d_turned_queries.reshape(-1, heads, HEAD_DIM), positions, -1.0))
    d_keys = low(rotate(d_turned_keys.reshape(-1, heads, HEAD_DIM), positions, -1.0))
    d_queries = d_queries.reshape(-1, cut)
    d_keys = d_keys.reshape(-1, cut)
    d_projected = jnp.concatenate([d_queries, d_keys, d_values], axis=1)
    d_normed_one = swap(matmul_nt(d_projected, merged_attend))
    unused, first_pull = jax.vjp(lambda v: root_norm(v, norm_gains[0]), floats)
    input_gradient = d_residual + first_pull(d_normed_one)[0]

    d_parts = (d_queries, d_keys, d_values, d_gate, d_lifted)
    parts = (queries, keys, values, gate, lifted)
    split_dots = jnp.concatenate(
        [jnp.sum(d.astype(jnp.float32) * y, axis=0) for d, y in zip(d_parts, parts)]
    )
    shared_dots = jnp.stack(
        [
            jnp.sum(d_residual_low.astype(jnp.float32) * attended, axis=0),
            jnp.sum(back * funneled, axis=0),
        ]
    )
    split_pull = split_dots / (split_norms * split_magnitudes)
    shared_pull = shared_dots / (shared_norms * loudness_value)

    down_gradients = []
    up_gradients = []
    inputs = (normed_one, normed_one, normed_one, normed_two, normed_two)
    weights = (
        attend_all[0],
        attend_all[1],
        attend_all[2],
        merged_gate,
        merged_widen,
    )
    offset = 0
    for i in range(5):
        out = weights[i].shape[1]
        ratio = split_ratio[offset : offset + out]
        pull = split_pull[offset : offset + out]
        offset += out
        low_lift = low(lifts[i] * ratio)
        pull_lift = low(lifts[i] * pull)
        lowered = low(matmul_nt(low_lift, d_parts[i]))
        down_gradients.append(
            ADAPTER_SCALE * (matmul(lowered, inputs[i]) - matmul_nt(pull_lift, weights[i]))
        )
        low_down = low(entry_value[i])
        reduced = low(matmul(inputs[i], low_down))
        up_gradients.append(
            ADAPTER_SCALE
            * (matmul_tn(reduced, d_parts[i]) * ratio - matmul_tn(low_down, weights[i]) * pull)
        )
    out_downs = []
    out_ups = []
    plan = (
        (mixed, d_residual_low, mixer_value, merged_mixer),
        (hidden, cotangent, funnel_value, merged_funnel),
    )
    for i, (source, d_out, down, weight) in enumerate(plan):
        low_lift = low(output_value[i] * shared_ratio[i])
        pull_lift = low(output_value[i] * shared_pull[i])
        lowered = low(matmul_nt(low_lift, d_out))
        out_downs.append(ADAPTER_SCALE * (matmul(lowered, source) - matmul(pull_lift, weight)))
        low_down = low(down)
        reduced = low(matmul(source, low_down))
        out_ups.append(
            ADAPTER_SCALE
            * (
                matmul_tn(reduced, d_out) * shared_ratio[i]
                - jnp.einsum("ir,ji->rj", low_down, weight, preferred_element_type=jnp.float32)
                * shared_pull[i]
            )
        )
    shared_terms = jnp.concatenate(down_gradients + out_ups, axis=1)
    split_terms = jnp.concatenate(up_gradients + out_downs, axis=1)
    shared_terms, split_terms, split_dots, shared_dots = lax.psum(
        (shared_terms, split_terms, split_dots, shared_dots), "dp"
    )
    split_scale = split_dots / split_magnitudes
    shared_scale = shared_dots / loudness_value
    split_total = jnp.sum(split_terms * split_terms) + jnp.sum(split_scale * split_scale)
    shared_terms, split_total = lax.psum((shared_terms, split_total), "tensor")
    totals = (
        jnp.stack([shared_terms[:, i * width : (i + 1) * width].T for i in range(5)]),
        jnp.stack([split_terms[:, i * cut : (i + 1) * cut] for i in range(3)]),
        jnp.stack([split_terms[:, 3 * cut + i * wide : 3 * cut + (i + 1) * wide] for i in range(2)]),
        split_terms[:, split_wide : split_wide + cut].T,
        split_terms[:, split_wide + cut :].T,
        jnp.stack([shared_terms[:, (5 + i) * width : (6 + i) * width] for i in range(2)]),
        split_scale[: 3 * cut].reshape(3, cut),
        split_scale[3 * cut :].reshape(2, wide),
        shared_scale,
    )
    gradient_norm = jnp.sqrt(split_total + squares_of((totals[0], totals[5], totals[8])))
    down_factor = jnp.minimum(1.0, CLIP / (gradient_norm + 1e-06))
    rates = (
        RATE_FACTOR,
        RATE_LIFT,
        RATE_LIFT,
        RATE_FACTOR,
        RATE_FACTOR,
        RATE_LIFT,
        RATE_SCALE,
        RATE_SCALE,
        RATE_LOUD,
    )
    updated = []
    momenta = []
    variances = []
    for value, gradient, first, second, rate in zip(params, totals, firsts, seconds, rates):
        fresh, momentum, variance = decoupled_update(
            value, gradient * down_factor, first, second, rate
        )
        updated.append(fresh)
        momenta.append(momentum)
        variances.append(variance)
    return (
        block_output,
        input_gradient,
        gradient_norm,
        updated[0],
        updated[1],
        updated[2],
        updated[3],
        updated[4],
        updated[5],
        updated[6],
        updated[7],
        updated[8],
        momenta[0],
        momenta[1],
        momenta[2],
        momenta[3],
        momenta[4],
        momenta[5],
        momenta[6],
        momenta[7],
        momenta[8],
        variances[0],
        variances[1],
        variances[2],
        variances[3],
        variances[4],
        variances[5],
        variances[6],
        variances[7],
        variances[8],
    )


def solution(mesh):
    return jax.shard_map(
        body,
        mesh=mesh,
        in_specs=(
            P("dp", None),
            P("dp", None),
            P("dp"),
            P("dp"),
            P(),
            P("dp", "tensor"),
            P("dp", "tensor"),
            P("dp", "tensor"),
            P("dp", "tensor"),
            P("dp", "tensor"),
            P("tensor", "dp"),
            P("tensor", "dp"),
            P(),
            P(None, None, "tensor"),
            P(None, None, "tensor"),
            P("tensor", None),
            P("tensor", None),
            P(),
            P(None, "tensor"),
            P(None, "tensor"),
            P(),
            P(),
            P(None, None, "tensor"),
            P(None, None, "tensor"),
            P("tensor", None),
            P("tensor", None),
            P(),
            P(None, "tensor"),
            P(None, "tensor"),
            P(),
            P(),
            P(None, None, "tensor"),
            P(None, None, "tensor"),
            P("tensor", None),
            P("tensor", None),
            P(),
            P(None, "tensor"),
            P(None, "tensor"),
            P(),
        ),
        out_specs=(
            P("dp", None),
            P("dp", None),
            P(),
            P(),
            P(None, None, "tensor"),
            P(None, None, "tensor"),
            P("tensor", None),
            P("tensor", None),
            P(),
            P(None, "tensor"),
            P(None, "tensor"),
            P(),
            P(),
            P(None, None, "tensor"),
            P(None, None, "tensor"),
            P("tensor", None),
            P("tensor", None),
            P(),
            P(None, "tensor"),
            P(None, "tensor"),
            P(),
            P(),
            P(None, None, "tensor"),
            P(None, None, "tensor"),
            P("tensor", None),
            P("tensor", None),
            P(),
            P(None, "tensor"),
            P(None, "tensor"),
            P(),
        ),
        check_vma=False,
    )
```

```python
import functools

import jax
import jax.numpy as jnp
from jax import lax
from jax.experimental import pallas as pl
from jax.experimental.pallas import tpu as pltpu
from jax.sharding import PartitionSpec as P

HEAD_DIM = 128
RANK = 16
SEQ = 256
STEP = 5


HIGH_PRECISION = lax.Precision.HIGHEST
ADAPTER_SCALE = 2.0
NORM_EPS = 1e-05
COLUMN_EPS = 1e-06
BETA_ONE = 0.9
BETA_TWO = 0.999
ADAM_EPS = 1e-08
DECAY = 0.01
CLIP = 1.0
RATE_FACTOR = 0.02
RATE_LIFT = 0.2
RATE_SCALE = 0.5
RATE_LOUD = 2.0
ROPE_BASE = 10000.0
MASKED = -1e30


def root_norm(values, gain):
    return values * lax.rsqrt(jnp.mean(values * values, axis=-1, keepdims=True) + NORM_EPS) * gain


def rotate(values, places, sign):
    half = values.shape[-1] // 2
    steps = jnp.arange(half, dtype=jnp.float32)
    frequency = ROPE_BASE ** (-2.0 * steps / values.shape[-1])
    angles = places.astype(jnp.float32)[:, None] * frequency[None, :]
    cosine = jnp.cos(angles)[:, None, :]
    sine = sign * jnp.sin(angles)[:, None, :]
    first = values[..., :half]
    second = values[..., half:]
    return jnp.concatenate(
        [first * cosine - second * sine, second * cosine + first * sine], axis=-1
    )


def allowed_of(padding, count):
    valid = padding.reshape(count, SEQ) > 0
    index = jnp.arange(SEQ)
    causal = index[:, None] >= index[None, :]
    itself = index[:, None] == index[None, :]
    return (causal[None] & valid[:, None, :] | itself[None])[:, None]


def squares_of(items):
    total = jnp.zeros((), jnp.float32)
    for param_entry in items:
        total = total + jnp.sum(param_entry * param_entry)
    return total


def decoupled_update(value, gradient, first, second, rate):
    momentum = BETA_ONE * first + (1.0 - BETA_ONE) * gradient
    variance = BETA_TWO * second + (1.0 - BETA_TWO) * gradient * gradient
    corrected = momentum / (1.0 - BETA_ONE**STEP)
    spread = jnp.sqrt(variance / (1.0 - BETA_TWO**STEP))
    return (value - rate * (corrected / (spread + ADAM_EPS) + DECAY * value), momentum, variance)


def swap(partial):
    low = partial.astype(jnp.bfloat16)
    size = lax.axis_size("tensor")
    total = low.astype(jnp.float32)
    for step in range(1, size):
        other = lax.ppermute(low, "tensor", [(i, (i + step) % size) for i in range(size)])
        total = total + other.astype(jnp.float32)
    return total


def matmul(left, right):
    return jnp.dot(left, right, preferred_element_type=jnp.float32)


def matmul_nt(left, right):
    return jnp.einsum("ik,jk->ij", left, right, preferred_element_type=jnp.float32)


def matmul_tn(left, right):
    return jnp.einsum("ki,kj->ij", left, right, preferred_element_type=jnp.float32)


def low(values):
    return values.astype(jnp.bfloat16)


MESH = pl.DeviceIdType.MESH
LANES = 1024
CHUNK = 256


def partners_of(size):
    me = lax.axis_index("dp")
    found = []
    bit = 1
    while bit < size:
        down = lax.rem(lax.div(me, bit), 2)
        found.append(me + bit - 2 * bit * down)
        bit *= 2
    return found


def double_sum(total, inbox, sends, receives, size, sides, shared_rows):
    targets = [({"dp": p}, total.shape[0]) for p in partners_of(size)]
    side = lax.axis_index("tensor")
    targets += [
        ({"tensor": lax.rem(side + step, sides)}, shared_rows) for step in range(1, sides)
    ]
    for step, (target, count) in enumerate(targets):
        kept = pl.ds(0, count)
        copy = pltpu.make_async_remote_copy(
            src_ref=total,
            dst_ref=inbox.at[step],
            send_sem=sends.at[step],
            recv_sem=receives.at[step],
            device_id=target,
            device_id_type=MESH,
        )
        copy.start()
        copy.wait()
        total[kept] += inbox[step, kept]


def greet_sum(size, sides):
    barrier = pltpu.get_barrier_semaphore()
    side = lax.axis_index("tensor")
    targets = [{"dp": p} for p in partners_of(size)]
    targets += [{"tensor": lax.rem(side + step, sides)} for step in range(1, sides)]
    for target in targets:
        pl.semaphore_signal(barrier, inc=1, device_id=target, device_id_type=MESH)
    pl.semaphore_wait(barrier, len(targets))


def merge_kernel(
    size,
    sides,
    query_ref,
    key_ref,
    value_ref,
    gate_ref,
    widen_ref,
    mixer_ref,
    funnel_ref,
    entry_ref,
    attend_ref,
    lift_ref,
    mixer_down_ref,
    funnel_down_ref,
    output_ref,
    magnitude_ref,
    shard_out,
    squares_out,
    total,
    inbox,
    direction_cut,
    direction_wide,
    direction_mixer,
    direction_funnel,
    sends,
    receives,
):
    greet_sum(size, sides)
    rows = query_ref.shape[0]
    wide = gate_ref.shape[1]
    me = lax.axis_index("dp")
    total[...] = jnp.zeros_like(total)

    def direction(base, down, up):
        return base.astype(jnp.float32) + ADAPTER_SCALE * jnp.dot(
            down, up, precision=HIGH_PRECISION, preferred_element_type=jnp.float32
        )

    group = LANES // rows
    lane_group = lax.broadcasted_iota(jnp.int32, (1, LANES), 1) // rows
    for i, (base, down) in enumerate(
        ((mixer_ref, mixer_down_ref), (funnel_ref, funnel_down_ref))
    ):
        held = (direction_mixer, direction_funnel)[i]
        sums = jnp.zeros((1, rows), jnp.float32)
        for start in range(0, base.shape[0], CHUNK):
            piece = pl.ds(start, CHUNK)
            part = direction(base[piece], down[piece], output_ref[i])
            held[piece] = part
            sums += jnp.sum(part * part, axis=0, keepdims=True)
        spread = jnp.concatenate([sums] * group, axis=1)
        for r in range(2):
            here = lane_group == me - r * group
            total[2 * i + r : 2 * i + r + 1, :] = jnp.where(here, spread, 0.0)
    for i, base in enumerate((query_ref, key_ref, value_ref)):
        for start in range(0, LANES, CHUNK):
            piece = pl.ds(start, CHUNK)
            part = direction(base[:, piece], entry_ref[i], attend_ref[i, :, piece])
            direction_cut[i, :, piece] = part
            total[4 + i : 5 + i, piece] = jnp.sum(part * part, axis=0, keepdims=True)
    for i, base in enumerate((gate_ref, widen_ref)):
        for start in range(0, wide, CHUNK):
            piece = pl.ds(start, CHUNK)
            part = direction(base[:, piece], entry_ref[3 + i], lift_ref[i, :, piece])
            direction_wide[i, :, piece] = part
            row = 7 + 3 * i + start // LANES
            total[row : row + 1, pl.ds(start % LANES, CHUNK)] = jnp.sum(
                part * part, axis=0, keepdims=True
            )
    double_sum(total, inbox, sends, receives, size, sides, 4)
    squares_out[...] = total[...]
    ratio = magnitude_ref[...] / jnp.sqrt(total[...] + COLUMN_EPS)
    near = LANES // CHUNK
    for i in range(3):
        for b in range(near):
            lanes = slice(b * CHUNK, (b + 1) * CHUNK)
            shard_out[near * i + b] = (
                direction_cut[i, :, lanes] * ratio[4 + i : 5 + i, lanes]
            ).astype(jnp.bfloat16)
    for i in range(2):
        for start in range(0, wide, CHUNK):
            row = 7 + 3 * i + start // LANES
            shard_out[4 * near + 3 * (start // CHUNK) + i] = (
                direction_wide[i, :, pl.ds(start, CHUNK)]
                * ratio[row : row + 1, start % LANES : start % LANES + CHUNK]
            ).astype(jnp.bfloat16)
    for i, held in enumerate((direction_mixer, direction_funnel)):
        own = jnp.zeros((1, rows), jnp.float32)
        for r in range(2):
            for g in range(group):
                own += jnp.where(
                    me == r * group + g,
                    ratio[2 * i + r : 2 * i + r + 1, g * rows : (g + 1) * rows],
                    0.0,
                )
        for start in range(0, held.shape[0], CHUNK):
            part = (held[pl.ds(start, CHUNK)] * own).T.astype(jnp.bfloat16)
            if i == 0:
                shard_out[3 * near + start // CHUNK] = part
            else:
                shard_out[4 * near + 3 * (start // CHUNK) + 2] = part


def merge(bases, entry_rows, attend, widen, mixer_down, funnel_down, output_columns, magnitudes):
    size = lax.axis_size("dp")
    sides = lax.axis_size("tensor")
    rows, cut = bases[0].shape
    wide = bases[3].shape[1]
    steps = len(bin(size)) - 3 + sides - 1
    lines = magnitudes.shape[0]
    return pl.pallas_call(
        functools.partial(merge_kernel, size, sides),
        name="merge",
        out_shape=(
            jax.ShapeDtypeStruct(((4 * cut + 3 * wide) // CHUNK, rows, CHUNK), jnp.bfloat16),
            jax.ShapeDtypeStruct((lines, LANES), jnp.float32),
        ),
        in_specs=[pl.BlockSpec(memory_space=pltpu.VMEM)] * 14,
        out_specs=[pl.BlockSpec(memory_space=pltpu.VMEM)] * 2,
        scratch_shapes=[
            pltpu.VMEM((lines, LANES), jnp.float32),
            pltpu.VMEM((steps, lines, LANES), jnp.float32),
            pltpu.VMEM((3, rows, cut), jnp.float32),
            pltpu.VMEM((2, rows, wide), jnp.float32),
            pltpu.VMEM((cut, rows), jnp.float32),
            pltpu.VMEM((wide, rows), jnp.float32),
            pltpu.SemaphoreType.DMA((steps,)),
            pltpu.SemaphoreType.DMA((steps,)),
        ],
        compiler_params=pltpu.CompilerParams(
            collective_id=0, has_side_effects=True, vmem_limit_bytes=48 * 1024 * 1024
        ),
    )(*bases, entry_rows, attend, widen, mixer_down, funnel_down, output_columns, magnitudes)


def dot_nn(left, right):
    return jnp.dot(left, right, preferred_element_type=jnp.float32)


def dot_nt(left, right):
    return lax.dot_general(
        left, right, (((1,), (1,)), ((), ())), preferred_element_type=jnp.float32
    )


BLOCKS = 3
HEAD_CHUNKS = 5
EXTRA_TICKS = 3


def gather_parts(size, shard, full, sems):
    line = size // 4
    early = 16
    late = shard.shape[1] - early
    me = lax.axis_index("dp")
    core, column, spot = lax.rem(me, 2), lax.rem(lax.div(me, 2), 2), lax.div(me, 4)
    right_sends, left_sends, right_gets, left_gets, pair_sems, core_sems, early_sems = sems

    def device(other_spot, other_column, other_core):
        return {"dp": (other_spot * 2 + other_column) * 2 + other_core}

    right = device(lax.rem(spot + 1, line), column, core)
    left = device(lax.rem(spot + line - 1, line), column, core)
    across = device(spot, 1 - column, core)
    twin = device(spot, column, 1 - core)

    def greet():
        barrier = pltpu.get_barrier_semaphore()
        ahead, behind = spot < line - 1, spot > 0

        @pl.when(ahead)
        def _():
            pl.semaphore_signal(barrier, inc=1, device_id=right, device_id_type=MESH)

        @pl.when(behind)
        def _():
            pl.semaphore_signal(barrier, inc=1, device_id=left, device_id_type=MESH)

        for target in (across, twin, {"tensor": 1 - lax.axis_index("tensor")}):
            pl.semaphore_signal(barrier, inc=1, device_id=target, device_id_type=MESH)
        peers = 3 + ahead.astype(jnp.int32) + behind.astype(jnp.int32)
        pl.semaphore_wait(barrier, peers)

    def remote(source, target, send, get, where):
        return pltpu.make_async_remote_copy(
            src_ref=source,
            dst_ref=target,
            send_sem=send,
            recv_sem=get,
            device_id=where,
            device_id_type=MESH,
        )

    def early_copy(part, owner):
        first = 1 + BLOCKS
        blocks = pl.ds(0, first) if part == 0 else pl.ds(first, shard.shape[0] - first)
        return remote(
            shard.at[blocks, pl.ds(0, early)],
            full.at[blocks, spot, owner, core, pl.ds(0, early)],
            early_sems.at[part, 0],
            early_sems.at[part, 1],
            across,
        )

    def early_start():
        for part in range(2):
            early_copy(part, column).start()

    def early_wait(part):
        early_copy(part, 1 - column).wait_recv()
        early_copy(part, column).wait_send()

    def place_of(part, origin, blocks):
        if part == 0:
            return full.at[blocks, origin, column, core, pl.ds(early, late)]
        return full.at[blocks, origin, :, core, pl.ds(0, early)]

    def moves(to_right, hop, chunk, start, count):
        sends, gets = (right_sends, right_gets) if to_right else (left_sends, left_gets)
        blocks = pl.ds(start, count)
        found = []
        for part in range(2):
            place = place_of(part, spot - hop if to_right else spot + hop, blocks)
            source = shard.at[blocks, pl.ds(early, late)] if hop == 0 and part == 0 else place
            found.append(
                remote(
                    source,
                    place,
                    sends.at[chunk, 2 * hop + part],
                    gets.at[chunk, 2 * hop + part],
                    right if to_right else left,
                )
            )
        return found

    def arrivals(to_right, hop, chunk, start, count):
        gets = right_gets if to_right else left_gets
        for part in range(2):
            place = place_of(part, spot - hop if to_right else spot + hop, pl.ds(start, count))
            kept = 2 * (hop - 1) + part
            remote(
                place, place, right_sends.at[chunk, kept], gets.at[chunk, kept], right
            ).wait_recv()

    def pair_copy(chunk, start, count, owner):
        place = full.at[pl.ds(start, count), :, owner, core, pl.ds(early, late)]
        return remote(place, place, pair_sems.at[chunk, 0], pair_sems.at[chunk, 1], across)

    def core_copy(chunk, start, count, owner):
        place = full.at[pl.ds(start, count), :, :, owner]
        return remote(place, place, core_sems.at[chunk, 0], core_sems.at[chunk, 1], twin)

    def send_on(hop, chunk, start, count):
        @pl.when((spot >= hop) & (spot < line - 1))
        def _():
            for copy in moves(True, hop, chunk, start, count):
                copy.start()

        @pl.when((spot < line - hop) & (spot > 0))
        def _():
            for copy in moves(False, hop, chunk, start, count):
                copy.start()

    def take_in(hop, chunk, start, count):
        @pl.when(spot >= hop)
        def _():
            arrivals(True, hop, chunk, start, count)

        @pl.when(spot < line - hop)
        def _():
            arrivals(False, hop, chunk, start, count)

    def step(phase, chunk, start, count):
        if 1 <= phase < line:
            take_in(phase, chunk, start, count)
        if phase < line - 1:
            send_on(phase, chunk, start, count)
        if phase == line - 1:
            pair_copy(chunk, start, count, column).start()
        elif phase == line + 1:
            pair_copy(chunk, start, count, 1 - column).wait_recv()
            core_copy(chunk, start, count, core).start()
        elif phase == line + 2:
            core_copy(chunk, start, count, 1 - core).wait_recv()
        elif phase == line + 3:
            finish(chunk, start, count)

    def finish(chunk, start, count):
        for hop in range(line - 1):

            @pl.when((spot >= hop) & (spot < line - 1))
            def _(hop=hop):
                for copy in moves(True, hop, chunk, start, count):
                    copy.wait_send()

            @pl.when((spot < line - hop) & (spot > 0))
            def _(hop=hop):
                for copy in moves(False, hop, chunk, start, count):
                    copy.wait_send()

        pair_copy(chunk, start, count, column).wait_send()
        core_copy(chunk, start, count, core).wait_send()

    return greet, step, early_start, early_wait, finish


def block_kernel(
    size,
    shard,
    normed_ref,
    rows_ref,
    back_ref,
    cosine_ref,
    sine_ref,
    keep_ref,
    gain_ref,
    entry_down_ref,
    funnel_down_ref,
    low_lift_ref,
    pull_lift_ref,
    ratio_ref,
    pull_ref,
    low_output_ref,
    full,
    turned_out,
    plain_out,
    mixed_out,
    residual_out,
    d_normed_out,
    funneled_out,
    up_out,
    down_out,
    funnel_down_out,
    funnel_up_out,
    funnel_seen_out,
    dots_out,
    normed,
    back,
    floats,
    turned,
    plain,
    mixed,
    heads_weight,
    feed_weight,
    residual,
    d_normed,
    funneled,
    outbox,
    inbox,
    lowered,
    reduced,
    funnel_lowered,
    funnel_reduced,
    right_sends,
    left_sends,
    right_gets,
    left_gets,
    pair_sems,
    core_sems,
    early_sems,
    local_sems,
    weight_sems,
    side_sends,
    side_gets,
    out_sems,
):
    line = size // 4
    total_blocks = full.shape[0]
    chunks = total_blocks // BLOCKS
    tokens, width = normed.shape[0] - 2 * RANK, normed.shape[1]
    count = tokens // SEQ
    sides = {"tensor": 1 - lax.axis_index("tensor")}
    sems = (right_sends, left_sends, right_gets, left_gets, pair_sems, core_sems, early_sems)
    greet, step, early_start, early_wait, finish = gather_parts(size, shard, full, sems)
    me = lax.axis_index("dp")
    core, column, spot = lax.rem(me, 2), lax.rem(lax.div(me, 2), 2), lax.div(me, 4)

    def tick(now):
        for phase in range(line + 4):
            chunk = now - phase
            start = 1 + BLOCKS * chunk
            if isinstance(now, int):
                if 0 <= chunk < chunks:
                    step(phase, chunk, start, BLOCKS)
            else:

                @pl.when((chunk >= 0) & (chunk < chunks))
                def _(phase=phase, chunk=chunk, start=start):
                    step(phase, chunk, start, BLOCKS)

    own = pltpu.make_async_copy(shard, full.at[:, spot, column, core], local_sems.at[0])
    own.start()
    loads = [
        pltpu.make_async_copy(normed_ref, normed.at[pl.ds(0, tokens)], local_sems.at[1]),
        pltpu.make_async_copy(back_ref, back, local_sems.at[2]),
        pltpu.make_async_copy(rows_ref, floats, local_sems.at[3]),
    ]
    for load in loads:
        load.start()
    greet()
    early_start()
    own.wait()
    early_wait(0)
    step(0, chunks, 0, 1)
    tick(0)
    early_wait(1)
    for now in range(1, line + 4):
        step(now, chunks, 0, 1)
        tick(now)
    ready = HEAD_CHUNKS - 2 + line + 2
    lax.fori_loop(line + 4, ready + 1, lambda now, carry: (tick(now), carry)[1], 0)
    for load in loads:
        load.wait()

    def head_load(block, slot):
        return pltpu.make_async_copy(
            full.at[block], heads_weight.at[slot], weight_sems.at[slot]
        )

    def head_weight(slot):
        return heads_weight[slot].reshape(width, CHUNK)

    cut_blocks = turned.shape[0] // 3
    head_load(0, 0).start()

    def project(block, carry):
        slot = lax.rem(block, 2)

        @pl.when(block < 3 * cut_blocks - 1)
        def _():
            head_load(block + 1, 1 - slot).start()

        head_load(block, slot).wait()
        for part in range(count):
            place = pl.ds(part * SEQ, SEQ)
            result = dot_nn(normed[place], head_weight(slot))
            plain[block, place] = result.astype(jnp.bfloat16)

            @pl.when(block < 2 * cut_blocks)
            def _(result=result, place=place):
                for half in range(CHUNK // HEAD_DIM):
                    lanes = slice(half * HEAD_DIM, (half + 1) * HEAD_DIM)
                    head = result[:, lanes]
                    turned[block, place, lanes] = (
                        head * cosine_ref[place]
                        + pltpu.roll(head, HEAD_DIM // 2, 1) * sine_ref[place]
                    ).astype(jnp.bfloat16)

            @pl.when(block >= 2 * cut_blocks)
            def _(result=result, place=place):
                turned[block, place] = result.astype(jnp.bfloat16)

        return carry

    lax.fori_loop(0, 3 * cut_blocks, project, 0)
    outs = [
        pltpu.make_async_copy(turned, turned_out, out_sems.at[0]),
        pltpu.make_async_copy(plain.at[pl.ds(0, 2 * cut_blocks)], plain_out, out_sems.at[1]),
    ]
    for out in outs:
        out.start()
    tick(ready + 1)

    mixer_loads = [
        pltpu.make_async_copy(
            full.at[3 * cut_blocks + b],
            feed_weight.at[:, :, :, :, pl.ds(b * CHUNK, CHUNK)],
            weight_sems.at[b],
        )
        for b in range(cut_blocks)
    ]
    for load in mixer_loads:
        load.start()
    line_up = lax.broadcasted_iota(jnp.int32, (SEQ, SEQ), 0)
    line_on = lax.broadcasted_iota(jnp.int32, (SEQ, SEQ), 1)

    def attend(block, carry):
        for part in range(count):
            place = pl.ds(part * SEQ, SEQ)
            allowed = ((line_up >= line_on) & (keep_ref[part] > 0)) | (line_up == line_on)
            for half in range(CHUNK // HEAD_DIM):
                lanes = slice(half * HEAD_DIM, (half + 1) * HEAD_DIM)
                scores = dot_nt(
                    turned[block, place, lanes], turned[cut_blocks + block, place, lanes]
                ) * (HEAD_DIM ** (-0.5))
                masked = jnp.where(allowed, scores, MASKED)
                top = jnp.max(masked, axis=1, keepdims=True)
                weight = jnp.exp(masked - top)
                attention = weight / jnp.sum(weight, axis=1, keepdims=True)
                mixed[block, place, lanes] = dot_nn(
                    attention.astype(jnp.bfloat16), turned[2 * cut_blocks + block, place, lanes]
                ).astype(jnp.bfloat16)
        return carry

    lax.fori_loop(0, cut_blocks, attend, 0)
    outs.append(pltpu.make_async_copy(mixed, mixed_out, out_sems.at[2]))
    outs[-1].start()
    tick(ready + 2)

    for load in mixer_loads:
        load.wait()

    def side_copy(part):
        place = pl.ds(part * SEQ, SEQ)
        return pltpu.make_async_remote_copy(
            src_ref=outbox.at[place],
            dst_ref=inbox.at[place],
            send_sem=side_sends.at[part],
            recv_sem=side_gets.at[part],
            device_id=sides,
            device_id_type=MESH,
        )

    for part in range(count):
        place = pl.ds(part * SEQ, SEQ)
        joined = jnp.concatenate([mixed[b, place] for b in range(cut_blocks)], axis=1)
        per = 512 // (4 * feed_weight.shape[3])
        for piece in range(width // 512):
            weight = feed_weight[pl.ds(piece * per, per), :, :, :, pl.ds(0, cut_blocks * CHUNK)]
            outbox[place, pl.ds(piece * 512, 512)] = dot_nt(
                joined, weight.reshape(512, cut_blocks * CHUNK)
            ).astype(jnp.bfloat16)
        side_copy(part).start()
    tick(ready + 3)

    tile = 32
    for part in range(count):
        side_copy(part).wait()

        def add_up(index, carry, part=part):
            place = pl.ds(pl.multiple_of(part * SEQ + index * tile, tile), tile)
            value = floats[place].astype(jnp.float32) + (
                outbox[place].astype(jnp.float32) + inbox[place].astype(jnp.float32)
            )
            residual[place] = value
            root = lax.rsqrt(jnp.mean(value * value, axis=1, keepdims=True) + NORM_EPS)
            normed[place] = (value * root * gain_ref[...]).astype(jnp.bfloat16)
            return carry

        lax.fori_loop(0, SEQ // tile, add_up, 0)
        if part == 0:
            tick(ready + 4)
    outs.append(pltpu.make_async_copy(residual, residual_out, out_sems.at[3]))
    outs[-1].start()
    normed[pl.ds(tokens, 2 * RANK)] = entry_down_ref[...]
    reduced[...] = dot_nt(entry_down_ref[...], normed[pl.ds(0, tokens)]).astype(jnp.bfloat16)
    funnel_lowered[...] = dot_nt(low_output_ref[...], back[...]).astype(jnp.bfloat16)
    d_normed[...] = jnp.zeros_like(d_normed)
    funneled[...] = jnp.zeros_like(funneled)
    lowered[...] = jnp.zeros_like(lowered)
    funnel_reduced[...] = jnp.zeros_like(funnel_reduced)

    def feed_load(index):
        return [
            pltpu.make_async_copy(
                full.at[4 * cut_blocks + BLOCKS * index + b],
                feed_weight.at[:, :, :, :, pl.ds(b * CHUNK, CHUNK)],
                weight_sems.at[b],
            )
            for b in range(BLOCKS)
        ]

    nothing = jnp.zeros((RANK, CHUNK), jnp.bfloat16)

    def feed(index, carry):
        @pl.when(index >= EXTRA_TICKS)
        def _():
            tick(index + HEAD_CHUNKS + line + 2)

        for load in feed_load(index):
            load.start()
        for load in feed_load(index):
            load.wait()
        columns = pl.ds(pl.multiple_of(index * CHUNK, CHUNK), CHUNK)
        weight = feed_weight[:, :, :, :, pl.ds(0, 2 * CHUNK)].reshape(width, 2 * CHUNK)
        both = dot_nn(normed[...], weight)
        gate, lifted = both[:tokens, :CHUNK], both[:tokens, CHUNK:]
        gate_seen = both[tokens : tokens + RANK, :CHUNK]
        lifted_seen = both[tokens + RANK :, CHUNK:]
        funnel = feed_weight[:, :, :, :, pl.ds(2 * CHUNK, CHUNK)].reshape(width, CHUNK)
        d_hidden = dot_nn(back[...], funnel)
        sigmoid = 1.0 / (1.0 + jnp.exp(-gate))
        silu = gate * sigmoid
        hidden = (silu * lifted).astype(jnp.bfloat16)
        d_gate = (d_hidden * lifted * (sigmoid * (1.0 + gate * (1.0 - sigmoid)))).astype(
            jnp.bfloat16
        )
        d_lifted = (d_hidden * silu).astype(jnp.bfloat16)
        gate_dots = jnp.sum(d_gate.astype(jnp.float32) * gate, axis=0, keepdims=True)
        lifted_dots = jnp.sum(d_lifted.astype(jnp.float32) * lifted, axis=0, keepdims=True)
        dots_out[0:1, columns] = gate_dots
        dots_out[1:2, columns] = lifted_dots
        gate_pull = (pull_lift_ref[0, :, columns] * gate_dots).astype(jnp.bfloat16)
        lifted_pull = (pull_lift_ref[1, :, columns] * lifted_dots).astype(jnp.bfloat16)
        up_out[0, :, columns] = ADAPTER_SCALE * (
            dot_nn(reduced[pl.ds(0, RANK)], d_gate) * ratio_ref[0:1, columns]
            - gate_seen * (pull_ref[0:1, columns] * gate_dots)
        )
        up_out[1, :, columns] = ADAPTER_SCALE * (
            dot_nn(reduced[pl.ds(RANK, RANK)], d_lifted) * ratio_ref[1:2, columns]
            - lifted_seen * (pull_ref[1:2, columns] * lifted_dots)
        )
        lowered[pl.ds(0, RANK)] += dot_nt(low_lift_ref[0, :, columns], d_gate)
        lowered[pl.ds(RANK, RANK)] += dot_nt(low_lift_ref[1, :, columns], d_lifted)
        funnel_down_out[:, columns] = ADAPTER_SCALE * dot_nn(funnel_lowered[...], hidden)
        funnel_down = funnel_down_ref[:, columns]
        funnel_reduced[...] += dot_nt(funnel_down, hidden)
        sources = jnp.concatenate([hidden, funnel_down], axis=0)
        gradients = jnp.concatenate(
            [
                jnp.concatenate([d_gate, d_lifted], axis=1),
                jnp.concatenate([gate_pull, nothing], axis=1),
                jnp.concatenate([nothing, lifted_pull], axis=1),
            ],
            axis=0,
        )
        per = 512 // (4 * feed_weight.shape[3])
        for piece in range(width // 512):
            near = pl.ds(piece * per, per)
            funnel_rows = feed_weight[near, :, :, :, pl.ds(2 * CHUNK, CHUNK)]
            gate_rows = feed_weight[near, :, :, :, pl.ds(0, 2 * CHUNK)]
            lanes = pl.ds(piece * 512, 512)
            funneled[:, lanes] += dot_nt(sources, funnel_rows.reshape(512, CHUNK))
            d_normed[:, lanes] += dot_nt(
                gradients, gate_rows.reshape(512, 2 * CHUNK)
            )
        return carry

    lax.fori_loop(0, chunks - HEAD_CHUNKS, feed, 0)
    outbox[...] = d_normed[pl.ds(0, tokens)].astype(jnp.bfloat16)
    outs.append(pltpu.make_async_copy(outbox, d_normed_out, out_sems.at[4]))
    outs[-1].start()
    down_out[...] = ADAPTER_SCALE * (
        dot_nn(lowered[...].astype(jnp.bfloat16), normed[pl.ds(0, tokens)])
        - d_normed[pl.ds(tokens, 2 * RANK)]
    )
    floats[...] = funneled[pl.ds(0, tokens)].astype(jnp.bfloat16)
    outs.append(pltpu.make_async_copy(floats, funneled_out, out_sems.at[5]))
    outs[-1].start()
    funnel_up_out[...] = dot_nn(funnel_reduced[...].astype(jnp.bfloat16), back[...])
    funnel_seen_out[...] = funneled[pl.ds(tokens, RANK)]
    finish(chunks - 1, 1 + BLOCKS * (chunks - 1), BLOCKS)
    for out in outs:
        out.wait()


def run_block(shard, normed_one, rows, back, cosine, sine, keep, gain, small):
    size = lax.axis_size("dp")
    line = size // 4
    tokens, width = rows.shape
    blocks, height, _ = shard.shape
    chunks = blocks // BLOCKS
    cut_blocks = (BLOCKS * HEAD_CHUNKS + 1) // 4
    wide = small[2].shape[2]
    anywhere = pl.BlockSpec(memory_space=pl.ANY)
    local = pl.BlockSpec(memory_space=pltpu.VMEM)
    low = jnp.bfloat16
    full = jnp.float32
    out_shape = (
        jax.ShapeDtypeStruct((blocks, line, 2, 2, height, CHUNK), low),
        jax.ShapeDtypeStruct((3 * cut_blocks, tokens, CHUNK), low),
        jax.ShapeDtypeStruct((2 * cut_blocks, tokens, CHUNK), low),
        jax.ShapeDtypeStruct((cut_blocks, tokens, CHUNK), low),
        jax.ShapeDtypeStruct((tokens, width), full),
        jax.ShapeDtypeStruct((tokens, width), low),
        jax.ShapeDtypeStruct((tokens, width), low),
        jax.ShapeDtypeStruct((2, RANK, wide), full),
        jax.ShapeDtypeStruct((2 * RANK, width), full),
        jax.ShapeDtypeStruct((RANK, wide), full),
        jax.ShapeDtypeStruct((RANK, width), full),
        jax.ShapeDtypeStruct((RANK, width), full),
        jax.ShapeDtypeStruct((2, wide), full),
    )
    scratch = [
        pltpu.VMEM((tokens + 2 * RANK, width), low),
        pltpu.VMEM((tokens, width), low),
        pltpu.VMEM((tokens, width), low),
        pltpu.VMEM((3 * cut_blocks, tokens, CHUNK), low),
        pltpu.VMEM((3 * cut_blocks, tokens, CHUNK), low),
        pltpu.VMEM((cut_blocks, tokens, CHUNK), low),
        pltpu.VMEM((2, line, 2, 2, height, CHUNK), low),
        pltpu.VMEM((line, 2, 2, height, 4 * CHUNK), low),
        pltpu.VMEM((tokens, width), full),
        pltpu.VMEM((tokens + 2 * RANK, width), full),
        pltpu.VMEM((tokens + RANK, width), full),
        pltpu.VMEM((tokens, width), low),
        pltpu.VMEM((tokens, width), low),
        pltpu.VMEM((2 * RANK, tokens), full),
        pltpu.VMEM((2 * RANK, tokens), low),
        pltpu.VMEM((RANK, tokens), low),
        pltpu.VMEM((RANK, tokens), full),
        pltpu.SemaphoreType.DMA((chunks + 1, 2 * (line - 1))),
        pltpu.SemaphoreType.DMA((chunks + 1, 2 * (line - 1))),
        pltpu.SemaphoreType.DMA((chunks + 1, 2 * (line - 1))),
        pltpu.SemaphoreType.DMA((chunks + 1, 2 * (line - 1))),
        pltpu.SemaphoreType.DMA((chunks + 1, 2)),
        pltpu.SemaphoreType.DMA((chunks + 1, 2)),
        pltpu.SemaphoreType.DMA((2, 2)),
        pltpu.SemaphoreType.DMA((4,)),
        pltpu.SemaphoreType.DMA((4,)),
        pltpu.SemaphoreType.DMA((tokens // SEQ,)),
        pltpu.SemaphoreType.DMA((tokens // SEQ,)),
        pltpu.SemaphoreType.DMA((6,)),
    ]
    return pl.pallas_call(
        functools.partial(block_kernel, size),
        name="block",
        out_shape=out_shape,
        in_specs=[local] + [anywhere] * 3 + [local] * 11,
        out_specs=[anywhere] * 7 + [local] * 6,
        scratch_shapes=scratch,
        compiler_params=pltpu.CompilerParams(
            collective_id=1, has_side_effects=True, vmem_limit_bytes=60 * 1024 * 1024
        ),
    )(shard, normed_one, rows, back, cosine, sine, keep, gain, *small)


def body(
    activations,
    cotangent,
    padding_mask,
    positions,
    norm_gains,
    base_query,
    base_key,
    base_value,
    base_gate,
    base_widen,
    base_mixer,
    base_funnel,
    entry_value,
    attend_value,
    widen_value,
    mixer_value,
    funnel_value,
    output_value,
    stature_value,
    amplitude_value,
    loudness_value,
    entry_first,
    attend_first,
    widen_first,
    mixer_first,
    funnel_first,
    output_first,
    stature_first,
    amplitude_first,
    loudness_first,
    entry_second,
    attend_second,
    widen_second,
    mixer_second,
    funnel_second,
    output_second,
    stature_second,
    amplitude_second,
    loudness_second,
):
    params = (
        entry_value,
        attend_value,
        widen_value,
        mixer_value,
        funnel_value,
        output_value,
        stature_value,
        amplitude_value,
        loudness_value,
    )
    firsts = (
        entry_first,
        attend_first,
        widen_first,
        mixer_first,
        funnel_first,
        output_first,
        stature_first,
        amplitude_first,
        loudness_first,
    )
    seconds = (
        entry_second,
        attend_second,
        widen_second,
        mixer_second,
        funnel_second,
        output_second,
        stature_second,
        amplitude_second,
        loudness_second,
    )
    rows = base_query.shape[0]
    width = activations.shape[1]
    place = lax.axis_index("dp") * rows
    cut = base_query.shape[1]
    wide = base_gate.shape[1]
    entry_rows = lax.dynamic_slice_in_dim(entry_value, place, rows, 1)
    output_columns = lax.dynamic_slice_in_dim(output_value, place, rows, 2)
    lifts = [attend_value[0], attend_value[1], attend_value[2], widen_value[0], widen_value[1]]
    pad = -wide % LANES
    magnitudes = jnp.concatenate(
        [
            loudness_value.reshape(-1, LANES),
            stature_value.reshape(-1, LANES),
            jnp.pad(amplitude_value, ((0, 0), (0, pad)), constant_values=1.0).reshape(-1, LANES),
        ]
    )
    magnitudes = jnp.pad(magnitudes, ((0, -magnitudes.shape[0] % 8), (0, 0)), constant_values=1.0)
    shard, squares = merge(
        (base_query, base_key, base_value, base_gate, base_widen, base_mixer, base_funnel),
        entry_rows,
        attend_value,
        widen_value,
        mixer_value,
        funnel_value,
        output_columns,
        magnitudes,
    )
    lines = (wide + pad) // LANES
    shared_norms = jnp.sqrt(squares[:4].reshape(2, width) + COLUMN_EPS)
    split_norms = jnp.sqrt(
        jnp.concatenate(
            [squares[4:7].reshape(-1)]
            + [
                squares[7 + i * lines : 7 + (i + 1) * lines].reshape(-1)[:wide]
                for i in range(2)
            ]
        )
        + COLUMN_EPS
    )
    split_wide = split_norms.shape[0]
    split_magnitudes = jnp.concatenate([stature_value.reshape(-1), amplitude_value.reshape(-1)])
    split_ratio = split_magnitudes / split_norms
    shared_ratio = loudness_value / shared_norms
    floats = activations.astype(jnp.float32)
    normed_one = low(root_norm(floats, norm_gains[0]))
    count = activations.shape[0] // SEQ
    half = jnp.arange(HEAD_DIM // 2, dtype=jnp.float32)
    angles = positions.astype(jnp.float32)[:, None] * (ROPE_BASE ** (-2.0 * half / HEAD_DIM))[None]
    cosine = jnp.tile(jnp.cos(angles), (1, 2))
    sine = jnp.sin(angles)
    sine = jnp.concatenate([-sine, sine], axis=1)
    keep = padding_mask.reshape(count, 1, SEQ)
    feed_ratio = split_ratio[3 * cut :].reshape(2, wide)
    feed_pull = 1.0 / (split_norms[3 * cut :] * split_magnitudes[3 * cut :]).reshape(2, wide)
    entry_down = low(jnp.swapaxes(entry_value, 1, 2))
    small = (
        entry_down[3:].reshape(2 * RANK, width),
        low(funnel_value.T),
        low(widen_value * feed_ratio[:, None]),
        widen_value * feed_pull[:, None],
        feed_ratio,
        feed_pull,
        low(output_value[1] * shared_ratio[1]),
    )
    (
        full,
        turned,
        plain,
        mixed,
        residual,
        d_normed_two,
        funneled,
        feed_ups,
        feed_downs,
        funnel_down,
        funnel_up,
        funnel_seen,
        feed_dots,
    ) = run_block(
        shard, normed_one, activations, cotangent, cosine, sine, keep, norm_gains[1:2], small
    )
    blocks = full.shape[0]
    near = cut // CHUNK
    heads = CHUNK // HEAD_DIM
    scale = HEAD_DIM ** (-0.5)
    full = full.reshape(blocks, width, CHUNK)
    d_normed_two = swap(d_normed_two)
    funneled = swap(funneled)
    attended = residual - floats
    block_output = low(residual + funneled)
    back = cotangent.astype(jnp.float32)
    unused, second_pull = jax.vjp(lambda v: root_norm(v, norm_gains[1]), residual)
    d_residual = back + second_pull(d_normed_two)[0]
    d_residual_low = low(d_residual)
    d_mixed = low(
        jnp.einsum(
            "td,gdc->gtc", d_residual_low, full[3 * near : 4 * near], preferred_element_type=jnp.float32
        )
    )
    split = (near, count, SEQ, heads, HEAD_DIM)
    d_mixed = d_mixed.reshape(split)
    turned_queries, turned_keys, values_low = (
        turned[i * near : (i + 1) * near].reshape(split) for i in range(3)
    )
    allowed = allowed_of(padding_mask, count)[None]

    def product(equation, left, right):
        return jnp.einsum(equation, left, right, preferred_element_type=jnp.float32)

    scores = product("gbqhd,gbkhd->gbhqk", turned_queries, turned_keys) * scale
    masked = jnp.where(allowed, scores, MASKED)
    top = jnp.max(masked, axis=-1, keepdims=True)
    log_total = top + jnp.log(jnp.sum(jnp.exp(masked - top), axis=-1, keepdims=True))
    attention = jnp.exp(masked - log_total)
    attention_low = low(attention)
    d_attention = product("gbqhd,gbkhd->gbhqk", d_mixed, values_low)
    d_values = low(product("gbhqk,gbqhd->gbkhd", attention_low, d_mixed))
    d_scores = attention * (d_attention - jnp.sum(attention * d_attention, axis=-1, keepdims=True))
    d_scores = low(d_scores)
    flat = (near, activations.shape[0], heads, HEAD_DIM)
    d_turned_queries = product("gbhqk,gbkhd->gbqhd", d_scores, turned_keys).reshape(flat) * scale
    d_turned_keys = product("gbhqk,gbqhd->gbkhd", d_scores, turned_queries).reshape(flat) * scale

    def turn_back(values):
        swapped = jnp.concatenate([values[..., HEAD_DIM // 2 :], values[..., : HEAD_DIM // 2]], -1)
        return low(values * cosine[None, :, None] - swapped * sine[None, :, None])

    d_heads = jnp.concatenate(
        [
            turn_back(d_turned_queries).reshape(near, -1, CHUNK),
            turn_back(d_turned_keys).reshape(near, -1, CHUNK),
            d_values.reshape(near, -1, CHUNK),
        ]
    )
    d_normed_one = swap(product("gtc,gdc->td", d_heads, full[: 3 * near]))
    unused, first_pull = jax.vjp(lambda v: root_norm(v, norm_gains[0]), floats)
    input_gradient = d_residual + first_pull(d_normed_one)[0]

    heads_plain = jnp.concatenate([plain, turned[2 * near :]]).astype(jnp.float32)
    head_dots = jnp.sum(d_heads.astype(jnp.float32) * heads_plain, axis=1).reshape(-1)
    split_dots = jnp.concatenate([head_dots, feed_dots.reshape(-1)])
    shared_dots = jnp.stack(
        [
            jnp.sum(d_residual_low.astype(jnp.float32) * attended, axis=0),
            jnp.sum(back * funneled, axis=0),
        ]
    )
    shared_pull = shared_dots / (shared_norms * loudness_value)
    head_pull = split_dots[: 3 * cut] / (split_norms[: 3 * cut] * split_magnitudes[: 3 * cut])
    down_gradients = []
    up_gradients = []
    for i in range(3):
        ratio = split_ratio[i * cut : (i + 1) * cut]
        pull = head_pull[i * cut : (i + 1) * cut]
        part = slice(i * near, (i + 1) * near)
        low_lift = low(attend_value[i] * ratio).reshape(RANK, near, CHUNK)
        pull_lift = low(attend_value[i] * pull).reshape(RANK, near, CHUNK)
        lowered = low(product("rgc,gtc->rt", low_lift, d_heads[part]))
        down_gradients.append(
            ADAPTER_SCALE
            * (matmul(lowered, normed_one) - product("rgc,gdc->rd", pull_lift, full[part]))
        )
        reduced = low(matmul_nt(entry_down[i], normed_one))
        main = product("rt,gtc->rgc", reduced, d_heads[part]).reshape(RANK, cut)
        seen = product("rd,gdc->rgc", entry_down[i], full[part]).reshape(RANK, cut)
        up_gradients.append(ADAPTER_SCALE * (main * ratio - seen * pull))
    down_gradients += [feed_downs[:RANK], feed_downs[RANK:]]
    up_gradients += [feed_ups[0], feed_ups[1]]
    low_lift = low(output_value[0] * shared_ratio[0])
    pull_lift = low(output_value[0] * shared_pull[0])
    lowered = low(matmul_nt(low_lift, d_residual_low))
    mixer_weight = full[3 * near : 4 * near]
    mixer_down = ADAPTER_SCALE * (
        product("rt,gtc->rgc", lowered, mixed) - product("rd,gdc->rgc", pull_lift, mixer_weight)
    ).reshape(RANK, cut)
    low_down = low(mixer_value.T).reshape(RANK, near, CHUNK)
    reduced = low(product("rgc,gtc->rt", low_down, mixed))
    mixer_up = ADAPTER_SCALE * (
        matmul(reduced, d_residual_low) * shared_ratio[0]
        - product("rgc,gdc->rd", low_down, mixer_weight) * shared_pull[0]
    )
    pull_lift = low(output_value[1] * shared_pull[1])
    funnel_weight = full[4 * near :].reshape(-1, BLOCKS, width, CHUNK)[:, 2]
    funnel_down = funnel_down - ADAPTER_SCALE * product(
        "rd,gdc->rgc", pull_lift, funnel_weight
    ).reshape(RANK, wide)
    funnel_up = ADAPTER_SCALE * (funnel_up * shared_ratio[1] - funnel_seen * shared_pull[1])
    shared_terms = jnp.concatenate(down_gradients + [mixer_up, funnel_up], axis=1)
    split_terms = jnp.concatenate(up_gradients + [mixer_down, funnel_down], axis=1)
    shared_terms, split_terms, split_dots, shared_dots = lax.psum(
        (shared_terms, split_terms, split_dots, shared_dots), "dp"
    )
    split_scale = split_dots / split_magnitudes
    shared_scale = shared_dots / loudness_value
    split_total = jnp.sum(split_terms * split_terms) + jnp.sum(split_scale * split_scale)
    shared_terms, split_total = lax.psum((shared_terms, split_total), "tensor")
    totals = (
        jnp.stack([shared_terms[:, i * width : (i + 1) * width].T for i in range(5)]),
        jnp.stack([split_terms[:, i * cut : (i + 1) * cut] for i in range(3)]),
        jnp.stack([split_terms[:, 3 * cut + i * wide : 3 * cut + (i + 1) * wide] for i in range(2)]),
        split_terms[:, split_wide : split_wide + cut].T,
        split_terms[:, split_wide + cut :].T,
        jnp.stack([shared_terms[:, (5 + i) * width : (6 + i) * width] for i in range(2)]),
        split_scale[: 3 * cut].reshape(3, cut),
        split_scale[3 * cut :].reshape(2, wide),
        shared_scale,
    )
    gradient_norm = jnp.sqrt(split_total + squares_of((totals[0], totals[5], totals[8])))
    down_factor = jnp.minimum(1.0, CLIP / (gradient_norm + 1e-06))
    rates = (
        RATE_FACTOR,
        RATE_LIFT,
        RATE_LIFT,
        RATE_FACTOR,
        RATE_FACTOR,
        RATE_LIFT,
        RATE_SCALE,
        RATE_SCALE,
        RATE_LOUD,
    )
    updated = []
    momenta = []
    variances = []
    for value, gradient, first, second, rate in zip(params, totals, firsts, seconds, rates):
        fresh, momentum, variance = decoupled_update(
            value, gradient * down_factor, first, second, rate
        )
        updated.append(fresh)
        momenta.append(momentum)
        variances.append(variance)
    return (
        block_output,
        input_gradient,
        gradient_norm,
        updated[0],
        updated[1],
        updated[2],
        updated[3],
        updated[4],
        updated[5],
        updated[6],
        updated[7],
        updated[8],
        momenta[0],
        momenta[1],
        momenta[2],
        momenta[3],
        momenta[4],
        momenta[5],
        momenta[6],
        momenta[7],
        momenta[8],
        variances[0],
        variances[1],
        variances[2],
        variances[3],
        variances[4],
        variances[5],
        variances[6],
        variances[7],
        variances[8],
    )


def solution(mesh):
    return jax.shard_map(
        body,
        mesh=mesh,
        in_specs=(
            P("dp", None),
            P("dp", None),
            P("dp"),
            P("dp"),
            P(),
            P("dp", "tensor"),
            P("dp", "tensor"),
            P("dp", "tensor"),
            P("dp", "tensor"),
            P("dp", "tensor"),
            P("tensor", "dp"),
            P("tensor", "dp"),
            P(),
            P(None, None, "tensor"),
            P(None, None, "tensor"),
            P("tensor", None),
            P("tensor", None),
            P(),
            P(None, "tensor"),
            P(None, "tensor"),
            P(),
            P(),
            P(None, None, "tensor"),
            P(None, None, "tensor"),
            P("tensor", None),
            P("tensor", None),
            P(),
            P(None, "tensor"),
            P(None, "tensor"),
            P(),
            P(),
            P(None, None, "tensor"),
            P(None, None, "tensor"),
            P("tensor", None),
            P("tensor", None),
            P(),
            P(None, "tensor"),
            P(None, "tensor"),
            P(),
        ),
        out_specs=(
            P("dp", None),
            P("dp", None),
            P(),
            P(),
            P(None, None, "tensor"),
            P(None, None, "tensor"),
            P("tensor", None),
            P("tensor", None),
            P(),
            P(None, "tensor"),
            P(None, "tensor"),
            P(),
            P(),
            P(None, None, "tensor"),
            P(None, None, "tensor"),
            P("tensor", None),
            P("tensor", None),
            P(),
            P(None, "tensor"),
            P(None, "tensor"),
            P(),
            P(),
            P(None, None, "tensor"),
            P(None, None, "tensor"),
            P("tensor", None),
            P("tensor", None),
            P(),
            P(None, "tensor"),
            P(None, "tensor"),
            P(),
        ),
        check_vma=False,
    )
```

```python
import functools

import jax
import jax.numpy as jnp
from jax import lax
from jax.experimental import pallas as pl
from jax.experimental.pallas import tpu as pltpu
from jax.sharding import PartitionSpec as P

HEAD_DIM = 128
RANK = 16
SEQ = 256
STEP = 5


HIGH_PRECISION = lax.Precision.HIGHEST
ADAPTER_SCALE = 2.0
NORM_EPS = 1e-05
COLUMN_EPS = 1e-06
BETA_ONE = 0.9
BETA_TWO = 0.999
ADAM_EPS = 1e-08
DECAY = 0.01
CLIP = 1.0
RATE_FACTOR = 0.02
RATE_LIFT = 0.2
RATE_SCALE = 0.5
RATE_LOUD = 2.0
ROPE_BASE = 10000.0
MASKED = -1e30


def root_norm(values, gain):
    return values * lax.rsqrt(jnp.mean(values * values, axis=-1, keepdims=True) + NORM_EPS) * gain


def rotate(values, places, sign):
    half = values.shape[-1] // 2
    steps = jnp.arange(half, dtype=jnp.float32)
    frequency = ROPE_BASE ** (-2.0 * steps / values.shape[-1])
    angles = places.astype(jnp.float32)[:, None] * frequency[None, :]
    cosine = jnp.cos(angles)[:, None, :]
    sine = sign * jnp.sin(angles)[:, None, :]
    first = values[..., :half]
    second = values[..., half:]
    return jnp.concatenate(
        [first * cosine - second * sine, second * cosine + first * sine], axis=-1
    )


def allowed_of(padding, count):
    valid = padding.reshape(count, SEQ) > 0
    index = jnp.arange(SEQ)
    causal = index[:, None] >= index[None, :]
    itself = index[:, None] == index[None, :]
    return (causal[None] & valid[:, None, :] | itself[None])[:, None]


def squares_of(items):
    total = jnp.zeros((), jnp.float32)
    for param_entry in items:
        total = total + jnp.sum(param_entry * param_entry)
    return total


def decoupled_update(value, gradient, first, second, rate):
    momentum = BETA_ONE * first + (1.0 - BETA_ONE) * gradient
    variance = BETA_TWO * second + (1.0 - BETA_TWO) * gradient * gradient
    corrected = momentum / (1.0 - BETA_ONE**STEP)
    spread = jnp.sqrt(variance / (1.0 - BETA_TWO**STEP))
    return (value - rate * (corrected / (spread + ADAM_EPS) + DECAY * value), momentum, variance)


def swap(partial):
    low = partial.astype(jnp.bfloat16)
    size = lax.axis_size("tensor")
    total = low.astype(jnp.float32)
    for step in range(1, size):
        other = lax.ppermute(low, "tensor", [(i, (i + step) % size) for i in range(size)])
        total = total + other.astype(jnp.float32)
    return total


def matmul(left, right):
    return jnp.dot(left, right, preferred_element_type=jnp.float32)


def matmul_nt(left, right):
    return jnp.einsum("ik,jk->ij", left, right, preferred_element_type=jnp.float32)


def matmul_tn(left, right):
    return jnp.einsum("ki,kj->ij", left, right, preferred_element_type=jnp.float32)


def low(values):
    return values.astype(jnp.bfloat16)


MESH = pl.DeviceIdType.MESH
LANES = 1024
CHUNK = 256


def partners_of(size):
    me = lax.axis_index("dp")
    found = []
    bit = 1
    while bit < size:
        down = lax.rem(lax.div(me, bit), 2)
        found.append(me + bit - 2 * bit * down)
        bit *= 2
    return found


def double_sum(total, inbox, sends, receives, size, sides, shared_rows):
    targets = [({"dp": p}, total.shape[0]) for p in partners_of(size)]
    side = lax.axis_index("tensor")
    targets += [
        ({"tensor": lax.rem(side + step, sides)}, shared_rows) for step in range(1, sides)
    ]
    for step, (target, count) in enumerate(targets):
        kept = pl.ds(0, count)
        copy = pltpu.make_async_remote_copy(
            src_ref=total,
            dst_ref=inbox.at[step],
            send_sem=sends.at[step],
            recv_sem=receives.at[step],
            device_id=target,
            device_id_type=MESH,
        )
        copy.start()
        copy.wait()
        total[kept] += inbox[step, kept]


def greet_sum(size, sides):
    barrier = pltpu.get_barrier_semaphore()
    side = lax.axis_index("tensor")
    targets = [{"dp": p} for p in partners_of(size)]
    targets += [{"tensor": lax.rem(side + step, sides)} for step in range(1, sides)]
    for target in targets:
        pl.semaphore_signal(barrier, inc=1, device_id=target, device_id_type=MESH)
    pl.semaphore_wait(barrier, len(targets))


def merge_kernel(
    size,
    sides,
    query_ref,
    key_ref,
    value_ref,
    gate_ref,
    widen_ref,
    mixer_ref,
    funnel_ref,
    entry_ref,
    attend_ref,
    lift_ref,
    mixer_down_ref,
    funnel_down_ref,
    output_ref,
    magnitude_ref,
    shard_out,
    squares_out,
    total,
    inbox,
    direction_cut,
    direction_wide,
    direction_mixer,
    direction_funnel,
    sends,
    receives,
):
    greet_sum(size, sides)
    rows = query_ref.shape[0]
    wide = gate_ref.shape[1]
    me = lax.axis_index("dp")
    total[...] = jnp.zeros_like(total)

    def direction(base, down, up):
        return base.astype(jnp.float32) + ADAPTER_SCALE * jnp.dot(
            down, up, precision=HIGH_PRECISION, preferred_element_type=jnp.float32
        )

    group = LANES // rows
    lane_group = lax.broadcasted_iota(jnp.int32, (1, LANES), 1) // rows
    for i, (base, down) in enumerate(
        ((mixer_ref, mixer_down_ref), (funnel_ref, funnel_down_ref))
    ):
        held = (direction_mixer, direction_funnel)[i]
        sums = jnp.zeros((1, rows), jnp.float32)
        for start in range(0, base.shape[0], CHUNK):
            piece = pl.ds(start, CHUNK)
            part = direction(base[piece], down[piece], output_ref[i])
            held[piece] = part
            sums += jnp.sum(part * part, axis=0, keepdims=True)
        spread = jnp.concatenate([sums] * group, axis=1)
        for r in range(2):
            here = lane_group == me - r * group
            total[2 * i + r : 2 * i + r + 1, :] = jnp.where(here, spread, 0.0)
    for i, base in enumerate((query_ref, key_ref, value_ref)):
        for start in range(0, LANES, CHUNK):
            piece = pl.ds(start, CHUNK)
            part = direction(base[:, piece], entry_ref[i], attend_ref[i, :, piece])
            direction_cut[i, :, piece] = part
            total[4 + i : 5 + i, piece] = jnp.sum(part * part, axis=0, keepdims=True)
    for i, base in enumerate((gate_ref, widen_ref)):
        for start in range(0, wide, CHUNK):
            piece = pl.ds(start, CHUNK)
            part = direction(base[:, piece], entry_ref[3 + i], lift_ref[i, :, piece])
            direction_wide[i, :, piece] = part
            row = 7 + 3 * i + start // LANES
            total[row : row + 1, pl.ds(start % LANES, CHUNK)] = jnp.sum(
                part * part, axis=0, keepdims=True
            )
    double_sum(total, inbox, sends, receives, size, sides, 4)
    squares_out[...] = total[...]
    ratio = magnitude_ref[...] / jnp.sqrt(total[...] + COLUMN_EPS)
    near = LANES // CHUNK
    for i in range(3):
        for b in range(near):
            lanes = slice(b * CHUNK, (b + 1) * CHUNK)
            shard_out[near * i + b] = (
                direction_cut[i, :, lanes] * ratio[4 + i : 5 + i, lanes]
            ).astype(jnp.bfloat16)
    for i in range(2):
        for start in range(0, wide, CHUNK):
            row = 7 + 3 * i + start // LANES
            shard_out[4 * near + 3 * (start // CHUNK) + i] = (
                direction_wide[i, :, pl.ds(start, CHUNK)]
                * ratio[row : row + 1, start % LANES : start % LANES + CHUNK]
            ).astype(jnp.bfloat16)
    for i, held in enumerate((direction_mixer, direction_funnel)):
        own = jnp.zeros((1, rows), jnp.float32)
        for r in range(2):
            for g in range(group):
                own += jnp.where(
                    me == r * group + g,
                    ratio[2 * i + r : 2 * i + r + 1, g * rows : (g + 1) * rows],
                    0.0,
                )
        for start in range(0, held.shape[0], CHUNK):
            part = (held[pl.ds(start, CHUNK)] * own).T.astype(jnp.bfloat16)
            if i == 0:
                shard_out[3 * near + start // CHUNK] = part
            else:
                shard_out[4 * near + 3 * (start // CHUNK) + 2] = part


def merge(bases, entry_rows, attend, widen, mixer_down, funnel_down, output_columns, magnitudes):
    size = lax.axis_size("dp")
    sides = lax.axis_size("tensor")
    rows, cut = bases[0].shape
    wide = bases[3].shape[1]
    steps = len(bin(size)) - 3 + sides - 1
    lines = magnitudes.shape[0]
    return pl.pallas_call(
        functools.partial(merge_kernel, size, sides),
        name="merge",
        out_shape=(
            jax.ShapeDtypeStruct(((4 * cut + 3 * wide) // CHUNK, rows, CHUNK), jnp.bfloat16),
            jax.ShapeDtypeStruct((lines, LANES), jnp.float32),
        ),
        in_specs=[pl.BlockSpec(memory_space=pltpu.VMEM)] * 14,
        out_specs=[pl.BlockSpec(memory_space=pltpu.VMEM)] * 2,
        scratch_shapes=[
            pltpu.VMEM((lines, LANES), jnp.float32),
            pltpu.VMEM((steps, lines, LANES), jnp.float32),
            pltpu.VMEM((3, rows, cut), jnp.float32),
            pltpu.VMEM((2, rows, wide), jnp.float32),
            pltpu.VMEM((cut, rows), jnp.float32),
            pltpu.VMEM((wide, rows), jnp.float32),
            pltpu.SemaphoreType.DMA((steps,)),
            pltpu.SemaphoreType.DMA((steps,)),
        ],
        compiler_params=pltpu.CompilerParams(
            collective_id=0, has_side_effects=True, vmem_limit_bytes=48 * 1024 * 1024
        ),
    )(*bases, entry_rows, attend, widen, mixer_down, funnel_down, output_columns, magnitudes)


def dot_nn(left, right):
    return jnp.dot(left, right, preferred_element_type=jnp.float32)


def dot_nt(left, right):
    return lax.dot_general(
        left, right, (((1,), (1,)), ((), ())), preferred_element_type=jnp.float32
    )


BLOCKS = 3
HEAD_CHUNKS = 5
EXTRA_TICKS = 3


def gather_parts(size, shard, full, sems):
    line = size // 4
    early = 16
    late = shard.shape[1] - early
    me = lax.axis_index("dp")
    core, column, spot = lax.rem(me, 2), lax.rem(lax.div(me, 2), 2), lax.div(me, 4)
    right_sends, left_sends, right_gets, left_gets, pair_sems, core_sems, early_sems = sems

    def device(other_spot, other_column, other_core):
        return {"dp": (other_spot * 2 + other_column) * 2 + other_core}

    right = device(lax.rem(spot + 1, line), column, core)
    left = device(lax.rem(spot + line - 1, line), column, core)
    across = device(spot, 1 - column, core)
    twin = device(spot, column, 1 - core)

    def greet():
        barrier = pltpu.get_barrier_semaphore()
        ahead, behind = spot < line - 1, spot > 0

        @pl.when(ahead)
        def _():
            pl.semaphore_signal(barrier, inc=1, device_id=right, device_id_type=MESH)

        @pl.when(behind)
        def _():
            pl.semaphore_signal(barrier, inc=1, device_id=left, device_id_type=MESH)

        for target in (across, twin, {"tensor": 1 - lax.axis_index("tensor")}):
            pl.semaphore_signal(barrier, inc=1, device_id=target, device_id_type=MESH)
        peers = 3 + ahead.astype(jnp.int32) + behind.astype(jnp.int32)
        pl.semaphore_wait(barrier, peers)

    def remote(source, target, send, get, where):
        return pltpu.make_async_remote_copy(
            src_ref=source,
            dst_ref=target,
            send_sem=send,
            recv_sem=get,
            device_id=where,
            device_id_type=MESH,
        )

    def early_copy(part, owner):
        first = 1 + BLOCKS
        blocks = pl.ds(0, first) if part == 0 else pl.ds(first, shard.shape[0] - first)
        return remote(
            shard.at[blocks, pl.ds(0, early)],
            full.at[blocks, spot, owner, core, pl.ds(0, early)],
            early_sems.at[part, 0],
            early_sems.at[part, 1],
            across,
        )

    def early_start():
        for part in range(2):
            early_copy(part, column).start()

    def early_wait(part):
        early_copy(part, 1 - column).wait_recv()
        early_copy(part, column).wait_send()

    def place_of(part, origin, blocks):
        if part == 0:
            return full.at[blocks, origin, column, core, pl.ds(early, late)]
        return full.at[blocks, origin, :, core, pl.ds(0, early)]

    def moves(to_right, hop, chunk, start, count):
        sends, gets = (right_sends, right_gets) if to_right else (left_sends, left_gets)
        blocks = pl.ds(start, count)
        found = []
        for part in range(2):
            place = place_of(part, spot - hop if to_right else spot + hop, blocks)
            source = shard.at[blocks, pl.ds(early, late)] if hop == 0 and part == 0 else place
            found.append(
                remote(
                    source,
                    place,
                    sends.at[chunk, 2 * hop + part],
                    gets.at[chunk, 2 * hop + part],
                    right if to_right else left,
                )
            )
        return found

    def arrivals(to_right, hop, chunk, start, count):
        gets = right_gets if to_right else left_gets
        for part in range(2):
            place = place_of(part, spot - hop if to_right else spot + hop, pl.ds(start, count))
            kept = 2 * (hop - 1) + part
            remote(
                place, place, right_sends.at[chunk, kept], gets.at[chunk, kept], right
            ).wait_recv()

    def pair_copy(chunk, start, count, owner):
        place = full.at[pl.ds(start, count), :, owner, core, pl.ds(early, late)]
        return remote(place, place, pair_sems.at[chunk, 0], pair_sems.at[chunk, 1], across)

    def core_copy(chunk, start, count, owner):
        place = full.at[pl.ds(start, count), :, :, owner]
        return remote(place, place, core_sems.at[chunk, 0], core_sems.at[chunk, 1], twin)

    def send_on(hop, chunk, start, count):
        @pl.when((spot >= hop) & (spot < line - 1))
        def _():
            for copy in moves(True, hop, chunk, start, count):
                copy.start()

        @pl.when((spot < line - hop) & (spot > 0))
        def _():
            for copy in moves(False, hop, chunk, start, count):
                copy.start()

    def take_in(hop, chunk, start, count):
        @pl.when(spot >= hop)
        def _():
            arrivals(True, hop, chunk, start, count)

        @pl.when(spot < line - hop)
        def _():
            arrivals(False, hop, chunk, start, count)

    def step(phase, chunk, start, count):
        if 1 <= phase < line:
            take_in(phase, chunk, start, count)
        if phase < line - 1:
            send_on(phase, chunk, start, count)
        if phase == line - 1:
            pair_copy(chunk, start, count, column).start()
        elif phase == line + 1:
            pair_copy(chunk, start, count, 1 - column).wait_recv()
            core_copy(chunk, start, count, core).start()
        elif phase == line + 2:
            core_copy(chunk, start, count, 1 - core).wait_recv()
        elif phase == line + 3:
            finish(chunk, start, count)

    def finish(chunk, start, count):
        for hop in range(line - 1):

            @pl.when((spot >= hop) & (spot < line - 1))
            def _(hop=hop):
                for copy in moves(True, hop, chunk, start, count):
                    copy.wait_send()

            @pl.when((spot < line - hop) & (spot > 0))
            def _(hop=hop):
                for copy in moves(False, hop, chunk, start, count):
                    copy.wait_send()

        pair_copy(chunk, start, count, column).wait_send()
        core_copy(chunk, start, count, core).wait_send()

    return greet, step, early_start, early_wait, finish


def block_kernel(
    size,
    shard,
    normed_ref,
    rows_ref,
    back_ref,
    cosine_ref,
    sine_ref,
    keep_ref,
    gain_ref,
    entry_down_ref,
    funnel_down_ref,
    low_lift_ref,
    pull_lift_ref,
    ratio_ref,
    pull_ref,
    low_output_ref,
    full,
    turned_out,
    plain_out,
    mixed_out,
    residual_out,
    d_normed_out,
    funneled_out,
    up_out,
    down_out,
    funnel_down_out,
    funnel_up_out,
    funnel_seen_out,
    dots_out,
    normed,
    back,
    floats,
    turned,
    plain,
    mixed,
    heads_weight,
    feed_weight,
    residual,
    d_normed,
    funneled,
    outbox,
    inbox,
    lowered,
    reduced,
    funnel_lowered,
    funnel_reduced,
    right_sends,
    left_sends,
    right_gets,
    left_gets,
    pair_sems,
    core_sems,
    early_sems,
    local_sems,
    weight_sems,
    side_sends,
    side_gets,
    out_sems,
):
    line = size // 4
    total_blocks = full.shape[0]
    chunks = total_blocks // BLOCKS
    tokens, width = normed.shape[0] - 2 * RANK, normed.shape[1]
    count = tokens // SEQ
    sides = {"tensor": 1 - lax.axis_index("tensor")}
    sems = (right_sends, left_sends, right_gets, left_gets, pair_sems, core_sems, early_sems)
    greet, step, early_start, early_wait, finish = gather_parts(size, shard, full, sems)
    me = lax.axis_index("dp")
    core, column, spot = lax.rem(me, 2), lax.rem(lax.div(me, 2), 2), lax.div(me, 4)

    def tick(now):
        for phase in range(line + 4):
            chunk = now - phase
            start = 1 + BLOCKS * chunk
            if isinstance(now, int):
                if 0 <= chunk < chunks:
                    step(phase, chunk, start, BLOCKS)
            else:

                @pl.when((chunk >= 0) & (chunk < chunks))
                def _(phase=phase, chunk=chunk, start=start):
                    step(phase, chunk, start, BLOCKS)

    own = pltpu.make_async_copy(shard, full.at[:, spot, column, core], local_sems.at[0])
    own.start()
    loads = [
        pltpu.make_async_copy(normed_ref, normed.at[pl.ds(0, tokens)], local_sems.at[1]),
        pltpu.make_async_copy(back_ref, back, local_sems.at[2]),
        pltpu.make_async_copy(rows_ref, floats, local_sems.at[3]),
    ]
    for load in loads:
        load.start()
    greet()
    early_start()
    own.wait()
    early_wait(0)
    step(0, chunks, 0, 1)
    tick(0)
    early_wait(1)
    for now in range(1, line + 4):
        step(now, chunks, 0, 1)
        tick(now)
    ready = HEAD_CHUNKS - 2 + line + 2
    lax.fori_loop(line + 4, ready + 1, lambda now, carry: (tick(now), carry)[1], 0)
    for load in loads:
        load.wait()

    def head_load(block, slot):
        return pltpu.make_async_copy(
            full.at[block], heads_weight.at[slot], weight_sems.at[slot]
        )

    def head_weight(slot):
        return heads_weight[slot].reshape(width, CHUNK)

    cut_blocks = turned.shape[0] // 3
    head_load(0, 0).start()

    def project(block, carry):
        slot = lax.rem(block, 2)

        @pl.when(block < 3 * cut_blocks - 1)
        def _():
            head_load(block + 1, 1 - slot).start()

        head_load(block, slot).wait()
        for part in range(count):
            place = pl.ds(part * SEQ, SEQ)
            result = dot_nn(normed[place], head_weight(slot))
            plain[block, place] = result.astype(jnp.bfloat16)

            @pl.when(block < 2 * cut_blocks)
            def _(result=result, place=place):
                for half in range(CHUNK // HEAD_DIM):
                    lanes = slice(half * HEAD_DIM, (half + 1) * HEAD_DIM)
                    head = result[:, lanes]
                    turned[block, place, lanes] = (
                        head * cosine_ref[place]
                        + pltpu.roll(head, HEAD_DIM // 2, 1) * sine_ref[place]
                    ).astype(jnp.bfloat16)

            @pl.when(block >= 2 * cut_blocks)
            def _(result=result, place=place):
                turned[block, place] = result.astype(jnp.bfloat16)

        return carry

    lax.fori_loop(0, 3 * cut_blocks, project, 0)
    outs = [
        pltpu.make_async_copy(turned, turned_out, out_sems.at[0]),
        pltpu.make_async_copy(plain.at[pl.ds(0, 2 * cut_blocks)], plain_out, out_sems.at[1]),
    ]
    for out in outs:
        out.start()
    tick(ready + 1)

    mixer_loads = [
        pltpu.make_async_copy(
            full.at[3 * cut_blocks + b],
            feed_weight.at[:, :, :, :, pl.ds(b * CHUNK, CHUNK)],
            weight_sems.at[b],
        )
        for b in range(cut_blocks)
    ]
    for load in mixer_loads:
        load.start()
    line_up = lax.broadcasted_iota(jnp.int32, (SEQ, SEQ), 0)
    line_on = lax.broadcasted_iota(jnp.int32, (SEQ, SEQ), 1)

    def attend(block, carry):
        for part in range(count):
            place = pl.ds(part * SEQ, SEQ)
            allowed = ((line_up >= line_on) & (keep_ref[part] > 0)) | (line_up == line_on)
            for half in range(CHUNK // HEAD_DIM):
                lanes = slice(half * HEAD_DIM, (half + 1) * HEAD_DIM)
                scores = dot_nt(
                    turned[block, place, lanes], turned[cut_blocks + block, place, lanes]
                ) * (HEAD_DIM ** (-0.5))
                masked = jnp.where(allowed, scores, MASKED)
                top = jnp.max(masked, axis=1, keepdims=True)
                weight = jnp.exp(masked - top)
                attention = weight / jnp.sum(weight, axis=1, keepdims=True)
                mixed[block, place, lanes] = dot_nn(
                    attention.astype(jnp.bfloat16), turned[2 * cut_blocks + block, place, lanes]
                ).astype(jnp.bfloat16)
        return carry

    lax.fori_loop(0, cut_blocks, attend, 0)
    outs.append(pltpu.make_async_copy(mixed, mixed_out, out_sems.at[2]))
    outs[-1].start()
    tick(ready + 2)

    for load in mixer_loads:
        load.wait()

    def side_copy(part):
        place = pl.ds(part * SEQ, SEQ)
        return pltpu.make_async_remote_copy(
            src_ref=outbox.at[place],
            dst_ref=inbox.at[place],
            send_sem=side_sends.at[part],
            recv_sem=side_gets.at[part],
            device_id=sides,
            device_id_type=MESH,
        )

    for part in range(count):
        place = pl.ds(part * SEQ, SEQ)
        joined = jnp.concatenate([mixed[b, place] for b in range(cut_blocks)], axis=1)
        per = 512 // (4 * feed_weight.shape[3])
        for piece in range(width // 512):
            weight = feed_weight[pl.ds(piece * per, per), :, :, :, pl.ds(0, cut_blocks * CHUNK)]
            outbox[place, pl.ds(piece * 512, 512)] = dot_nt(
                joined, weight.reshape(512, cut_blocks * CHUNK)
            ).astype(jnp.bfloat16)
        side_copy(part).start()
    tick(ready + 3)

    tile = 32
    for part in range(count):
        side_copy(part).wait()

        def add_up(index, carry, part=part):
            place = pl.ds(pl.multiple_of(part * SEQ + index * tile, tile), tile)
            value = floats[place].astype(jnp.float32) + (
                outbox[place].astype(jnp.float32) + inbox[place].astype(jnp.float32)
            )
            residual[place] = value
            root = lax.rsqrt(jnp.mean(value * value, axis=1, keepdims=True) + NORM_EPS)
            normed[place] = (value * root * gain_ref[...]).astype(jnp.bfloat16)
            return carry

        lax.fori_loop(0, SEQ // tile, add_up, 0)
        if part == 0:
            tick(ready + 4)
    outs.append(pltpu.make_async_copy(residual, residual_out, out_sems.at[3]))
    outs[-1].start()
    normed[pl.ds(tokens, 2 * RANK)] = entry_down_ref[...]
    reduced[...] = dot_nt(entry_down_ref[...], normed[pl.ds(0, tokens)]).astype(jnp.bfloat16)
    funnel_lowered[...] = dot_nt(low_output_ref[...], back[...]).astype(jnp.bfloat16)
    d_normed[...] = jnp.zeros_like(d_normed)
    funneled[...] = jnp.zeros_like(funneled)
    lowered[...] = jnp.zeros_like(lowered)
    funnel_reduced[...] = jnp.zeros_like(funnel_reduced)

    def feed_load(index):
        return [
            pltpu.make_async_copy(
                full.at[4 * cut_blocks + BLOCKS * index + b],
                feed_weight.at[:, :, :, :, pl.ds(b * CHUNK, CHUNK)],
                weight_sems.at[b],
            )
            for b in range(BLOCKS)
        ]

    nothing = jnp.zeros((RANK, CHUNK), jnp.bfloat16)

    def feed(index, carry):
        @pl.when(index >= EXTRA_TICKS)
        def _():
            tick(index + HEAD_CHUNKS + line + 2)

        for load in feed_load(index):
            load.start()
        for load in feed_load(index):
            load.wait()
        columns = pl.ds(pl.multiple_of(index * CHUNK, CHUNK), CHUNK)
        weight = feed_weight[:, :, :, :, pl.ds(0, 2 * CHUNK)].reshape(width, 2 * CHUNK)
        both = dot_nn(normed[...], weight)
        gate, lifted = both[:tokens, :CHUNK], both[:tokens, CHUNK:]
        gate_seen = both[tokens : tokens + RANK, :CHUNK]
        lifted_seen = both[tokens + RANK :, CHUNK:]
        funnel = feed_weight[:, :, :, :, pl.ds(2 * CHUNK, CHUNK)].reshape(width, CHUNK)
        d_hidden = dot_nn(back[...], funnel)
        sigmoid = 1.0 / (1.0 + jnp.exp(-gate))
        silu = gate * sigmoid
        hidden = (silu * lifted).astype(jnp.bfloat16)
        d_gate = (d_hidden * lifted * (sigmoid * (1.0 + gate * (1.0 - sigmoid)))).astype(
            jnp.bfloat16
        )
        d_lifted = (d_hidden * silu).astype(jnp.bfloat16)
        gate_dots = jnp.sum(d_gate.astype(jnp.float32) * gate, axis=0, keepdims=True)
        lifted_dots = jnp.sum(d_lifted.astype(jnp.float32) * lifted, axis=0, keepdims=True)
        dots_out[0:1, columns] = gate_dots
        dots_out[1:2, columns] = lifted_dots
        gate_pull = (pull_lift_ref[0, :, columns] * gate_dots).astype(jnp.bfloat16)
        lifted_pull = (pull_lift_ref[1, :, columns] * lifted_dots).astype(jnp.bfloat16)
        up_out[0, :, columns] = ADAPTER_SCALE * (
            dot_nn(reduced[pl.ds(0, RANK)], d_gate) * ratio_ref[0:1, columns]
            - gate_seen * (pull_ref[0:1, columns] * gate_dots)
        )
        up_out[1, :, columns] = ADAPTER_SCALE * (
            dot_nn(reduced[pl.ds(RANK, RANK)], d_lifted) * ratio_ref[1:2, columns]
            - lifted_seen * (pull_ref[1:2, columns] * lifted_dots)
        )
        lowered[pl.ds(0, RANK)] += dot_nt(low_lift_ref[0, :, columns], d_gate)
        lowered[pl.ds(RANK, RANK)] += dot_nt(low_lift_ref[1, :, columns], d_lifted)
        funnel_down_out[:, columns] = ADAPTER_SCALE * dot_nn(funnel_lowered[...], hidden)
        funnel_down = funnel_down_ref[:, columns]
        funnel_reduced[...] += dot_nt(funnel_down, hidden)
        sources = jnp.concatenate([hidden, funnel_down], axis=0)
        gradients = jnp.concatenate(
            [
                jnp.concatenate([d_gate, d_lifted], axis=1),
                jnp.concatenate([gate_pull, nothing], axis=1),
                jnp.concatenate([nothing, lifted_pull], axis=1),
            ],
            axis=0,
        )
        per = 512 // (4 * feed_weight.shape[3])
        for piece in range(width // 512):
            near = pl.ds(piece * per, per)
            funnel_rows = feed_weight[near, :, :, :, pl.ds(2 * CHUNK, CHUNK)]
            gate_rows = feed_weight[near, :, :, :, pl.ds(0, 2 * CHUNK)]
            lanes = pl.ds(piece * 512, 512)
            funneled[:, lanes] += dot_nt(sources, funnel_rows.reshape(512, CHUNK))
            d_normed[:, lanes] += dot_nt(
                gradients, gate_rows.reshape(512, 2 * CHUNK)
            )
        return carry

    lax.fori_loop(0, chunks - HEAD_CHUNKS, feed, 0)
    outbox[...] = d_normed[pl.ds(0, tokens)].astype(jnp.bfloat16)
    outs.append(pltpu.make_async_copy(outbox, d_normed_out, out_sems.at[4]))
    outs[-1].start()
    down_out[...] = ADAPTER_SCALE * (
        dot_nn(lowered[...].astype(jnp.bfloat16), normed[pl.ds(0, tokens)])
        - d_normed[pl.ds(tokens, 2 * RANK)]
    )
    floats[...] = funneled[pl.ds(0, tokens)].astype(jnp.bfloat16)
    outs.append(pltpu.make_async_copy(floats, funneled_out, out_sems.at[5]))
    outs[-1].start()
    funnel_up_out[...] = dot_nn(funnel_reduced[...].astype(jnp.bfloat16), back[...])
    funnel_seen_out[...] = funneled[pl.ds(tokens, RANK)]
    finish(chunks - 1, 1 + BLOCKS * (chunks - 1), BLOCKS)
    for out in outs:
        out.wait()


def run_block(shard, normed_one, rows, back, cosine, sine, keep, gain, small):
    size = lax.axis_size("dp")
    line = size // 4
    tokens, width = rows.shape
    blocks, height, _ = shard.shape
    chunks = blocks // BLOCKS
    cut_blocks = (BLOCKS * HEAD_CHUNKS + 1) // 4
    wide = small[2].shape[2]
    anywhere = pl.BlockSpec(memory_space=pl.ANY)
    local = pl.BlockSpec(memory_space=pltpu.VMEM)
    low = jnp.bfloat16
    full = jnp.float32
    out_shape = (
        jax.ShapeDtypeStruct((blocks, line, 2, 2, height, CHUNK), low),
        jax.ShapeDtypeStruct((3 * cut_blocks, tokens, CHUNK), low),
        jax.ShapeDtypeStruct((2 * cut_blocks, tokens, CHUNK), low),
        jax.ShapeDtypeStruct((cut_blocks, tokens, CHUNK), low),
        jax.ShapeDtypeStruct((tokens, width), full),
        jax.ShapeDtypeStruct((tokens, width), low),
        jax.ShapeDtypeStruct((tokens, width), low),
        jax.ShapeDtypeStruct((2, RANK, wide), full),
        jax.ShapeDtypeStruct((2 * RANK, width), full),
        jax.ShapeDtypeStruct((RANK, wide), full),
        jax.ShapeDtypeStruct((RANK, width), full),
        jax.ShapeDtypeStruct((RANK, width), full),
        jax.ShapeDtypeStruct((2, wide), full),
    )
    scratch = [
        pltpu.VMEM((tokens + 2 * RANK, width), low),
        pltpu.VMEM((tokens, width), low),
        pltpu.VMEM((tokens, width), low),
        pltpu.VMEM((3 * cut_blocks, tokens, CHUNK), low),
        pltpu.VMEM((3 * cut_blocks, tokens, CHUNK), low),
        pltpu.VMEM((cut_blocks, tokens, CHUNK), low),
        pltpu.VMEM((2, line, 2, 2, height, CHUNK), low),
        pltpu.VMEM((line, 2, 2, height, 4 * CHUNK), low),
        pltpu.VMEM((tokens, width), full),
        pltpu.VMEM((tokens + 2 * RANK, width), full),
        pltpu.VMEM((tokens + RANK, width), full),
        pltpu.VMEM((tokens, width), low),
        pltpu.VMEM((tokens, width), low),
        pltpu.VMEM((2 * RANK, tokens), full),
        pltpu.VMEM((2 * RANK, tokens), low),
        pltpu.VMEM((RANK, tokens), low),
        pltpu.VMEM((RANK, tokens), full),
        pltpu.SemaphoreType.DMA((chunks + 1, 2 * (line - 1))),
        pltpu.SemaphoreType.DMA((chunks + 1, 2 * (line - 1))),
        pltpu.SemaphoreType.DMA((chunks + 1, 2 * (line - 1))),
        pltpu.SemaphoreType.DMA((chunks + 1, 2 * (line - 1))),
        pltpu.SemaphoreType.DMA((chunks + 1, 2)),
        pltpu.SemaphoreType.DMA((chunks + 1, 2)),
        pltpu.SemaphoreType.DMA((2, 2)),
        pltpu.SemaphoreType.DMA((4,)),
        pltpu.SemaphoreType.DMA((4,)),
        pltpu.SemaphoreType.DMA((tokens // SEQ,)),
        pltpu.SemaphoreType.DMA((tokens // SEQ,)),
        pltpu.SemaphoreType.DMA((6,)),
    ]
    return pl.pallas_call(
        functools.partial(block_kernel, size),
        name="block",
        out_shape=out_shape,
        in_specs=[local] + [anywhere] * 3 + [local] * 11,
        out_specs=[anywhere] * 7 + [local] * 6,
        scratch_shapes=scratch,
        compiler_params=pltpu.CompilerParams(
            collective_id=1, has_side_effects=True, vmem_limit_bytes=60 * 1024 * 1024
        ),
    )(shard, normed_one, rows, back, cosine, sine, keep, gain, *small)


def tail_kernel(
    full,
    turned_ref,
    plain_ref,
    mixed_ref,
    residual_ref,
    d_normed_ref,
    funneled_ref,
    back_ref,
    rows_ref,
    normed_ref,
    cosine_ref,
    sine_ref,
    keep_ref,
    gain_ref,
    entry_down_ref,
    low_lift_ref,
    pull_lift_ref,
    ratio_ref,
    pull_ref,
    mixer_down_ref,
    low_output_ref,
    pull_output_ref,
    output_ratio_ref,
    output_pull_ref,
    funnel_down_ref,
    funnel_up_ref,
    funnel_seen_ref,
    feed_dots_ref,
    partial_out,
    d_residual_out,
    funneled_out,
    down_out,
    up_out,
    mixer_down_out,
    mixer_up_out,
    funnel_down_out,
    funnel_up_out,
    dots_out,
    weights,
    residual,
    floats,
    back,
    normed,
    turned,
    plain,
    mixed,
    own,
    inbox,
    funneled,
    attention,
    d_low,
    d_heads,
    funnel_weight,
    dots_box,
    mixer_dots,
    load_sems,
    weight_sems,
    funnel_sems,
    side_sends,
    side_gets,
    out_sems,
):
    tokens, width = back.shape
    count = tokens // SEQ
    cut = d_heads.shape[2]
    near = cut // CHUNK
    wide = funnel_down_ref.shape[1]
    scale = HEAD_DIM ** (-0.5)
    other = {"tensor": 1 - lax.axis_index("tensor")}
    halves = CHUNK // HEAD_DIM

    loads = [
        pltpu.make_async_copy(source, target, load_sems.at[i])
        for i, (source, target) in enumerate(
            (
                (funneled_ref, funneled),
                (back_ref, back),
                (turned_ref, turned),
                (normed_ref, normed),
                (d_normed_ref, own),
                (residual_ref, residual),
                (rows_ref, floats),
                (mixed_ref, mixed),
                (plain_ref, plain),
            )
        )
    ]
    weight_loads = [
        pltpu.make_async_copy(
            full.at[near * i + b],
            weights.at[i, :, :, :, :, pl.ds(b * CHUNK, CHUNK)],
            weight_sems.at[near * i + b],
        )
        for i in range(4)
        for b in range(near)
    ]
    for load in loads[:3]:
        load.start()
    barrier = pltpu.get_barrier_semaphore()
    pl.semaphore_signal(barrier, inc=1, device_id=other, device_id_type=MESH)
    pl.semaphore_wait(barrier, 1)

    def remote(source, target, index):
        return pltpu.make_async_remote_copy(
            src_ref=source,
            dst_ref=target,
            send_sem=side_sends.at[index],
            recv_sem=side_gets.at[index],
            device_id=other,
            device_id_type=MESH,
        )

    def rows_of(part):
        return pl.ds(part * SEQ, SEQ)

    part_copies = [
        remote(d_normed_ref.at[rows_of(part)], inbox.at[rows_of(part)], part)
        for part in range(count)
    ]
    part_copies[0].start()
    for load in loads[3:] + weight_loads:
        load.start()
    dots_copy = remote(dots_box.at[0], dots_box.at[1], count)
    funneled_copy = remote(funneled_ref, funneled_out, count + 1)

    def weight_of(i):
        return weights[i].reshape(width, cut)

    loads[0].wait()
    loads[1].wait()
    tile = 64

    def count_dots(index, total):
        place = pl.ds(pl.multiple_of(index * tile, tile), tile)
        return total + jnp.sum(
            back[place].astype(jnp.float32) * funneled[place].astype(jnp.float32),
            axis=0,
            keepdims=True,
        )

    funnel_dots = lax.fori_loop(
        0, tokens // tile, count_dots, jnp.zeros((1, width), jnp.float32)
    )
    dots_box[0] = jnp.broadcast_to(funnel_dots, dots_box.shape[1:])
    dots_copy.start()
    loads[2].wait()
    line_up = lax.broadcasted_iota(jnp.int32, (SEQ, SEQ), 0)
    line_on = lax.broadcasted_iota(jnp.int32, (SEQ, SEQ), 1)

    def attend(block, carry):
        for part in range(count):
            place = rows_of(part)
            allowed = ((line_up >= line_on) & (keep_ref[part] > 0)) | (line_up == line_on)
            for half in range(halves):
                lanes = slice(half * HEAD_DIM, (half + 1) * HEAD_DIM)
                scores = dot_nt(
                    turned[block, place, lanes], turned[near + block, place, lanes]
                ) * scale
                masked = jnp.where(allowed, scores, MASKED)
                top = jnp.max(masked, axis=1, keepdims=True)
                weight = jnp.exp(masked - top)
                attention[part, halves * block + half] = weight / jnp.sum(
                    weight, axis=1, keepdims=True
                )
        return carry

    lax.fori_loop(0, near, attend, 0)
    for copy in part_copies[1:]:
        copy.start()

    def funnel_load(block, slot):
        return pltpu.make_async_copy(
            full.at[4 * near + BLOCKS * block + 2], funnel_weight.at[slot], funnel_sems.at[slot]
        )

    funnel_load(0, 0).start()
    for load in loads[3:] + weight_loads:
        load.wait()
    head_seen = [
        dot_nn(entry_down_ref[pl.ds(RANK * i, RANK)], weight_of(i)) for i in range(3)
    ]
    mixer_seen = dot_nt(mixer_down_ref[...], weight_of(3))
    reduced = dot_nt(entry_down_ref[...], normed[...]).astype(jnp.bfloat16)
    dots_copy.wait()
    funnel_dots = dots_box[0, 0:1] + dots_box[1, 0:1]
    funnel_pull = (pull_output_ref[1] * funnel_dots).astype(jnp.bfloat16)

    def correct(block, carry):
        slot = lax.rem(block, 2)

        @pl.when(block < wide // CHUNK - 1)
        def _():
            funnel_load(block + 1, 1 - slot).start()

        funnel_load(block, slot).wait()
        columns = pl.ds(pl.multiple_of(block * CHUNK, CHUNK), CHUNK)
        funnel_down_out[:, columns] = funnel_down_ref[:, columns] - ADAPTER_SCALE * dot_nn(
            funnel_pull, funnel_weight[slot].reshape(width, CHUNK)
        )
        return carry

    lax.fori_loop(0, wide // CHUNK, correct, 0)
    funnel_up_out[...] = ADAPTER_SCALE * (
        funnel_up_ref[...] * output_ratio_ref[1:2]
        - funnel_seen_ref[...] * (output_pull_ref[1:2] * funnel_dots)
    )
    mixer_dots[...] = jnp.zeros_like(mixer_dots)
    small = 32
    for part in range(count):
        part_copies[part].wait()
        if part == count - 1:
            funneled_copy.start()

        def pull_back(index, carry, part=part):
            place = pl.ds(pl.multiple_of(part * SEQ + index * small, small), small)
            value = residual[place]
            weighted = gain_ref[...] * (
                own[place].astype(jnp.float32) + inbox[place].astype(jnp.float32)
            )
            root = lax.rsqrt(jnp.mean(value * value, axis=1, keepdims=True) + NORM_EPS)
            along = jnp.mean(value * weighted, axis=1, keepdims=True)
            gradient = back[place].astype(jnp.float32) + (
                root * weighted - value * (root * root * root * along)
            )
            rounded = gradient.astype(jnp.bfloat16)
            d_low[place] = rounded
            attended = value - floats[place].astype(jnp.float32)
            mixer_dots[...] += jnp.sum(
                (rounded.astype(jnp.float32) * attended).reshape(small // 8, 8, width), axis=0
            )
            residual[place] = gradient
            return carry

        lax.fori_loop(0, SEQ // small, pull_back, 0)
        place = rows_of(part)

        def attend_back(block, carry, part=part, place=place):
            columns = pl.ds(pl.multiple_of(block * CHUNK, CHUNK), CHUNK)
            mixer = weights[3, :, :, :, :, columns].reshape(width, CHUNK)
            d_mixed = dot_nn(d_low[place], mixer).astype(jnp.bfloat16)
            for half in range(halves):
                lanes = slice(half * HEAD_DIM, (half + 1) * HEAD_DIM)
                spot = pl.ds(
                    pl.multiple_of(block * CHUNK + half * HEAD_DIM, HEAD_DIM), HEAD_DIM
                )
                weight = attention[part, halves * block + half]
                d_head = d_mixed[:, lanes]
                d_attention = dot_nt(d_head, turned[2 * near + block, place, lanes])
                d_heads[2, place, spot] = dot_nn(
                    weight.astype(jnp.bfloat16).T, d_head
                ).astype(jnp.bfloat16)
                inner = jnp.sum(weight * d_attention, axis=1, keepdims=True)
                d_scores = (weight * (d_attention - inner)).astype(jnp.bfloat16)
                d_query = dot_nn(d_scores, turned[near + block, place, lanes]) * scale
                d_key = dot_nn(d_scores.T, turned[block, place, lanes]) * scale
                for i, value in ((0, d_query), (1, d_key)):
                    d_heads[i, place, spot] = (
                        value * cosine_ref[place]
                        - pltpu.roll(value, HEAD_DIM // 2, 1) * sine_ref[place]
                    ).astype(jnp.bfloat16)
            return carry

        lax.fori_loop(0, near, attend_back, 0)
    d_residual_copy = pltpu.make_async_copy(residual, d_residual_out, out_sems.at[0])
    d_residual_copy.start()
    per = 512 // (4 * weights.shape[4])
    for i in range(3):
        dots = []
        for block in range(near):
            lanes = slice(block * CHUNK, (block + 1) * CHUNK)
            source = plain if i < 2 else turned
            dots.append(
                jnp.sum(
                    d_heads[i, :tokens, lanes].astype(jnp.float32)
                    * source[near * i + block].astype(jnp.float32),
                    axis=0,
                    keepdims=True,
                )
            )
        dots = jnp.concatenate(dots, axis=1)
        dots_out[4 + i : 5 + i] = dots
        pulled = (pull_lift_ref[i] * dots).astype(jnp.bfloat16)
        up_out[i] = ADAPTER_SCALE * (
            dot_nn(reduced[RANK * i : RANK * (i + 1)], d_heads[i, :tokens]) * ratio_ref[i : i + 1]
            - head_seen[i] * (pull_ref[i : i + 1] * dots)
        )
        lowered = dot_nt(low_lift_ref[i], d_heads[i, :tokens]).astype(jnp.bfloat16)
        down_out[pl.ds(RANK * i, RANK)] = ADAPTER_SCALE * dot_nn(lowered, normed[...])
        d_heads[i, tokens:] = pulled
    for piece in range(width // 512):
        lanes = slice(piece * 512, (piece + 1) * 512)
        results = [
            dot_nt(d_heads[i], weights[i, pl.ds(piece * per, per)].reshape(512, cut))
            for i in range(3)
        ]
        own[:, lanes] = (
            results[0][:tokens] + results[1][:tokens] + results[2][:tokens]
        ).astype(jnp.bfloat16)
        for i in range(3):
            down_out[pl.ds(RANK * i, RANK), lanes] -= ADAPTER_SCALE * results[i][tokens:]
    partial_copy = pltpu.make_async_copy(own, partial_out, out_sems.at[1])
    partial_copy.start()
    mixer_total = jnp.sum(mixer_dots[...], axis=0, keepdims=True)
    joined = jnp.concatenate([mixed[b] for b in range(near)], axis=1)
    lowered = dot_nt(low_output_ref[...], d_low[...]).astype(jnp.bfloat16)
    pulled = (pull_output_ref[0] * mixer_total).astype(jnp.bfloat16)
    mixer_down_out[...] = ADAPTER_SCALE * (
        dot_nn(lowered, joined) - dot_nn(pulled, weight_of(3))
    )
    reduced_mixed = dot_nt(mixer_down_ref[...], joined).astype(jnp.bfloat16)
    mixer_up_out[...] = ADAPTER_SCALE * (
        dot_nn(reduced_mixed, d_low[...]) * output_ratio_ref[0:1]
        - mixer_seen * (output_pull_ref[0:1] * mixer_total)
    )
    for i, value in enumerate((mixer_total, funnel_dots)):
        for r in range(2):
            dots_out[2 * i + r : 2 * i + r + 1] = value[:, r * LANES : (r + 1) * LANES]
    row = 7
    for i in range(2):
        for start in range(0, wide, LANES):
            size = min(LANES, wide - start)
            dots_out[row : row + 1, pl.ds(0, size)] = feed_dots_ref[
                i : i + 1, pl.ds(start, size)
            ]
            if size < LANES:
                dots_out[row : row + 1, pl.ds(size, LANES - size)] = jnp.zeros(
                    (1, LANES - size), jnp.float32
                )
            row += 1
    if row < dots_out.shape[0]:
        dots_out[row:] = jnp.zeros((dots_out.shape[0] - row, LANES), jnp.float32)
    d_residual_copy.wait()
    partial_copy.wait()
    funneled_copy.wait()


def run_tail(big, small, lines):
    full, turned, plain, mixed, residual = big[:5]
    tokens, width = residual.shape
    line, height = full.shape[1], full.shape[4]
    near = mixed.shape[0]
    cut = near * CHUNK
    wide = small[14].shape[1]
    count = tokens // SEQ
    anywhere = pl.BlockSpec(memory_space=pl.ANY)
    local = pl.BlockSpec(memory_space=pltpu.VMEM)
    low, full_type = jnp.bfloat16, jnp.float32
    heads = cut // HEAD_DIM
    return pl.pallas_call(
        tail_kernel,
        name="tail",
        out_shape=(
            jax.ShapeDtypeStruct((tokens, width), low),
            jax.ShapeDtypeStruct((tokens, width), full_type),
            jax.ShapeDtypeStruct((tokens, width), low),
            jax.ShapeDtypeStruct((3 * RANK, width), full_type),
            jax.ShapeDtypeStruct((3, RANK, cut), full_type),
            jax.ShapeDtypeStruct((RANK, cut), full_type),
            jax.ShapeDtypeStruct((RANK, width), full_type),
            jax.ShapeDtypeStruct((RANK, wide), full_type),
            jax.ShapeDtypeStruct((RANK, width), full_type),
            jax.ShapeDtypeStruct((lines, LANES), full_type),
        ),
        in_specs=[anywhere] * 10 + [local] * 18,
        out_specs=[anywhere] * 3 + [local] * 7,
        scratch_shapes=[
            pltpu.VMEM((4, line, 2, 2, height, cut), low),
            pltpu.VMEM((tokens, width), full_type),
            pltpu.VMEM((tokens, width), low),
            pltpu.VMEM((tokens, width), low),
            pltpu.VMEM((tokens, width), low),
            pltpu.VMEM(turned.shape, low),
            pltpu.VMEM(plain.shape, low),
            pltpu.VMEM(mixed.shape, low),
            pltpu.VMEM((tokens, width), low),
            pltpu.VMEM((tokens, width), low),
            pltpu.VMEM((tokens, width), low),
            pltpu.VMEM((count, heads, SEQ, SEQ), full_type),
            pltpu.VMEM((tokens, width), low),
            pltpu.VMEM((3, tokens + RANK, cut), low),
            pltpu.VMEM((2, line, 2, 2, height, CHUNK), low),
            pltpu.VMEM((2, 8, width), full_type),
            pltpu.VMEM((8, width), full_type),
            pltpu.SemaphoreType.DMA((9,)),
            pltpu.SemaphoreType.DMA((4 * near,)),
            pltpu.SemaphoreType.DMA((2,)),
            pltpu.SemaphoreType.DMA((count + 2,)),
            pltpu.SemaphoreType.DMA((count + 2,)),
            pltpu.SemaphoreType.DMA((2,)),
        ],
        compiler_params=pltpu.CompilerParams(
            collective_id=2, has_side_effects=True, vmem_limit_bytes=62 * 1024 * 1024
        ),
    )(*big, *small)


def place_in(target, base, offset, value):
    width = target.shape[1]
    start = 0
    while start < value.shape[1]:
        group, lane = divmod(offset + start, width)
        size = min(value.shape[1] - start, width - lane)
        target[pl.ds(base + RANK * group, RANK), pl.ds(lane, size)] = value[
            :, start : start + size
        ].astype(target.dtype)
        start += size


def take_from(source, base, offset, size):
    width = source.shape[1]
    pieces = []
    start = 0
    while start < size:
        group, lane = divmod(offset + start, width)
        count = min(size - start, width - lane)
        pieces.append(
            source[pl.ds(base + RANK * group, RANK), pl.ds(lane, count)].astype(jnp.float32)
        )
        start += count
    return pieces[0] if len(pieces) == 1 else jnp.concatenate(pieces, axis=1)


def sum_kernel(
    size,
    sides,
    widths,
    down_ref,
    feed_down_ref,
    mixer_up_ref,
    funnel_up_ref,
    up_ref,
    feed_up_ref,
    mixer_down_ref,
    funnel_down_ref,
    dots_ref,
    magnitude_ref,
    total,
    norm_out,
    gathered,
    side_box,
    norm_box,
    *rest,
):
    bits = len(widths)
    outboxes, inboxes = rest[:bits], rest[bits : 2 * bits]
    sends, receives = rest[2 * bits :]
    half = gathered.shape[0] // 2
    me = lax.axis_index("dp")
    side = lax.axis_index("tensor")
    partners = partners_of(size)
    greet_sum(size, sides)

    def remote(source, target, index, where):
        return pltpu.make_async_remote_copy(
            src_ref=source,
            dst_ref=target,
            send_sem=sends.at[index],
            recv_sem=receives.at[index],
            device_id=where,
            device_id_type=MESH,
        )

    row = 0
    for ref in (down_ref, feed_down_ref, mixer_up_ref, funnel_up_ref):
        gathered[pl.ds(row, ref.shape[0])] = ref[...]
        row += ref.shape[0]
    offset = 0
    split = [up_ref[i] for i in range(3)] + [feed_up_ref[i] for i in range(2)]
    split += [mixer_down_ref[...], funnel_down_ref[...], dots_ref[...]]
    for value in split:
        place_in(gathered, half, offset, value)
        offset += value.shape[1]
    rest_columns = half // RANK * gathered.shape[1] - offset
    place_in(gathered, half, offset, jnp.zeros((RANK, rest_columns), jnp.float32))

    start = 0
    width = gathered.shape[1]
    marks = []
    for step in range(bits):
        bit = lax.rem(lax.div(me, 2**step), 2)
        where = {"dp": partners[step]}
        if widths[step] < width:
            width = widths[step]
            marks.append((step, bit, width))
            mine = pl.ds(pl.multiple_of(start + bit * width, 128), width)
            theirs = pl.ds(pl.multiple_of(start + (1 - bit) * width, 128), width)
            outboxes[step][...] = gathered[:, theirs].astype(jnp.bfloat16)
            copy = remote(outboxes[step], inboxes[step], step, where)
            copy.start()
            copy.wait()
            gathered[:, mine] += inboxes[step][...].astype(jnp.float32)
            start = start + bit * width
        else:
            mine = pl.ds(pl.multiple_of(start, 128), width)
            outboxes[step][...] = gathered[:, mine].astype(jnp.bfloat16)
            copy = remote(outboxes[step], inboxes[step], step, where)
            copy.start()
            copy.wait()
            gathered[:, mine] = outboxes[step][...].astype(jnp.float32) + inboxes[step][
                ...
            ].astype(jnp.float32)
    mine = pl.ds(pl.multiple_of(start, 128), width)
    side_box[0] = gathered[pl.ds(0, half), mine].astype(jnp.bfloat16)
    shared = side_box[0].astype(jnp.float32)
    for step in range(1, sides):
        copy = remote(
            side_box.at[0],
            side_box.at[step],
            bits + step - 1,
            {"tensor": lax.rem(side + step, sides)},
        )
        copy.start()
        copy.wait()
        shared += side_box[step].astype(jnp.float32)
    total[pl.ds(0, half), mine] = shared.astype(jnp.bfloat16)
    total[pl.ds(half, half), mine] = gathered[pl.ds(half, half), mine].astype(jnp.bfloat16)
    index = bits + sides - 1
    for step, bit, width in reversed(marks):
        mine = pl.ds(pl.multiple_of(start, 128), width)
        copy = remote(
            total.at[:, mine], total.at[:, mine], index, {"dp": partners[step]}
        )
        copy.start()
        copy.wait()
        index += 1
        start = start - bit * width
    squares = jnp.zeros((RANK, 1), jnp.float32)
    for row in range(0, half, RANK):
        value = total[pl.ds(row, RANK)].astype(jnp.float32)
        squares += jnp.sum(value * value, axis=1, keepdims=True)
    lines = dots_ref.shape[1]
    dots_offset = offset - lines
    dots = take_from(total, half, dots_offset, lines) / magnitude_ref[...]
    dots = jnp.sum(dots * dots, axis=1, keepdims=True)
    shared_total = jnp.sum(squares) + jnp.sum(dots[:4])
    split_squares = jnp.zeros((RANK, 1), jnp.float32)
    start = 0
    while start < dots_offset:
        count = min(dots_offset - start, gathered.shape[1])
        value = take_from(total, half, start, count)
        split_squares += jnp.sum(value * value, axis=1, keepdims=True)
        start += count
    split_total = jnp.sum(split_squares) + jnp.sum(dots[4:])
    norm_box[0] = jnp.full(norm_box.shape[1:], split_total, jnp.float32)
    for step in range(1, sides):
        copy = remote(
            norm_box.at[0],
            norm_box.at[step],
            index + step - 1,
            {"tensor": lax.rem(side + step, sides)},
        )
        copy.start()
        copy.wait()
    split_sum = norm_box[0]
    for step in range(1, sides):
        split_sum = split_sum + norm_box[step]
    norm_out[...] = jnp.sqrt(split_sum + shared_total)


def sum_all(parts, magnitudes):
    size = lax.axis_size("dp")
    sides = lax.axis_size("tensor")
    width = parts[0].shape[1]
    rows = sum(part.shape[0] for part in parts[:4])
    bits = len(bin(size)) - 3
    widths = [max(width >> (step + 1), 128) for step in range(bits)]
    halvings = sum(1 for step in range(bits) if width >> (step + 1) >= 128)
    boxes = [pltpu.VMEM((2 * rows, w), jnp.bfloat16) for w in widths]
    copies = bits + halvings + 2 * (sides - 1)
    return pl.pallas_call(
        functools.partial(sum_kernel, size, sides, widths),
        name="sum",
        out_shape=(
            jax.ShapeDtypeStruct((2 * rows, width), jnp.bfloat16),
            jax.ShapeDtypeStruct((8, 128), jnp.float32),
        ),
        in_specs=[pl.BlockSpec(memory_space=pltpu.VMEM)] * 10,
        out_specs=[pl.BlockSpec(memory_space=pltpu.VMEM)] * 2,
        scratch_shapes=[
            pltpu.VMEM((2 * rows, width), jnp.float32),
            pltpu.VMEM((sides, rows, widths[-1]), jnp.bfloat16),
            pltpu.VMEM((sides, 8, 128), jnp.float32),
            *boxes,
            *boxes,
            pltpu.SemaphoreType.DMA((copies,)),
            pltpu.SemaphoreType.DMA((copies,)),
        ],
        compiler_params=pltpu.CompilerParams(
            collective_id=3, has_side_effects=True, vmem_limit_bytes=32 * 1024 * 1024
        ),
    )(*parts, magnitudes)


def update_kernel(*refs):
    total, norm_ref = refs[:2]
    values, firsts, seconds = refs[2:11], refs[11:20], refs[20:29]
    fresh, momenta, variances = refs[29:38], refs[38:47], refs[47:56]
    factor = jnp.minimum(1.0, CLIP / (norm_ref[0:1, 0:1] + 1e-06))
    half = total.shape[0] // 2
    cut, wide = values[1].shape[2], values[2].shape[2]

    def update(index, rate, piece, gradient):
        value, momentum, variance = decoupled_update(
            values[index][piece], gradient * factor, firsts[index][piece], seconds[index][piece], rate
        )
        fresh[index][piece] = value
        momenta[index][piece] = momentum
        variances[index][piece] = variance

    def shared(group):
        return total[pl.ds(RANK * group, RANK)].astype(jnp.float32)

    for i in range(5):
        update(0, RATE_FACTOR, i, shared(i))
    for i in range(2):
        update(5, RATE_LIFT, i, shared(5 + i))
    offset = 0
    for i in range(3):
        update(1, RATE_LIFT, i, take_from(total, half, offset, cut))
        offset += cut
    for i in range(2):
        update(2, RATE_LIFT, i, take_from(total, half, offset, wide))
        offset += wide
    update(3, RATE_FACTOR, Ellipsis, take_from(total, half, offset, cut))
    offset += cut
    update(4, RATE_FACTOR, Ellipsis, take_from(total, half, offset, wide))
    offset += wide
    dots = take_from(total, half, offset, LANES)

    def long(row, size):
        count = -(-size // LANES)
        return jnp.concatenate([dots[row + r : row + r + 1] for r in range(count)], axis=1)[
            :, :size
        ]

    width = total.shape[1]
    for i in range(2):
        piece = slice(i, i + 1)
        update(8, RATE_LOUD, piece, long(2 * i, width) / values[8][piece])
    for i in range(3):
        piece = slice(i, i + 1)
        update(6, RATE_SCALE, piece, long(4 + i, cut) / values[6][piece])
    lines = -(-wide // LANES)
    for i in range(2):
        piece = slice(i, i + 1)
        update(7, RATE_SCALE, piece, long(7 + lines * i, wide) / values[7][piece])


def update_all(total, norm, params, firsts, seconds):
    shapes = tuple(jax.ShapeDtypeStruct(p.shape, p.dtype) for p in params)
    return pl.pallas_call(
        update_kernel,
        name="update",
        out_shape=shapes * 3,
        in_specs=[pl.BlockSpec(memory_space=pltpu.VMEM)] * 29,
        out_specs=[pl.BlockSpec(memory_space=pltpu.VMEM)] * 27,
        compiler_params=pltpu.CompilerParams(vmem_limit_bytes=48 * 1024 * 1024),
    )(total, norm, *params, *firsts, *seconds)


def body(
    activations,
    cotangent,
    padding_mask,
    positions,
    norm_gains,
    base_query,
    base_key,
    base_value,
    base_gate,
    base_widen,
    base_mixer,
    base_funnel,
    entry_value,
    attend_value,
    widen_value,
    mixer_value,
    funnel_value,
    output_value,
    stature_value,
    amplitude_value,
    loudness_value,
    entry_first,
    attend_first,
    widen_first,
    mixer_first,
    funnel_first,
    output_first,
    stature_first,
    amplitude_first,
    loudness_first,
    entry_second,
    attend_second,
    widen_second,
    mixer_second,
    funnel_second,
    output_second,
    stature_second,
    amplitude_second,
    loudness_second,
):
    params = (
        entry_value,
        attend_value,
        widen_value,
        mixer_value,
        funnel_value,
        output_value,
        stature_value,
        amplitude_value,
        loudness_value,
    )
    firsts = (
        entry_first,
        attend_first,
        widen_first,
        mixer_first,
        funnel_first,
        output_first,
        stature_first,
        amplitude_first,
        loudness_first,
    )
    seconds = (
        entry_second,
        attend_second,
        widen_second,
        mixer_second,
        funnel_second,
        output_second,
        stature_second,
        amplitude_second,
        loudness_second,
    )
    rows = base_query.shape[0]
    width = activations.shape[1]
    place = lax.axis_index("dp") * rows
    cut = base_query.shape[1]
    wide = base_gate.shape[1]
    entry_rows = lax.dynamic_slice_in_dim(entry_value, place, rows, 1)
    output_columns = lax.dynamic_slice_in_dim(output_value, place, rows, 2)
    lifts = [attend_value[0], attend_value[1], attend_value[2], widen_value[0], widen_value[1]]
    pad = -wide % LANES
    magnitudes = jnp.concatenate(
        [
            loudness_value.reshape(-1, LANES),
            stature_value.reshape(-1, LANES),
            jnp.pad(amplitude_value, ((0, 0), (0, pad)), constant_values=1.0).reshape(-1, LANES),
        ]
    )
    magnitudes = jnp.pad(magnitudes, ((0, -magnitudes.shape[0] % 8), (0, 0)), constant_values=1.0)
    shard, squares = merge(
        (base_query, base_key, base_value, base_gate, base_widen, base_mixer, base_funnel),
        entry_rows,
        attend_value,
        widen_value,
        mixer_value,
        funnel_value,
        output_columns,
        magnitudes,
    )
    lines = (wide + pad) // LANES
    shared_norms = jnp.sqrt(squares[:4].reshape(2, width) + COLUMN_EPS)
    split_norms = jnp.sqrt(
        jnp.concatenate(
            [squares[4:7].reshape(-1)]
            + [
                squares[7 + i * lines : 7 + (i + 1) * lines].reshape(-1)[:wide]
                for i in range(2)
            ]
        )
        + COLUMN_EPS
    )
    split_wide = split_norms.shape[0]
    split_magnitudes = jnp.concatenate([stature_value.reshape(-1), amplitude_value.reshape(-1)])
    split_ratio = split_magnitudes / split_norms
    shared_ratio = loudness_value / shared_norms
    floats = activations.astype(jnp.float32)
    normed_one = low(root_norm(floats, norm_gains[0]))
    count = activations.shape[0] // SEQ
    half = jnp.arange(HEAD_DIM // 2, dtype=jnp.float32)
    angles = positions.astype(jnp.float32)[:, None] * (ROPE_BASE ** (-2.0 * half / HEAD_DIM))[None]
    cosine = jnp.tile(jnp.cos(angles), (1, 2))
    sine = jnp.sin(angles)
    sine = jnp.concatenate([-sine, sine], axis=1)
    keep = padding_mask.reshape(count, 1, SEQ)
    feed_ratio = split_ratio[3 * cut :].reshape(2, wide)
    feed_pull = 1.0 / (split_norms[3 * cut :] * split_magnitudes[3 * cut :]).reshape(2, wide)
    entry_down = low(jnp.swapaxes(entry_value, 1, 2))
    small = (
        entry_down[3:].reshape(2 * RANK, width),
        low(funnel_value.T),
        low(widen_value * feed_ratio[:, None]),
        widen_value * feed_pull[:, None],
        feed_ratio,
        feed_pull,
        low(output_value[1] * shared_ratio[1]),
    )
    (
        full,
        turned,
        plain,
        mixed,
        residual,
        d_normed_two,
        funneled,
        feed_ups,
        feed_downs,
        funnel_down,
        funnel_up,
        funnel_seen,
        feed_dots,
    ) = run_block(
        shard, normed_one, activations, cotangent, cosine, sine, keep, norm_gains[1:2], small
    )
    head_pull = 1.0 / (split_norms[: 3 * cut] * split_magnitudes[: 3 * cut]).reshape(3, cut)
    head_ratio = split_ratio[: 3 * cut].reshape(3, cut)
    shared_pull = 1.0 / (shared_norms * loudness_value)
    small = (
        cosine,
        sine,
        keep,
        norm_gains[1:2],
        entry_down[:3].reshape(3 * RANK, width),
        low(attend_value * head_ratio[:, None]),
        attend_value * head_pull[:, None],
        head_ratio,
        head_pull,
        low(mixer_value.T),
        low(output_value[0] * shared_ratio[0]),
        output_value * shared_pull[:, None],
        shared_ratio,
        shared_pull,
        funnel_down,
        funnel_up,
        funnel_seen,
        feed_dots,
    )
    big = (
        full,
        turned,
        plain,
        mixed,
        residual,
        d_normed_two,
        funneled,
        cotangent,
        activations,
        normed_one,
    )
    (
        partial,
        d_residual,
        funneled_other,
        head_downs,
        head_ups,
        mixer_down,
        mixer_up,
        funnel_down,
        funnel_up,
        dots,
    ) = run_tail(big, small, squares.shape[0])
    d_normed_one = swap(partial)
    total, norm = sum_all(
        (
            head_downs,
            feed_downs,
            mixer_up,
            funnel_up,
            head_ups,
            feed_ups,
            mixer_down,
            funnel_down,
            dots,
        ),
        magnitudes,
    )

    def turned_over(items):
        return [
            jnp.swapaxes(item, -1, -2) if i in (0, 3, 4) else item for i, item in enumerate(items)
        ]

    results = update_all(total, norm, turned_over(params), turned_over(firsts), turned_over(seconds))
    updated, momenta, variances = (turned_over(results[i : i + 9]) for i in (0, 9, 18))
    gradient_norm = norm[0, 0]
    block_output = low(
        residual + (funneled.astype(jnp.float32) + funneled_other.astype(jnp.float32))
    )
    unused, first_pull = jax.vjp(lambda v: root_norm(v, norm_gains[0]), floats)
    input_gradient = d_residual + first_pull(d_normed_one)[0]
    return (
        block_output,
        input_gradient,
        gradient_norm,
        updated[0],
        updated[1],
        updated[2],
        updated[3],
        updated[4],
        updated[5],
        updated[6],
        updated[7],
        updated[8],
        momenta[0],
        momenta[1],
        momenta[2],
        momenta[3],
        momenta[4],
        momenta[5],
        momenta[6],
        momenta[7],
        momenta[8],
        variances[0],
        variances[1],
        variances[2],
        variances[3],
        variances[4],
        variances[5],
        variances[6],
        variances[7],
        variances[8],
    )


def solution(mesh):
    return jax.shard_map(
        body,
        mesh=mesh,
        in_specs=(
            P("dp", None),
            P("dp", None),
            P("dp"),
            P("dp"),
            P(),
            P("dp", "tensor"),
            P("dp", "tensor"),
            P("dp", "tensor"),
            P("dp", "tensor"),
            P("dp", "tensor"),
            P("tensor", "dp"),
            P("tensor", "dp"),
            P(),
            P(None, None, "tensor"),
            P(None, None, "tensor"),
            P("tensor", None),
            P("tensor", None),
            P(),
            P(None, "tensor"),
            P(None, "tensor"),
            P(),
            P(),
            P(None, None, "tensor"),
            P(None, None, "tensor"),
            P("tensor", None),
            P("tensor", None),
            P(),
            P(None, "tensor"),
            P(None, "tensor"),
            P(),
            P(),
            P(None, None, "tensor"),
            P(None, None, "tensor"),
            P("tensor", None),
            P("tensor", None),
            P(),
            P(None, "tensor"),
            P(None, "tensor"),
            P(),
        ),
        out_specs=(
            P("dp", None),
            P("dp", None),
            P(),
            P(),
            P(None, None, "tensor"),
            P(None, None, "tensor"),
            P("tensor", None),
            P("tensor", None),
            P(),
            P(None, "tensor"),
            P(None, "tensor"),
            P(),
            P(),
            P(None, None, "tensor"),
            P(None, None, "tensor"),
            P("tensor", None),
            P("tensor", None),
            P(),
            P(None, "tensor"),
            P(None, "tensor"),
            P(),
            P(),
            P(None, None, "tensor"),
            P(None, None, "tensor"),
            P("tensor", None),
            P("tensor", None),
            P(),
            P(None, "tensor"),
            P(None, "tensor"),
            P(),
        ),
        check_vma=False,
    )
```

```python
import functools

import jax
import jax.numpy as jnp
from jax import lax
from jax.experimental import pallas as pl
from jax.experimental.pallas import tpu as pltpu
from jax.sharding import PartitionSpec as P

HEAD_DIM = 128
RANK = 16
SEQ = 256
STEP = 5


HIGH_PRECISION = lax.Precision.HIGHEST
ADAPTER_SCALE = 2.0
NORM_EPS = 1e-05
COLUMN_EPS = 1e-06
BETA_ONE = 0.9
BETA_TWO = 0.999
ADAM_EPS = 1e-08
DECAY = 0.01
CLIP = 1.0
RATE_FACTOR = 0.02
RATE_LIFT = 0.2
RATE_SCALE = 0.5
RATE_LOUD = 2.0
ROPE_BASE = 10000.0
MASKED = -1e30


def root_norm(values, gain):
    return values * lax.rsqrt(jnp.mean(values * values, axis=-1, keepdims=True) + NORM_EPS) * gain


def decoupled_update(value, gradient, first, second, rate):
    momentum = BETA_ONE * first + (1.0 - BETA_ONE) * gradient
    variance = BETA_TWO * second + (1.0 - BETA_TWO) * gradient * gradient
    corrected = momentum / (1.0 - BETA_ONE**STEP)
    spread = jnp.sqrt(variance / (1.0 - BETA_TWO**STEP))
    return (value - rate * (corrected / (spread + ADAM_EPS) + DECAY * value), momentum, variance)


def low(values):
    return values.astype(jnp.bfloat16)


MESH = pl.DeviceIdType.MESH
LANES = 1024
VMEM = 62 * 1024 * 1024
CHUNK = 256


def partners_of(size):
    me = lax.axis_index("dp")
    found = []
    bit = 1
    while bit < size:
        down = lax.rem(lax.div(me, bit), 2)
        found.append(me + bit - 2 * bit * down)
        bit *= 2
    return found


def double_sum(total, inbox, sends, receives, size, sides, shared_rows):
    targets = [({"dp": p}, total.shape[0]) for p in partners_of(size)]
    side = lax.axis_index("tensor")
    targets += [
        ({"tensor": lax.rem(side + step, sides)}, shared_rows) for step in range(1, sides)
    ]
    for step, (target, count) in enumerate(targets):
        kept = pl.ds(0, count)
        copy = pltpu.make_async_remote_copy(
            src_ref=total,
            dst_ref=inbox.at[step],
            send_sem=sends.at[step],
            recv_sem=receives.at[step],
            device_id=target,
            device_id_type=MESH,
        )
        copy.start()
        copy.wait()
        total[kept] += inbox[step, kept]


def greet_sum(size, sides):
    barrier = pltpu.get_barrier_semaphore()
    side = lax.axis_index("tensor")
    targets = [{"dp": p} for p in partners_of(size)]
    targets += [{"tensor": lax.rem(side + step, sides)} for step in range(1, sides)]
    for target in targets:
        pl.semaphore_signal(barrier, inc=1, device_id=target, device_id_type=MESH)
    pl.semaphore_wait(barrier, len(targets))


def merge_kernel(
    size,
    sides,
    query_ref,
    key_ref,
    value_ref,
    gate_ref,
    widen_ref,
    mixer_ref,
    funnel_ref,
    entry_ref,
    attend_ref,
    lift_ref,
    mixer_down_ref,
    funnel_down_ref,
    output_ref,
    stature_ref,
    amplitude_ref,
    loudness_ref,
    shard_out,
    squares_out,
    magnitudes_out,
    total,
    inbox,
    direction_cut,
    direction_wide,
    direction_mixer,
    direction_funnel,
    sends,
    receives,
):
    greet_sum(size, sides)
    rows = query_ref.shape[0]
    wide = gate_ref.shape[1]
    me = lax.axis_index("dp")
    total[...] = jnp.zeros_like(total)

    def direction(base, down, up):
        return base.astype(jnp.float32) + ADAPTER_SCALE * lax.dot_general(
            down,
            up,
            (((0,), (0,)), ((), ())),
            precision=HIGH_PRECISION,
            preferred_element_type=jnp.float32,
        )

    magnitudes_out[...] = jnp.ones_like(magnitudes_out)
    for i in range(2):
        for r in range(2):
            magnitudes_out[2 * i + r : 2 * i + r + 1, :] = loudness_ref[
                i : i + 1, r * LANES : (r + 1) * LANES
            ]
    for i in range(3):
        magnitudes_out[4 + i : 5 + i, :] = stature_ref[i : i + 1, :]
    for i in range(2):
        for start in range(0, wide, CHUNK):
            row = 7 + 3 * i + start // LANES
            magnitudes_out[row : row + 1, pl.ds(start % LANES, CHUNK)] = amplitude_ref[
                i : i + 1, pl.ds(start, CHUNK)
            ]

    group = LANES // rows
    lane_group = lax.broadcasted_iota(jnp.int32, (1, LANES), 1) // rows
    for i, (base, down) in enumerate(
        ((mixer_ref, mixer_down_ref), (funnel_ref, funnel_down_ref))
    ):
        held = (direction_mixer, direction_funnel)[i]
        sums = jnp.zeros((1, rows), jnp.float32)
        for start in range(0, base.shape[0], CHUNK):
            piece = pl.ds(start, CHUNK)
            part = direction(base[piece], down[:, piece], output_ref[i])
            held[piece] = part
            sums += jnp.sum(part * part, axis=0, keepdims=True)
        spread = jnp.concatenate([sums] * group, axis=1)
        for r in range(2):
            here = lane_group == me - r * group
            total[2 * i + r : 2 * i + r + 1, :] = jnp.where(here, spread, 0.0)
    for i, base in enumerate((query_ref, key_ref, value_ref)):
        for start in range(0, LANES, CHUNK):
            piece = pl.ds(start, CHUNK)
            part = direction(base[:, piece], entry_ref[i], attend_ref[i, :, piece])
            direction_cut[i, :, piece] = part
            total[4 + i : 5 + i, piece] = jnp.sum(part * part, axis=0, keepdims=True)
    for i, base in enumerate((gate_ref, widen_ref)):
        for start in range(0, wide, CHUNK):
            piece = pl.ds(start, CHUNK)
            part = direction(base[:, piece], entry_ref[3 + i], lift_ref[i, :, piece])
            direction_wide[i, :, piece] = part
            row = 7 + 3 * i + start // LANES
            total[row : row + 1, pl.ds(start % LANES, CHUNK)] = jnp.sum(
                part * part, axis=0, keepdims=True
            )
    double_sum(total, inbox, sends, receives, size, sides, 4)
    squares_out[...] = total[...]
    ratio = magnitudes_out[...] / jnp.sqrt(total[...] + COLUMN_EPS)
    near = LANES // CHUNK
    for i in range(3):
        for b in range(near):
            lanes = slice(b * CHUNK, (b + 1) * CHUNK)
            shard_out[near * i + b] = (
                direction_cut[i, :, lanes] * ratio[4 + i : 5 + i, lanes]
            ).astype(jnp.bfloat16)
    for i in range(2):
        for start in range(0, wide, CHUNK):
            row = 7 + 3 * i + start // LANES
            shard_out[4 * near + 3 * (start // CHUNK) + i] = (
                direction_wide[i, :, pl.ds(start, CHUNK)]
                * ratio[row : row + 1, start % LANES : start % LANES + CHUNK]
            ).astype(jnp.bfloat16)
    for i, held in enumerate((direction_mixer, direction_funnel)):
        own = jnp.zeros((1, rows), jnp.float32)
        for r in range(2):
            for g in range(group):
                own += jnp.where(
                    me == r * group + g,
                    ratio[2 * i + r : 2 * i + r + 1, g * rows : (g + 1) * rows],
                    0.0,
                )
        for start in range(0, held.shape[0], CHUNK):
            part = (held[pl.ds(start, CHUNK)] * own).T.astype(jnp.bfloat16)
            if i == 0:
                shard_out[3 * near + start // CHUNK] = part
            else:
                shard_out[4 * near + 3 * (start // CHUNK) + 2] = part


def merge(bases, entry_rows, attend, widen, mixer_down, funnel_down, output_columns, scales):
    size = lax.axis_size("dp")
    sides = lax.axis_size("tensor")
    rows, cut = bases[0].shape
    wide = bases[3].shape[1]
    steps = len(bin(size)) - 3 + sides - 1
    lines = 16
    return pl.pallas_call(
        functools.partial(merge_kernel, size, sides),
        name="merge",
        out_shape=(
            jax.ShapeDtypeStruct(((4 * cut + 3 * wide) // CHUNK, rows, CHUNK), jnp.bfloat16),
            jax.ShapeDtypeStruct((lines, LANES), jnp.float32),
            jax.ShapeDtypeStruct((lines, LANES), jnp.float32),
        ),
        in_specs=[pl.BlockSpec(memory_space=pltpu.VMEM)] * 16,
        out_specs=[pl.BlockSpec(memory_space=pltpu.VMEM)] * 3,
        scratch_shapes=[
            pltpu.VMEM((lines, LANES), jnp.float32),
            pltpu.VMEM((steps, lines, LANES), jnp.float32),
            pltpu.VMEM((3, rows, cut), jnp.float32),
            pltpu.VMEM((2, rows, wide), jnp.float32),
            pltpu.VMEM((cut, rows), jnp.float32),
            pltpu.VMEM((wide, rows), jnp.float32),
            pltpu.SemaphoreType.DMA((steps,)),
            pltpu.SemaphoreType.DMA((steps,)),
        ],
        compiler_params=pltpu.CompilerParams(
            collective_id=0, has_side_effects=True, vmem_limit_bytes=VMEM
        ),
    )(*bases, entry_rows, attend, widen, mixer_down, funnel_down, output_columns, *scales)


def dot_nn(left, right):
    return jnp.dot(left, right, preferred_element_type=jnp.float32)


def dot_nt(left, right):
    return lax.dot_general(
        left, right, (((1,), (1,)), ((), ())), preferred_element_type=jnp.float32
    )


def long_row(lines, row, size):
    count = -(-size // LANES)
    return jnp.concatenate([lines[row + r : row + r + 1] for r in range(count)], axis=1)[:, :size]


BLOCKS = 3
HEAD_CHUNKS = 5
EXTRA_TICKS = 3


def gather_parts(size, shard, full, sems):
    line = size // 4
    early = 16
    late = shard.shape[1] - early
    me = lax.axis_index("dp")
    core, column, spot = lax.rem(me, 2), lax.rem(lax.div(me, 2), 2), lax.div(me, 4)
    right_sends, left_sends, right_gets, left_gets, pair_sems, core_sems, early_sems = sems

    def device(other_spot, other_column, other_core):
        return {"dp": (other_spot * 2 + other_column) * 2 + other_core}

    right = device(lax.rem(spot + 1, line), column, core)
    left = device(lax.rem(spot + line - 1, line), column, core)
    across = device(spot, 1 - column, core)
    twin = device(spot, column, 1 - core)

    def greet():
        barrier = pltpu.get_barrier_semaphore()
        ahead, behind = spot < line - 1, spot > 0

        @pl.when(ahead)
        def _():
            pl.semaphore_signal(barrier, inc=1, device_id=right, device_id_type=MESH)

        @pl.when(behind)
        def _():
            pl.semaphore_signal(barrier, inc=1, device_id=left, device_id_type=MESH)

        for target in (across, twin, {"tensor": 1 - lax.axis_index("tensor")}):
            pl.semaphore_signal(barrier, inc=1, device_id=target, device_id_type=MESH)
        peers = 3 + ahead.astype(jnp.int32) + behind.astype(jnp.int32)
        pl.semaphore_wait(barrier, peers)

    def remote(source, target, send, get, where):
        return pltpu.make_async_remote_copy(
            src_ref=source,
            dst_ref=target,
            send_sem=send,
            recv_sem=get,
            device_id=where,
            device_id_type=MESH,
        )

    def early_copy(part, owner):
        first = 1 + BLOCKS
        blocks = pl.ds(0, first) if part == 0 else pl.ds(first, shard.shape[0] - first)
        return remote(
            shard.at[blocks, pl.ds(0, early)],
            full.at[blocks, spot, owner, core, pl.ds(0, early)],
            early_sems.at[part, 0],
            early_sems.at[part, 1],
            across,
        )

    def early_start():
        for part in range(2):
            early_copy(part, column).start()

    def early_wait(part):
        early_copy(part, 1 - column).wait_recv()
        early_copy(part, column).wait_send()

    def place_of(part, origin, blocks):
        if part == 0:
            return full.at[blocks, origin, column, core, pl.ds(early, late)]
        return full.at[blocks, origin, :, core, pl.ds(0, early)]

    def moves(to_right, hop, chunk, start, count):
        sends, gets = (right_sends, right_gets) if to_right else (left_sends, left_gets)
        blocks = pl.ds(start, count)
        found = []
        for part in range(2):
            place = place_of(part, spot - hop if to_right else spot + hop, blocks)
            source = shard.at[blocks, pl.ds(early, late)] if hop == 0 and part == 0 else place
            found.append(
                remote(
                    source,
                    place,
                    sends.at[chunk, 2 * hop + part],
                    gets.at[chunk, 2 * hop + part],
                    right if to_right else left,
                )
            )
        return found

    def arrivals(to_right, hop, chunk, start, count):
        gets = right_gets if to_right else left_gets
        for part in range(2):
            place = place_of(part, spot - hop if to_right else spot + hop, pl.ds(start, count))
            kept = 2 * (hop - 1) + part
            remote(
                place, place, right_sends.at[chunk, kept], gets.at[chunk, kept], right
            ).wait_recv()

    def pair_copy(chunk, start, count, owner):
        place = full.at[pl.ds(start, count), :, owner, core, pl.ds(early, late)]
        return remote(place, place, pair_sems.at[chunk, 0], pair_sems.at[chunk, 1], across)

    def core_copy(chunk, start, count, owner):
        place = full.at[pl.ds(start, count), :, :, owner]
        return remote(place, place, core_sems.at[chunk, 0], core_sems.at[chunk, 1], twin)

    def send_on(hop, chunk, start, count):
        @pl.when((spot >= hop) & (spot < line - 1))
        def _():
            for copy in moves(True, hop, chunk, start, count):
                copy.start()

        @pl.when((spot < line - hop) & (spot > 0))
        def _():
            for copy in moves(False, hop, chunk, start, count):
                copy.start()

    def take_in(hop, chunk, start, count):
        @pl.when(spot >= hop)
        def _():
            arrivals(True, hop, chunk, start, count)

        @pl.when(spot < line - hop)
        def _():
            arrivals(False, hop, chunk, start, count)

    def step(phase, chunk, start, count):
        if 1 <= phase < line:
            take_in(phase, chunk, start, count)
        if phase < line - 1:
            send_on(phase, chunk, start, count)
        if phase == line - 1:
            pair_copy(chunk, start, count, column).start()
        elif phase == line + 1:
            pair_copy(chunk, start, count, 1 - column).wait_recv()
            core_copy(chunk, start, count, core).start()
        elif phase == line + 2:
            core_copy(chunk, start, count, 1 - core).wait_recv()
        elif phase == line + 3:
            finish(chunk, start, count)

    def finish(chunk, start, count):
        for hop in range(line - 1):

            @pl.when((spot >= hop) & (spot < line - 1))
            def _(hop=hop):
                for copy in moves(True, hop, chunk, start, count):
                    copy.wait_send()

            @pl.when((spot < line - hop) & (spot > 0))
            def _(hop=hop):
                for copy in moves(False, hop, chunk, start, count):
                    copy.wait_send()

        pair_copy(chunk, start, count, column).wait_send()
        core_copy(chunk, start, count, core).wait_send()

    return greet, step, early_start, early_wait, finish


def block_kernel(
    size,
    shard,
    rows_ref,
    back_ref,
    cosine_ref,
    sine_ref,
    keep_ref,
    gain_ref,
    entry_ref,
    funnel_ref,
    lift_ref,
    output_ref,
    squares_ref,
    magnitudes_ref,
    full,
    normed_out,
    turned_out,
    plain_out,
    mixed_out,
    residual_out,
    d_normed_out,
    funneled_out,
    up_out,
    down_out,
    funnel_down_out,
    funnel_up_out,
    funnel_seen_out,
    dots_out,
    normed,
    back,
    floats,
    turned,
    plain,
    mixed,
    heads_weight,
    feed_weight,
    residual,
    d_normed,
    funneled,
    outbox,
    inbox,
    lowered,
    reduced,
    funnel_lowered,
    funnel_reduced,
    low_lift_ref,
    pull_lift_ref,
    ratio_ref,
    pull_ref,
    funnel_down_ref,
    right_sends,
    left_sends,
    right_gets,
    left_gets,
    pair_sems,
    core_sems,
    early_sems,
    local_sems,
    weight_sems,
    side_sends,
    side_gets,
    out_sems,
):
    line = size // 4
    total_blocks = full.shape[0]
    chunks = total_blocks // BLOCKS
    tokens, width = normed.shape[0] - 2 * RANK, normed.shape[1]
    count = tokens // SEQ
    sides = {"tensor": 1 - lax.axis_index("tensor")}
    sems = (right_sends, left_sends, right_gets, left_gets, pair_sems, core_sems, early_sems)
    greet, step, early_start, early_wait, finish = gather_parts(size, shard, full, sems)
    me = lax.axis_index("dp")
    core, column, spot = lax.rem(me, 2), lax.rem(lax.div(me, 2), 2), lax.div(me, 4)

    def tick(now):
        for phase in range(line + 4):
            chunk = now - phase
            start = 1 + BLOCKS * chunk
            if isinstance(now, int):
                if 0 <= chunk < chunks:
                    step(phase, chunk, start, BLOCKS)
            else:

                @pl.when((chunk >= 0) & (chunk < chunks))
                def _(phase=phase, chunk=chunk, start=start):
                    step(phase, chunk, start, BLOCKS)

    own = pltpu.make_async_copy(shard, full.at[:, spot, column, core], local_sems.at[0])
    own.start()
    loads = [
        pltpu.make_async_copy(rows_ref, floats, local_sems.at[1]),
        pltpu.make_async_copy(back_ref, back, local_sems.at[2]),
    ]
    for load in loads:
        load.start()
    greet()
    early_start()
    own.wait()
    early_wait(0)
    step(0, chunks, 0, 1)
    tick(0)
    early_wait(1)
    for load in loads:
        load.wait()
    tile = 32

    def norm_rows(index, carry):
        place = pl.ds(pl.multiple_of(index * tile, tile), tile)
        value = floats[place].astype(jnp.float32)
        root = lax.rsqrt(jnp.mean(value * value, axis=1, keepdims=True) + NORM_EPS)
        normed[place] = (value * root * gain_ref[0:1]).astype(jnp.bfloat16)
        return carry

    def prepare():
        lax.fori_loop(0, tokens // tile, norm_rows, 0)
        norms = jnp.sqrt(squares_ref[...] + COLUMN_EPS)
        ratios = magnitudes_ref[...] / norms
        pulls = 1.0 / (norms * magnitudes_ref[...])
        wide = funnel_down_ref.shape[1]
        lines = -(-wide // LANES)
        for i in range(2):
            ratio = long_row(ratios, 7 + lines * i, wide)
            pull = long_row(pulls, 7 + lines * i, wide)
            ratio_ref[i : i + 1] = ratio
            pull_ref[i : i + 1] = pull
            low_lift_ref[i] = (lift_ref[i] * ratio).astype(jnp.bfloat16)
            pull_lift_ref[i] = lift_ref[i] * pull
        funnel_down_ref[...] = funnel_ref[...].astype(jnp.bfloat16)
        low_output = (output_ref[1] * long_row(ratios, 2, width)).astype(jnp.bfloat16)
        funnel_lowered[...] = dot_nt(low_output, back[...]).astype(jnp.bfloat16)
        for i in range(2):
            normed[pl.ds(tokens + RANK * i, RANK)] = entry_ref[3 + i].astype(jnp.bfloat16)

    for now in range(1, line + 4):
        step(now, chunks, 0, 1)
        tick(now)
        if now == 1:
            prepare()
    normed_copy = pltpu.make_async_copy(
        normed.at[pl.ds(0, tokens)], normed_out, local_sems.at[3]
    )
    normed_copy.start()
    ready = HEAD_CHUNKS - 2 + line + 2
    lax.fori_loop(line + 4, ready + 1, lambda now, carry: (tick(now), carry)[1], 0)

    def head_load(block, slot):
        return pltpu.make_async_copy(
            full.at[block], heads_weight.at[slot], weight_sems.at[slot]
        )

    def head_weight(slot):
        return heads_weight[slot].reshape(width, CHUNK)

    cut_blocks = turned.shape[0] // 3
    head_load(0, 0).start()

    def project(block, carry):
        slot = lax.rem(block, 2)

        @pl.when(block < 3 * cut_blocks - 1)
        def _():
            head_load(block + 1, 1 - slot).start()

        head_load(block, slot).wait()
        for part in range(count):
            place = pl.ds(part * SEQ, SEQ)
            result = dot_nn(normed[place], head_weight(slot))
            plain[block, place] = result.astype(jnp.bfloat16)

            @pl.when(block < 2 * cut_blocks)
            def _(result=result, place=place):
                for half in range(CHUNK // HEAD_DIM):
                    lanes = slice(half * HEAD_DIM, (half + 1) * HEAD_DIM)
                    head = result[:, lanes]
                    turned[block, place, lanes] = (
                        head * cosine_ref[place]
                        + pltpu.roll(head, HEAD_DIM // 2, 1) * sine_ref[place]
                    ).astype(jnp.bfloat16)

            @pl.when(block >= 2 * cut_blocks)
            def _(result=result, place=place):
                turned[block, place] = result.astype(jnp.bfloat16)

        return carry

    lax.fori_loop(0, 3 * cut_blocks, project, 0)
    outs = [
        pltpu.make_async_copy(turned, turned_out, out_sems.at[0]),
        pltpu.make_async_copy(plain.at[pl.ds(0, 2 * cut_blocks)], plain_out, out_sems.at[1]),
    ]
    for out in outs:
        out.start()
    tick(ready + 1)

    mixer_loads = [
        pltpu.make_async_copy(
            full.at[3 * cut_blocks + b],
            feed_weight.at[:, :, :, :, pl.ds(b * CHUNK, CHUNK)],
            weight_sems.at[b],
        )
        for b in range(cut_blocks)
    ]
    for load in mixer_loads:
        load.start()
    line_up = lax.broadcasted_iota(jnp.int32, (SEQ, SEQ), 0)
    line_on = lax.broadcasted_iota(jnp.int32, (SEQ, SEQ), 1)

    def attend(block, carry):
        for part in range(count):
            place = pl.ds(part * SEQ, SEQ)
            allowed = ((line_up >= line_on) & (keep_ref[part] > 0)) | (line_up == line_on)
            for half in range(CHUNK // HEAD_DIM):
                lanes = slice(half * HEAD_DIM, (half + 1) * HEAD_DIM)
                scores = dot_nt(
                    turned[block, place, lanes], turned[cut_blocks + block, place, lanes]
                ) * (HEAD_DIM ** (-0.5))
                masked = jnp.where(allowed, scores, MASKED)
                top = jnp.max(masked, axis=1, keepdims=True)
                weight = jnp.exp(masked - top)
                attention = weight / jnp.sum(weight, axis=1, keepdims=True)
                mixed[block, place, lanes] = dot_nn(
                    attention.astype(jnp.bfloat16), turned[2 * cut_blocks + block, place, lanes]
                ).astype(jnp.bfloat16)
        return carry

    lax.fori_loop(0, cut_blocks, attend, 0)
    outs.append(pltpu.make_async_copy(mixed, mixed_out, out_sems.at[2]))
    outs[-1].start()
    tick(ready + 2)

    for load in mixer_loads:
        load.wait()

    def side_copy(part):
        place = pl.ds(part * SEQ, SEQ)
        return pltpu.make_async_remote_copy(
            src_ref=outbox.at[place],
            dst_ref=inbox.at[place],
            send_sem=side_sends.at[part],
            recv_sem=side_gets.at[part],
            device_id=sides,
            device_id_type=MESH,
        )

    for part in range(count):
        place = pl.ds(part * SEQ, SEQ)
        joined = jnp.concatenate([mixed[b, place] for b in range(cut_blocks)], axis=1)
        per = 512 // (4 * feed_weight.shape[3])
        for piece in range(width // 512):
            weight = feed_weight[pl.ds(piece * per, per), :, :, :, pl.ds(0, cut_blocks * CHUNK)]
            outbox[place, pl.ds(piece * 512, 512)] = dot_nt(
                joined, weight.reshape(512, cut_blocks * CHUNK)
            ).astype(jnp.bfloat16)
        side_copy(part).start()
    tick(ready + 3)

    normed_copy.wait()
    for part in range(count):
        side_copy(part).wait()

        def add_up(index, carry, part=part):
            place = pl.ds(pl.multiple_of(part * SEQ + index * tile, tile), tile)
            value = floats[place].astype(jnp.float32) + (
                outbox[place].astype(jnp.float32) + inbox[place].astype(jnp.float32)
            )
            residual[place] = value
            root = lax.rsqrt(jnp.mean(value * value, axis=1, keepdims=True) + NORM_EPS)
            normed[place] = (value * root * gain_ref[1:2]).astype(jnp.bfloat16)
            return carry

        lax.fori_loop(0, SEQ // tile, add_up, 0)
        if part == 0:
            tick(ready + 4)
    outs.append(pltpu.make_async_copy(residual, residual_out, out_sems.at[3]))
    outs[-1].start()
    reduced[...] = dot_nt(normed[pl.ds(tokens, 2 * RANK)], normed[pl.ds(0, tokens)]).astype(
        jnp.bfloat16
    )
    d_normed[...] = jnp.zeros_like(d_normed)
    funneled[...] = jnp.zeros_like(funneled)
    lowered[...] = jnp.zeros_like(lowered)
    funnel_reduced[...] = jnp.zeros_like(funnel_reduced)

    def feed_load(index):
        return [
            pltpu.make_async_copy(
                full.at[4 * cut_blocks + BLOCKS * index + b],
                feed_weight.at[:, :, :, :, pl.ds(b * CHUNK, CHUNK)],
                weight_sems.at[b],
            )
            for b in range(BLOCKS)
        ]

    nothing = jnp.zeros((RANK, CHUNK), jnp.bfloat16)

    def feed(index, carry):
        @pl.when(index >= EXTRA_TICKS)
        def _():
            tick(index + HEAD_CHUNKS + line + 2)

        for load in feed_load(index):
            load.start()
        for load in feed_load(index):
            load.wait()
        columns = pl.ds(pl.multiple_of(index * CHUNK, CHUNK), CHUNK)
        weight = feed_weight[:, :, :, :, pl.ds(0, 2 * CHUNK)].reshape(width, 2 * CHUNK)
        both = dot_nn(normed[...], weight)
        gate, lifted = both[:tokens, :CHUNK], both[:tokens, CHUNK:]
        gate_seen = both[tokens : tokens + RANK, :CHUNK]
        lifted_seen = both[tokens + RANK :, CHUNK:]
        funnel = feed_weight[:, :, :, :, pl.ds(2 * CHUNK, CHUNK)].reshape(width, CHUNK)
        d_hidden = dot_nn(back[...], funnel)
        sigmoid = 1.0 / (1.0 + jnp.exp(-gate))
        silu = gate * sigmoid
        hidden = (silu * lifted).astype(jnp.bfloat16)
        d_gate = (d_hidden * lifted * (sigmoid * (1.0 + gate * (1.0 - sigmoid)))).astype(
            jnp.bfloat16
        )
        d_lifted = (d_hidden * silu).astype(jnp.bfloat16)
        gate_dots = jnp.sum(d_gate.astype(jnp.float32) * gate, axis=0, keepdims=True)
        lifted_dots = jnp.sum(d_lifted.astype(jnp.float32) * lifted, axis=0, keepdims=True)
        dots_out[0:1, columns] = gate_dots
        dots_out[1:2, columns] = lifted_dots
        gate_pull = (pull_lift_ref[0, :, columns] * gate_dots).astype(jnp.bfloat16)
        lifted_pull = (pull_lift_ref[1, :, columns] * lifted_dots).astype(jnp.bfloat16)
        up_out[0, :, columns] = ADAPTER_SCALE * (
            dot_nn(reduced[pl.ds(0, RANK)], d_gate) * ratio_ref[0:1, columns]
            - gate_seen * (pull_ref[0:1, columns] * gate_dots)
        )
        up_out[1, :, columns] = ADAPTER_SCALE * (
            dot_nn(reduced[pl.ds(RANK, RANK)], d_lifted) * ratio_ref[1:2, columns]
            - lifted_seen * (pull_ref[1:2, columns] * lifted_dots)
        )
        lowered[pl.ds(0, RANK)] += dot_nt(low_lift_ref[0, :, columns], d_gate)
        lowered[pl.ds(RANK, RANK)] += dot_nt(low_lift_ref[1, :, columns], d_lifted)
        funnel_down_out[:, columns] = ADAPTER_SCALE * dot_nn(funnel_lowered[...], hidden)
        funnel_down = funnel_down_ref[:, columns]
        funnel_reduced[...] += dot_nt(funnel_down, hidden)
        sources = jnp.concatenate([hidden, funnel_down], axis=0)
        gradients = jnp.concatenate(
            [
                jnp.concatenate([d_gate, d_lifted], axis=1),
                jnp.concatenate([gate_pull, nothing], axis=1),
                jnp.concatenate([nothing, lifted_pull], axis=1),
            ],
            axis=0,
        )
        per = 512 // (4 * feed_weight.shape[3])
        for piece in range(width // 512):
            near = pl.ds(piece * per, per)
            funnel_rows = feed_weight[near, :, :, :, pl.ds(2 * CHUNK, CHUNK)]
            gate_rows = feed_weight[near, :, :, :, pl.ds(0, 2 * CHUNK)]
            lanes = pl.ds(piece * 512, 512)
            funneled[:, lanes] += dot_nt(sources, funnel_rows.reshape(512, CHUNK))
            d_normed[:, lanes] += dot_nt(
                gradients, gate_rows.reshape(512, 2 * CHUNK)
            )
        return carry

    lax.fori_loop(0, chunks - HEAD_CHUNKS, feed, 0)
    outbox[...] = d_normed[pl.ds(0, tokens)].astype(jnp.bfloat16)
    outs.append(pltpu.make_async_copy(outbox, d_normed_out, out_sems.at[4]))
    outs[-1].start()
    down_out[...] = ADAPTER_SCALE * (
        dot_nn(lowered[...].astype(jnp.bfloat16), normed[pl.ds(0, tokens)])
        - d_normed[pl.ds(tokens, 2 * RANK)]
    )
    floats[...] = funneled[pl.ds(0, tokens)].astype(jnp.bfloat16)
    outs.append(pltpu.make_async_copy(floats, funneled_out, out_sems.at[5]))
    outs[-1].start()
    funnel_up_out[...] = dot_nn(funnel_reduced[...].astype(jnp.bfloat16), back[...])
    funnel_seen_out[...] = funneled[pl.ds(tokens, RANK)]
    finish(chunks - 1, 1 + BLOCKS * (chunks - 1), BLOCKS)
    for out in outs:
        out.wait()


def run_block(shard, rows, back, small):
    size = lax.axis_size("dp")
    line = size // 4
    tokens, width = rows.shape
    blocks, height, _ = shard.shape
    chunks = blocks // BLOCKS
    cut_blocks = (BLOCKS * HEAD_CHUNKS + 1) // 4
    wide = small[6].shape[2]
    anywhere = pl.BlockSpec(memory_space=pl.ANY)
    local = pl.BlockSpec(memory_space=pltpu.VMEM)
    low = jnp.bfloat16
    full = jnp.float32
    out_shape = (
        jax.ShapeDtypeStruct((blocks, line, 2, 2, height, CHUNK), low),
        jax.ShapeDtypeStruct((tokens, width), low),
        jax.ShapeDtypeStruct((3 * cut_blocks, tokens, CHUNK), low),
        jax.ShapeDtypeStruct((2 * cut_blocks, tokens, CHUNK), low),
        jax.ShapeDtypeStruct((cut_blocks, tokens, CHUNK), low),
        jax.ShapeDtypeStruct((tokens, width), full),
        jax.ShapeDtypeStruct((tokens, width), low),
        jax.ShapeDtypeStruct((tokens, width), low),
        jax.ShapeDtypeStruct((2, RANK, wide), full),
        jax.ShapeDtypeStruct((2 * RANK, width), full),
        jax.ShapeDtypeStruct((RANK, wide), full),
        jax.ShapeDtypeStruct((RANK, width), full),
        jax.ShapeDtypeStruct((RANK, width), full),
        jax.ShapeDtypeStruct((2, wide), full),
    )
    scratch = [
        pltpu.VMEM((tokens + 2 * RANK, width), low),
        pltpu.VMEM((tokens, width), low),
        pltpu.VMEM((tokens, width), low),
        pltpu.VMEM((3 * cut_blocks, tokens, CHUNK), low),
        pltpu.VMEM((3 * cut_blocks, tokens, CHUNK), low),
        pltpu.VMEM((cut_blocks, tokens, CHUNK), low),
        pltpu.VMEM((2, line, 2, 2, height, CHUNK), low),
        pltpu.VMEM((line, 2, 2, height, 4 * CHUNK), low),
        pltpu.VMEM((tokens, width), full),
        pltpu.VMEM((tokens + 2 * RANK, width), full),
        pltpu.VMEM((tokens + RANK, width), full),
        pltpu.VMEM((tokens, width), low),
        pltpu.VMEM((tokens, width), low),
        pltpu.VMEM((2 * RANK, tokens), full),
        pltpu.VMEM((2 * RANK, tokens), low),
        pltpu.VMEM((RANK, tokens), low),
        pltpu.VMEM((RANK, tokens), full),
        pltpu.VMEM((2, RANK, wide), low),
        pltpu.VMEM((2, RANK, wide), full),
        pltpu.VMEM((2, wide), full),
        pltpu.VMEM((2, wide), full),
        pltpu.VMEM((RANK, wide), low),
        pltpu.SemaphoreType.DMA((chunks + 1, 2 * (line - 1))),
        pltpu.SemaphoreType.DMA((chunks + 1, 2 * (line - 1))),
        pltpu.SemaphoreType.DMA((chunks + 1, 2 * (line - 1))),
        pltpu.SemaphoreType.DMA((chunks + 1, 2 * (line - 1))),
        pltpu.SemaphoreType.DMA((chunks + 1, 2)),
        pltpu.SemaphoreType.DMA((chunks + 1, 2)),
        pltpu.SemaphoreType.DMA((2, 2)),
        pltpu.SemaphoreType.DMA((4,)),
        pltpu.SemaphoreType.DMA((4,)),
        pltpu.SemaphoreType.DMA((tokens // SEQ,)),
        pltpu.SemaphoreType.DMA((tokens // SEQ,)),
        pltpu.SemaphoreType.DMA((6,)),
    ]
    return pl.pallas_call(
        functools.partial(block_kernel, size),
        name="block",
        out_shape=out_shape,
        in_specs=[local] + [anywhere] * 2 + [local] * 10,
        out_specs=[anywhere] * 8 + [local] * 6,
        scratch_shapes=scratch,
        compiler_params=pltpu.CompilerParams(
            collective_id=1, has_side_effects=True, vmem_limit_bytes=VMEM
        ),
    )(shard, rows, back, *small)


def tail_kernel(
    size,
    sides,
    widths,
    full,
    turned_ref,
    plain_ref,
    mixed_ref,
    residual_ref,
    d_normed_ref,
    funneled_ref,
    back_ref,
    rows_ref,
    normed_ref,
    cosine_ref,
    sine_ref,
    keep_ref,
    gain_ref,
    entry_ref,
    attend_ref,
    mixer_ref,
    output_ref,
    squares_ref,
    magnitudes_ref,
    funnel_down_ref,
    funnel_up_ref,
    funnel_seen_ref,
    feed_dots_ref,
    feed_down_ref,
    feed_up_ref,
    partial_out,
    partial_other,
    d_residual_out,
    funneled_out,
    total,
    norm_out,
    weights,
    residual,
    floats,
    back,
    normed,
    turned,
    plain,
    mixed,
    own,
    inbox,
    funneled,
    attention,
    d_low,
    d_heads,
    funnel_weight,
    dots_box,
    mixer_dots,
    entry_down_ref,
    funnel_down,
    gathered,
    dots_out,
    side_box,
    norm_box,
    load_sems,
    weight_sems,
    funnel_sems,
    side_sends,
    side_gets,
    out_sems,
    *sum_refs,
):
    tokens, width = back.shape
    count = tokens // SEQ
    cut = d_heads.shape[2]
    near = cut // CHUNK
    wide = funnel_down_ref.shape[1]
    scale = HEAD_DIM ** (-0.5)
    other = {"tensor": lax.rem(lax.axis_index("tensor") + 1, sides)}
    halves = CHUNK // HEAD_DIM
    half_rows = gathered.shape[0] // 2

    loads = [
        pltpu.make_async_copy(source, target, load_sems.at[i])
        for i, (source, target) in enumerate(
            (
                (funneled_ref, funneled),
                (back_ref, back),
                (turned_ref, turned),
                (normed_ref, normed),
                (d_normed_ref, own),
                (residual_ref, residual),
                (rows_ref, floats),
                (mixed_ref, mixed),
                (plain_ref, plain),
            )
        )
    ]
    weight_loads = [
        pltpu.make_async_copy(
            full.at[near * i + b],
            weights.at[i, :, :, :, :, pl.ds(b * CHUNK, CHUNK)],
            weight_sems.at[near * i + b],
        )
        for i in range(4)
        for b in range(near)
    ]
    for load in loads[:3]:
        load.start()
    greet_sum(size, sides)

    def remote(source, target, index):
        return pltpu.make_async_remote_copy(
            src_ref=source,
            dst_ref=target,
            send_sem=side_sends.at[index],
            recv_sem=side_gets.at[index],
            device_id=other,
            device_id_type=MESH,
        )

    def rows_of(part):
        return pl.ds(part * SEQ, SEQ)

    part_copies = [
        remote(d_normed_ref.at[rows_of(part)], inbox.at[rows_of(part)], part)
        for part in range(count)
    ]
    part_copies[0].start()
    for load in loads[3:] + weight_loads:
        load.start()
    dots_copy = remote(dots_box.at[0], dots_box.at[1], count)
    funneled_copy = remote(funneled_ref, funneled_out, count + 1)
    partial_copy = remote(own, partial_other, count + 2)
    norms = jnp.sqrt(squares_ref[...] + COLUMN_EPS)
    ratios = magnitudes_ref[...] / norms
    pulls = 1.0 / (norms * magnitudes_ref[...])
    for i in range(3):
        entry_down_ref[pl.ds(RANK * i, RANK)] = entry_ref[i].astype(jnp.bfloat16)
    mixer_low = mixer_ref[...].astype(jnp.bfloat16)
    output_ratio = [long_row(ratios, 2 * i, width) for i in range(2)]
    output_pull = [long_row(pulls, 2 * i, width) for i in range(2)]

    def weight_of(i):
        return weights[i].reshape(width, cut)

    loads[0].wait()
    loads[1].wait()
    tile = 64

    def count_dots(index, total):
        place = pl.ds(pl.multiple_of(index * tile, tile), tile)
        return total + jnp.sum(
            back[place].astype(jnp.float32) * funneled[place].astype(jnp.float32),
            axis=0,
            keepdims=True,
        )

    funnel_dots = lax.fori_loop(
        0, tokens // tile, count_dots, jnp.zeros((1, width), jnp.float32)
    )
    dots_box[0] = jnp.broadcast_to(funnel_dots, dots_box.shape[1:])
    dots_copy.start()
    loads[2].wait()
    line_up = lax.broadcasted_iota(jnp.int32, (SEQ, SEQ), 0)
    line_on = lax.broadcasted_iota(jnp.int32, (SEQ, SEQ), 1)

    def attend(block, carry):
        for part in range(count):
            place = rows_of(part)
            allowed = ((line_up >= line_on) & (keep_ref[part] > 0)) | (line_up == line_on)
            for half in range(halves):
                lanes = slice(half * HEAD_DIM, (half + 1) * HEAD_DIM)
                scores = dot_nt(
                    turned[block, place, lanes], turned[near + block, place, lanes]
                ) * scale
                masked = jnp.where(allowed, scores, MASKED)
                top = jnp.max(masked, axis=1, keepdims=True)
                weight = jnp.exp(masked - top)
                attention[part, halves * block + half] = weight / jnp.sum(
                    weight, axis=1, keepdims=True
                )
        return carry

    lax.fori_loop(0, near, attend, 0)
    for copy in part_copies[1:]:
        copy.start()

    def funnel_load(block, slot):
        return pltpu.make_async_copy(
            full.at[4 * near + BLOCKS * block + 2], funnel_weight.at[slot], funnel_sems.at[slot]
        )

    funnel_load(0, 0).start()
    for load in loads[3:] + weight_loads:
        load.wait()
    head_seen = [
        dot_nn(entry_down_ref[pl.ds(RANK * i, RANK)], weight_of(i)) for i in range(3)
    ]
    mixer_seen = dot_nt(mixer_low, weight_of(3))
    reduced = dot_nt(entry_down_ref[...], normed[...]).astype(jnp.bfloat16)
    dots_copy.wait()
    funnel_dots = dots_box[0, 0:1] + dots_box[1, 0:1]
    funnel_pull = (output_ref[1] * (output_pull[1] * funnel_dots)).astype(jnp.bfloat16)

    def correct(block, carry):
        slot = lax.rem(block, 2)

        @pl.when(block < wide // CHUNK - 1)
        def _():
            funnel_load(block + 1, 1 - slot).start()

        funnel_load(block, slot).wait()
        columns = pl.ds(pl.multiple_of(block * CHUNK, CHUNK), CHUNK)
        funnel_down[:, columns] = funnel_down_ref[:, columns] - ADAPTER_SCALE * dot_nn(
            funnel_pull, funnel_weight[slot].reshape(width, CHUNK)
        )
        return carry

    lax.fori_loop(0, wide // CHUNK, correct, 0)
    gathered[pl.ds(6 * RANK, RANK)] = ADAPTER_SCALE * (
        funnel_up_ref[...] * output_ratio[1]
        - funnel_seen_ref[...] * (output_pull[1] * funnel_dots)
    )
    gathered[pl.ds(3 * RANK, 2 * RANK)] = feed_down_ref[...]
    mixer_dots[...] = jnp.zeros_like(mixer_dots)
    small = 32
    for part in range(count):
        part_copies[part].wait()
        if part == count - 1:
            funneled_copy.start()

        def pull_back(index, carry, part=part):
            place = pl.ds(pl.multiple_of(part * SEQ + index * small, small), small)
            value = residual[place]
            weighted = gain_ref[1:2] * (
                own[place].astype(jnp.float32) + inbox[place].astype(jnp.float32)
            )
            root = lax.rsqrt(jnp.mean(value * value, axis=1, keepdims=True) + NORM_EPS)
            along = jnp.mean(value * weighted, axis=1, keepdims=True)
            gradient = back[place].astype(jnp.float32) + (
                root * weighted - value * (root * root * root * along)
            )
            rounded = gradient.astype(jnp.bfloat16)
            d_low[place] = rounded
            attended = value - floats[place].astype(jnp.float32)
            mixer_dots[...] += jnp.sum(
                (rounded.astype(jnp.float32) * attended).reshape(small // 8, 8, width), axis=0
            )
            residual[place] = gradient
            return carry

        lax.fori_loop(0, SEQ // small, pull_back, 0)
        place = rows_of(part)

        def attend_back(block, carry, part=part, place=place):
            columns = pl.ds(pl.multiple_of(block * CHUNK, CHUNK), CHUNK)
            mixer = weights[3, :, :, :, :, columns].reshape(width, CHUNK)
            d_mixed = dot_nn(d_low[place], mixer).astype(jnp.bfloat16)
            for half in range(halves):
                lanes = slice(half * HEAD_DIM, (half + 1) * HEAD_DIM)
                spot = pl.ds(
                    pl.multiple_of(block * CHUNK + half * HEAD_DIM, HEAD_DIM), HEAD_DIM
                )
                weight = attention[part, halves * block + half]
                d_head = d_mixed[:, lanes]
                d_attention = dot_nt(d_head, turned[2 * near + block, place, lanes])
                d_heads[2, place, spot] = dot_nn(
                    weight.astype(jnp.bfloat16).T, d_head
                ).astype(jnp.bfloat16)
                inner = jnp.sum(weight * d_attention, axis=1, keepdims=True)
                d_scores = (weight * (d_attention - inner)).astype(jnp.bfloat16)
                d_query = dot_nn(d_scores, turned[near + block, place, lanes]) * scale
                d_key = dot_nn(d_scores.T, turned[block, place, lanes]) * scale
                for i, value in ((0, d_query), (1, d_key)):
                    d_heads[i, place, spot] = (
                        value * cosine_ref[place]
                        - pltpu.roll(value, HEAD_DIM // 2, 1) * sine_ref[place]
                    ).astype(jnp.bfloat16)
            return carry

        lax.fori_loop(0, near, attend_back, 0)
    d_residual_copy = pltpu.make_async_copy(residual, d_residual_out, out_sems.at[0])
    d_residual_copy.start()
    per = 512 // (4 * weights.shape[4])
    for i in range(3):
        dots = []
        for block in range(near):
            lanes = slice(block * CHUNK, (block + 1) * CHUNK)
            source = plain if i < 2 else turned
            dots.append(
                jnp.sum(
                    d_heads[i, :tokens, lanes].astype(jnp.float32)
                    * source[near * i + block].astype(jnp.float32),
                    axis=0,
                    keepdims=True,
                )
            )
        dots = jnp.concatenate(dots, axis=1)
        dots_out[4 + i : 5 + i] = dots
        head_ratio = ratios[4 + i : 5 + i]
        pulled = (attend_ref[i] * (pulls[4 + i : 5 + i] * dots)).astype(jnp.bfloat16)
        place_in(
            gathered,
            half_rows,
            cut * i,
            ADAPTER_SCALE
            * (
                dot_nn(reduced[RANK * i : RANK * (i + 1)], d_heads[i, :tokens]) * head_ratio
                - head_seen[i] * (pulls[4 + i : 5 + i] * dots)
            ),
        )
        low_lift = (attend_ref[i] * head_ratio).astype(jnp.bfloat16)
        lowered = dot_nt(low_lift, d_heads[i, :tokens]).astype(jnp.bfloat16)
        gathered[pl.ds(RANK * i, RANK)] = ADAPTER_SCALE * dot_nn(lowered, normed[...])
        d_heads[i, tokens:] = pulled
    for piece in range(width // 512):
        lanes = slice(piece * 512, (piece + 1) * 512)
        results = [
            dot_nt(d_heads[i], weights[i, pl.ds(piece * per, per)].reshape(512, cut))
            for i in range(3)
        ]
        own[:, lanes] = (
            results[0][:tokens] + results[1][:tokens] + results[2][:tokens]
        ).astype(jnp.bfloat16)
        for i in range(3):
            gathered[pl.ds(RANK * i, RANK), lanes] -= ADAPTER_SCALE * results[i][tokens:]
    partial_copy.start()
    partial_save = pltpu.make_async_copy(own, partial_out, out_sems.at[1])
    partial_save.start()
    mixer_total = jnp.sum(mixer_dots[...], axis=0, keepdims=True)
    joined = jnp.concatenate([mixed[b] for b in range(near)], axis=1)
    low_output = (output_ref[0] * output_ratio[0]).astype(jnp.bfloat16)
    lowered = dot_nt(low_output, d_low[...]).astype(jnp.bfloat16)
    pulled = (output_ref[0] * (output_pull[0] * mixer_total)).astype(jnp.bfloat16)
    mixer_down = ADAPTER_SCALE * (dot_nn(lowered, joined) - dot_nn(pulled, weight_of(3)))
    reduced_mixed = dot_nt(mixer_low, joined).astype(jnp.bfloat16)
    gathered[pl.ds(5 * RANK, RANK)] = ADAPTER_SCALE * (
        dot_nn(reduced_mixed, d_low[...]) * output_ratio[0]
        - mixer_seen * (output_pull[0] * mixer_total)
    )
    for i, value in enumerate((mixer_total, funnel_dots)):
        for r in range(2):
            dots_out[2 * i + r : 2 * i + r + 1] = value[:, r * LANES : (r + 1) * LANES]
    row = 7
    for i in range(2):
        for start in range(0, wide, LANES):
            size = min(LANES, wide - start)
            dots_out[row : row + 1, pl.ds(0, size)] = feed_dots_ref[
                i : i + 1, pl.ds(start, size)
            ]
            if size < LANES:
                dots_out[row : row + 1, pl.ds(size, LANES - size)] = jnp.zeros(
                    (1, LANES - size), jnp.float32
                )
            row += 1
    if row < dots_out.shape[0]:
        dots_out[row:] = jnp.zeros((dots_out.shape[0] - row, LANES), jnp.float32)
    offset = 3 * cut
    for value in (feed_up_ref[0], feed_up_ref[1], mixer_down, funnel_down[...], dots_out[...]):
        place_in(gathered, half_rows, offset, value)
        offset += value.shape[1]
    rest_columns = half_rows // RANK * width - offset
    place_in(gathered, half_rows, offset, jnp.zeros((RANK, rest_columns), jnp.float32))
    sum_up(
        size, sides, widths, offset, magnitudes_ref, total, norm_out, gathered, side_box, norm_box,
        *sum_refs,
    )
    d_residual_copy.wait()
    partial_save.wait()
    funneled_copy.wait()
    partial_copy.wait()


def run_tail(big, small):
    size = lax.axis_size("dp")
    sides = lax.axis_size("tensor")
    full, turned, plain, mixed, residual = big[:5]
    tokens, width = residual.shape
    line, height = full.shape[1], full.shape[4]
    near = mixed.shape[0]
    cut = near * CHUNK
    wide = small[10].shape[1]
    lines = small[8].shape[0]
    count = tokens // SEQ
    anywhere = pl.BlockSpec(memory_space=pl.ANY)
    local = pl.BlockSpec(memory_space=pltpu.VMEM)
    low, full_type = jnp.bfloat16, jnp.float32
    heads = cut // HEAD_DIM
    rows = 7 * RANK
    bits = len(bin(size)) - 3
    widths = [max(width >> (step + 1), 128) for step in range(bits)]
    halvings = sum(1 for step in range(bits) if width >> (step + 1) >= 128)
    boxes = [pltpu.VMEM((2 * rows, w), low) for w in widths]
    copies = bits + halvings + 2 * (sides - 1)
    return pl.pallas_call(
        functools.partial(tail_kernel, size, sides, widths),
        name="tail",
        out_shape=(
            jax.ShapeDtypeStruct((tokens, width), low),
            jax.ShapeDtypeStruct((tokens, width), low),
            jax.ShapeDtypeStruct((tokens, width), full_type),
            jax.ShapeDtypeStruct((tokens, width), low),
            jax.ShapeDtypeStruct((2 * rows, width), low),
            jax.ShapeDtypeStruct((8, 128), full_type),
        ),
        in_specs=[anywhere] * 10 + [local] * 16,
        out_specs=[anywhere] * 4 + [local] * 2,
        scratch_shapes=[
            pltpu.VMEM((4, line, 2, 2, height, cut), low),
            pltpu.VMEM((tokens, width), full_type),
            pltpu.VMEM((tokens, width), low),
            pltpu.VMEM((tokens, width), low),
            pltpu.VMEM((tokens, width), low),
            pltpu.VMEM(turned.shape, low),
            pltpu.VMEM(plain.shape, low),
            pltpu.VMEM(mixed.shape, low),
            pltpu.VMEM((tokens, width), low),
            pltpu.VMEM((tokens, width), low),
            pltpu.VMEM((tokens, width), low),
            pltpu.VMEM((count, heads, SEQ, SEQ), full_type),
            pltpu.VMEM((tokens, width), low),
            pltpu.VMEM((3, tokens + RANK, cut), low),
            pltpu.VMEM((2, line, 2, 2, height, CHUNK), low),
            pltpu.VMEM((2, 8, width), full_type),
            pltpu.VMEM((8, width), full_type),
            pltpu.VMEM((3 * RANK, width), low),
            pltpu.VMEM((RANK, wide), full_type),
            pltpu.VMEM((2 * rows, width), full_type),
            pltpu.VMEM((lines, LANES), full_type),
            pltpu.VMEM((sides, rows, widths[-1]), low),
            pltpu.VMEM((sides, 8, 128), full_type),
            pltpu.SemaphoreType.DMA((9,)),
            pltpu.SemaphoreType.DMA((4 * near,)),
            pltpu.SemaphoreType.DMA((2,)),
            pltpu.SemaphoreType.DMA((count + 3,)),
            pltpu.SemaphoreType.DMA((count + 3,)),
            pltpu.SemaphoreType.DMA((2,)),
            *boxes,
            *boxes,
            pltpu.SemaphoreType.DMA((copies,)),
            pltpu.SemaphoreType.DMA((copies,)),
        ],
        compiler_params=pltpu.CompilerParams(
            collective_id=2, has_side_effects=True, vmem_limit_bytes=VMEM
        ),
    )(*big, *small)


def place_in(target, base, offset, value):
    width = target.shape[1]
    start = 0
    while start < value.shape[1]:
        group, lane = divmod(offset + start, width)
        size = min(value.shape[1] - start, width - lane)
        target[pl.ds(base + RANK * group, RANK), pl.ds(lane, size)] = value[
            :, start : start + size
        ].astype(target.dtype)
        start += size


def take_from(source, base, offset, size):
    width = source.shape[1]
    pieces = []
    start = 0
    while start < size:
        group, lane = divmod(offset + start, width)
        count = min(size - start, width - lane)
        pieces.append(
            source[pl.ds(base + RANK * group, RANK), pl.ds(lane, count)].astype(jnp.float32)
        )
        start += count
    return pieces[0] if len(pieces) == 1 else jnp.concatenate(pieces, axis=1)


def sum_up(
    size,
    sides,
    widths,
    offset,
    magnitude_ref,
    total,
    norm_out,
    gathered,
    side_box,
    norm_box,
    *rest,
):
    bits = len(widths)
    outboxes, inboxes = rest[:bits], rest[bits : 2 * bits]
    sends, receives = rest[2 * bits :]
    half = gathered.shape[0] // 2
    me = lax.axis_index("dp")
    side = lax.axis_index("tensor")
    partners = partners_of(size)

    def remote(source, target, index, where):
        return pltpu.make_async_remote_copy(
            src_ref=source,
            dst_ref=target,
            send_sem=sends.at[index],
            recv_sem=receives.at[index],
            device_id=where,
            device_id_type=MESH,
        )

    start = 0
    width = gathered.shape[1]
    marks = []
    for step in range(bits):
        bit = lax.rem(lax.div(me, 2**step), 2)
        where = {"dp": partners[step]}
        if widths[step] < width:
            width = widths[step]
            marks.append((step, bit, width))
            mine = pl.ds(pl.multiple_of(start + bit * width, 128), width)
            theirs = pl.ds(pl.multiple_of(start + (1 - bit) * width, 128), width)
            outboxes[step][...] = gathered[:, theirs].astype(jnp.bfloat16)
            copy = remote(outboxes[step], inboxes[step], step, where)
            copy.start()
            copy.wait()
            gathered[:, mine] += inboxes[step][...].astype(jnp.float32)
            start = start + bit * width
        else:
            mine = pl.ds(pl.multiple_of(start, 128), width)
            outboxes[step][...] = gathered[:, mine].astype(jnp.bfloat16)
            copy = remote(outboxes[step], inboxes[step], step, where)
            copy.start()
            copy.wait()
            gathered[:, mine] = outboxes[step][...].astype(jnp.float32) + inboxes[step][
                ...
            ].astype(jnp.float32)
    mine = pl.ds(pl.multiple_of(start, 128), width)
    side_box[0] = gathered[pl.ds(0, half), mine].astype(jnp.bfloat16)
    shared = side_box[0].astype(jnp.float32)
    for step in range(1, sides):
        copy = remote(
            side_box.at[0],
            side_box.at[step],
            bits + step - 1,
            {"tensor": lax.rem(side + step, sides)},
        )
        copy.start()
        copy.wait()
        shared += side_box[step].astype(jnp.float32)
    total[pl.ds(0, half), mine] = shared.astype(jnp.bfloat16)
    total[pl.ds(half, half), mine] = gathered[pl.ds(half, half), mine].astype(jnp.bfloat16)
    index = bits + sides - 1
    for step, bit, width in reversed(marks):
        mine = pl.ds(pl.multiple_of(start, 128), width)
        copy = remote(
            total.at[:, mine], total.at[:, mine], index, {"dp": partners[step]}
        )
        copy.start()
        copy.wait()
        index += 1
        start = start - bit * width
    squares = jnp.zeros((RANK, 1), jnp.float32)
    for row in range(0, half, RANK):
        value = total[pl.ds(row, RANK)].astype(jnp.float32)
        squares += jnp.sum(value * value, axis=1, keepdims=True)
    dots_offset = offset - LANES
    dots = take_from(total, half, dots_offset, LANES) / magnitude_ref[...]
    dots = jnp.sum(dots * dots, axis=1, keepdims=True)
    shared_total = jnp.sum(squares) + jnp.sum(dots[:4])
    split_squares = jnp.zeros((RANK, 1), jnp.float32)
    start = 0
    while start < dots_offset:
        count = min(dots_offset - start, gathered.shape[1])
        value = take_from(total, half, start, count)
        split_squares += jnp.sum(value * value, axis=1, keepdims=True)
        start += count
    split_total = jnp.sum(split_squares) + jnp.sum(dots[4:])
    norm_box[0] = jnp.full(norm_box.shape[1:], split_total, jnp.float32)
    for step in range(1, sides):
        copy = remote(
            norm_box.at[0],
            norm_box.at[step],
            index + step - 1,
            {"tensor": lax.rem(side + step, sides)},
        )
        copy.start()
        copy.wait()
    split_sum = norm_box[0]
    for step in range(1, sides):
        split_sum = split_sum + norm_box[step]
    norm_out[...] = jnp.sqrt(split_sum + shared_total)


def update_kernel(*refs):
    total, norm_ref = refs[:2]
    values, firsts, seconds = refs[2:11], refs[11:20], refs[20:29]
    fresh, momenta, variances = refs[29:38], refs[38:47], refs[47:56]
    factor = jnp.minimum(1.0, CLIP / (norm_ref[0:1, 0:1] + 1e-06))
    half = total.shape[0] // 2
    cut, wide = values[1].shape[2], values[2].shape[2]

    def update(index, rate, piece, gradient):
        value, momentum, variance = decoupled_update(
            values[index][piece], gradient * factor, firsts[index][piece], seconds[index][piece], rate
        )
        fresh[index][piece] = value
        momenta[index][piece] = momentum
        variances[index][piece] = variance

    def shared(group):
        return total[pl.ds(RANK * group, RANK)].astype(jnp.float32)

    for i in range(5):
        update(0, RATE_FACTOR, i, shared(i))
    for i in range(2):
        update(5, RATE_LIFT, i, shared(5 + i))
    offset = 0
    for i in range(3):
        update(1, RATE_LIFT, i, take_from(total, half, offset, cut))
        offset += cut
    for i in range(2):
        update(2, RATE_LIFT, i, take_from(total, half, offset, wide))
        offset += wide
    update(3, RATE_FACTOR, Ellipsis, take_from(total, half, offset, cut))
    offset += cut
    update(4, RATE_FACTOR, Ellipsis, take_from(total, half, offset, wide))
    offset += wide
    dots = take_from(total, half, offset, LANES)

    def long(row, size):
        count = -(-size // LANES)
        return jnp.concatenate([dots[row + r : row + r + 1] for r in range(count)], axis=1)[
            :, :size
        ]

    width = total.shape[1]
    for i in range(2):
        piece = slice(i, i + 1)
        update(8, RATE_LOUD, piece, long(2 * i, width) / values[8][piece])
    for i in range(3):
        piece = slice(i, i + 1)
        update(6, RATE_SCALE, piece, long(4 + i, cut) / values[6][piece])
    lines = -(-wide // LANES)
    for i in range(2):
        piece = slice(i, i + 1)
        update(7, RATE_SCALE, piece, long(7 + lines * i, wide) / values[7][piece])


def update_all(total, norm, params, firsts, seconds):
    shapes = tuple(jax.ShapeDtypeStruct(p.shape, p.dtype) for p in params)
    return pl.pallas_call(
        update_kernel,
        name="update",
        out_shape=shapes * 3,
        in_specs=[pl.BlockSpec(memory_space=pltpu.VMEM)] * 29,
        out_specs=[pl.BlockSpec(memory_space=pltpu.VMEM)] * 27,
        compiler_params=pltpu.CompilerParams(vmem_limit_bytes=VMEM),
    )(total, norm, *params, *firsts, *seconds)


def body(
    activations,
    cotangent,
    padding_mask,
    positions,
    norm_gains,
    base_query,
    base_key,
    base_value,
    base_gate,
    base_widen,
    base_mixer,
    base_funnel,
    entry_value,
    attend_value,
    widen_value,
    mixer_value,
    funnel_value,
    output_value,
    stature_value,
    amplitude_value,
    loudness_value,
    entry_first,
    attend_first,
    widen_first,
    mixer_first,
    funnel_first,
    output_first,
    stature_first,
    amplitude_first,
    loudness_first,
    entry_second,
    attend_second,
    widen_second,
    mixer_second,
    funnel_second,
    output_second,
    stature_second,
    amplitude_second,
    loudness_second,
):
    params = (
        entry_value,
        attend_value,
        widen_value,
        mixer_value,
        funnel_value,
        output_value,
        stature_value,
        amplitude_value,
        loudness_value,
    )
    firsts = (
        entry_first,
        attend_first,
        widen_first,
        mixer_first,
        funnel_first,
        output_first,
        stature_first,
        amplitude_first,
        loudness_first,
    )
    seconds = (
        entry_second,
        attend_second,
        widen_second,
        mixer_second,
        funnel_second,
        output_second,
        stature_second,
        amplitude_second,
        loudness_second,
    )
    rows, cut = base_query.shape
    width = activations.shape[1]
    place = lax.axis_index("dp") * rows
    entry_down = jnp.swapaxes(entry_value, 1, 2)
    shard, squares, magnitudes = merge(
        (base_query, base_key, base_value, base_gate, base_widen, base_mixer, base_funnel),
        lax.dynamic_slice_in_dim(entry_down, place, rows, 2),
        attend_value,
        widen_value,
        mixer_value.T,
        funnel_value.T,
        lax.dynamic_slice_in_dim(output_value, place, rows, 2),
        (stature_value, amplitude_value, loudness_value),
    )
    count = activations.shape[0] // SEQ
    half = HEAD_DIM // 2
    lane = jnp.arange(HEAD_DIM)
    frequency = ROPE_BASE ** (-2.0 * (lane % half).astype(jnp.float32) / HEAD_DIM)
    angles = positions.astype(jnp.float32)[:, None] * frequency[None]
    cosine = jnp.cos(angles)
    sine = jnp.sin(angles) * jnp.where(lane < half, -1.0, 1.0)[None]
    keep = padding_mask.reshape(count, 1, SEQ)
    (
        full,
        normed_one,
        turned,
        plain,
        mixed,
        residual,
        d_normed_two,
        funneled,
        feed_ups,
        feed_downs,
        funnel_down,
        funnel_up,
        funnel_seen,
        feed_dots,
    ) = run_block(
        shard,
        activations,
        cotangent,
        (
            cosine,
            sine,
            keep,
            norm_gains,
            entry_down,
            funnel_value.T,
            widen_value,
            output_value,
            squares,
            magnitudes,
        ),
    )
    partial, partial_other, d_residual, funneled_other, total, norm = run_tail(
        (
            full,
            turned,
            plain,
            mixed,
            residual,
            d_normed_two,
            funneled,
            cotangent,
            activations,
            normed_one,
        ),
        (
            cosine,
            sine,
            keep,
            norm_gains,
            entry_down,
            attend_value,
            mixer_value.T,
            output_value,
            squares,
            magnitudes,
            funnel_down,
            funnel_up,
            funnel_seen,
            feed_dots,
            feed_downs,
            feed_ups,
        ),
    )

    def turned_over(items):
        return [
            jnp.swapaxes(item, -1, -2) if i in (0, 3, 4) else item for i, item in enumerate(items)
        ]

    results = update_all(total, norm, turned_over(params), turned_over(firsts), turned_over(seconds))
    updated, momenta, variances = (turned_over(results[i : i + 9]) for i in (0, 9, 18))
    gradient_norm = norm[0, 0]
    block_output = low(
        residual + (funneled.astype(jnp.float32) + funneled_other.astype(jnp.float32))
    )
    floats = activations.astype(jnp.float32)
    d_normed_one = partial.astype(jnp.float32) + partial_other.astype(jnp.float32)
    unused, first_pull = jax.vjp(lambda v: root_norm(v, norm_gains[0]), floats)
    input_gradient = d_residual + first_pull(d_normed_one)[0]
    return (
        block_output,
        input_gradient,
        gradient_norm,
        updated[0],
        updated[1],
        updated[2],
        updated[3],
        updated[4],
        updated[5],
        updated[6],
        updated[7],
        updated[8],
        momenta[0],
        momenta[1],
        momenta[2],
        momenta[3],
        momenta[4],
        momenta[5],
        momenta[6],
        momenta[7],
        momenta[8],
        variances[0],
        variances[1],
        variances[2],
        variances[3],
        variances[4],
        variances[5],
        variances[6],
        variances[7],
        variances[8],
    )


def solution(mesh):
    return jax.shard_map(
        body,
        mesh=mesh,
        in_specs=(
            P("dp", None),
            P("dp", None),
            P("dp"),
            P("dp"),
            P(),
            P("dp", "tensor"),
            P("dp", "tensor"),
            P("dp", "tensor"),
            P("dp", "tensor"),
            P("dp", "tensor"),
            P("tensor", "dp"),
            P("tensor", "dp"),
            P(),
            P(None, None, "tensor"),
            P(None, None, "tensor"),
            P("tensor", None),
            P("tensor", None),
            P(),
            P(None, "tensor"),
            P(None, "tensor"),
            P(),
            P(),
            P(None, None, "tensor"),
            P(None, None, "tensor"),
            P("tensor", None),
            P("tensor", None),
            P(),
            P(None, "tensor"),
            P(None, "tensor"),
            P(),
            P(),
            P(None, None, "tensor"),
            P(None, None, "tensor"),
            P("tensor", None),
            P("tensor", None),
            P(),
            P(None, "tensor"),
            P(None, "tensor"),
            P(),
        ),
        out_specs=(
            P("dp", None),
            P("dp", None),
            P(),
            P(),
            P(None, None, "tensor"),
            P(None, None, "tensor"),
            P("tensor", None),
            P("tensor", None),
            P(),
            P(None, "tensor"),
            P(None, "tensor"),
            P(),
            P(),
            P(None, None, "tensor"),
            P(None, None, "tensor"),
            P("tensor", None),
            P("tensor", None),
            P(),
            P(None, "tensor"),
            P(None, "tensor"),
            P(),
            P(),
            P(None, None, "tensor"),
            P(None, None, "tensor"),
            P("tensor", None),
            P("tensor", None),
            P(),
            P(None, "tensor"),
            P(None, "tensor"),
            P(),
        ),
        check_vma=False,
    )
```

```python
import functools

import jax
import jax.numpy as jnp
from jax import lax
from jax.experimental import pallas as pl
from jax.experimental.pallas import tpu as pltpu
from jax.sharding import PartitionSpec as P

HEAD_DIM = 128
RANK = 16
SEQ = 256
STEP = 5


HIGH_PRECISION = lax.Precision.HIGHEST
ADAPTER_SCALE = 2.0
NORM_EPS = 1e-05
COLUMN_EPS = 1e-06
BETA_ONE = 0.9
BETA_TWO = 0.999
ADAM_EPS = 1e-08
DECAY = 0.01
CLIP = 1.0
RATE_FACTOR = 0.02
RATE_LIFT = 0.2
RATE_SCALE = 0.5
RATE_LOUD = 2.0
ROPE_BASE = 10000.0
MASKED = -1e30


def decoupled_update(value, gradient, first, second, rate):
    momentum = BETA_ONE * first + (1.0 - BETA_ONE) * gradient
    variance = BETA_TWO * second + (1.0 - BETA_TWO) * gradient * gradient
    corrected = momentum / (1.0 - BETA_ONE**STEP)
    spread = jnp.sqrt(variance / (1.0 - BETA_TWO**STEP))
    return (value - rate * (corrected / (spread + ADAM_EPS) + DECAY * value), momentum, variance)


MESH = pl.DeviceIdType.MESH
LANES = 1024
VMEM = 62 * 1024 * 1024
CHUNK = 256


def partners_of(size):
    me = lax.axis_index("dp")
    found = []
    bit = 1
    while bit < size:
        down = lax.rem(lax.div(me, bit), 2)
        found.append(me + bit - 2 * bit * down)
        bit *= 2
    return found


def double_sum(total, inbox, sends, receives, size, sides, shared_rows):
    targets = [({"dp": p}, total.shape[0]) for p in partners_of(size)]
    side = lax.axis_index("tensor")
    targets += [
        ({"tensor": lax.rem(side + step, sides)}, shared_rows) for step in range(1, sides)
    ]
    for step, (target, count) in enumerate(targets):
        kept = pl.ds(0, count)
        copy = pltpu.make_async_remote_copy(
            src_ref=total,
            dst_ref=inbox.at[step],
            send_sem=sends.at[step],
            recv_sem=receives.at[step],
            device_id=target,
            device_id_type=MESH,
        )
        copy.start()
        copy.wait()
        total[kept] += inbox[step, kept]


def greet_sum(size, sides):
    barrier = pltpu.get_barrier_semaphore()
    side = lax.axis_index("tensor")
    targets = [{"dp": p} for p in partners_of(size)]
    targets += [{"tensor": lax.rem(side + step, sides)} for step in range(1, sides)]
    for target in targets:
        pl.semaphore_signal(barrier, inc=1, device_id=target, device_id_type=MESH)
    pl.semaphore_wait(barrier, len(targets))


def merge_kernel(
    size,
    sides,
    query_ref,
    key_ref,
    value_ref,
    gate_ref,
    widen_ref,
    mixer_ref,
    funnel_ref,
    entry_ref,
    attend_ref,
    lift_ref,
    mixer_down_ref,
    funnel_down_ref,
    output_ref,
    stature_ref,
    amplitude_ref,
    loudness_ref,
    shard_out,
    squares_out,
    magnitudes_out,
    total,
    inbox,
    direction_cut,
    direction_wide,
    direction_mixer,
    direction_funnel,
    sends,
    receives,
):
    greet_sum(size, sides)
    rows = query_ref.shape[0]
    wide = gate_ref.shape[1]
    me = lax.axis_index("dp")
    total[...] = jnp.zeros_like(total)

    def direction(base, down, up):
        return base.astype(jnp.float32) + ADAPTER_SCALE * lax.dot_general(
            down,
            up,
            (((0,), (0,)), ((), ())),
            precision=HIGH_PRECISION,
            preferred_element_type=jnp.float32,
        )

    magnitudes_out[...] = jnp.ones_like(magnitudes_out)
    for i in range(2):
        for r in range(2):
            magnitudes_out[2 * i + r : 2 * i + r + 1, :] = loudness_ref[
                i : i + 1, r * LANES : (r + 1) * LANES
            ]
    for i in range(3):
        magnitudes_out[4 + i : 5 + i, :] = stature_ref[i : i + 1, :]
    for i in range(2):
        for start in range(0, wide, CHUNK):
            row = 7 + 3 * i + start // LANES
            magnitudes_out[row : row + 1, pl.ds(start % LANES, CHUNK)] = amplitude_ref[
                i : i + 1, pl.ds(start, CHUNK)
            ]

    group = LANES // rows
    lane_group = lax.broadcasted_iota(jnp.int32, (1, LANES), 1) // rows
    for i, (base, down) in enumerate(
        ((mixer_ref, mixer_down_ref), (funnel_ref, funnel_down_ref))
    ):
        held = (direction_mixer, direction_funnel)[i]
        sums = jnp.zeros((1, rows), jnp.float32)
        for start in range(0, base.shape[0], CHUNK):
            piece = pl.ds(start, CHUNK)
            part = direction(base[piece], down[:, piece], output_ref[i])
            held[piece] = part
            sums += jnp.sum(part * part, axis=0, keepdims=True)
        spread = jnp.concatenate([sums] * group, axis=1)
        for r in range(2):
            here = lane_group == me - r * group
            total[2 * i + r : 2 * i + r + 1, :] = jnp.where(here, spread, 0.0)
    for i, base in enumerate((query_ref, key_ref, value_ref)):
        for start in range(0, LANES, CHUNK):
            piece = pl.ds(start, CHUNK)
            part = direction(base[:, piece], entry_ref[i], attend_ref[i, :, piece])
            direction_cut[i, :, piece] = part
            total[4 + i : 5 + i, piece] = jnp.sum(part * part, axis=0, keepdims=True)
    for i, base in enumerate((gate_ref, widen_ref)):
        for start in range(0, wide, CHUNK):
            piece = pl.ds(start, CHUNK)
            part = direction(base[:, piece], entry_ref[3 + i], lift_ref[i, :, piece])
            direction_wide[i, :, piece] = part
            row = 7 + 3 * i + start // LANES
            total[row : row + 1, pl.ds(start % LANES, CHUNK)] = jnp.sum(
                part * part, axis=0, keepdims=True
            )
    double_sum(total, inbox, sends, receives, size, sides, 4)
    squares_out[...] = total[...]
    ratio = magnitudes_out[...] / jnp.sqrt(total[...] + COLUMN_EPS)
    near = LANES // CHUNK
    for i in range(3):
        for b in range(near):
            lanes = slice(b * CHUNK, (b + 1) * CHUNK)
            shard_out[near * i + b] = (
                direction_cut[i, :, lanes] * ratio[4 + i : 5 + i, lanes]
            ).astype(jnp.bfloat16)
    for i in range(2):
        for start in range(0, wide, CHUNK):
            row = 7 + 3 * i + start // LANES
            shard_out[4 * near + 3 * (start // CHUNK) + i] = (
                direction_wide[i, :, pl.ds(start, CHUNK)]
                * ratio[row : row + 1, start % LANES : start % LANES + CHUNK]
            ).astype(jnp.bfloat16)
    for i, held in enumerate((direction_mixer, direction_funnel)):
        own = jnp.zeros((1, rows), jnp.float32)
        for r in range(2):
            for g in range(group):
                own += jnp.where(
                    me == r * group + g,
                    ratio[2 * i + r : 2 * i + r + 1, g * rows : (g + 1) * rows],
                    0.0,
                )
        for start in range(0, held.shape[0], CHUNK):
            part = (held[pl.ds(start, CHUNK)] * own).T.astype(jnp.bfloat16)
            if i == 0:
                shard_out[3 * near + start // CHUNK] = part
            else:
                shard_out[4 * near + 3 * (start // CHUNK) + 2] = part


def merge(bases, entry_rows, attend, widen, mixer_down, funnel_down, output_columns, scales):
    size = lax.axis_size("dp")
    sides = lax.axis_size("tensor")
    rows, cut = bases[0].shape
    wide = bases[3].shape[1]
    steps = len(bin(size)) - 3 + sides - 1
    lines = 16
    return pl.pallas_call(
        functools.partial(merge_kernel, size, sides),
        name="merge",
        out_shape=(
            jax.ShapeDtypeStruct(((4 * cut + 3 * wide) // CHUNK, rows, CHUNK), jnp.bfloat16),
            jax.ShapeDtypeStruct((lines, LANES), jnp.float32),
            jax.ShapeDtypeStruct((lines, LANES), jnp.float32),
        ),
        in_specs=[pl.BlockSpec(memory_space=pltpu.VMEM)] * 16,
        out_specs=[pl.BlockSpec(memory_space=pltpu.VMEM)] * 3,
        scratch_shapes=[
            pltpu.VMEM((lines, LANES), jnp.float32),
            pltpu.VMEM((steps, lines, LANES), jnp.float32),
            pltpu.VMEM((3, rows, cut), jnp.float32),
            pltpu.VMEM((2, rows, wide), jnp.float32),
            pltpu.VMEM((cut, rows), jnp.float32),
            pltpu.VMEM((wide, rows), jnp.float32),
            pltpu.SemaphoreType.DMA((steps,)),
            pltpu.SemaphoreType.DMA((steps,)),
        ],
        compiler_params=pltpu.CompilerParams(
            collective_id=0, has_side_effects=True, vmem_limit_bytes=VMEM
        ),
    )(*bases, entry_rows, attend, widen, mixer_down, funnel_down, output_columns, *scales)


def dot_nn(left, right):
    return jnp.dot(left, right, preferred_element_type=jnp.float32)


def dot_nt(left, right):
    return lax.dot_general(
        left, right, (((1,), (1,)), ((), ())), preferred_element_type=jnp.float32
    )


def long_row(lines, row, size):
    count = -(-size // LANES)
    return jnp.concatenate([lines[row + r : row + r + 1] for r in range(count)], axis=1)[:, :size]


BLOCKS = 3
HEAD_CHUNKS = 5
EXTRA_TICKS = 2


def gather_parts(size, shard, full, sems):
    line = size // 4
    early = 16
    late = shard.shape[1] - early
    me = lax.axis_index("dp")
    core, column, spot = lax.rem(me, 2), lax.rem(lax.div(me, 2), 2), lax.div(me, 4)
    right_sends, left_sends, right_gets, left_gets, pair_sems, core_sems, early_sems = sems

    def device(other_spot, other_column, other_core):
        return {"dp": (other_spot * 2 + other_column) * 2 + other_core}

    right = device(lax.rem(spot + 1, line), column, core)
    left = device(lax.rem(spot + line - 1, line), column, core)
    across = device(spot, 1 - column, core)
    twin = device(spot, column, 1 - core)

    def greet():
        barrier = pltpu.get_barrier_semaphore()
        peers = jnp.int32(3)
        for near, target in ((spot < line - 1, right), (spot > 0, left)):

            @pl.when(near)
            def _(target=target):
                pl.semaphore_signal(barrier, inc=1, device_id=target, device_id_type=MESH)

            peers += near.astype(jnp.int32)
        for target in (across, twin, {"tensor": 1 - lax.axis_index("tensor")}):
            pl.semaphore_signal(barrier, inc=1, device_id=target, device_id_type=MESH)
        pl.semaphore_wait(barrier, peers)

    def remote(source, target, send, get, where):
        return pltpu.make_async_remote_copy(
            src_ref=source,
            dst_ref=target,
            send_sem=send,
            recv_sem=get,
            device_id=where,
            device_id_type=MESH,
        )

    def early_copy(part, owner):
        first = 1 + BLOCKS
        blocks = pl.ds(0, first) if part == 0 else pl.ds(first, shard.shape[0] - first)
        return remote(
            shard.at[blocks, pl.ds(0, early)],
            full.at[blocks, spot, owner, core, pl.ds(0, early)],
            early_sems.at[part, 0],
            early_sems.at[part, 1],
            across,
        )

    def early_start():
        for part in range(2):
            early_copy(part, column).start()

    def early_wait(part):
        early_copy(part, 1 - column).wait_recv()
        early_copy(part, column).wait_send()

    def place_of(part, origin, blocks):
        if part == 0:
            return full.at[blocks, origin, column, core, pl.ds(early, late)]
        return full.at[blocks, origin, :, core, pl.ds(0, early)]

    def move(to_right, part, distance, chunk, start, count):
        sends, gets = (right_sends, right_gets) if to_right else (left_sends, left_gets)
        hop = distance - 1
        blocks = pl.ds(start, count)
        place = place_of(part, spot - hop if to_right else spot + hop, blocks)
        source = shard.at[blocks, pl.ds(early, late)] if hop == 0 and part == 0 else place
        kept = 2 * hop + part
        where = right if to_right else left
        return remote(source, place, sends.at[chunk, kept], gets.at[chunk, kept], where)

    def arrivals(to_right, distance, chunk, start, count):
        gets = right_gets if to_right else left_gets
        for part in range(2):
            origin = spot - distance if to_right else spot + distance
            place = place_of(part, origin, pl.ds(start, count))
            kept = 2 * (distance - 1) + part
            remote(
                place, place, right_sends.at[chunk, kept], gets.at[chunk, kept], right
            ).wait_recv()

    def reaches(to_right, distance):
        if to_right:
            return (spot >= distance - 1) & (spot < line - 1)
        return (spot <= line - distance) & (spot > 0)

    def pair_copy(chunk, start, count, owner):
        place = full.at[pl.ds(start, count), :, owner, core, pl.ds(early, late)]
        return remote(place, place, pair_sems.at[chunk, 0], pair_sems.at[chunk, 1], across)

    def core_copy(chunk, start, count, owner):
        place = full.at[pl.ds(start, count), :, :, owner]
        return remote(place, place, core_sems.at[chunk, 0], core_sems.at[chunk, 1], twin)

    def send(distances, parts, chunk, start, count):
        for to_right in (True, False):
            for distance in distances:

                @pl.when(reaches(to_right, distance))
                def _(to_right=to_right, distance=distance):
                    for part in parts:
                        move(to_right, part, distance, chunk, start, count).start()

    def take_in(distance, chunk, start, count):
        @pl.when(spot >= distance)
        def _():
            arrivals(True, distance, chunk, start, count)

        @pl.when(spot < line - distance)
        def _():
            arrivals(False, distance, chunk, start, count)

    def own(parts, chunk, start, count):
        send((1,), parts, chunk, start, count)

    def turn(distance, chunk, start, count):
        take_in(distance, chunk, start, count)
        if distance < line - 1:
            send((distance + 1,), (0, 1), chunk, start, count)
        else:
            pair_copy(chunk, start, count, column).start()

    def pair_done(chunk, start, count):
        pair_copy(chunk, start, count, 1 - column).wait_recv()
        core_copy(chunk, start, count, core).start()

    def core_done(chunk, start, count):
        core_copy(chunk, start, count, 1 - core).wait_recv()

    def finish(chunk, start, count):
        for to_right in (True, False):
            for distance in range(1, line):

                @pl.when(reaches(to_right, distance))
                def _(to_right=to_right, distance=distance):
                    for part in range(2):
                        move(to_right, part, distance, chunk, start, count).wait_send()

        pair_copy(chunk, start, count, column).wait_send()
        core_copy(chunk, start, count, core).wait_send()

    def stages(pace):
        found = {0: functools.partial(own, (0, 1))}
        for distance in range(1, line):
            found[pace * distance] = functools.partial(turn, distance)
        last = pace * (line - 1)
        found[last + 2] = pair_done
        found[last + 3] = core_done
        found[last + 4] = finish
        return found

    return greet, own, stages, early_start, early_wait, finish


def block_kernel(
    size,
    shard,
    rows_ref,
    back_ref,
    cosine_ref,
    sine_ref,
    keep_ref,
    gain_ref,
    entry_ref,
    funnel_ref,
    lift_ref,
    output_ref,
    squares_ref,
    magnitudes_ref,
    full,
    normed_out,
    turned_out,
    plain_out,
    mixed_out,
    residual_out,
    d_normed_out,
    funneled_out,
    up_out,
    down_out,
    funnel_down_out,
    funnel_up_out,
    funnel_seen_out,
    dots_out,
    normed,
    back,
    floats,
    turned,
    plain,
    mixed,
    heads_weight,
    feed_weight,
    residual,
    d_normed,
    funneled,
    outbox,
    inbox,
    lowered,
    reduced,
    funnel_lowered,
    funnel_reduced,
    low_lift_ref,
    pull_lift_ref,
    ratio_ref,
    pull_ref,
    funnel_down_ref,
    right_sends,
    left_sends,
    right_gets,
    left_gets,
    pair_sems,
    core_sems,
    early_sems,
    local_sems,
    weight_sems,
    feed_sems,
    side_sends,
    side_gets,
    out_sems,
):
    line = size // 4
    total_blocks = full.shape[0]
    chunks = total_blocks // BLOCKS
    tokens, width = normed.shape[0] - 2 * RANK, normed.shape[1]
    count = tokens // SEQ
    sides = {"tensor": 1 - lax.axis_index("tensor")}
    sems = (right_sends, left_sends, right_gets, left_gets, pair_sems, core_sems, early_sems)
    greet, send_own, stages, early_start, early_wait, finish = gather_parts(
        size, shard, full, sems
    )
    me = lax.axis_index("dp")
    core, column, spot = lax.rem(me, 2), lax.rem(lax.div(me, 2), 2), lax.div(me, 4)

    slow, fast = stages(1), stages(1)
    lag = (line - 1) + 3

    def tick(now, sends=True):
        for phase, stage in slow.items():
            chunk = now - phase
            if phase == 0 and not sends:
                continue
            start = 1 + BLOCKS * chunk
            if isinstance(now, int):
                if 1 <= chunk < chunks:
                    stage(chunk, start, BLOCKS)
            else:

                @pl.when((chunk >= 1) & (chunk < chunks))
                def _(stage=stage, chunk=chunk, start=start):
                    stage(chunk, start, BLOCKS)

    def first_ticks(now):
        if now in fast:
            fast[now](chunks, 0, 1)
            fast[now](0, 1, BLOCKS)

    own = pltpu.make_async_copy(shard, full.at[:, spot, column, core], local_sems.at[0])
    own.start()
    loads = [
        pltpu.make_async_copy(rows_ref, floats, local_sems.at[1]),
        pltpu.make_async_copy(back_ref, back, local_sems.at[2]),
    ]
    for load in loads:
        load.start()
    greet()
    early_start()
    send_own((0,), chunks, 0, 1)
    send_own((0,), 0, 1, BLOCKS)
    own.wait()
    early_wait(0)
    send_own((1,), chunks, 0, 1)
    send_own((1,), 0, 1, BLOCKS)
    early_wait(1)
    for load in loads:
        load.wait()
    tile = 32

    def norm_rows(index, carry):
        place = pl.ds(pl.multiple_of(index * tile, tile), tile)
        value = floats[place].astype(jnp.float32)
        root = lax.rsqrt(jnp.mean(value * value, axis=1, keepdims=True) + NORM_EPS)
        normed[place] = (value * root * gain_ref[0:1]).astype(jnp.bfloat16)
        return carry

    def prepare():
        lax.fori_loop(0, tokens // tile, norm_rows, 0)
        norms = jnp.sqrt(squares_ref[...] + COLUMN_EPS)
        ratios = magnitudes_ref[...] / norms
        pulls = 1.0 / (norms * magnitudes_ref[...])
        wide = funnel_down_ref.shape[1]
        lines = -(-wide // LANES)
        for i in range(2):
            ratio = long_row(ratios, 7 + lines * i, wide)
            pull = long_row(pulls, 7 + lines * i, wide)
            ratio_ref[i : i + 1] = ratio
            pull_ref[i : i + 1] = pull
            low_lift_ref[i] = (lift_ref[i] * ratio).astype(jnp.bfloat16)
            pull_lift_ref[i] = lift_ref[i] * pull
        funnel_down_ref[...] = funnel_ref[...].astype(jnp.bfloat16)
        low_output = (output_ref[1] * long_row(ratios, 2, width)).astype(jnp.bfloat16)
        funnel_lowered[...] = dot_nt(low_output, back[...]).astype(jnp.bfloat16)
        for i in range(2):
            normed[pl.ds(tokens + RANK * i, RANK)] = entry_ref[3 + i].astype(jnp.bfloat16)

    head_ticks = max(fast) + 1
    for now in range(1, head_ticks):
        first_ticks(now)
        tick(now)
        if now == 1:
            prepare()
    normed_copy = pltpu.make_async_copy(
        normed.at[pl.ds(0, tokens)], normed_out, local_sems.at[3]
    )
    normed_copy.start()
    ready = HEAD_CHUNKS - 2 + lag
    lax.fori_loop(head_ticks, ready + 1, lambda now, carry: (tick(now), carry)[1], 0)

    def head_load(block, slot):
        return pltpu.make_async_copy(
            full.at[block], heads_weight.at[slot], weight_sems.at[slot]
        )

    def head_weight(slot):
        return heads_weight[slot].reshape(width, CHUNK)

    cut_blocks = turned.shape[0] // 3
    head_load(0, 0).start()

    def project(block, carry):
        slot = lax.rem(block, 2)

        @pl.when(block < 3 * cut_blocks - 1)
        def _():
            head_load(block + 1, 1 - slot).start()

        head_load(block, slot).wait()
        for part in range(count):
            place = pl.ds(part * SEQ, SEQ)
            result = dot_nn(normed[place], head_weight(slot))
            plain[block, place] = result.astype(jnp.bfloat16)

            @pl.when(block < 2 * cut_blocks)
            def _(result=result, place=place):
                for half in range(CHUNK // HEAD_DIM):
                    lanes = slice(half * HEAD_DIM, (half + 1) * HEAD_DIM)
                    head = result[:, lanes]
                    turned[block, place, lanes] = (
                        head * cosine_ref[place]
                        + pltpu.roll(head, HEAD_DIM // 2, 1) * sine_ref[place]
                    ).astype(jnp.bfloat16)

            @pl.when(block >= 2 * cut_blocks)
            def _(result=result, place=place):
                turned[block, place] = result.astype(jnp.bfloat16)

        return carry

    lax.fori_loop(0, 3 * cut_blocks, project, 0)
    outs = [
        pltpu.make_async_copy(turned, turned_out, out_sems.at[0]),
        pltpu.make_async_copy(plain.at[pl.ds(0, 2 * cut_blocks)], plain_out, out_sems.at[1]),
    ]
    for out in outs:
        out.start()
    tick(ready + 1)

    mixer_loads = [
        pltpu.make_async_copy(
            full.at[3 * cut_blocks + b],
            feed_weight.at[0, :, :, :, :, pl.ds(b * CHUNK, CHUNK)],
            weight_sems.at[b],
        )
        for b in range(cut_blocks)
    ]
    for load in mixer_loads:
        load.start()
    line_up = lax.broadcasted_iota(jnp.int32, (SEQ, SEQ), 0)
    line_on = lax.broadcasted_iota(jnp.int32, (SEQ, SEQ), 1)

    def attend(block, carry):
        for part in range(count):
            place = pl.ds(part * SEQ, SEQ)
            allowed = ((line_up >= line_on) & (keep_ref[part] > 0)) | (line_up == line_on)
            for half in range(CHUNK // HEAD_DIM):
                lanes = slice(half * HEAD_DIM, (half + 1) * HEAD_DIM)
                scores = dot_nt(
                    turned[block, place, lanes], turned[cut_blocks + block, place, lanes]
                ) * (HEAD_DIM ** (-0.5))
                masked = jnp.where(allowed, scores, MASKED)
                top = jnp.max(masked, axis=1, keepdims=True)
                weight = jnp.exp(masked - top)
                attention = weight / jnp.sum(weight, axis=1, keepdims=True)
                mixed[block, place, lanes] = dot_nn(
                    attention.astype(jnp.bfloat16), turned[2 * cut_blocks + block, place, lanes]
                ).astype(jnp.bfloat16)
        return carry

    lax.fori_loop(0, cut_blocks, attend, 0)
    outs.append(pltpu.make_async_copy(mixed, mixed_out, out_sems.at[2]))
    outs[-1].start()
    tick(ready + 2)

    for load in mixer_loads:
        load.wait()

    def side_copy(part):
        place = pl.ds(part * SEQ, SEQ)
        return pltpu.make_async_remote_copy(
            src_ref=outbox.at[place],
            dst_ref=inbox.at[place],
            send_sem=side_sends.at[part],
            recv_sem=side_gets.at[part],
            device_id=sides,
            device_id_type=MESH,
        )

    for part in range(count):
        place = pl.ds(part * SEQ, SEQ)
        joined = jnp.concatenate([mixed[b, place] for b in range(cut_blocks)], axis=1)
        per = 512 // (4 * feed_weight.shape[4])
        for piece in range(width // 512):
            weight = feed_weight[0, pl.ds(piece * per, per), :, :, :, pl.ds(0, cut_blocks * CHUNK)]
            outbox[place, pl.ds(piece * 512, 512)] = dot_nt(
                joined, weight.reshape(512, cut_blocks * CHUNK)
            ).astype(jnp.bfloat16)
        side_copy(part).start()
    tick(ready + 3)

    normed_copy.wait()
    for part in range(count):
        side_copy(part).wait()

        def add_up(index, carry, part=part):
            place = pl.ds(pl.multiple_of(part * SEQ + index * tile, tile), tile)
            value = floats[place].astype(jnp.float32) + (
                outbox[place].astype(jnp.float32) + inbox[place].astype(jnp.float32)
            )
            residual[place] = value
            root = lax.rsqrt(jnp.mean(value * value, axis=1, keepdims=True) + NORM_EPS)
            normed[place] = (value * root * gain_ref[1:2]).astype(jnp.bfloat16)
            return carry

        lax.fori_loop(0, SEQ // tile, add_up, 0)
        if part == 0:
            tick(ready + 4)
    outs.append(pltpu.make_async_copy(residual, residual_out, out_sems.at[3]))
    outs[-1].start()
    reduced[...] = dot_nt(normed[pl.ds(tokens, 2 * RANK)], normed[pl.ds(0, tokens)]).astype(
        jnp.bfloat16
    )
    d_normed[...] = jnp.zeros_like(d_normed)
    funneled[...] = jnp.zeros_like(funneled)
    lowered[...] = jnp.zeros_like(lowered)
    funnel_reduced[...] = jnp.zeros_like(funnel_reduced)

    def feed_load(index, slot, owner):
        return [
            pltpu.make_async_copy(
                full.at[4 * cut_blocks + BLOCKS * index + b, :, :, owner],
                feed_weight.at[slot, :, :, owner, :, pl.ds(b * CHUNK, CHUNK)],
                feed_sems.at[slot, owner, b],
            )
            for b in range(BLOCKS)
        ]

    for load in feed_load(0, 0, core):
        load.start()
    nothing = jnp.zeros((RANK, CHUNK), jnp.bfloat16)

    def feed(index, carry):
        now = index + HEAD_CHUNKS + lag
        first = ready + 5
        for early_step in range(EXTRA_TICKS):

            @pl.when(index == 2 * early_step + 1)
            def _(early_step=early_step):
                tick(first + early_step)

        @pl.when(now >= first + EXTRA_TICKS)
        def _():
            tick(now)

        slot = lax.rem(index, 2)
        for load in feed_load(index, slot, 1 - core):
            load.start()

        @pl.when(index < chunks - HEAD_CHUNKS - 1)
        def _():
            for load in feed_load(index + 1, 1 - slot, core):
                load.start()

        for owner in (core, 1 - core):
            for load in feed_load(index, slot, owner):
                load.wait()
        columns = pl.ds(pl.multiple_of(index * CHUNK, CHUNK), CHUNK)
        weight = feed_weight[slot, :, :, :, :, pl.ds(0, 2 * CHUNK)].reshape(width, 2 * CHUNK)
        both = dot_nn(normed[...], weight)
        gate, lifted = both[:tokens, :CHUNK], both[:tokens, CHUNK:]
        gate_seen = both[tokens : tokens + RANK, :CHUNK]
        lifted_seen = both[tokens + RANK :, CHUNK:]
        funnel = feed_weight[slot, :, :, :, :, pl.ds(2 * CHUNK, CHUNK)].reshape(width, CHUNK)
        d_hidden = dot_nn(back[...], funnel)
        sigmoid = 1.0 / (1.0 + jnp.exp(-gate))
        silu = gate * sigmoid
        hidden = (silu * lifted).astype(jnp.bfloat16)
        d_gate = (d_hidden * lifted * (sigmoid * (1.0 + gate * (1.0 - sigmoid)))).astype(
            jnp.bfloat16
        )
        d_lifted = (d_hidden * silu).astype(jnp.bfloat16)
        gate_dots = jnp.sum(d_gate.astype(jnp.float32) * gate, axis=0, keepdims=True)
        lifted_dots = jnp.sum(d_lifted.astype(jnp.float32) * lifted, axis=0, keepdims=True)
        dots_out[0:1, columns] = gate_dots
        dots_out[1:2, columns] = lifted_dots
        gate_pull = (pull_lift_ref[0, :, columns] * gate_dots).astype(jnp.bfloat16)
        lifted_pull = (pull_lift_ref[1, :, columns] * lifted_dots).astype(jnp.bfloat16)
        up_out[0, :, columns] = ADAPTER_SCALE * (
            dot_nn(reduced[pl.ds(0, RANK)], d_gate) * ratio_ref[0:1, columns]
            - gate_seen * (pull_ref[0:1, columns] * gate_dots)
        )
        up_out[1, :, columns] = ADAPTER_SCALE * (
            dot_nn(reduced[pl.ds(RANK, RANK)], d_lifted) * ratio_ref[1:2, columns]
            - lifted_seen * (pull_ref[1:2, columns] * lifted_dots)
        )
        lowered[pl.ds(0, RANK)] += dot_nt(low_lift_ref[0, :, columns], d_gate)
        lowered[pl.ds(RANK, RANK)] += dot_nt(low_lift_ref[1, :, columns], d_lifted)
        funnel_down_out[:, columns] = ADAPTER_SCALE * dot_nn(funnel_lowered[...], hidden)
        funnel_down = funnel_down_ref[:, columns]
        funnel_reduced[...] += dot_nt(funnel_down, hidden)
        sources = jnp.concatenate([hidden, funnel_down], axis=0)
        gradients = jnp.concatenate(
            [
                jnp.concatenate([d_gate, d_lifted], axis=1),
                jnp.concatenate([gate_pull, nothing], axis=1),
                jnp.concatenate([nothing, lifted_pull], axis=1),
            ],
            axis=0,
        )
        per = 512 // (4 * feed_weight.shape[4])
        for piece in range(width // 512):
            near = pl.ds(piece * per, per)
            funnel_rows = feed_weight[slot, near, :, :, :, pl.ds(2 * CHUNK, CHUNK)]
            gate_rows = feed_weight[slot, near, :, :, :, pl.ds(0, 2 * CHUNK)]
            lanes = pl.ds(piece * 512, 512)
            funneled[:, lanes] += dot_nt(sources, funnel_rows.reshape(512, CHUNK))
            d_normed[:, lanes] += dot_nt(
                gradients, gate_rows.reshape(512, 2 * CHUNK)
            )
        return carry

    lax.fori_loop(0, chunks - HEAD_CHUNKS, feed, 0)
    outbox[...] = d_normed[pl.ds(0, tokens)].astype(jnp.bfloat16)
    outs.append(pltpu.make_async_copy(outbox, d_normed_out, out_sems.at[4]))
    outs[-1].start()
    down_out[...] = ADAPTER_SCALE * (
        dot_nn(lowered[...].astype(jnp.bfloat16), normed[pl.ds(0, tokens)])
        - d_normed[pl.ds(tokens, 2 * RANK)]
    )
    floats[...] = funneled[pl.ds(0, tokens)].astype(jnp.bfloat16)
    outs.append(pltpu.make_async_copy(floats, funneled_out, out_sems.at[5]))
    outs[-1].start()
    funnel_up_out[...] = dot_nn(funnel_reduced[...].astype(jnp.bfloat16), back[...])
    funnel_seen_out[...] = funneled[pl.ds(tokens, RANK)]
    finish(chunks - 1, 1 + BLOCKS * (chunks - 1), BLOCKS)
    for out in outs:
        out.wait()


def run_block(shard, rows, back, small):
    size = lax.axis_size("dp")
    line = size // 4
    tokens, width = rows.shape
    blocks, height, _ = shard.shape
    chunks = blocks // BLOCKS
    cut_blocks = (BLOCKS * HEAD_CHUNKS + 1) // 4
    wide = small[6].shape[2]
    anywhere = pl.BlockSpec(memory_space=pl.ANY)
    local = pl.BlockSpec(memory_space=pltpu.VMEM)
    low = jnp.bfloat16
    full = jnp.float32
    out_shape = (
        jax.ShapeDtypeStruct((blocks, line, 2, 2, height, CHUNK), low),
        jax.ShapeDtypeStruct((tokens, width), low),
        jax.ShapeDtypeStruct((3 * cut_blocks, tokens, CHUNK), low),
        jax.ShapeDtypeStruct((2 * cut_blocks, tokens, CHUNK), low),
        jax.ShapeDtypeStruct((cut_blocks, tokens, CHUNK), low),
        jax.ShapeDtypeStruct((tokens, width), full),
        jax.ShapeDtypeStruct((tokens, width), low),
        jax.ShapeDtypeStruct((tokens, width), low),
        jax.ShapeDtypeStruct((2, RANK, wide), full),
        jax.ShapeDtypeStruct((2 * RANK, width), full),
        jax.ShapeDtypeStruct((RANK, wide), full),
        jax.ShapeDtypeStruct((RANK, width), full),
        jax.ShapeDtypeStruct((RANK, width), full),
        jax.ShapeDtypeStruct((2, wide), full),
    )
    scratch = [
        pltpu.VMEM((tokens + 2 * RANK, width), low),
        pltpu.VMEM((tokens, width), low),
        pltpu.VMEM((tokens, width), low),
        pltpu.VMEM((3 * cut_blocks, tokens, CHUNK), low),
        pltpu.VMEM((3 * cut_blocks, tokens, CHUNK), low),
        pltpu.VMEM((cut_blocks, tokens, CHUNK), low),
        pltpu.VMEM((2, line, 2, 2, height, CHUNK), low),
        pltpu.VMEM((2, line, 2, 2, height, 4 * CHUNK), low),
        pltpu.VMEM((tokens, width), full),
        pltpu.VMEM((tokens + 2 * RANK, width), full),
        pltpu.VMEM((tokens + RANK, width), full),
        pltpu.VMEM((tokens, width), low),
        pltpu.VMEM((tokens, width), low),
        pltpu.VMEM((2 * RANK, tokens), full),
        pltpu.VMEM((2 * RANK, tokens), low),
        pltpu.VMEM((RANK, tokens), low),
        pltpu.VMEM((RANK, tokens), full),
        pltpu.VMEM((2, RANK, wide), low),
        pltpu.VMEM((2, RANK, wide), full),
        pltpu.VMEM((2, wide), full),
        pltpu.VMEM((2, wide), full),
        pltpu.VMEM((RANK, wide), low),
        pltpu.SemaphoreType.DMA((chunks + 1, 2 * (line - 1))),
        pltpu.SemaphoreType.DMA((chunks + 1, 2 * (line - 1))),
        pltpu.SemaphoreType.DMA((chunks + 1, 2 * (line - 1))),
        pltpu.SemaphoreType.DMA((chunks + 1, 2 * (line - 1))),
        pltpu.SemaphoreType.DMA((chunks + 1, 2)),
        pltpu.SemaphoreType.DMA((chunks + 1, 2)),
        pltpu.SemaphoreType.DMA((2, 2)),
        pltpu.SemaphoreType.DMA((4,)),
        pltpu.SemaphoreType.DMA((4,)),
        pltpu.SemaphoreType.DMA((2, 2, BLOCKS)),
        pltpu.SemaphoreType.DMA((tokens // SEQ,)),
        pltpu.SemaphoreType.DMA((tokens // SEQ,)),
        pltpu.SemaphoreType.DMA((6,)),
    ]
    return pl.pallas_call(
        functools.partial(block_kernel, size),
        name="block",
        out_shape=out_shape,
        in_specs=[local] + [anywhere] * 2 + [local] * 10,
        out_specs=[anywhere] * 8 + [local] * 6,
        scratch_shapes=scratch,
        compiler_params=pltpu.CompilerParams(
            collective_id=1, has_side_effects=True, vmem_limit_bytes=VMEM
        ),
    )(shard, rows, back, *small)


def tail_kernel(
    size,
    sides,
    widths,
    full,
    turned_ref,
    plain_ref,
    mixed_ref,
    residual_ref,
    d_normed_ref,
    funneled_ref,
    back_ref,
    rows_ref,
    normed_ref,
    cosine_ref,
    sine_ref,
    keep_ref,
    gain_ref,
    entry_ref,
    attend_ref,
    mixer_ref,
    output_ref,
    squares_ref,
    magnitudes_ref,
    funnel_down_ref,
    funnel_up_ref,
    funnel_seen_ref,
    feed_dots_ref,
    feed_down_ref,
    feed_up_ref,
    gradient_out,
    block_out,
    funneled_out,
    total,
    norm_out,
    weights,
    residual,
    floats,
    back,
    normed,
    turned,
    plain,
    mixed,
    own,
    inbox,
    last_inbox,
    funneled,
    attention,
    d_low,
    d_heads,
    funnel_weight,
    dots_box,
    mixer_dots,
    entry_down_ref,
    funnel_down,
    gathered,
    dots_out,
    side_box,
    norm_box,
    kept_rows,
    other_rows,
    load_sems,
    weight_sems,
    funnel_sems,
    side_sends,
    side_gets,
    out_sems,
    kept_sems,
    *sum_refs,
):
    tokens, width = back.shape
    count = tokens // SEQ
    cut = d_heads.shape[2]
    near = cut // CHUNK
    wide = funnel_down_ref.shape[1]
    scale = HEAD_DIM ** (-0.5)
    other = {"tensor": lax.rem(lax.axis_index("tensor") + 1, sides)}
    halves = CHUNK // HEAD_DIM
    half_rows = gathered.shape[0] // 2

    loads = [
        pltpu.make_async_copy(source, target, load_sems.at[i])
        for i, (source, target) in enumerate(
            (
                (funneled_ref, funneled),
                (back_ref, back),
                (turned_ref, turned),
                (normed_ref, normed),
                (d_normed_ref, own),
                (residual_ref, residual),
                (rows_ref, floats),
                (mixed_ref, mixed),
                (plain_ref, plain),
            )
        )
    ]
    weight_loads = [
        pltpu.make_async_copy(
            full.at[near * i + b],
            weights.at[i, :, :, :, :, pl.ds(b * CHUNK, CHUNK)],
            weight_sems.at[near * i + b],
        )
        for i in range(4)
        for b in range(near)
    ]
    for load in loads[:3]:
        load.start()
    greet_sum(size, sides)

    def remote(source, target, index):
        return pltpu.make_async_remote_copy(
            src_ref=source,
            dst_ref=target,
            send_sem=side_sends.at[index],
            recv_sem=side_gets.at[index],
            device_id=other,
            device_id_type=MESH,
        )

    def rows_of(part):
        return pl.ds(part * SEQ, SEQ)

    part_copies = [
        remote(d_normed_ref.at[rows_of(part)], inbox.at[rows_of(part)], part)
        for part in range(count)
    ]
    part_copies[0].start()
    for load in loads[3:] + weight_loads:
        load.start()
    dots_copy = remote(dots_box.at[0], dots_box.at[1], count)
    funneled_copies = [
        remote(funneled_ref.at[rows_of(part)], funneled_out.at[rows_of(part)], count + 1 + part)
        for part in range(count)
    ]
    last_copies = [
        remote(own.at[rows_of(part)], last_inbox.at[rows_of(part)], 2 * count + 1 + part)
        for part in range(count)
    ]
    norms = jnp.sqrt(squares_ref[...] + COLUMN_EPS)
    ratios = magnitudes_ref[...] / norms
    pulls = 1.0 / (norms * magnitudes_ref[...])
    for i in range(3):
        entry_down_ref[pl.ds(RANK * i, RANK)] = entry_ref[i].astype(jnp.bfloat16)
    mixer_low = mixer_ref[...].astype(jnp.bfloat16)
    output_ratio = [long_row(ratios, 2 * i, width) for i in range(2)]
    output_pull = [long_row(pulls, 2 * i, width) for i in range(2)]

    def weight_of(i):
        return weights[i].reshape(width, cut)

    loads[0].wait()
    loads[1].wait()
    tile = 64

    def count_dots(index, total):
        place = pl.ds(pl.multiple_of(index * tile, tile), tile)
        return total + jnp.sum(
            back[place].astype(jnp.float32) * funneled[place].astype(jnp.float32),
            axis=0,
            keepdims=True,
        )

    funnel_dots = lax.fori_loop(
        0, tokens // tile, count_dots, jnp.zeros((1, width), jnp.float32)
    )
    dots_box[0] = jnp.broadcast_to(funnel_dots, dots_box.shape[1:])
    dots_copy.start()
    loads[2].wait()
    line_up = lax.broadcasted_iota(jnp.int32, (SEQ, SEQ), 0)
    line_on = lax.broadcasted_iota(jnp.int32, (SEQ, SEQ), 1)

    def attend(block, carry):
        for part in range(count):
            place = rows_of(part)
            allowed = ((line_up >= line_on) & (keep_ref[part] > 0)) | (line_up == line_on)
            for half in range(halves):
                lanes = slice(half * HEAD_DIM, (half + 1) * HEAD_DIM)
                scores = dot_nt(
                    turned[block, place, lanes], turned[near + block, place, lanes]
                ) * scale
                masked = jnp.where(allowed, scores, MASKED)
                top = jnp.max(masked, axis=1, keepdims=True)
                weight = jnp.exp(masked - top)
                attention[part, halves * block + half] = weight / jnp.sum(
                    weight, axis=1, keepdims=True
                )
        return carry

    lax.fori_loop(0, near, attend, 0)
    for copy in part_copies[1:]:
        copy.start()

    def funnel_lanes(block):
        half = 0 if isinstance(block, int) else lax.rem(block, 2) * (CHUNK // 2)
        return pl.ds(pl.multiple_of(half, CHUNK // 2), CHUNK // 2)

    def funnel_load(block, slot):
        return pltpu.make_async_copy(
            full.at[4 * near + BLOCKS * lax.div(block, 2) + 2, :, :, :, :, funnel_lanes(block)],
            funnel_weight.at[slot],
            funnel_sems.at[slot],
        )

    funnel_load(0, 0).start()
    for load in loads[3:] + weight_loads:
        load.wait()
    head_seen = [
        dot_nn(entry_down_ref[pl.ds(RANK * i, RANK)], weight_of(i)) for i in range(3)
    ]
    mixer_seen = dot_nt(mixer_low, weight_of(3))
    reduced = dot_nt(entry_down_ref[...], normed[...]).astype(jnp.bfloat16)
    dots_copy.wait()
    funnel_dots = dots_box[0, 0:1] + dots_box[1, 0:1]
    funnel_pull = (output_ref[1] * (output_pull[1] * funnel_dots)).astype(jnp.bfloat16)

    def correct(block, carry):
        slot = lax.rem(block, 2)

        @pl.when(block < 2 * wide // CHUNK - 1)
        def _():
            funnel_load(block + 1, 1 - slot).start()

        funnel_load(block, slot).wait()
        columns = pl.ds(pl.multiple_of(block * (CHUNK // 2), CHUNK // 2), CHUNK // 2)
        funnel_down[:, columns] = funnel_down_ref[:, columns] - ADAPTER_SCALE * dot_nn(
            funnel_pull, funnel_weight[slot].reshape(width, CHUNK // 2)
        )
        return carry

    lax.fori_loop(0, 2 * wide // CHUNK, correct, 0)
    gathered[pl.ds(6 * RANK, RANK)] = ADAPTER_SCALE * (
        funnel_up_ref[...] * output_ratio[1]
        - funnel_seen_ref[...] * (output_pull[1] * funnel_dots)
    )
    gathered[pl.ds(3 * RANK, 2 * RANK)] = feed_down_ref[...]
    mixer_dots[...] = jnp.zeros_like(mixer_dots)
    small = 32
    for part in range(count):
        part_copies[part].wait()
        if part == count - 1:
            funneled_copies[0].start()

        def pull_back(index, carry, part=part):
            place = pl.ds(pl.multiple_of(part * SEQ + index * small, small), small)
            value = residual[place]
            weighted = gain_ref[1:2] * (
                own[place].astype(jnp.float32) + inbox[place].astype(jnp.float32)
            )
            root = lax.rsqrt(jnp.mean(value * value, axis=1, keepdims=True) + NORM_EPS)
            along = jnp.mean(value * weighted, axis=1, keepdims=True)
            gradient = back[place].astype(jnp.float32) + (
                root * weighted - value * (root * root * root * along)
            )
            rounded = gradient.astype(jnp.bfloat16)
            d_low[place] = rounded
            attended = value - floats[place].astype(jnp.float32)
            mixer_dots[...] += jnp.sum(
                (rounded.astype(jnp.float32) * attended).reshape(small // 8, 8, width), axis=0
            )
            residual[place] = gradient
            return carry

        lax.fori_loop(0, SEQ // small, pull_back, 0)
        place = rows_of(part)

        def attend_back(block, carry, part=part, place=place):
            columns = pl.ds(pl.multiple_of(block * CHUNK, CHUNK), CHUNK)
            mixer = weights[3, :, :, :, :, columns].reshape(width, CHUNK)
            d_mixed = dot_nn(d_low[place], mixer).astype(jnp.bfloat16)
            for half in range(halves):
                lanes = slice(half * HEAD_DIM, (half + 1) * HEAD_DIM)
                spot = pl.ds(
                    pl.multiple_of(block * CHUNK + half * HEAD_DIM, HEAD_DIM), HEAD_DIM
                )
                weight = attention[part, halves * block + half]
                d_head = d_mixed[:, lanes]
                d_attention = dot_nt(d_head, turned[2 * near + block, place, lanes])
                d_heads[2, place, spot] = dot_nn(
                    weight.astype(jnp.bfloat16).T, d_head
                ).astype(jnp.bfloat16)
                inner = jnp.sum(weight * d_attention, axis=1, keepdims=True)
                d_scores = (weight * (d_attention - inner)).astype(jnp.bfloat16)
                d_query = dot_nn(d_scores, turned[near + block, place, lanes]) * scale
                d_key = dot_nn(d_scores.T, turned[block, place, lanes]) * scale
                for i, value in ((0, d_query), (1, d_key)):
                    d_heads[i, place, spot] = (
                        value * cosine_ref[place]
                        - pltpu.roll(value, HEAD_DIM // 2, 1) * sine_ref[place]
                    ).astype(jnp.bfloat16)
            return carry

        lax.fori_loop(0, near, attend_back, 0)
    per = 512 // (4 * weights.shape[4])
    for i in range(3):
        dots = []
        for block in range(near):
            lanes = slice(block * CHUNK, (block + 1) * CHUNK)
            source = plain if i < 2 else turned
            dots.append(
                jnp.sum(
                    d_heads[i, :tokens, lanes].astype(jnp.float32)
                    * source[near * i + block].astype(jnp.float32),
                    axis=0,
                    keepdims=True,
                )
            )
        dots = jnp.concatenate(dots, axis=1)
        dots_out[4 + i : 5 + i] = dots
        head_ratio = ratios[4 + i : 5 + i]
        pulled = (attend_ref[i] * (pulls[4 + i : 5 + i] * dots)).astype(jnp.bfloat16)
        place_in(
            gathered,
            half_rows,
            cut * i,
            ADAPTER_SCALE
            * (
                dot_nn(reduced[RANK * i : RANK * (i + 1)], d_heads[i, :tokens]) * head_ratio
                - head_seen[i] * (pulls[4 + i : 5 + i] * dots)
            ),
        )
        low_lift = (attend_ref[i] * head_ratio).astype(jnp.bfloat16)
        lowered = dot_nt(low_lift, d_heads[i, :tokens]).astype(jnp.bfloat16)
        gathered[pl.ds(RANK * i, RANK)] = ADAPTER_SCALE * dot_nn(lowered, normed[...])
        d_heads[i, tokens:] = pulled
    for piece in range(width // 512):
        lanes = slice(piece * 512, (piece + 1) * 512)
        results = [
            dot_nt(d_heads[i], weights[i, pl.ds(piece * per, per)].reshape(512, cut))
            for i in range(3)
        ]
        own[:, lanes] = (
            results[0][:tokens] + results[1][:tokens] + results[2][:tokens]
        ).astype(jnp.bfloat16)
        for i in range(3):
            gathered[pl.ds(RANK * i, RANK), lanes] -= ADAPTER_SCALE * results[i][tokens:]
    last_copies[0].start()
    mixer_total = jnp.sum(mixer_dots[...], axis=0, keepdims=True)
    joined = jnp.concatenate([mixed[b] for b in range(near)], axis=1)
    low_output = (output_ref[0] * output_ratio[0]).astype(jnp.bfloat16)
    lowered = dot_nt(low_output, d_low[...]).astype(jnp.bfloat16)
    pulled = (output_ref[0] * (output_pull[0] * mixer_total)).astype(jnp.bfloat16)
    mixer_down = ADAPTER_SCALE * (dot_nn(lowered, joined) - dot_nn(pulled, weight_of(3)))
    reduced_mixed = dot_nt(mixer_low, joined).astype(jnp.bfloat16)
    gathered[pl.ds(5 * RANK, RANK)] = ADAPTER_SCALE * (
        dot_nn(reduced_mixed, d_low[...]) * output_ratio[0]
        - mixer_seen * (output_pull[0] * mixer_total)
    )
    for i, value in enumerate((mixer_total, funnel_dots)):
        for r in range(2):
            dots_out[2 * i + r : 2 * i + r + 1] = value[:, r * LANES : (r + 1) * LANES]
    row = 7
    for i in range(2):
        for start in range(0, wide, LANES):
            size = min(LANES, wide - start)
            dots_out[row : row + 1, pl.ds(0, size)] = feed_dots_ref[
                i : i + 1, pl.ds(start, size)
            ]
            if size < LANES:
                dots_out[row : row + 1, pl.ds(size, LANES - size)] = jnp.zeros(
                    (1, LANES - size), jnp.float32
                )
            row += 1
    if row < dots_out.shape[0]:
        dots_out[row:] = jnp.zeros((dots_out.shape[0] - row, LANES), jnp.float32)
    offset = 3 * cut
    scales = dots_out[...] / magnitudes_ref[...]
    for value in (feed_up_ref[0], feed_up_ref[1], mixer_down, funnel_down[...], scales):
        place_in(gathered, half_rows, offset, value)
        offset += value.shape[1]
    rest_columns = half_rows // RANK * width - offset
    place_in(gathered, half_rows, offset, jnp.zeros((RANK, rest_columns), jnp.float32))
    def meanwhile():
        for copy in last_copies[1:] + funneled_copies[1:]:
            copy.start()

    sum_up(
        size, sides, widths, offset - LANES, total, norm_out, gathered, side_box, norm_box,
        meanwhile, *sum_refs,
    )
    tile = kept_rows.shape[1]
    steps = SEQ // tile

    def kept_loads(part, index, slot):
        place = pl.ds(pl.multiple_of(part * SEQ + index * tile, tile), tile)
        return [
            pltpu.make_async_copy(residual_ref.at[place], kept_rows.at[slot], kept_sems.at[0, slot]),
            pltpu.make_async_copy(funneled_out.at[place], other_rows.at[slot], kept_sems.at[1, slot]),
        ]

    gradient_copies = []
    for part in range(count):
        last_copies[part].wait()

        def pull_rows(index, carry, part=part):
            place = pl.ds(pl.multiple_of(part * SEQ + index * small, small), small)
            value = floats[place].astype(jnp.float32)
            weighted = gain_ref[0:1] * (
                own[place].astype(jnp.float32) + last_inbox[place].astype(jnp.float32)
            )
            root = lax.rsqrt(jnp.mean(value * value, axis=1, keepdims=True) + NORM_EPS)
            along = jnp.mean(value * weighted, axis=1, keepdims=True)
            residual[place] += root * weighted - value * (root * root * root * along)
            return carry

        lax.fori_loop(0, SEQ // small, pull_rows, 0)
        gradient_copies.append(
            pltpu.make_async_copy(
                residual.at[rows_of(part)], gradient_out.at[rows_of(part)], out_sems.at[part]
            )
        )
        gradient_copies[-1].start()
    for part in range(count):
        funneled_copies[part].wait()
        for load in kept_loads(part, 0, 0):
            load.start()

        def end_rows(index, carry, part=part):
            slot = lax.rem(index, 2)

            @pl.when(index < steps - 1)
            def _():
                for load in kept_loads(part, index + 1, 1 - slot):
                    load.start()

            for load in kept_loads(part, index, slot):
                load.wait()
            place = pl.ds(pl.multiple_of(part * SEQ + index * tile, tile), tile)
            d_low[place] = (
                kept_rows[slot]
                + (funneled[place].astype(jnp.float32) + other_rows[slot].astype(jnp.float32))
            ).astype(jnp.bfloat16)
            return carry

        lax.fori_loop(0, steps, end_rows, 0)
        gradient_copies.append(
            pltpu.make_async_copy(
                d_low.at[rows_of(part)], block_out.at[rows_of(part)], out_sems.at[count + part]
            )
        )
        gradient_copies[-1].start()
    for copy in gradient_copies:
        copy.wait()


def run_tail(big, small):
    size = lax.axis_size("dp")
    sides = lax.axis_size("tensor")
    full, turned, plain, mixed, residual = big[:5]
    tokens, width = residual.shape
    line, height = full.shape[1], full.shape[4]
    near = mixed.shape[0]
    cut = near * CHUNK
    wide = small[10].shape[1]
    lines = small[8].shape[0]
    count = tokens // SEQ
    anywhere = pl.BlockSpec(memory_space=pl.ANY)
    local = pl.BlockSpec(memory_space=pltpu.VMEM)
    low, full_type = jnp.bfloat16, jnp.float32
    heads = cut // HEAD_DIM
    rows = 7 * RANK
    bits = len(bin(size)) - 3
    widths = [max(width >> (step + 1), 128) for step in range(bits)]
    halvings = sum(1 for step in range(bits) if width >> (step + 1) >= 128)
    boxes = [pltpu.VMEM((2 * rows, w), low) for w in widths]
    copies = bits + halvings + 2 * (sides - 1)
    return pl.pallas_call(
        functools.partial(tail_kernel, size, sides, widths),
        name="tail",
        out_shape=(
            jax.ShapeDtypeStruct((tokens, width), full_type),
            jax.ShapeDtypeStruct((tokens, width), low),
            jax.ShapeDtypeStruct((tokens, width), low),
            jax.ShapeDtypeStruct((2 * rows + RANK, width), low),
            jax.ShapeDtypeStruct((8, 128), full_type),
        ),
        in_specs=[anywhere] * 10 + [local] * 16,
        out_specs=[anywhere] * 3 + [local] * 2,
        scratch_shapes=[
            pltpu.VMEM((4, line, 2, 2, height, cut), low),
            pltpu.VMEM((tokens, width), full_type),
            pltpu.VMEM((tokens, width), low),
            pltpu.VMEM((tokens, width), low),
            pltpu.VMEM((tokens, width), low),
            pltpu.VMEM(turned.shape, low),
            pltpu.VMEM(plain.shape, low),
            pltpu.VMEM(mixed.shape, low),
            pltpu.VMEM((tokens, width), low),
            pltpu.VMEM((tokens, width), low),
            pltpu.VMEM((tokens, width), low),
            pltpu.VMEM((tokens, width), low),
            pltpu.VMEM((count, heads, SEQ, SEQ), full_type),
            pltpu.VMEM((tokens, width), low),
            pltpu.VMEM((3, tokens + RANK, cut), low),
            pltpu.VMEM((2, line, 2, 2, height, CHUNK // 2), low),
            pltpu.VMEM((2, 8, width), full_type),
            pltpu.VMEM((8, width), full_type),
            pltpu.VMEM((3 * RANK, width), low),
            pltpu.VMEM((RANK, wide), full_type),
            pltpu.VMEM((2 * rows, width), full_type),
            pltpu.VMEM((lines, LANES), full_type),
            pltpu.VMEM((sides, rows, widths[-1]), low),
            pltpu.VMEM((sides, 8, 128), full_type),
            pltpu.VMEM((2, 32, width), full_type),
            pltpu.VMEM((2, 32, width), low),
            pltpu.SemaphoreType.DMA((9,)),
            pltpu.SemaphoreType.DMA((4 * near,)),
            pltpu.SemaphoreType.DMA((2,)),
            pltpu.SemaphoreType.DMA((3 * count + 1,)),
            pltpu.SemaphoreType.DMA((3 * count + 1,)),
            pltpu.SemaphoreType.DMA((2 * count,)),
            pltpu.SemaphoreType.DMA((2, 2)),
            *boxes,
            *boxes,
            pltpu.SemaphoreType.DMA((copies,)),
            pltpu.SemaphoreType.DMA((copies,)),
        ],
        compiler_params=pltpu.CompilerParams(
            collective_id=2, has_side_effects=True, vmem_limit_bytes=VMEM
        ),
    )(*big, *small)


def place_in(target, base, offset, value):
    width = target.shape[1]
    start = 0
    while start < value.shape[1]:
        group, lane = divmod(offset + start, width)
        size = min(value.shape[1] - start, width - lane)
        target[pl.ds(base + RANK * group, RANK), pl.ds(lane, size)] = value[
            :, start : start + size
        ].astype(target.dtype)
        start += size


def take_from(source, base, offset, size):
    width = source.shape[1]
    pieces = []
    start = 0
    while start < size:
        group, lane = divmod(offset + start, width)
        count = min(size - start, width - lane)
        pieces.append(
            source[pl.ds(base + RANK * group, RANK), pl.ds(lane, count)].astype(jnp.float32)
        )
        start += count
    return pieces[0] if len(pieces) == 1 else jnp.concatenate(pieces, axis=1)


def sum_up(
    size,
    sides,
    widths,
    scales_offset,
    total,
    norm_out,
    gathered,
    side_box,
    norm_box,
    meanwhile,
    *rest,
):
    bits = len(widths)
    outboxes, inboxes = rest[:bits], rest[bits : 2 * bits]
    sends, receives = rest[2 * bits :]
    half = gathered.shape[0] // 2
    me = lax.axis_index("dp")
    side = lax.axis_index("tensor")
    partners = partners_of(size)

    def remote(source, target, index, where):
        return pltpu.make_async_remote_copy(
            src_ref=source,
            dst_ref=target,
            send_sem=sends.at[index],
            recv_sem=receives.at[index],
            device_id=where,
            device_id_type=MESH,
        )

    start = 0
    width = gathered.shape[1]
    marks = []
    for step in range(bits):
        bit = lax.rem(lax.div(me, 2**step), 2)
        where = {"dp": partners[step]}
        if widths[step] < width:
            width = widths[step]
            marks.append((step, bit, width))
            mine = pl.ds(pl.multiple_of(start + bit * width, 128), width)
            theirs = pl.ds(pl.multiple_of(start + (1 - bit) * width, 128), width)
            outboxes[step][...] = gathered[:, theirs].astype(jnp.bfloat16)
            copy = remote(outboxes[step], inboxes[step], step, where)
            copy.start()
            copy.wait()
            gathered[:, mine] += inboxes[step][...].astype(jnp.float32)
            start = start + bit * width
        else:
            mine = pl.ds(pl.multiple_of(start, 128), width)
            outboxes[step][...] = gathered[:, mine].astype(jnp.bfloat16)
            copy = remote(outboxes[step], inboxes[step], step, where)
            copy.start()
            copy.wait()
            gathered[:, mine] = outboxes[step][...].astype(jnp.float32) + inboxes[step][
                ...
            ].astype(jnp.float32)
    mine = pl.ds(pl.multiple_of(start, 128), width)
    side_box[0] = gathered[pl.ds(0, half), mine].astype(jnp.bfloat16)
    split = gathered[pl.ds(half, half), mine].astype(jnp.bfloat16)
    value = split.astype(jnp.float32)
    group, lane = divmod(scales_offset, gathered.shape[1])
    row = lax.broadcasted_iota(jnp.int32, value.shape, 0) - RANK * group
    column = lax.broadcasted_iota(jnp.int32, value.shape, 1) + start - lane
    both_hold = (row >= 0) & (row < 4) & (column >= 0) & (column < LANES)
    norm_box[0] = jnp.full(
        norm_box.shape[1:],
        jnp.sum(jnp.where(both_hold, value * value / sides, value * value)),
        jnp.float32,
    )
    copies = []
    for step in range(1, sides):
        where = {"tensor": lax.rem(side + step, sides)}
        copies.append(remote(side_box.at[0], side_box.at[step], bits + 2 * step - 2, where))
        copies.append(remote(norm_box.at[0], norm_box.at[step], bits + 2 * step - 1, where))
    for copy in copies:
        copy.start()
    meanwhile()
    for copy in copies:
        copy.wait()
    shared = side_box[0].astype(jnp.float32)
    squares = norm_box[0]
    for step in range(1, sides):
        shared += side_box[step].astype(jnp.float32)
        squares += norm_box[step]
    shared = shared.astype(jnp.bfloat16)
    total[pl.ds(0, half), mine] = shared
    total[pl.ds(half, half), mine] = split
    value = shared.astype(jnp.float32)
    rest_of = jnp.full((1, width), jnp.sum(value * value)) + squares[0:1, 0:1]
    pieces = []
    for _ in range(3):
        pieces.append(rest_of.astype(jnp.bfloat16))
        rest_of = rest_of - pieces[-1].astype(jnp.float32)
    pieces.append(jnp.zeros((RANK - 3, width), jnp.bfloat16))
    total[pl.ds(2 * half, RANK), mine] = jnp.concatenate(pieces, axis=0)
    index = bits + 2 * (sides - 1)
    for step, bit, width in reversed(marks):
        mine = pl.ds(pl.multiple_of(start, 128), width)
        copy = remote(
            total.at[:, mine], total.at[:, mine], index, {"dp": partners[step]}
        )
        copy.start()
        copy.wait()
        index += 1
        start = start - bit * width
    pieces = total[pl.ds(2 * half, RANK)].astype(jnp.float32)
    norm = jnp.sqrt(jnp.sum(pieces) / widths[-1])
    norm_out[...] = jnp.full(norm_out.shape, norm, jnp.float32)


def update_kernel(*refs):
    total, norm_ref = refs[:2]
    values, firsts, seconds = refs[2:11], refs[11:20], refs[20:29]
    fresh, momenta, variances = refs[29:38], refs[38:47], refs[47:56]
    factor = jnp.minimum(1.0, CLIP / (norm_ref[0:1, 0:1] + 1e-06))
    half = total.shape[0] // 2 - RANK // 2
    cut, wide = values[1].shape[2], values[2].shape[2]

    def update(index, rate, piece, gradient):
        value, momentum, variance = decoupled_update(
            values[index][piece], gradient * factor, firsts[index][piece], seconds[index][piece], rate
        )
        fresh[index][piece] = value
        momenta[index][piece] = momentum
        variances[index][piece] = variance

    def shared(group):
        return total[pl.ds(RANK * group, RANK)].astype(jnp.float32)

    for i in range(5):
        update(0, RATE_FACTOR, i, shared(i))
    for i in range(2):
        update(5, RATE_LIFT, i, shared(5 + i))
    offset = 0
    for i in range(3):
        update(1, RATE_LIFT, i, take_from(total, half, offset, cut))
        offset += cut
    for i in range(2):
        update(2, RATE_LIFT, i, take_from(total, half, offset, wide))
        offset += wide
    update(3, RATE_FACTOR, Ellipsis, take_from(total, half, offset, cut))
    offset += cut
    update(4, RATE_FACTOR, Ellipsis, take_from(total, half, offset, wide))
    offset += wide
    dots = take_from(total, half, offset, LANES)

    def long(row, size):
        count = -(-size // LANES)
        return jnp.concatenate([dots[row + r : row + r + 1] for r in range(count)], axis=1)[
            :, :size
        ]

    width = total.shape[1]
    for i in range(2):
        piece = slice(i, i + 1)
        update(8, RATE_LOUD, piece, long(2 * i, width))
    for i in range(3):
        piece = slice(i, i + 1)
        update(6, RATE_SCALE, piece, long(4 + i, cut))
    lines = -(-wide // LANES)
    for i in range(2):
        piece = slice(i, i + 1)
        update(7, RATE_SCALE, piece, long(7 + lines * i, wide))


def update_all(total, norm, params, firsts, seconds):
    shapes = tuple(jax.ShapeDtypeStruct(p.shape, p.dtype) for p in params)
    return pl.pallas_call(
        update_kernel,
        name="update",
        out_shape=shapes * 3,
        in_specs=[pl.BlockSpec(memory_space=pltpu.VMEM)] * 29,
        out_specs=[pl.BlockSpec(memory_space=pltpu.VMEM)] * 27,
        compiler_params=pltpu.CompilerParams(vmem_limit_bytes=VMEM),
    )(total, norm, *params, *firsts, *seconds)


def body(
    activations,
    cotangent,
    padding_mask,
    positions,
    norm_gains,
    base_query,
    base_key,
    base_value,
    base_gate,
    base_widen,
    base_mixer,
    base_funnel,
    entry_value,
    attend_value,
    widen_value,
    mixer_value,
    funnel_value,
    output_value,
    stature_value,
    amplitude_value,
    loudness_value,
    entry_first,
    attend_first,
    widen_first,
    mixer_first,
    funnel_first,
    output_first,
    stature_first,
    amplitude_first,
    loudness_first,
    entry_second,
    attend_second,
    widen_second,
    mixer_second,
    funnel_second,
    output_second,
    stature_second,
    amplitude_second,
    loudness_second,
):
    params = (
        entry_value,
        attend_value,
        widen_value,
        mixer_value,
        funnel_value,
        output_value,
        stature_value,
        amplitude_value,
        loudness_value,
    )
    firsts = (
        entry_first,
        attend_first,
        widen_first,
        mixer_first,
        funnel_first,
        output_first,
        stature_first,
        amplitude_first,
        loudness_first,
    )
    seconds = (
        entry_second,
        attend_second,
        widen_second,
        mixer_second,
        funnel_second,
        output_second,
        stature_second,
        amplitude_second,
        loudness_second,
    )
    rows, cut = base_query.shape
    width = activations.shape[1]
    place = lax.axis_index("dp") * rows
    entry_down = jnp.swapaxes(entry_value, 1, 2)
    shard, squares, magnitudes = merge(
        (base_query, base_key, base_value, base_gate, base_widen, base_mixer, base_funnel),
        lax.dynamic_slice_in_dim(entry_down, place, rows, 2),
        attend_value,
        widen_value,
        mixer_value.T,
        funnel_value.T,
        lax.dynamic_slice_in_dim(output_value, place, rows, 2),
        (stature_value, amplitude_value, loudness_value),
    )
    count = activations.shape[0] // SEQ
    half = HEAD_DIM // 2
    lane = jnp.arange(HEAD_DIM)
    frequency = ROPE_BASE ** (-2.0 * (lane % half).astype(jnp.float32) / HEAD_DIM)
    angles = positions.astype(jnp.float32)[:, None] * frequency[None]
    cosine = jnp.cos(angles)
    sine = jnp.sin(angles) * jnp.where(lane < half, -1.0, 1.0)[None]
    keep = padding_mask.reshape(count, 1, SEQ)
    (
        full,
        normed_one,
        turned,
        plain,
        mixed,
        residual,
        d_normed_two,
        funneled,
        feed_ups,
        feed_downs,
        funnel_down,
        funnel_up,
        funnel_seen,
        feed_dots,
    ) = run_block(
        shard,
        activations,
        cotangent,
        (
            cosine,
            sine,
            keep,
            norm_gains,
            entry_down,
            funnel_value.T,
            widen_value,
            output_value,
            squares,
            magnitudes,
        ),
    )
    input_gradient, block_output, _, total, norm = run_tail(
        (
            full,
            turned,
            plain,
            mixed,
            residual,
            d_normed_two,
            funneled,
            cotangent,
            activations,
            normed_one,
        ),
        (
            cosine,
            sine,
            keep,
            norm_gains,
            entry_down,
            attend_value,
            mixer_value.T,
            output_value,
            squares,
            magnitudes,
            funnel_down,
            funnel_up,
            funnel_seen,
            feed_dots,
            feed_downs,
            feed_ups,
        ),
    )

    def turned_over(items):
        return [
            jnp.swapaxes(item, -1, -2) if i in (0, 3, 4) else item for i, item in enumerate(items)
        ]

    results = update_all(total, norm, turned_over(params), turned_over(firsts), turned_over(seconds))
    updated, momenta, variances = (turned_over(results[i : i + 9]) for i in (0, 9, 18))
    gradient_norm = norm[0, 0]
    return (
        block_output,
        input_gradient,
        gradient_norm,
        updated[0],
        updated[1],
        updated[2],
        updated[3],
        updated[4],
        updated[5],
        updated[6],
        updated[7],
        updated[8],
        momenta[0],
        momenta[1],
        momenta[2],
        momenta[3],
        momenta[4],
        momenta[5],
        momenta[6],
        momenta[7],
        momenta[8],
        variances[0],
        variances[1],
        variances[2],
        variances[3],
        variances[4],
        variances[5],
        variances[6],
        variances[7],
        variances[8],
    )


def solution(mesh):
    return jax.shard_map(
        body,
        mesh=mesh,
        in_specs=(
            P("dp", None),
            P("dp", None),
            P("dp"),
            P("dp"),
            P(),
            P("dp", "tensor"),
            P("dp", "tensor"),
            P("dp", "tensor"),
            P("dp", "tensor"),
            P("dp", "tensor"),
            P("tensor", "dp"),
            P("tensor", "dp"),
            P(),
            P(None, None, "tensor"),
            P(None, None, "tensor"),
            P("tensor", None),
            P("tensor", None),
            P(),
            P(None, "tensor"),
            P(None, "tensor"),
            P(),
            P(),
            P(None, None, "tensor"),
            P(None, None, "tensor"),
            P("tensor", None),
            P("tensor", None),
            P(),
            P(None, "tensor"),
            P(None, "tensor"),
            P(),
            P(),
            P(None, None, "tensor"),
            P(None, None, "tensor"),
            P("tensor", None),
            P("tensor", None),
            P(),
            P(None, "tensor"),
            P(None, "tensor"),
            P(),
        ),
        out_specs=(
            P("dp", None),
            P("dp", None),
            P(),
            P(),
            P(None, None, "tensor"),
            P(None, None, "tensor"),
            P("tensor", None),
            P("tensor", None),
            P(),
            P(None, "tensor"),
            P(None, "tensor"),
            P(),
            P(),
            P(None, None, "tensor"),
            P(None, None, "tensor"),
            P("tensor", None),
            P("tensor", None),
            P(),
            P(None, "tensor"),
            P(None, "tensor"),
            P(),
            P(),
            P(None, None, "tensor"),
            P(None, None, "tensor"),
            P("tensor", None),
            P("tensor", None),
            P(),
            P(None, "tensor"),
            P(None, "tensor"),
            P(),
        ),
        check_vma=False,
    )
```

```python
import functools

import jax
import jax.numpy as jnp
from jax import lax
from jax.experimental import pallas as pl
from jax.experimental.pallas import tpu as pltpu
from jax.sharding import PartitionSpec as P

HEAD_DIM = 128
RANK = 16
SEQ = 256
STEP = 5


HIGH_PRECISION = lax.Precision.HIGHEST
ADAPTER_SCALE = 2.0
NORM_EPS = 1e-05
COLUMN_EPS = 1e-06
BETA_ONE = 0.9
BETA_TWO = 0.999
ADAM_EPS = 1e-08
DECAY = 0.01
CLIP = 1.0
RATE_FACTOR = 0.02
RATE_LIFT = 0.2
RATE_SCALE = 0.5
RATE_LOUD = 2.0
ROPE_BASE = 10000.0
MASKED = -1e30


def decoupled_update(value, gradient, first, second, rate):
    momentum = BETA_ONE * first + (1.0 - BETA_ONE) * gradient
    variance = BETA_TWO * second + (1.0 - BETA_TWO) * gradient * gradient
    corrected = momentum / (1.0 - BETA_ONE**STEP)
    spread = jnp.sqrt(variance / (1.0 - BETA_TWO**STEP))
    return (value - rate * (corrected / (spread + ADAM_EPS) + DECAY * value), momentum, variance)


MESH = pl.DeviceIdType.MESH
LANES = 1024
VMEM = 62 * 1024 * 1024
CHUNK = 256


def staged(kernel, before, inside):
    def run(*refs):
        sources, boxes, sems = refs[before : before + inside], refs[-inside - 1 : -1], refs[-1]
        copies = [
            pltpu.make_async_copy(source, box, sems.at[i])
            for i, (source, box) in enumerate(zip(sources, boxes))
        ]
        kernel(copies, *refs[:before], *boxes, *refs[before + inside : -inside - 1])

    return run


def stage_of(operands):
    boxes = [pltpu.VMEM(operand.shape, operand.dtype) for operand in operands]
    return boxes + [pltpu.SemaphoreType.DMA((len(operands),))]


def partners_of(size):
    me = lax.axis_index("dp")
    found = []
    bit = 1
    while bit < size:
        down = lax.rem(lax.div(me, bit), 2)
        found.append(me + bit - 2 * bit * down)
        bit *= 2
    return found


def double_sum(total, inbox, sends, receives, size, sides, shared_rows):
    targets = [({"dp": p}, total.shape[0]) for p in partners_of(size)]
    side = lax.axis_index("tensor")
    targets += [
        ({"tensor": lax.rem(side + step, sides)}, shared_rows) for step in range(1, sides)
    ]
    for step, (target, count) in enumerate(targets):
        kept = pl.ds(0, count)
        copy = pltpu.make_async_remote_copy(
            src_ref=total,
            dst_ref=inbox.at[step],
            send_sem=sends.at[step],
            recv_sem=receives.at[step],
            device_id=target,
            device_id_type=MESH,
        )
        copy.start()
        copy.wait()
        total[kept] += inbox[step, kept]


def greet_sum(size, sides):
    barrier = pltpu.get_barrier_semaphore()
    side = lax.axis_index("tensor")
    targets = [{"dp": p} for p in partners_of(size)]
    targets += [{"tensor": lax.rem(side + step, sides)} for step in range(1, sides)]
    for target in targets:
        pl.semaphore_signal(barrier, inc=1, device_id=target, device_id_type=MESH)
    pl.semaphore_wait(barrier, len(targets))


def merge_kernel(
    size,
    sides,
    copies,
    query_ref,
    key_ref,
    value_ref,
    gate_ref,
    widen_ref,
    mixer_ref,
    funnel_ref,
    entry_ref,
    attend_ref,
    lift_ref,
    mixer_down_ref,
    funnel_down_ref,
    output_ref,
    stature_ref,
    amplitude_ref,
    loudness_ref,
    shard_out,
    squares_out,
    magnitudes_out,
    total,
    inbox,
    direction_cut,
    direction_wide,
    direction_mixer,
    direction_funnel,
    sends,
    receives,
):
    for copy in copies:
        copy.start()
    greet_sum(size, sides)
    for copy in copies:
        copy.wait()
    rows = query_ref.shape[0]
    wide = gate_ref.shape[1]
    me = lax.axis_index("dp")
    total[...] = jnp.zeros_like(total)

    def direction(base, down, up):
        return base.astype(jnp.float32) + ADAPTER_SCALE * lax.dot_general(
            down,
            up,
            (((0,), (0,)), ((), ())),
            precision=HIGH_PRECISION,
            preferred_element_type=jnp.float32,
        )

    magnitudes_out[...] = jnp.ones_like(magnitudes_out)
    for i in range(2):
        for r in range(2):
            magnitudes_out[2 * i + r : 2 * i + r + 1, :] = loudness_ref[
                i : i + 1, r * LANES : (r + 1) * LANES
            ]
    for i in range(3):
        magnitudes_out[4 + i : 5 + i, :] = stature_ref[i : i + 1, :]
    for i in range(2):
        for start in range(0, wide, CHUNK):
            row = 7 + 3 * i + start // LANES
            magnitudes_out[row : row + 1, pl.ds(start % LANES, CHUNK)] = amplitude_ref[
                i : i + 1, pl.ds(start, CHUNK)
            ]

    group = LANES // rows
    lane_group = lax.broadcasted_iota(jnp.int32, (1, LANES), 1) // rows
    for i, (base, down) in enumerate(
        ((mixer_ref, mixer_down_ref), (funnel_ref, funnel_down_ref))
    ):
        held = (direction_mixer, direction_funnel)[i]
        sums = jnp.zeros((1, rows), jnp.float32)
        for start in range(0, base.shape[0], CHUNK):
            piece = pl.ds(start, CHUNK)
            part = direction(base[piece], down[:, piece], output_ref[i])
            held[piece] = part
            sums += jnp.sum(part * part, axis=0, keepdims=True)
        spread = jnp.concatenate([sums] * group, axis=1)
        for r in range(2):
            here = lane_group == me - r * group
            total[2 * i + r : 2 * i + r + 1, :] = jnp.where(here, spread, 0.0)
    for i, base in enumerate((query_ref, key_ref, value_ref)):
        for start in range(0, LANES, CHUNK):
            piece = pl.ds(start, CHUNK)
            part = direction(base[:, piece], entry_ref[i], attend_ref[i, :, piece])
            direction_cut[i, :, piece] = part
            total[4 + i : 5 + i, piece] = jnp.sum(part * part, axis=0, keepdims=True)
    for i, base in enumerate((gate_ref, widen_ref)):
        for start in range(0, wide, CHUNK):
            piece = pl.ds(start, CHUNK)
            part = direction(base[:, piece], entry_ref[3 + i], lift_ref[i, :, piece])
            direction_wide[i, :, piece] = part
            row = 7 + 3 * i + start // LANES
            total[row : row + 1, pl.ds(start % LANES, CHUNK)] = jnp.sum(
                part * part, axis=0, keepdims=True
            )
    double_sum(total, inbox, sends, receives, size, sides, 4)
    squares_out[...] = total[...]
    ratio = magnitudes_out[...] / jnp.sqrt(total[...] + COLUMN_EPS)
    near = LANES // CHUNK
    for i in range(3):
        for b in range(near):
            lanes = slice(b * CHUNK, (b + 1) * CHUNK)
            shard_out[near * i + b] = (
                direction_cut[i, :, lanes] * ratio[4 + i : 5 + i, lanes]
            ).astype(jnp.bfloat16)
    for i in range(2):
        for start in range(0, wide, CHUNK):
            row = 7 + 3 * i + start // LANES
            shard_out[4 * near + 3 * (start // CHUNK) + i] = (
                direction_wide[i, :, pl.ds(start, CHUNK)]
                * ratio[row : row + 1, start % LANES : start % LANES + CHUNK]
            ).astype(jnp.bfloat16)
    for i, held in enumerate((direction_mixer, direction_funnel)):
        own = jnp.zeros((1, rows), jnp.float32)
        for r in range(2):
            for g in range(group):
                own += jnp.where(
                    me == r * group + g,
                    ratio[2 * i + r : 2 * i + r + 1, g * rows : (g + 1) * rows],
                    0.0,
                )
        for start in range(0, held.shape[0], CHUNK):
            part = (held[pl.ds(start, CHUNK)] * own).T.astype(jnp.bfloat16)
            if i == 0:
                shard_out[3 * near + start // CHUNK] = part
            else:
                shard_out[4 * near + 3 * (start // CHUNK) + 2] = part


def merge(bases, entry_rows, attend, widen, mixer_down, funnel_down, output_columns, scales):
    size = lax.axis_size("dp")
    sides = lax.axis_size("tensor")
    rows, cut = bases[0].shape
    wide = bases[3].shape[1]
    steps = len(bin(size)) - 3 + sides - 1
    lines = 16
    operands = (*bases, entry_rows, attend, widen, mixer_down, funnel_down, output_columns, *scales)
    return pl.pallas_call(
        staged(functools.partial(merge_kernel, size, sides), 0, len(operands)),
        name="merge",
        out_shape=(
            jax.ShapeDtypeStruct(((4 * cut + 3 * wide) // CHUNK, rows, CHUNK), jnp.bfloat16),
            jax.ShapeDtypeStruct((lines, LANES), jnp.float32),
            jax.ShapeDtypeStruct((lines, LANES), jnp.float32),
        ),
        in_specs=[pl.BlockSpec(memory_space=pl.ANY)] * len(operands),
        out_specs=[pl.BlockSpec(memory_space=pltpu.VMEM)] * 3,
        scratch_shapes=[
            pltpu.VMEM((lines, LANES), jnp.float32),
            pltpu.VMEM((steps, lines, LANES), jnp.float32),
            pltpu.VMEM((3, rows, cut), jnp.float32),
            pltpu.VMEM((2, rows, wide), jnp.float32),
            pltpu.VMEM((cut, rows), jnp.float32),
            pltpu.VMEM((wide, rows), jnp.float32),
            pltpu.SemaphoreType.DMA((steps,)),
            pltpu.SemaphoreType.DMA((steps,)),
            *stage_of(operands),
        ],
        compiler_params=pltpu.CompilerParams(
            collective_id=0, has_side_effects=True, vmem_limit_bytes=VMEM
        ),
    )(*operands)


def dot_nn(left, right):
    return jnp.dot(left, right, preferred_element_type=jnp.float32)


def dot_nt(left, right):
    return lax.dot_general(
        left, right, (((1,), (1,)), ((), ())), preferred_element_type=jnp.float32
    )


def long_row(lines, row, size):
    count = -(-size // LANES)
    return jnp.concatenate([lines[row + r : row + r + 1] for r in range(count)], axis=1)[:, :size]


BLOCKS = 3
HEAD_CHUNKS = 5
EXTRA_TICKS = 3


def gather_parts(size, shard, full, sems):
    line = size // 4
    early = 16
    late = shard.shape[1] - early
    me = lax.axis_index("dp")
    core, column, spot = lax.rem(me, 2), lax.rem(lax.div(me, 2), 2), lax.div(me, 4)
    right_sends, left_sends, right_gets, left_gets, pair_sems, core_sems, early_sems = sems

    def device(other_spot, other_column, other_core):
        return {"dp": (other_spot * 2 + other_column) * 2 + other_core}

    right = device(lax.rem(spot + 1, line), column, core)
    left = device(lax.rem(spot + line - 1, line), column, core)
    across = device(spot, 1 - column, core)
    twin = device(spot, column, 1 - core)

    def greet():
        barrier = pltpu.get_barrier_semaphore()
        peers = jnp.int32(3)
        for near, target in ((spot < line - 1, right), (spot > 0, left)):

            @pl.when(near)
            def _(target=target):
                pl.semaphore_signal(barrier, inc=1, device_id=target, device_id_type=MESH)

            peers += near.astype(jnp.int32)
        for target in (across, twin, {"tensor": 1 - lax.axis_index("tensor")}):
            pl.semaphore_signal(barrier, inc=1, device_id=target, device_id_type=MESH)
        pl.semaphore_wait(barrier, peers)

    def remote(source, target, send, get, where):
        return pltpu.make_async_remote_copy(
            src_ref=source,
            dst_ref=target,
            send_sem=send,
            recv_sem=get,
            device_id=where,
            device_id_type=MESH,
        )

    def early_copy(part, owner):
        first = 1 + BLOCKS
        blocks = pl.ds(0, first) if part == 0 else pl.ds(first, shard.shape[0] - first)
        return remote(
            shard.at[blocks, pl.ds(0, early)],
            full.at[blocks, spot, owner, core, pl.ds(0, early)],
            early_sems.at[part, 0],
            early_sems.at[part, 1],
            across,
        )

    def early_start():
        for part in range(2):
            early_copy(part, column).start()

    def early_wait(part):
        early_copy(part, 1 - column).wait_recv()
        early_copy(part, column).wait_send()

    def place_of(part, origin, blocks):
        if part == 0:
            return full.at[blocks, origin, column, core, pl.ds(early, late)]
        return full.at[blocks, origin, :, core, pl.ds(0, early)]

    def move(to_right, part, distance, chunk, start, count):
        sends, gets = (right_sends, right_gets) if to_right else (left_sends, left_gets)
        hop = distance - 1
        blocks = pl.ds(start, count)
        place = place_of(part, spot - hop if to_right else spot + hop, blocks)
        source = shard.at[blocks, pl.ds(early, late)] if hop == 0 and part == 0 else place
        kept = 2 * hop + part
        where = right if to_right else left
        return remote(source, place, sends.at[chunk, kept], gets.at[chunk, kept], where)

    def arrivals(to_right, distance, chunk, start, count):
        gets = right_gets if to_right else left_gets
        for part in range(2):
            origin = spot - distance if to_right else spot + distance
            place = place_of(part, origin, pl.ds(start, count))
            kept = 2 * (distance - 1) + part
            remote(
                place, place, right_sends.at[chunk, kept], gets.at[chunk, kept], right
            ).wait_recv()

    def reaches(to_right, distance):
        if to_right:
            return (spot >= distance - 1) & (spot < line - 1)
        return (spot <= line - distance) & (spot > 0)

    def pair_copy(chunk, start, count, owner):
        place = full.at[pl.ds(start, count), :, owner, core, pl.ds(early, late)]
        return remote(place, place, pair_sems.at[chunk, 0], pair_sems.at[chunk, 1], across)

    def core_copy(chunk, start, count, owner):
        place = full.at[pl.ds(start, count), :, :, owner]
        return remote(place, place, core_sems.at[chunk, 0], core_sems.at[chunk, 1], twin)

    def send(distances, parts, chunk, start, count):
        for to_right in (True, False):
            for distance in distances:

                @pl.when(reaches(to_right, distance))
                def _(to_right=to_right, distance=distance):
                    for part in parts:
                        move(to_right, part, distance, chunk, start, count).start()

    def take_in(distance, chunk, start, count):
        @pl.when(spot >= distance)
        def _():
            arrivals(True, distance, chunk, start, count)

        @pl.when(spot < line - distance)
        def _():
            arrivals(False, distance, chunk, start, count)

    def own(parts, chunk, start, count):
        send((1,), parts, chunk, start, count)

    def turn(distance, chunk, start, count):
        take_in(distance, chunk, start, count)
        if distance < line - 1:
            send((distance + 1,), (0, 1), chunk, start, count)
        else:
            pair_copy(chunk, start, count, column).start()

    def pair_done(chunk, start, count):
        pair_copy(chunk, start, count, 1 - column).wait_recv()
        core_copy(chunk, start, count, core).start()

    def core_done(chunk, start, count):
        core_copy(chunk, start, count, 1 - core).wait_recv()

    def finish(chunk, start, count):
        for to_right in (True, False):
            for distance in range(1, line):

                @pl.when(reaches(to_right, distance))
                def _(to_right=to_right, distance=distance):
                    for part in range(2):
                        move(to_right, part, distance, chunk, start, count).wait_send()

        pair_copy(chunk, start, count, column).wait_send()
        core_copy(chunk, start, count, core).wait_send()

    def stages(pace):
        found = {0: functools.partial(own, (0, 1))}
        for distance in range(1, line):
            found[pace * distance] = functools.partial(turn, distance)
        last = pace * (line - 1)
        found[last + 2] = pair_done
        found[last + 3] = core_done
        found[last + 4] = finish
        return found

    return greet, own, stages, early_start, early_wait, finish


def block_kernel(
    size,
    copies,
    rows_ref,
    back_ref,
    shard,
    cosine_ref,
    sine_ref,
    keep_ref,
    gain_ref,
    entry_ref,
    funnel_ref,
    lift_ref,
    output_ref,
    squares_ref,
    magnitudes_ref,
    full,
    normed_out,
    turned_out,
    plain_out,
    mixed_out,
    residual_out,
    d_normed_out,
    d_normed_other,
    funneled_out,
    up_out,
    down_out,
    funnel_down_out,
    funnel_up_out,
    funnel_seen_out,
    dots_out,
    normed,
    back,
    floats,
    turned,
    plain,
    mixed,
    heads_weight,
    feed_weight,
    residual,
    d_normed,
    funneled,
    outbox,
    inbox,
    lowered,
    reduced,
    funnel_lowered,
    funnel_reduced,
    low_lift_ref,
    pull_lift_ref,
    ratio_ref,
    pull_ref,
    funnel_down_ref,
    right_sends,
    left_sends,
    right_gets,
    left_gets,
    pair_sems,
    core_sems,
    early_sems,
    local_sems,
    weight_sems,
    feed_sems,
    side_sends,
    side_gets,
    out_sems,
):
    line = size // 4
    total_blocks = full.shape[0]
    chunks = total_blocks // BLOCKS
    tokens, width = normed.shape[0] - 2 * RANK, normed.shape[1]
    count = tokens // SEQ
    sides = {"tensor": 1 - lax.axis_index("tensor")}
    sems = (right_sends, left_sends, right_gets, left_gets, pair_sems, core_sems, early_sems)
    greet, send_own, stages, early_start, early_wait, finish = gather_parts(
        size, shard, full, sems
    )
    me = lax.axis_index("dp")
    core, column, spot = lax.rem(me, 2), lax.rem(lax.div(me, 2), 2), lax.div(me, 4)

    slow, fast = stages(1), stages(1)
    lag = (line - 1) + 3

    def tick(now, sends=True):
        for phase, stage in slow.items():
            chunk = now - phase
            if phase == 0 and not sends:
                continue
            start = 1 + BLOCKS * chunk
            if isinstance(now, int):
                if 1 <= chunk < chunks:
                    stage(chunk, start, BLOCKS)
            else:

                @pl.when((chunk >= 1) & (chunk < chunks))
                def _(stage=stage, chunk=chunk, start=start):
                    stage(chunk, start, BLOCKS)

    def first_ticks(now):
        if now in fast:
            fast[now](chunks, 0, 1)
            fast[now](0, 1, BLOCKS)

    for copy in copies:
        copy.start()
    own = pltpu.make_async_copy(shard, full.at[:, spot, column, core], local_sems.at[0])
    loads = [
        pltpu.make_async_copy(rows_ref, floats, local_sems.at[1]),
        pltpu.make_async_copy(back_ref, back, local_sems.at[2]),
    ]
    for load in loads:
        load.start()
    greet()
    copies[0].wait()
    early_start()
    send_own((0,), chunks, 0, 1)
    send_own((0,), 0, 1, BLOCKS)
    own.start()
    own.wait()
    early_wait(0)
    send_own((1,), chunks, 0, 1)
    send_own((1,), 0, 1, BLOCKS)
    early_wait(1)
    for load in loads + copies[1:]:
        load.wait()
    tile = 32

    def norm_rows(index, carry):
        place = pl.ds(pl.multiple_of(index * tile, tile), tile)
        value = floats[place].astype(jnp.float32)
        root = lax.rsqrt(jnp.mean(value * value, axis=1, keepdims=True) + NORM_EPS)
        normed[place] = (value * root * gain_ref[0:1]).astype(jnp.bfloat16)
        return carry

    def prepare():
        lax.fori_loop(0, tokens // tile, norm_rows, 0)
        norms = jnp.sqrt(squares_ref[...] + COLUMN_EPS)
        ratios = magnitudes_ref[...] / norms
        pulls = 1.0 / (norms * magnitudes_ref[...])
        wide = funnel_down_ref.shape[1]
        lines = -(-wide // LANES)
        for i in range(2):
            ratio = long_row(ratios, 7 + lines * i, wide)
            pull = long_row(pulls, 7 + lines * i, wide)
            ratio_ref[i : i + 1] = ratio
            pull_ref[i : i + 1] = pull
            low_lift_ref[i] = (lift_ref[i] * ratio).astype(jnp.bfloat16)
            pull_lift_ref[i] = lift_ref[i] * pull
        funnel_down_ref[...] = funnel_ref[...].astype(jnp.bfloat16)
        low_output = (output_ref[1] * long_row(ratios, 2, width)).astype(jnp.bfloat16)
        funnel_lowered[...] = dot_nt(low_output, back[...]).astype(jnp.bfloat16)
        for i in range(2):
            normed[pl.ds(tokens + RANK * i, RANK)] = entry_ref[3 + i].astype(jnp.bfloat16)

    head_ticks = max(fast) + 1
    for now in range(1, head_ticks):
        first_ticks(now)
        tick(now)
        if now == 1:
            prepare()
    normed_copy = pltpu.make_async_copy(
        normed.at[pl.ds(0, tokens)], normed_out, local_sems.at[3]
    )
    normed_copy.start()
    ready = HEAD_CHUNKS - 2 + lag
    lax.fori_loop(head_ticks, ready + 1, lambda now, carry: (tick(now), carry)[1], 0)

    def head_load(block, slot):
        return pltpu.make_async_copy(
            full.at[block], heads_weight.at[slot], weight_sems.at[slot]
        )

    def head_weight(slot):
        return heads_weight[slot].reshape(width, CHUNK)

    cut_blocks = turned.shape[0] // 3
    head_load(0, 0).start()

    def project(block, carry):
        slot = lax.rem(block, 2)

        @pl.when(block < 3 * cut_blocks - 1)
        def _():
            head_load(block + 1, 1 - slot).start()

        head_load(block, slot).wait()
        for part in range(count):
            place = pl.ds(part * SEQ, SEQ)
            result = dot_nn(normed[place], head_weight(slot))
            plain[block, place] = result.astype(jnp.bfloat16)

            @pl.when(block < 2 * cut_blocks)
            def _(result=result, place=place):
                for half in range(CHUNK // HEAD_DIM):
                    lanes = slice(half * HEAD_DIM, (half + 1) * HEAD_DIM)
                    head = result[:, lanes]
                    turned[block, place, lanes] = (
                        head * cosine_ref[place]
                        + pltpu.roll(head, HEAD_DIM // 2, 1) * sine_ref[place]
                    ).astype(jnp.bfloat16)

            @pl.when(block >= 2 * cut_blocks)
            def _(result=result, place=place):
                turned[block, place] = result.astype(jnp.bfloat16)

        return carry

    lax.fori_loop(0, 3 * cut_blocks, project, 0)
    outs = [
        pltpu.make_async_copy(turned, turned_out, out_sems.at[0]),
        pltpu.make_async_copy(plain.at[pl.ds(0, 2 * cut_blocks)], plain_out, out_sems.at[1]),
    ]
    for out in outs:
        out.start()
    tick(ready + 1)

    mixer_loads = [
        pltpu.make_async_copy(
            full.at[3 * cut_blocks + b],
            feed_weight.at[0, :, :, :, :, pl.ds(b * CHUNK, CHUNK)],
            weight_sems.at[b],
        )
        for b in range(cut_blocks)
    ]
    for load in mixer_loads:
        load.start()
    line_up = lax.broadcasted_iota(jnp.int32, (SEQ, SEQ), 0)
    line_on = lax.broadcasted_iota(jnp.int32, (SEQ, SEQ), 1)

    def attend(block, carry):
        for part in range(count):
            place = pl.ds(part * SEQ, SEQ)
            allowed = ((line_up >= line_on) & (keep_ref[part] > 0)) | (line_up == line_on)
            for half in range(CHUNK // HEAD_DIM):
                lanes = slice(half * HEAD_DIM, (half + 1) * HEAD_DIM)
                scores = dot_nt(
                    turned[block, place, lanes], turned[cut_blocks + block, place, lanes]
                ) * (HEAD_DIM ** (-0.5))
                masked = jnp.where(allowed, scores, MASKED)
                top = jnp.max(masked, axis=1, keepdims=True)
                weight = jnp.exp(masked - top)
                attention = weight / jnp.sum(weight, axis=1, keepdims=True)
                mixed[block, place, lanes] = dot_nn(
                    attention.astype(jnp.bfloat16), turned[2 * cut_blocks + block, place, lanes]
                ).astype(jnp.bfloat16)
        return carry

    lax.fori_loop(0, cut_blocks, attend, 0)
    outs.append(pltpu.make_async_copy(mixed, mixed_out, out_sems.at[2]))
    outs[-1].start()
    tick(ready + 2)

    for load in mixer_loads:
        load.wait()

    def side_copy(part):
        place = pl.ds(part * SEQ, SEQ)
        return pltpu.make_async_remote_copy(
            src_ref=outbox.at[place],
            dst_ref=inbox.at[place],
            send_sem=side_sends.at[part],
            recv_sem=side_gets.at[part],
            device_id=sides,
            device_id_type=MESH,
        )

    for part in range(count):
        place = pl.ds(part * SEQ, SEQ)
        joined = jnp.concatenate([mixed[b, place] for b in range(cut_blocks)], axis=1)
        per = 512 // (4 * feed_weight.shape[4])
        for piece in range(width // 512):
            weight = feed_weight[0, pl.ds(piece * per, per), :, :, :, pl.ds(0, cut_blocks * CHUNK)]
            outbox[place, pl.ds(piece * 512, 512)] = dot_nt(
                joined, weight.reshape(512, cut_blocks * CHUNK)
            ).astype(jnp.bfloat16)
        side_copy(part).start()
    tick(ready + 3)

    normed_copy.wait()
    for part in range(count):
        side_copy(part).wait()

        def add_up(index, carry, part=part):
            place = pl.ds(pl.multiple_of(part * SEQ + index * tile, tile), tile)
            value = floats[place].astype(jnp.float32) + (
                outbox[place].astype(jnp.float32) + inbox[place].astype(jnp.float32)
            )
            residual[place] = value
            root = lax.rsqrt(jnp.mean(value * value, axis=1, keepdims=True) + NORM_EPS)
            normed[place] = (value * root * gain_ref[1:2]).astype(jnp.bfloat16)
            return carry

        lax.fori_loop(0, SEQ // tile, add_up, 0)
        if part == 0:
            tick(ready + 4)
            tick(ready + 5)
    outs.append(pltpu.make_async_copy(residual, residual_out, out_sems.at[3]))
    outs[-1].start()
    reduced[...] = dot_nt(normed[pl.ds(tokens, 2 * RANK)], normed[pl.ds(0, tokens)]).astype(
        jnp.bfloat16
    )
    d_normed[...] = jnp.zeros_like(d_normed)
    funneled[...] = jnp.zeros_like(funneled)
    lowered[...] = jnp.zeros_like(lowered)
    funnel_reduced[...] = jnp.zeros_like(funnel_reduced)

    def feed_load(index, slot, owner):
        return [
            pltpu.make_async_copy(
                full.at[4 * cut_blocks + BLOCKS * index + b, :, :, owner],
                feed_weight.at[slot, :, :, owner, :, pl.ds(b * CHUNK, CHUNK)],
                feed_sems.at[slot, owner, b],
            )
            for b in range(BLOCKS)
        ]

    for load in feed_load(0, 0, core):
        load.start()
    nothing = jnp.zeros((RANK, CHUNK), jnp.bfloat16)
    ahead_copy = pltpu.make_async_remote_copy(
        src_ref=outbox.at[:, pl.ds(0, 512)],
        dst_ref=d_normed_other,
        send_sem=side_sends.at[count],
        recv_sem=side_gets.at[count],
        device_id=sides,
        device_id_type=MESH,
    )

    def feed(index, carry):
        now = index + HEAD_CHUNKS + lag
        first = ready + 6
        for early_step in range(EXTRA_TICKS):

            @pl.when(index == 2 * early_step + 1)
            def _(early_step=early_step):
                tick(first + early_step)

        @pl.when(now >= first + EXTRA_TICKS)
        def _():
            tick(now)

        slot = lax.rem(index, 2)
        for load in feed_load(index, slot, 1 - core):
            load.start()

        @pl.when(index < chunks - HEAD_CHUNKS - 1)
        def _():
            for load in feed_load(index + 1, 1 - slot, core):
                load.start()

        for owner in (core, 1 - core):
            for load in feed_load(index, slot, owner):
                load.wait()
        columns = pl.ds(pl.multiple_of(index * CHUNK, CHUNK), CHUNK)
        weight = feed_weight[slot, :, :, :, :, pl.ds(0, 2 * CHUNK)].reshape(width, 2 * CHUNK)
        both = dot_nn(normed[...], weight)
        gate, lifted = both[:tokens, :CHUNK], both[:tokens, CHUNK:]
        gate_seen = both[tokens : tokens + RANK, :CHUNK]
        lifted_seen = both[tokens + RANK :, CHUNK:]
        funnel = feed_weight[slot, :, :, :, :, pl.ds(2 * CHUNK, CHUNK)].reshape(width, CHUNK)
        d_hidden = dot_nn(back[...], funnel)
        sigmoid = 1.0 / (1.0 + jnp.exp(-gate))
        silu = gate * sigmoid
        hidden = (silu * lifted).astype(jnp.bfloat16)
        d_gate = (d_hidden * lifted * (sigmoid * (1.0 + gate * (1.0 - sigmoid)))).astype(
            jnp.bfloat16
        )
        d_lifted = (d_hidden * silu).astype(jnp.bfloat16)
        gate_dots = jnp.sum(d_gate.astype(jnp.float32) * gate, axis=0, keepdims=True)
        lifted_dots = jnp.sum(d_lifted.astype(jnp.float32) * lifted, axis=0, keepdims=True)
        dots_out[0:1, columns] = gate_dots
        dots_out[1:2, columns] = lifted_dots
        gate_pull = (pull_lift_ref[0, :, columns] * gate_dots).astype(jnp.bfloat16)
        lifted_pull = (pull_lift_ref[1, :, columns] * lifted_dots).astype(jnp.bfloat16)
        up_out[0, :, columns] = ADAPTER_SCALE * (
            dot_nn(reduced[pl.ds(0, RANK)], d_gate) * ratio_ref[0:1, columns]
            - gate_seen * (pull_ref[0:1, columns] * gate_dots)
        )
        up_out[1, :, columns] = ADAPTER_SCALE * (
            dot_nn(reduced[pl.ds(RANK, RANK)], d_lifted) * ratio_ref[1:2, columns]
            - lifted_seen * (pull_ref[1:2, columns] * lifted_dots)
        )
        lowered[pl.ds(0, RANK)] += dot_nt(low_lift_ref[0, :, columns], d_gate)
        lowered[pl.ds(RANK, RANK)] += dot_nt(low_lift_ref[1, :, columns], d_lifted)
        funnel_down_out[:, columns] = ADAPTER_SCALE * dot_nn(funnel_lowered[...], hidden)
        funnel_down = funnel_down_ref[:, columns]
        funnel_reduced[...] += dot_nt(funnel_down, hidden)
        sources = jnp.concatenate([hidden, funnel_down], axis=0)
        gradients = jnp.concatenate(
            [
                jnp.concatenate([d_gate, d_lifted], axis=1),
                jnp.concatenate([gate_pull, nothing], axis=1),
                jnp.concatenate([nothing, lifted_pull], axis=1),
            ],
            axis=0,
        )
        per = 512 // (4 * feed_weight.shape[4])
        for piece in range(width // 512):
            gate_rows = feed_weight[slot, pl.ds(piece * per, per), :, :, :, pl.ds(0, 2 * CHUNK)]
            lanes = pl.ds(piece * 512, 512)
            d_normed[:, lanes] += dot_nt(
                gradients, gate_rows.reshape(512, 2 * CHUNK)
            )
            if piece == 0:

                @pl.when(index == chunks - HEAD_CHUNKS - 1)
                def _():
                    outbox[:, pl.ds(0, 512)] = d_normed[pl.ds(0, tokens), pl.ds(0, 512)].astype(
                        jnp.bfloat16
                    )
                    ahead_copy.start()

        for piece in range(width // 512):
            funnel_rows = feed_weight[
                slot, pl.ds(piece * per, per), :, :, :, pl.ds(2 * CHUNK, CHUNK)
            ]
            lanes = pl.ds(piece * 512, 512)
            funneled[:, lanes] += dot_nt(sources, funnel_rows.reshape(512, CHUNK))
        return carry

    lax.fori_loop(0, chunks - HEAD_CHUNKS, feed, 0)
    late = pl.ds(512, width - 512)
    outbox[:, late] = d_normed[pl.ds(0, tokens), late].astype(jnp.bfloat16)
    outs.append(pltpu.make_async_copy(outbox, d_normed_out, out_sems.at[4]))
    outs[-1].start()
    down_out[...] = ADAPTER_SCALE * (
        dot_nn(lowered[...].astype(jnp.bfloat16), normed[pl.ds(0, tokens)])
        - d_normed[pl.ds(tokens, 2 * RANK)]
    )
    floats[...] = funneled[pl.ds(0, tokens)].astype(jnp.bfloat16)
    outs.append(pltpu.make_async_copy(floats, funneled_out, out_sems.at[5]))
    outs[-1].start()
    funnel_up_out[...] = dot_nn(funnel_reduced[...].astype(jnp.bfloat16), back[...])
    funnel_seen_out[...] = funneled[pl.ds(tokens, RANK)]
    finish(chunks - 1, 1 + BLOCKS * (chunks - 1), BLOCKS)
    for out in outs:
        out.wait()
    ahead_copy.wait()


def run_block(shard, rows, back, small):
    size = lax.axis_size("dp")
    line = size // 4
    tokens, width = rows.shape
    blocks, height, _ = shard.shape
    chunks = blocks // BLOCKS
    cut_blocks = (BLOCKS * HEAD_CHUNKS + 1) // 4
    wide = small[6].shape[2]
    anywhere = pl.BlockSpec(memory_space=pl.ANY)
    local = pl.BlockSpec(memory_space=pltpu.VMEM)
    low = jnp.bfloat16
    full = jnp.float32
    out_shape = (
        jax.ShapeDtypeStruct((blocks, line, 2, 2, height, CHUNK), low),
        jax.ShapeDtypeStruct((tokens, width), low),
        jax.ShapeDtypeStruct((3 * cut_blocks, tokens, CHUNK), low),
        jax.ShapeDtypeStruct((2 * cut_blocks, tokens, CHUNK), low),
        jax.ShapeDtypeStruct((cut_blocks, tokens, CHUNK), low),
        jax.ShapeDtypeStruct((tokens, width), full),
        jax.ShapeDtypeStruct((tokens, width), low),
        jax.ShapeDtypeStruct((tokens, 512), low),
        jax.ShapeDtypeStruct((tokens, width), low),
        jax.ShapeDtypeStruct((2, RANK, wide), full),
        jax.ShapeDtypeStruct((2 * RANK, width), full),
        jax.ShapeDtypeStruct((RANK, wide), full),
        jax.ShapeDtypeStruct((RANK, width), full),
        jax.ShapeDtypeStruct((RANK, width), full),
        jax.ShapeDtypeStruct((2, wide), full),
    )
    scratch = [
        pltpu.VMEM((tokens + 2 * RANK, width), low),
        pltpu.VMEM((tokens, width), low),
        pltpu.VMEM((tokens, width), low),
        pltpu.VMEM((3 * cut_blocks, tokens, CHUNK), low),
        pltpu.VMEM((3 * cut_blocks, tokens, CHUNK), low),
        pltpu.VMEM((cut_blocks, tokens, CHUNK), low),
        pltpu.VMEM((2, line, 2, 2, height, CHUNK), low),
        pltpu.VMEM((2, line, 2, 2, height, 4 * CHUNK), low),
        pltpu.VMEM((tokens, width), full),
        pltpu.VMEM((tokens + 2 * RANK, width), full),
        pltpu.VMEM((tokens + RANK, width), full),
        pltpu.VMEM((tokens, width), low),
        pltpu.VMEM((tokens, width), low),
        pltpu.VMEM((2 * RANK, tokens), full),
        pltpu.VMEM((2 * RANK, tokens), low),
        pltpu.VMEM((RANK, tokens), low),
        pltpu.VMEM((RANK, tokens), full),
        pltpu.VMEM((2, RANK, wide), low),
        pltpu.VMEM((2, RANK, wide), full),
        pltpu.VMEM((2, wide), full),
        pltpu.VMEM((2, wide), full),
        pltpu.VMEM((RANK, wide), low),
        pltpu.SemaphoreType.DMA((chunks + 1, 2 * (line - 1))),
        pltpu.SemaphoreType.DMA((chunks + 1, 2 * (line - 1))),
        pltpu.SemaphoreType.DMA((chunks + 1, 2 * (line - 1))),
        pltpu.SemaphoreType.DMA((chunks + 1, 2 * (line - 1))),
        pltpu.SemaphoreType.DMA((chunks + 1, 2)),
        pltpu.SemaphoreType.DMA((chunks + 1, 2)),
        pltpu.SemaphoreType.DMA((2, 2)),
        pltpu.SemaphoreType.DMA((4,)),
        pltpu.SemaphoreType.DMA((4,)),
        pltpu.SemaphoreType.DMA((2, 2, BLOCKS)),
        pltpu.SemaphoreType.DMA((tokens // SEQ + 1,)),
        pltpu.SemaphoreType.DMA((tokens // SEQ + 1,)),
        pltpu.SemaphoreType.DMA((6,)),
        *stage_of((shard, *small)),
    ]
    return pl.pallas_call(
        staged(functools.partial(block_kernel, size), 2, 1 + len(small)),
        name="block",
        out_shape=out_shape,
        in_specs=[anywhere] * (3 + len(small)),
        out_specs=[anywhere] * 9 + [local] * 6,
        scratch_shapes=scratch,
        compiler_params=pltpu.CompilerParams(
            collective_id=1, has_side_effects=True, vmem_limit_bytes=VMEM
        ),
    )(rows, back, shard, *small)


def tail_kernel(
    size,
    sides,
    widths,
    copies,
    full,
    turned_ref,
    plain_ref,
    mixed_ref,
    residual_ref,
    d_normed_ref,
    d_normed_other,
    funneled_ref,
    back_ref,
    rows_ref,
    normed_ref,
    cosine_ref,
    sine_ref,
    keep_ref,
    gain_ref,
    entry_ref,
    attend_ref,
    mixer_ref,
    output_ref,
    squares_ref,
    magnitudes_ref,
    funnel_down_ref,
    funnel_up_ref,
    funnel_seen_ref,
    feed_dots_ref,
    feed_down_ref,
    feed_up_ref,
    gradient_out,
    block_out,
    funneled_out,
    total,
    norm_out,
    weights,
    residual,
    floats,
    back,
    normed,
    turned,
    plain,
    mixed,
    own,
    inbox,
    last_inbox,
    funneled,
    attention,
    d_low,
    d_heads,
    funnel_weight,
    dots_box,
    mixer_dots,
    entry_down_ref,
    funnel_down,
    gathered,
    dots_out,
    side_box,
    norm_box,
    kept_rows,
    other_rows,
    load_sems,
    weight_sems,
    funnel_sems,
    side_sends,
    side_gets,
    out_sems,
    kept_sems,
    *sum_refs,
):
    tokens, width = back.shape
    count = tokens // SEQ
    cut = d_heads.shape[2]
    near = cut // CHUNK
    wide = funnel_down_ref.shape[1]
    scale = HEAD_DIM ** (-0.5)
    other = {"tensor": lax.rem(lax.axis_index("tensor") + 1, sides)}
    halves = CHUNK // HEAD_DIM
    half_rows = gathered.shape[0] // 2

    loads = [
        pltpu.make_async_copy(source, target, load_sems.at[i])
        for i, (source, target) in enumerate(
            (
                (funneled_ref, funneled),
                (back_ref, back),
                (turned_ref, turned),
                (normed_ref, normed),
                (d_normed_ref, own),
                (residual_ref, residual),
                (rows_ref, floats),
                (mixed_ref, mixed),
                (plain_ref, plain),
                (d_normed_other, inbox.at[:, pl.ds(0, 512)]),
            )
        )
    ]
    weight_loads = [
        pltpu.make_async_copy(
            full.at[near * i + b],
            weights.at[i, :, :, :, :, pl.ds(b * CHUNK, CHUNK)],
            weight_sems.at[near * i + b],
        )
        for i in range(4)
        for b in range(near)
    ]
    for load in loads[:3] + copies:
        load.start()
    greet_sum(size, sides)

    def remote(source, target, index):
        return pltpu.make_async_remote_copy(
            src_ref=source,
            dst_ref=target,
            send_sem=side_sends.at[index],
            recv_sem=side_gets.at[index],
            device_id=other,
            device_id_type=MESH,
        )

    def rows_of(part):
        return pl.ds(part * SEQ, SEQ)

    part_copies = [
        remote(
            d_normed_ref.at[rows_of(part), pl.ds(512, width - 512)],
            inbox.at[rows_of(part), pl.ds(512, width - 512)],
            part,
        )
        for part in range(count)
    ]
    part_copies[0].start()
    for load in loads[3:] + weight_loads:
        load.start()
    dots_copy = remote(dots_box.at[0], dots_box.at[1], count)
    funneled_copies = [
        remote(funneled_ref.at[rows_of(part)], funneled_out.at[rows_of(part)], count + 1 + part)
        for part in range(count)
    ]
    last_copies = [
        remote(own.at[rows_of(part)], last_inbox.at[rows_of(part)], 2 * count + 1 + part)
        for part in range(count)
    ]
    for copy in copies:
        copy.wait()
    norms = jnp.sqrt(squares_ref[...] + COLUMN_EPS)
    ratios = magnitudes_ref[...] / norms
    pulls = 1.0 / (norms * magnitudes_ref[...])
    for i in range(3):
        entry_down_ref[pl.ds(RANK * i, RANK)] = entry_ref[i].astype(jnp.bfloat16)
    mixer_low = mixer_ref[...].astype(jnp.bfloat16)
    output_ratio = [long_row(ratios, 2 * i, width) for i in range(2)]
    output_pull = [long_row(pulls, 2 * i, width) for i in range(2)]

    def weight_of(i):
        return weights[i].reshape(width, cut)

    loads[0].wait()
    loads[1].wait()
    tile = 64

    def count_dots(index, total):
        place = pl.ds(pl.multiple_of(index * tile, tile), tile)
        return total + jnp.sum(
            back[place].astype(jnp.float32) * funneled[place].astype(jnp.float32),
            axis=0,
            keepdims=True,
        )

    funnel_dots = lax.fori_loop(
        0, tokens // tile, count_dots, jnp.zeros((1, width), jnp.float32)
    )
    dots_box[0] = jnp.broadcast_to(funnel_dots, dots_box.shape[1:])
    dots_copy.start()
    loads[2].wait()
    line_up = lax.broadcasted_iota(jnp.int32, (SEQ, SEQ), 0)
    line_on = lax.broadcasted_iota(jnp.int32, (SEQ, SEQ), 1)

    def attend(block, carry):
        for part in range(count):
            place = rows_of(part)
            allowed = ((line_up >= line_on) & (keep_ref[part] > 0)) | (line_up == line_on)
            for half in range(halves):
                lanes = slice(half * HEAD_DIM, (half + 1) * HEAD_DIM)
                scores = dot_nt(
                    turned[block, place, lanes], turned[near + block, place, lanes]
                ) * scale
                masked = jnp.where(allowed, scores, MASKED)
                top = jnp.max(masked, axis=1, keepdims=True)
                weight = jnp.exp(masked - top)
                attention[part, halves * block + half] = weight / jnp.sum(
                    weight, axis=1, keepdims=True
                )
        return carry

    lax.fori_loop(0, near, attend, 0)
    for copy in part_copies[1:]:
        copy.start()

    def funnel_lanes(block):
        half = 0 if isinstance(block, int) else lax.rem(block, 2) * (CHUNK // 2)
        return pl.ds(pl.multiple_of(half, CHUNK // 2), CHUNK // 2)

    def funnel_load(block, slot):
        return pltpu.make_async_copy(
            full.at[4 * near + BLOCKS * lax.div(block, 2) + 2, :, :, :, :, funnel_lanes(block)],
            funnel_weight.at[slot],
            funnel_sems.at[slot],
        )

    funnel_load(0, 0).start()
    for load in loads[3:] + weight_loads:
        load.wait()
    head_seen = [
        dot_nn(entry_down_ref[pl.ds(RANK * i, RANK)], weight_of(i)) for i in range(3)
    ]
    mixer_seen = dot_nt(mixer_low, weight_of(3))
    reduced = dot_nt(entry_down_ref[...], normed[...]).astype(jnp.bfloat16)
    dots_copy.wait()
    funnel_dots = dots_box[0, 0:1] + dots_box[1, 0:1]
    funnel_pull = (output_ref[1] * (output_pull[1] * funnel_dots)).astype(jnp.bfloat16)

    def correct(block, carry):
        slot = lax.rem(block, 2)

        @pl.when(block < 2 * wide // CHUNK - 1)
        def _():
            funnel_load(block + 1, 1 - slot).start()

        funnel_load(block, slot).wait()
        columns = pl.ds(pl.multiple_of(block * (CHUNK // 2), CHUNK // 2), CHUNK // 2)
        funnel_down[:, columns] = funnel_down_ref[:, columns] - ADAPTER_SCALE * dot_nn(
            funnel_pull, funnel_weight[slot].reshape(width, CHUNK // 2)
        )
        return carry

    lax.fori_loop(0, 2 * wide // CHUNK, correct, 0)
    gathered[pl.ds(6 * RANK, RANK)] = ADAPTER_SCALE * (
        funnel_up_ref[...] * output_ratio[1]
        - funnel_seen_ref[...] * (output_pull[1] * funnel_dots)
    )
    gathered[pl.ds(3 * RANK, 2 * RANK)] = feed_down_ref[...]
    mixer_dots[...] = jnp.zeros_like(mixer_dots)
    small = 32
    for part in range(count):
        part_copies[part].wait()
        if part == count - 1:
            funneled_copies[0].start()

        def pull_back(index, carry, part=part):
            place = pl.ds(pl.multiple_of(part * SEQ + index * small, small), small)
            value = residual[place]
            weighted = gain_ref[1:2] * (
                own[place].astype(jnp.float32) + inbox[place].astype(jnp.float32)
            )
            root = lax.rsqrt(jnp.mean(value * value, axis=1, keepdims=True) + NORM_EPS)
            along = jnp.mean(value * weighted, axis=1, keepdims=True)
            gradient = back[place].astype(jnp.float32) + (
                root * weighted - value * (root * root * root * along)
            )
            rounded = gradient.astype(jnp.bfloat16)
            d_low[place] = rounded
            attended = value - floats[place].astype(jnp.float32)
            mixer_dots[...] += jnp.sum(
                (rounded.astype(jnp.float32) * attended).reshape(small // 8, 8, width), axis=0
            )
            residual[place] = gradient
            return carry

        lax.fori_loop(0, SEQ // small, pull_back, 0)
        place = rows_of(part)

        def attend_back(block, carry, part=part, place=place):
            columns = pl.ds(pl.multiple_of(block * CHUNK, CHUNK), CHUNK)
            mixer = weights[3, :, :, :, :, columns].reshape(width, CHUNK)
            d_mixed = dot_nn(d_low[place], mixer).astype(jnp.bfloat16)
            for half in range(halves):
                lanes = slice(half * HEAD_DIM, (half + 1) * HEAD_DIM)
                spot = pl.ds(
                    pl.multiple_of(block * CHUNK + half * HEAD_DIM, HEAD_DIM), HEAD_DIM
                )
                weight = attention[part, halves * block + half]
                d_head = d_mixed[:, lanes]
                d_attention = dot_nt(d_head, turned[2 * near + block, place, lanes])
                d_heads[2, place, spot] = dot_nn(
                    weight.astype(jnp.bfloat16).T, d_head
                ).astype(jnp.bfloat16)
                inner = jnp.sum(weight * d_attention, axis=1, keepdims=True)
                d_scores = (weight * (d_attention - inner)).astype(jnp.bfloat16)
                d_query = dot_nn(d_scores, turned[near + block, place, lanes]) * scale
                d_key = dot_nn(d_scores.T, turned[block, place, lanes]) * scale
                for i, value in ((0, d_query), (1, d_key)):
                    d_heads[i, place, spot] = (
                        value * cosine_ref[place]
                        - pltpu.roll(value, HEAD_DIM // 2, 1) * sine_ref[place]
                    ).astype(jnp.bfloat16)
            return carry

        lax.fori_loop(0, near, attend_back, 0)
    per = 512 // (4 * weights.shape[4])
    for i in range(3):
        dots = []
        for block in range(near):
            lanes = slice(block * CHUNK, (block + 1) * CHUNK)
            source = plain if i < 2 else turned
            dots.append(
                jnp.sum(
                    d_heads[i, :tokens, lanes].astype(jnp.float32)
                    * source[near * i + block].astype(jnp.float32),
                    axis=0,
                    keepdims=True,
                )
            )
        dots = jnp.concatenate(dots, axis=1)
        dots_out[4 + i : 5 + i] = dots
        head_ratio = ratios[4 + i : 5 + i]
        pulled = (attend_ref[i] * (pulls[4 + i : 5 + i] * dots)).astype(jnp.bfloat16)
        place_in(
            gathered,
            half_rows,
            cut * i,
            ADAPTER_SCALE
            * (
                dot_nn(reduced[RANK * i : RANK * (i + 1)], d_heads[i, :tokens]) * head_ratio
                - head_seen[i] * (pulls[4 + i : 5 + i] * dots)
            ),
        )
        low_lift = (attend_ref[i] * head_ratio).astype(jnp.bfloat16)
        lowered = dot_nt(low_lift, d_heads[i, :tokens]).astype(jnp.bfloat16)
        gathered[pl.ds(RANK * i, RANK)] = ADAPTER_SCALE * dot_nn(lowered, normed[...])
        d_heads[i, tokens:] = pulled
    for piece in range(width // 512):
        lanes = slice(piece * 512, (piece + 1) * 512)
        results = [
            dot_nt(d_heads[i], weights[i, pl.ds(piece * per, per)].reshape(512, cut))
            for i in range(3)
        ]
        own[:, lanes] = (
            results[0][:tokens] + results[1][:tokens] + results[2][:tokens]
        ).astype(jnp.bfloat16)
        for i in range(3):
            gathered[pl.ds(RANK * i, RANK), lanes] -= ADAPTER_SCALE * results[i][tokens:]
    last_copies[0].start()
    mixer_total = jnp.sum(mixer_dots[...], axis=0, keepdims=True)
    joined = jnp.concatenate([mixed[b] for b in range(near)], axis=1)
    low_output = (output_ref[0] * output_ratio[0]).astype(jnp.bfloat16)
    lowered = dot_nt(low_output, d_low[...]).astype(jnp.bfloat16)
    pulled = (output_ref[0] * (output_pull[0] * mixer_total)).astype(jnp.bfloat16)
    mixer_down = ADAPTER_SCALE * (dot_nn(lowered, joined) - dot_nn(pulled, weight_of(3)))
    reduced_mixed = dot_nt(mixer_low, joined).astype(jnp.bfloat16)
    gathered[pl.ds(5 * RANK, RANK)] = ADAPTER_SCALE * (
        dot_nn(reduced_mixed, d_low[...]) * output_ratio[0]
        - mixer_seen * (output_pull[0] * mixer_total)
    )
    for i, value in enumerate((mixer_total, funnel_dots)):
        for r in range(2):
            dots_out[2 * i + r : 2 * i + r + 1] = value[:, r * LANES : (r + 1) * LANES]
    row = 7
    for i in range(2):
        for start in range(0, wide, LANES):
            size = min(LANES, wide - start)
            dots_out[row : row + 1, pl.ds(0, size)] = feed_dots_ref[
                i : i + 1, pl.ds(start, size)
            ]
            if size < LANES:
                dots_out[row : row + 1, pl.ds(size, LANES - size)] = jnp.zeros(
                    (1, LANES - size), jnp.float32
                )
            row += 1
    if row < dots_out.shape[0]:
        dots_out[row:] = jnp.zeros((dots_out.shape[0] - row, LANES), jnp.float32)
    offset = 3 * cut
    scales = dots_out[...] / magnitudes_ref[...]
    for value in (feed_up_ref[0], feed_up_ref[1], mixer_down, funnel_down[...], scales):
        place_in(gathered, half_rows, offset, value)
        offset += value.shape[1]
    rest_columns = half_rows // RANK * width - offset
    place_in(gathered, half_rows, offset, jnp.zeros((RANK, rest_columns), jnp.float32))
    def meanwhile():
        for copy in last_copies[1:] + funneled_copies[1:]:
            copy.start()

    sum_up(
        size, sides, widths, offset - LANES, total, norm_out, gathered, side_box, norm_box,
        meanwhile, *sum_refs,
    )
    tile = kept_rows.shape[1]
    steps = SEQ // tile

    def kept_loads(part, index, slot):
        place = pl.ds(pl.multiple_of(part * SEQ + index * tile, tile), tile)
        return [
            pltpu.make_async_copy(residual_ref.at[place], kept_rows.at[slot], kept_sems.at[0, slot]),
            pltpu.make_async_copy(funneled_out.at[place], other_rows.at[slot], kept_sems.at[1, slot]),
        ]

    gradient_copies = []
    for part in range(count):
        last_copies[part].wait()

        def pull_rows(index, carry, part=part):
            place = pl.ds(pl.multiple_of(part * SEQ + index * small, small), small)
            value = floats[place].astype(jnp.float32)
            weighted = gain_ref[0:1] * (
                own[place].astype(jnp.float32) + last_inbox[place].astype(jnp.float32)
            )
            root = lax.rsqrt(jnp.mean(value * value, axis=1, keepdims=True) + NORM_EPS)
            along = jnp.mean(value * weighted, axis=1, keepdims=True)
            residual[place] += root * weighted - value * (root * root * root * along)
            return carry

        lax.fori_loop(0, SEQ // small, pull_rows, 0)
        gradient_copies.append(
            pltpu.make_async_copy(
                residual.at[rows_of(part)], gradient_out.at[rows_of(part)], out_sems.at[part]
            )
        )
        gradient_copies[-1].start()
    for part in range(count):
        funneled_copies[part].wait()
        for load in kept_loads(part, 0, 0):
            load.start()

        def end_rows(index, carry, part=part):
            slot = lax.rem(index, 2)

            @pl.when(index < steps - 1)
            def _():
                for load in kept_loads(part, index + 1, 1 - slot):
                    load.start()

            for load in kept_loads(part, index, slot):
                load.wait()
            place = pl.ds(pl.multiple_of(part * SEQ + index * tile, tile), tile)
            d_low[place] = (
                kept_rows[slot]
                + (funneled[place].astype(jnp.float32) + other_rows[slot].astype(jnp.float32))
            ).astype(jnp.bfloat16)
            return carry

        lax.fori_loop(0, steps, end_rows, 0)
        gradient_copies.append(
            pltpu.make_async_copy(
                d_low.at[rows_of(part)], block_out.at[rows_of(part)], out_sems.at[count + part]
            )
        )
        gradient_copies[-1].start()
    for copy in gradient_copies:
        copy.wait()


def run_tail(big, small):
    size = lax.axis_size("dp")
    sides = lax.axis_size("tensor")
    full, turned, plain, mixed, residual = big[:5]
    tokens, width = residual.shape
    line, height = full.shape[1], full.shape[4]
    near = mixed.shape[0]
    cut = near * CHUNK
    wide = small[10].shape[1]
    lines = small[8].shape[0]
    count = tokens // SEQ
    anywhere = pl.BlockSpec(memory_space=pl.ANY)
    local = pl.BlockSpec(memory_space=pltpu.VMEM)
    low, full_type = jnp.bfloat16, jnp.float32
    heads = cut // HEAD_DIM
    rows = 7 * RANK
    bits = len(bin(size)) - 3
    widths = [max(width >> (step + 1), 128) for step in range(bits)]
    halvings = sum(1 for step in range(bits) if width >> (step + 1) >= 128)
    boxes = [pltpu.VMEM((2 * rows, w), low) for w in widths]
    copies = bits + halvings + 2 * (sides - 1)
    return pl.pallas_call(
        staged(functools.partial(tail_kernel, size, sides, widths), len(big), len(small)),
        name="tail",
        out_shape=(
            jax.ShapeDtypeStruct((tokens, width), full_type),
            jax.ShapeDtypeStruct((tokens, width), low),
            jax.ShapeDtypeStruct((tokens, width), low),
            jax.ShapeDtypeStruct((2 * rows + RANK, width), low),
            jax.ShapeDtypeStruct((8, 128), full_type),
        ),
        in_specs=[anywhere] * (len(big) + len(small)),
        out_specs=[anywhere] * 3 + [local] * 2,
        scratch_shapes=[
            pltpu.VMEM((4, line, 2, 2, height, cut), low),
            pltpu.VMEM((tokens, width), full_type),
            pltpu.VMEM((tokens, width), low),
            pltpu.VMEM((tokens, width), low),
            pltpu.VMEM((tokens, width), low),
            pltpu.VMEM(turned.shape, low),
            pltpu.VMEM(plain.shape, low),
            pltpu.VMEM(mixed.shape, low),
            pltpu.VMEM((tokens, width), low),
            pltpu.VMEM((tokens, width), low),
            pltpu.VMEM((tokens, width), low),
            pltpu.VMEM((tokens, width), low),
            pltpu.VMEM((count, heads, SEQ, SEQ), full_type),
            pltpu.VMEM((tokens, width), low),
            pltpu.VMEM((3, tokens + RANK, cut), low),
            pltpu.VMEM((2, line, 2, 2, height, CHUNK // 2), low),
            pltpu.VMEM((2, 8, width), full_type),
            pltpu.VMEM((8, width), full_type),
            pltpu.VMEM((3 * RANK, width), low),
            pltpu.VMEM((RANK, wide), full_type),
            pltpu.VMEM((2 * rows, width), full_type),
            pltpu.VMEM((lines, LANES), full_type),
            pltpu.VMEM((sides, rows, widths[-1]), low),
            pltpu.VMEM((sides, 8, 128), full_type),
            pltpu.VMEM((2, 32, width), full_type),
            pltpu.VMEM((2, 32, width), low),
            pltpu.SemaphoreType.DMA((10,)),
            pltpu.SemaphoreType.DMA((4 * near,)),
            pltpu.SemaphoreType.DMA((2,)),
            pltpu.SemaphoreType.DMA((3 * count + 1,)),
            pltpu.SemaphoreType.DMA((3 * count + 1,)),
            pltpu.SemaphoreType.DMA((2 * count,)),
            pltpu.SemaphoreType.DMA((2, 2)),
            *boxes,
            *boxes,
            pltpu.SemaphoreType.DMA((copies,)),
            pltpu.SemaphoreType.DMA((copies,)),
            *stage_of(small),
        ],
        compiler_params=pltpu.CompilerParams(
            collective_id=2, has_side_effects=True, vmem_limit_bytes=VMEM
        ),
    )(*big, *small)


def place_in(target, base, offset, value):
    width = target.shape[1]
    start = 0
    while start < value.shape[1]:
        group, lane = divmod(offset + start, width)
        size = min(value.shape[1] - start, width - lane)
        target[pl.ds(base + RANK * group, RANK), pl.ds(lane, size)] = value[
            :, start : start + size
        ].astype(target.dtype)
        start += size


def take_from(source, base, offset, size):
    width = source.shape[1]
    pieces = []
    start = 0
    while start < size:
        group, lane = divmod(offset + start, width)
        count = min(size - start, width - lane)
        pieces.append(
            source[pl.ds(base + RANK * group, RANK), pl.ds(lane, count)].astype(jnp.float32)
        )
        start += count
    return pieces[0] if len(pieces) == 1 else jnp.concatenate(pieces, axis=1)


def sum_up(
    size,
    sides,
    widths,
    scales_offset,
    total,
    norm_out,
    gathered,
    side_box,
    norm_box,
    meanwhile,
    *rest,
):
    bits = len(widths)
    outboxes, inboxes = rest[:bits], rest[bits : 2 * bits]
    sends, receives = rest[2 * bits :]
    half = gathered.shape[0] // 2
    me = lax.axis_index("dp")
    side = lax.axis_index("tensor")
    partners = partners_of(size)

    def remote(source, target, index, where):
        return pltpu.make_async_remote_copy(
            src_ref=source,
            dst_ref=target,
            send_sem=sends.at[index],
            recv_sem=receives.at[index],
            device_id=where,
            device_id_type=MESH,
        )

    start = 0
    width = gathered.shape[1]
    marks = []
    for step in range(bits):
        bit = lax.rem(lax.div(me, 2**step), 2)
        where = {"dp": partners[step]}
        if widths[step] < width:
            width = widths[step]
            marks.append((step, bit, width))
            mine = pl.ds(pl.multiple_of(start + bit * width, 128), width)
            theirs = pl.ds(pl.multiple_of(start + (1 - bit) * width, 128), width)
            outboxes[step][...] = gathered[:, theirs].astype(jnp.bfloat16)
            copy = remote(outboxes[step], inboxes[step], step, where)
            copy.start()
            copy.wait()
            gathered[:, mine] += inboxes[step][...].astype(jnp.float32)
            start = start + bit * width
        else:
            mine = pl.ds(pl.multiple_of(start, 128), width)
            outboxes[step][...] = gathered[:, mine].astype(jnp.bfloat16)
            copy = remote(outboxes[step], inboxes[step], step, where)
            copy.start()
            copy.wait()
            gathered[:, mine] = outboxes[step][...].astype(jnp.float32) + inboxes[step][
                ...
            ].astype(jnp.float32)
    mine = pl.ds(pl.multiple_of(start, 128), width)
    side_box[0] = gathered[pl.ds(0, half), mine].astype(jnp.bfloat16)
    split = gathered[pl.ds(half, half), mine].astype(jnp.bfloat16)
    value = split.astype(jnp.float32)
    group, lane = divmod(scales_offset, gathered.shape[1])
    row = lax.broadcasted_iota(jnp.int32, value.shape, 0) - RANK * group
    column = lax.broadcasted_iota(jnp.int32, value.shape, 1) + start - lane
    both_hold = (row >= 0) & (row < 4) & (column >= 0) & (column < LANES)
    norm_box[0] = jnp.full(
        norm_box.shape[1:],
        jnp.sum(jnp.where(both_hold, value * value / sides, value * value)),
        jnp.float32,
    )
    copies = []
    for step in range(1, sides):
        where = {"tensor": lax.rem(side + step, sides)}
        copies.append(remote(side_box.at[0], side_box.at[step], bits + 2 * step - 2, where))
        copies.append(remote(norm_box.at[0], norm_box.at[step], bits + 2 * step - 1, where))
    for copy in copies:
        copy.start()
    meanwhile()
    for copy in copies:
        copy.wait()
    shared = side_box[0].astype(jnp.float32)
    squares = norm_box[0]
    for step in range(1, sides):
        shared += side_box[step].astype(jnp.float32)
        squares += norm_box[step]
    shared = shared.astype(jnp.bfloat16)
    total[pl.ds(0, half), mine] = shared
    total[pl.ds(half, half), mine] = split
    value = shared.astype(jnp.float32)
    rest_of = jnp.full((1, width), jnp.sum(value * value)) + squares[0:1, 0:1]
    pieces = []
    for _ in range(3):
        pieces.append(rest_of.astype(jnp.bfloat16))
        rest_of = rest_of - pieces[-1].astype(jnp.float32)
    pieces.append(jnp.zeros((RANK - 3, width), jnp.bfloat16))
    total[pl.ds(2 * half, RANK), mine] = jnp.concatenate(pieces, axis=0)
    index = bits + 2 * (sides - 1)
    for step, bit, width in reversed(marks):
        mine = pl.ds(pl.multiple_of(start, 128), width)
        copy = remote(
            total.at[:, mine], total.at[:, mine], index, {"dp": partners[step]}
        )
        copy.start()
        copy.wait()
        index += 1
        start = start - bit * width
    pieces = total[pl.ds(2 * half, RANK)].astype(jnp.float32)
    norm = jnp.sqrt(jnp.sum(pieces) / widths[-1])
    norm_out[...] = jnp.full(norm_out.shape, norm, jnp.float32)


def update_kernel(*refs):
    total, norm_ref = refs[:2]
    values, firsts, seconds = refs[2:11], refs[11:20], refs[20:29]
    fresh, momenta, variances = refs[31:40], refs[40:49], refs[49:58]
    norm_out, boxes, sems = refs[60], refs[61:63], refs[63]
    ins = [pltpu.make_async_copy(refs[29 + i], boxes[i], sems.at[i]) for i in range(2)]
    outs = [pltpu.make_async_copy(boxes[i], refs[58 + i], sems.at[2 + i]) for i in range(2)]
    for copy in ins:
        copy.start()
    norm_out[...] = norm_ref[0:1, 0:1]
    factor = jnp.minimum(1.0, CLIP / (norm_ref[0:1, 0:1] + 1e-06))
    half = total.shape[0] // 2 - RANK // 2
    cut, wide = values[1].shape[2], values[2].shape[2]

    def update(index, rate, piece, gradient):
        value, momentum, variance = decoupled_update(
            values[index][piece], gradient * factor, firsts[index][piece], seconds[index][piece], rate
        )
        fresh[index][piece] = value
        momenta[index][piece] = momentum
        variances[index][piece] = variance

    def shared(group):
        return total[pl.ds(RANK * group, RANK)].astype(jnp.float32)

    for i in range(5):
        update(0, RATE_FACTOR, i, shared(i))
    for i in range(2):
        ins[i].wait()
        outs[i].start()
    for i in range(2):
        update(5, RATE_LIFT, i, shared(5 + i))
    offset = 0
    for i in range(3):
        update(1, RATE_LIFT, i, take_from(total, half, offset, cut))
        offset += cut
    for i in range(2):
        update(2, RATE_LIFT, i, take_from(total, half, offset, wide))
        offset += wide
    update(3, RATE_FACTOR, Ellipsis, take_from(total, half, offset, cut))
    offset += cut
    update(4, RATE_FACTOR, Ellipsis, take_from(total, half, offset, wide))
    offset += wide
    dots = take_from(total, half, offset, LANES)

    def long(row, size):
        count = -(-size // LANES)
        return jnp.concatenate([dots[row + r : row + r + 1] for r in range(count)], axis=1)[
            :, :size
        ]

    width = total.shape[1]
    for i in range(2):
        piece = slice(i, i + 1)
        update(8, RATE_LOUD, piece, long(2 * i, width))
    for i in range(3):
        piece = slice(i, i + 1)
        update(6, RATE_SCALE, piece, long(4 + i, cut))
    lines = -(-wide // LANES)
    for i in range(2):
        piece = slice(i, i + 1)
        update(7, RATE_SCALE, piece, long(7 + lines * i, wide))
    for copy in outs:
        copy.wait()


def update_all(total, norm, params, firsts, seconds, large):
    shapes = tuple(jax.ShapeDtypeStruct(p.shape, p.dtype) for p in params)
    large_shapes = tuple(jax.ShapeDtypeStruct(p.shape, p.dtype) for p in large)
    anywhere = pl.BlockSpec(memory_space=pl.ANY)
    local = pl.BlockSpec(memory_space=pltpu.VMEM)
    return pl.pallas_call(
        update_kernel,
        name="update",
        out_shape=shapes * 3 + large_shapes + (jax.ShapeDtypeStruct((1, 1), jnp.float32),),
        in_specs=[local] * 29 + [anywhere] * 2,
        out_specs=[local] * 27 + [anywhere] * 2 + [local],
        scratch_shapes=[
            *(pltpu.VMEM(p.shape, p.dtype) for p in large),
            pltpu.SemaphoreType.DMA((4,)),
        ],
        compiler_params=pltpu.CompilerParams(vmem_limit_bytes=VMEM),
    )(total, norm, *params, *firsts, *seconds, *large)


def body(
    activations,
    cotangent,
    padding_mask,
    positions,
    norm_gains,
    base_query,
    base_key,
    base_value,
    base_gate,
    base_widen,
    base_mixer,
    base_funnel,
    entry_value,
    attend_value,
    widen_value,
    mixer_value,
    funnel_value,
    output_value,
    stature_value,
    amplitude_value,
    loudness_value,
    entry_first,
    attend_first,
    widen_first,
    mixer_first,
    funnel_first,
    output_first,
    stature_first,
    amplitude_first,
    loudness_first,
    entry_second,
    attend_second,
    widen_second,
    mixer_second,
    funnel_second,
    output_second,
    stature_second,
    amplitude_second,
    loudness_second,
):
    params = (
        entry_value,
        attend_value,
        widen_value,
        mixer_value,
        funnel_value,
        output_value,
        stature_value,
        amplitude_value,
        loudness_value,
    )
    firsts = (
        entry_first,
        attend_first,
        widen_first,
        mixer_first,
        funnel_first,
        output_first,
        stature_first,
        amplitude_first,
        loudness_first,
    )
    seconds = (
        entry_second,
        attend_second,
        widen_second,
        mixer_second,
        funnel_second,
        output_second,
        stature_second,
        amplitude_second,
        loudness_second,
    )
    rows, cut = base_query.shape
    width = activations.shape[1]
    place = lax.axis_index("dp") * rows
    entry_down = jnp.swapaxes(entry_value, 1, 2)
    shard, squares, magnitudes = merge(
        (base_query, base_key, base_value, base_gate, base_widen, base_mixer, base_funnel),
        lax.dynamic_slice_in_dim(entry_down, place, rows, 2),
        attend_value,
        widen_value,
        mixer_value.T,
        funnel_value.T,
        lax.dynamic_slice_in_dim(output_value, place, rows, 2),
        (stature_value, amplitude_value, loudness_value),
    )
    count = activations.shape[0] // SEQ
    half = HEAD_DIM // 2
    lane = jnp.arange(HEAD_DIM)
    frequency = ROPE_BASE ** (-2.0 * (lane % half).astype(jnp.float32) / HEAD_DIM)
    angles = positions.astype(jnp.float32)[:, None] * frequency[None]
    cosine = jnp.cos(angles)
    sine = jnp.sin(angles) * jnp.where(lane < half, -1.0, 1.0)[None]
    keep = padding_mask.reshape(count, 1, SEQ)
    (
        full,
        normed_one,
        turned,
        plain,
        mixed,
        residual,
        d_normed_two,
        d_normed_other,
        funneled,
        feed_ups,
        feed_downs,
        funnel_down,
        funnel_up,
        funnel_seen,
        feed_dots,
    ) = run_block(
        shard,
        activations,
        cotangent,
        (
            cosine,
            sine,
            keep,
            norm_gains,
            entry_down,
            funnel_value.T,
            widen_value,
            output_value,
            squares,
            magnitudes,
        ),
    )
    input_gradient, block_output, _, total, norm = run_tail(
        (
            full,
            turned,
            plain,
            mixed,
            residual,
            d_normed_two,
            d_normed_other,
            funneled,
            cotangent,
            activations,
            normed_one,
        ),
        (
            cosine,
            sine,
            keep,
            norm_gains,
            entry_down,
            attend_value,
            mixer_value.T,
            output_value,
            squares,
            magnitudes,
            funnel_down,
            funnel_up,
            funnel_seen,
            feed_dots,
            feed_downs,
            feed_ups,
        ),
    )

    def turned_over(items):
        return [
            jnp.swapaxes(item, -1, -2) if i in (0, 3, 4) else item for i, item in enumerate(items)
        ]

    results = update_all(
        total,
        norm,
        turned_over(params),
        turned_over(firsts),
        turned_over(seconds),
        (input_gradient, block_output),
    )
    input_gradient, block_output, gradient_norm = results[27:]
    updated, momenta, variances = (turned_over(results[i : i + 9]) for i in (0, 9, 18))
    gradient_norm = gradient_norm.reshape(())
    return (
        block_output,
        input_gradient,
        gradient_norm,
        updated[0],
        updated[1],
        updated[2],
        updated[3],
        updated[4],
        updated[5],
        updated[6],
        updated[7],
        updated[8],
        momenta[0],
        momenta[1],
        momenta[2],
        momenta[3],
        momenta[4],
        momenta[5],
        momenta[6],
        momenta[7],
        momenta[8],
        variances[0],
        variances[1],
        variances[2],
        variances[3],
        variances[4],
        variances[5],
        variances[6],
        variances[7],
        variances[8],
    )


def solution(mesh):
    return jax.shard_map(
        body,
        mesh=mesh,
        in_specs=(
            P("dp", None),
            P("dp", None),
            P("dp"),
            P("dp"),
            P(),
            P("dp", "tensor"),
            P("dp", "tensor"),
            P("dp", "tensor"),
            P("dp", "tensor"),
            P("dp", "tensor"),
            P("tensor", "dp"),
            P("tensor", "dp"),
            P(),
            P(None, None, "tensor"),
            P(None, None, "tensor"),
            P("tensor", None),
            P("tensor", None),
            P(),
            P(None, "tensor"),
            P(None, "tensor"),
            P(),
            P(),
            P(None, None, "tensor"),
            P(None, None, "tensor"),
            P("tensor", None),
            P("tensor", None),
            P(),
            P(None, "tensor"),
            P(None, "tensor"),
            P(),
            P(),
            P(None, None, "tensor"),
            P(None, None, "tensor"),
            P("tensor", None),
            P("tensor", None),
            P(),
            P(None, "tensor"),
            P(None, "tensor"),
            P(),
        ),
        out_specs=(
            P("dp", None),
            P("dp", None),
            P(),
            P(),
            P(None, None, "tensor"),
            P(None, None, "tensor"),
            P("tensor", None),
            P("tensor", None),
            P(),
            P(None, "tensor"),
            P(None, "tensor"),
            P(),
            P(),
            P(None, None, "tensor"),
            P(None, None, "tensor"),
            P("tensor", None),
            P("tensor", None),
            P(),
            P(None, "tensor"),
            P(None, "tensor"),
            P(),
            P(),
            P(None, None, "tensor"),
            P(None, None, "tensor"),
            P("tensor", None),
            P("tensor", None),
            P(),
            P(None, "tensor"),
            P(None, "tensor"),
            P(),
        ),
        check_vma=False,
    )
```

```python
import functools

import jax
import jax.numpy as jnp
from jax import lax
from jax.experimental import pallas as pl
from jax.experimental.pallas import tpu as pltpu
from jax.sharding import PartitionSpec as P

HEAD_DIM = 128
RANK = 16
SEQ = 256
STEP = 5


HIGH_PRECISION = lax.Precision.HIGHEST
ADAPTER_SCALE = 2.0
NORM_EPS = 1e-05
COLUMN_EPS = 1e-06
BETA_ONE = 0.9
BETA_TWO = 0.999
ADAM_EPS = 1e-08
DECAY = 0.01
CLIP = 1.0
RATE_FACTOR = 0.02
RATE_LIFT = 0.2
RATE_SCALE = 0.5
RATE_LOUD = 2.0
ROPE_BASE = 10000.0
MASKED = -1e30


def decoupled_update(value, gradient, first, second, rate):
    momentum = BETA_ONE * first + (1.0 - BETA_ONE) * gradient
    variance = BETA_TWO * second + (1.0 - BETA_TWO) * gradient * gradient
    corrected = momentum / (1.0 - BETA_ONE**STEP)
    spread = jnp.sqrt(variance / (1.0 - BETA_TWO**STEP))
    return (value - rate * (corrected / (spread + ADAM_EPS) + DECAY * value), momentum, variance)


MESH = pl.DeviceIdType.MESH
LANES = 1024
VMEM = 62 * 1024 * 1024
CHUNK = 256


def staged(kernel, before, inside, view=None):
    def run(*refs):
        sources, boxes, sems = refs[before : before + inside], refs[-inside - 1 : -1], refs[-1]
        copies = [
            pltpu.make_async_copy(view(i, source) if view else source, box, sems.at[i])
            for i, (source, box) in enumerate(zip(sources, boxes))
        ]
        kernel(copies, *refs[:before], *boxes, *refs[before + inside : -inside - 1])

    return run


def stage_of(operands, shapes=()):
    shapes = dict(shapes)
    boxes = [
        pltpu.VMEM(shapes.get(i, operand.shape), operand.dtype)
        for i, operand in enumerate(operands)
    ]
    return boxes + [pltpu.SemaphoreType.DMA((len(operands),))]


def partners_of(size):
    me = lax.axis_index("dp")
    found = []
    bit = 1
    while bit < size:
        down = lax.rem(lax.div(me, bit), 2)
        found.append(me + bit - 2 * bit * down)
        bit *= 2
    return found


def double_sum(total, inbox, sends, receives, size, sides, shared_rows):
    targets = [({"dp": p}, total.shape[0]) for p in partners_of(size)]
    side = lax.axis_index("tensor")
    targets += [
        ({"tensor": lax.rem(side + step, sides)}, shared_rows) for step in range(1, sides)
    ]
    for step, (target, count) in enumerate(targets):
        kept = pl.ds(0, count)
        copy = pltpu.make_async_remote_copy(
            src_ref=total,
            dst_ref=inbox.at[step],
            send_sem=sends.at[step],
            recv_sem=receives.at[step],
            device_id=target,
            device_id_type=MESH,
        )
        copy.start()
        copy.wait()
        total[kept] += inbox[step, kept]


def greet_sum(size, sides):
    barrier = pltpu.get_barrier_semaphore()
    side = lax.axis_index("tensor")
    targets = [{"dp": p} for p in partners_of(size)]
    targets += [{"tensor": lax.rem(side + step, sides)} for step in range(1, sides)]
    for target in targets:
        pl.semaphore_signal(barrier, inc=1, device_id=target, device_id_type=MESH)
    pl.semaphore_wait(barrier, len(targets))


def merge_kernel(
    size,
    sides,
    copies,
    query_ref,
    key_ref,
    value_ref,
    gate_ref,
    widen_ref,
    mixer_ref,
    funnel_ref,
    entry_ref,
    attend_ref,
    lift_ref,
    mixer_down_ref,
    funnel_down_ref,
    output_ref,
    stature_ref,
    amplitude_ref,
    loudness_ref,
    shard_out,
    squares_out,
    magnitudes_out,
    total,
    inbox,
    direction_cut,
    direction_wide,
    direction_mixer,
    direction_funnel,
    sends,
    receives,
):
    for copy in copies:
        copy.start()
    greet_sum(size, sides)
    for copy in copies:
        copy.wait()
    rows = query_ref.shape[0]
    wide = gate_ref.shape[1]
    me = lax.axis_index("dp")
    total[...] = jnp.zeros_like(total)

    def direction(base, down, up):
        return base.astype(jnp.float32) + ADAPTER_SCALE * lax.dot_general(
            down,
            up,
            (((0,), (0,)), ((), ())),
            precision=HIGH_PRECISION,
            preferred_element_type=jnp.float32,
        )

    magnitudes_out[...] = jnp.ones_like(magnitudes_out)
    for i in range(2):
        for r in range(2):
            magnitudes_out[2 * i + r : 2 * i + r + 1, :] = loudness_ref[
                i : i + 1, r * LANES : (r + 1) * LANES
            ]
    for i in range(3):
        magnitudes_out[4 + i : 5 + i, :] = stature_ref[i : i + 1, :]
    for i in range(2):
        for start in range(0, wide, CHUNK):
            row = 7 + 3 * i + start // LANES
            magnitudes_out[row : row + 1, pl.ds(start % LANES, CHUNK)] = amplitude_ref[
                i : i + 1, pl.ds(start, CHUNK)
            ]

    group = LANES // rows
    lane_group = lax.broadcasted_iota(jnp.int32, (1, LANES), 1) // rows
    for i, (base, down) in enumerate(
        ((mixer_ref, mixer_down_ref), (funnel_ref, funnel_down_ref))
    ):
        held = (direction_mixer, direction_funnel)[i]
        sums = jnp.zeros((1, rows), jnp.float32)
        for start in range(0, base.shape[0], CHUNK):
            piece = pl.ds(start, CHUNK)
            part = direction(base[piece], down[:, piece], output_ref[i])
            held[piece] = part
            sums += jnp.sum(part * part, axis=0, keepdims=True)
        spread = jnp.concatenate([sums] * group, axis=1)
        for r in range(2):
            here = lane_group == me - r * group
            total[2 * i + r : 2 * i + r + 1, :] = jnp.where(here, spread, 0.0)
    for i, base in enumerate((query_ref, key_ref, value_ref)):
        for start in range(0, LANES, CHUNK):
            piece = pl.ds(start, CHUNK)
            part = direction(base[:, piece], entry_ref[i], attend_ref[i, :, piece])
            direction_cut[i, :, piece] = part
            total[4 + i : 5 + i, piece] = jnp.sum(part * part, axis=0, keepdims=True)
    for i, base in enumerate((gate_ref, widen_ref)):
        for start in range(0, wide, CHUNK):
            piece = pl.ds(start, CHUNK)
            part = direction(base[:, piece], entry_ref[3 + i], lift_ref[i, :, piece])
            direction_wide[i, :, piece] = part
            row = 7 + 3 * i + start // LANES
            total[row : row + 1, pl.ds(start % LANES, CHUNK)] = jnp.sum(
                part * part, axis=0, keepdims=True
            )
    double_sum(total, inbox, sends, receives, size, sides, 4)
    squares_out[...] = total[...]
    ratio = magnitudes_out[...] / jnp.sqrt(total[...] + COLUMN_EPS)
    near = LANES // CHUNK
    for i in range(3):
        for b in range(near):
            lanes = slice(b * CHUNK, (b + 1) * CHUNK)
            shard_out[near * i + b] = (
                direction_cut[i, :, lanes] * ratio[4 + i : 5 + i, lanes]
            ).astype(jnp.bfloat16)
    for i in range(2):
        for start in range(0, wide, CHUNK):
            row = 7 + 3 * i + start // LANES
            shard_out[4 * near + 3 * (start // CHUNK) + i] = (
                direction_wide[i, :, pl.ds(start, CHUNK)]
                * ratio[row : row + 1, start % LANES : start % LANES + CHUNK]
            ).astype(jnp.bfloat16)
    for i, held in enumerate((direction_mixer, direction_funnel)):
        own = jnp.zeros((1, rows), jnp.float32)
        for r in range(2):
            for g in range(group):
                own += jnp.where(
                    me == r * group + g,
                    ratio[2 * i + r : 2 * i + r + 1, g * rows : (g + 1) * rows],
                    0.0,
                )
        for start in range(0, held.shape[0], CHUNK):
            part = (held[pl.ds(start, CHUNK)] * own).T.astype(jnp.bfloat16)
            if i == 0:
                shard_out[3 * near + start // CHUNK] = part
            else:
                shard_out[4 * near + 3 * (start // CHUNK) + 2] = part


def merge(bases, entry, attend, widen, mixer_down, funnel_down, output, scales):
    size = lax.axis_size("dp")
    sides = lax.axis_size("tensor")
    rows, cut = bases[0].shape
    wide = bases[3].shape[1]
    steps = len(bin(size)) - 3 + sides - 1
    lines = 16
    shapes = {7: (*entry.shape[:2], rows), 12: (*output.shape[:2], rows)}
    direct = rows % 128 == 0
    if not direct:
        place = lax.axis_index("dp") * rows
        entry, output = (
            lax.dynamic_slice_in_dim(item, place, rows, 2) for item in (entry, output)
        )
    operands = (*bases, entry, attend, widen, mixer_down, funnel_down, output, *scales)

    def view(index, ref):
        if not direct or index not in shapes:
            return ref
        return ref.at[:, :, pl.ds(pl.multiple_of(lax.axis_index("dp") * rows, 128), rows)]

    return pl.pallas_call(
        staged(functools.partial(merge_kernel, size, sides), 0, len(operands), view),
        name="merge",
        out_shape=(
            jax.ShapeDtypeStruct(((4 * cut + 3 * wide) // CHUNK, rows, CHUNK), jnp.bfloat16),
            jax.ShapeDtypeStruct((lines, LANES), jnp.float32),
            jax.ShapeDtypeStruct((lines, LANES), jnp.float32),
        ),
        in_specs=[pl.BlockSpec(memory_space=pl.ANY)] * len(operands),
        out_specs=[pl.BlockSpec(memory_space=pltpu.VMEM)] * 3,
        scratch_shapes=[
            pltpu.VMEM((lines, LANES), jnp.float32),
            pltpu.VMEM((steps, lines, LANES), jnp.float32),
            pltpu.VMEM((3, rows, cut), jnp.float32),
            pltpu.VMEM((2, rows, wide), jnp.float32),
            pltpu.VMEM((cut, rows), jnp.float32),
            pltpu.VMEM((wide, rows), jnp.float32),
            pltpu.SemaphoreType.DMA((steps,)),
            pltpu.SemaphoreType.DMA((steps,)),
            *stage_of(operands, shapes),
        ],
        compiler_params=pltpu.CompilerParams(
            collective_id=0, has_side_effects=True, vmem_limit_bytes=VMEM
        ),
    )(*operands)


def dot_nn(left, right):
    return jnp.dot(left, right, preferred_element_type=jnp.float32)


def dot_nt(left, right):
    return lax.dot_general(
        left, right, (((1,), (1,)), ((), ())), preferred_element_type=jnp.float32
    )


def long_row(lines, row, size):
    count = -(-size // LANES)
    return jnp.concatenate([lines[row + r : row + r + 1] for r in range(count)], axis=1)[:, :size]


BLOCKS = 3
HEAD_CHUNKS = 5
EXTRA_TICKS = 3


def gather_parts(size, shard, full, sems):
    line = size // 4
    early = 16
    late = shard.shape[1] - early
    me = lax.axis_index("dp")
    core, column, spot = lax.rem(me, 2), lax.rem(lax.div(me, 2), 2), lax.div(me, 4)
    right_sends, left_sends, right_gets, left_gets, pair_sems, core_sems, early_sems = sems

    def device(other_spot, other_column, other_core):
        return {"dp": (other_spot * 2 + other_column) * 2 + other_core}

    right = device(lax.rem(spot + 1, line), column, core)
    left = device(lax.rem(spot + line - 1, line), column, core)
    across = device(spot, 1 - column, core)
    twin = device(spot, column, 1 - core)

    def greet():
        barrier = pltpu.get_barrier_semaphore()
        peers = jnp.int32(3)
        for near, target in ((spot < line - 1, right), (spot > 0, left)):

            @pl.when(near)
            def _(target=target):
                pl.semaphore_signal(barrier, inc=1, device_id=target, device_id_type=MESH)

            peers += near.astype(jnp.int32)
        for target in (across, twin, {"tensor": 1 - lax.axis_index("tensor")}):
            pl.semaphore_signal(barrier, inc=1, device_id=target, device_id_type=MESH)
        pl.semaphore_wait(barrier, peers)

    def remote(source, target, send, get, where):
        return pltpu.make_async_remote_copy(
            src_ref=source,
            dst_ref=target,
            send_sem=send,
            recv_sem=get,
            device_id=where,
            device_id_type=MESH,
        )

    def early_copy(part, owner):
        first = 1 + BLOCKS
        blocks = pl.ds(0, first) if part == 0 else pl.ds(first, shard.shape[0] - first)
        return remote(
            shard.at[blocks, pl.ds(0, early)],
            full.at[blocks, spot, owner, core, pl.ds(0, early)],
            early_sems.at[part, 0],
            early_sems.at[part, 1],
            across,
        )

    def early_start():
        for part in range(2):
            early_copy(part, column).start()

    def early_wait(part):
        early_copy(part, 1 - column).wait_recv()
        early_copy(part, column).wait_send()

    def place_of(part, origin, blocks):
        if part == 0:
            return full.at[blocks, origin, column, core, pl.ds(early, late)]
        return full.at[blocks, origin, :, core, pl.ds(0, early)]

    def move(to_right, part, distance, chunk, start, count):
        sends, gets = (right_sends, right_gets) if to_right else (left_sends, left_gets)
        hop = distance - 1
        blocks = pl.ds(start, count)
        place = place_of(part, spot - hop if to_right else spot + hop, blocks)
        source = shard.at[blocks, pl.ds(early, late)] if hop == 0 and part == 0 else place
        kept = 2 * hop + part
        where = right if to_right else left
        return remote(source, place, sends.at[chunk, kept], gets.at[chunk, kept], where)

    def arrivals(to_right, distance, chunk, start, count):
        gets = right_gets if to_right else left_gets
        for part in range(2):
            origin = spot - distance if to_right else spot + distance
            place = place_of(part, origin, pl.ds(start, count))
            kept = 2 * (distance - 1) + part
            remote(
                place, place, right_sends.at[chunk, kept], gets.at[chunk, kept], right
            ).wait_recv()

    def reaches(to_right, distance):
        if to_right:
            return (spot >= distance - 1) & (spot < line - 1)
        return (spot <= line - distance) & (spot > 0)

    def pair_copy(chunk, start, count, owner):
        place = full.at[pl.ds(start, count), :, owner, core, pl.ds(early, late)]
        return remote(place, place, pair_sems.at[chunk, 0], pair_sems.at[chunk, 1], across)

    def core_copy(chunk, start, count, owner):
        place = full.at[pl.ds(start, count), :, :, owner]
        return remote(place, place, core_sems.at[chunk, 0], core_sems.at[chunk, 1], twin)

    def send(distances, parts, chunk, start, count):
        for to_right in (True, False):
            for distance in distances:

                @pl.when(reaches(to_right, distance))
                def _(to_right=to_right, distance=distance):
                    for part in parts:
                        move(to_right, part, distance, chunk, start, count).start()

    def take_in(distance, chunk, start, count):
        @pl.when(spot >= distance)
        def _():
            arrivals(True, distance, chunk, start, count)

        @pl.when(spot < line - distance)
        def _():
            arrivals(False, distance, chunk, start, count)

    def own(parts, chunk, start, count):
        send((1,), parts, chunk, start, count)

    def turn(distance, chunk, start, count):
        take_in(distance, chunk, start, count)
        if distance < line - 1:
            send((distance + 1,), (0, 1), chunk, start, count)
        else:
            pair_copy(chunk, start, count, column).start()

    def pair_done(chunk, start, count):
        pair_copy(chunk, start, count, 1 - column).wait_recv()
        core_copy(chunk, start, count, core).start()

    def core_done(chunk, start, count):
        core_copy(chunk, start, count, 1 - core).wait_recv()

    def finish(chunk, start, count):
        for to_right in (True, False):
            for distance in range(1, line):

                @pl.when(reaches(to_right, distance))
                def _(to_right=to_right, distance=distance):
                    for part in range(2):
                        move(to_right, part, distance, chunk, start, count).wait_send()

        pair_copy(chunk, start, count, column).wait_send()
        core_copy(chunk, start, count, core).wait_send()

    def stages(pace):
        found = {0: functools.partial(own, (0, 1))}
        for distance in range(1, line):
            found[pace * distance] = functools.partial(turn, distance)
        last = pace * (line - 1)
        found[last + 2] = pair_done
        found[last + 3] = core_done
        found[last + 4] = finish
        return found

    return greet, own, stages, early_start, early_wait, finish


def block_kernel(
    size,
    copies,
    rows_ref,
    back_ref,
    shard,
    positions_ref,
    frequency_ref,
    keep_ref,
    gain_ref,
    entry_ref,
    funnel_ref,
    lift_ref,
    output_ref,
    squares_ref,
    magnitudes_ref,
    full,
    cosine_out,
    sine_out,
    normed_out,
    turned_out,
    plain_out,
    mixed_out,
    residual_out,
    d_normed_out,
    d_normed_other,
    funneled_out,
    up_out,
    down_out,
    funnel_down_out,
    funnel_up_out,
    funnel_seen_out,
    dots_out,
    normed,
    back,
    floats,
    turned,
    plain,
    mixed,
    heads_weight,
    feed_weight,
    residual,
    d_normed,
    funneled,
    outbox,
    inbox,
    lowered,
    reduced,
    funnel_lowered,
    funnel_reduced,
    low_lift_ref,
    pull_lift_ref,
    ratio_ref,
    pull_ref,
    funnel_down_ref,
    cosine_ref,
    sine_ref,
    right_sends,
    left_sends,
    right_gets,
    left_gets,
    pair_sems,
    core_sems,
    early_sems,
    local_sems,
    weight_sems,
    feed_sems,
    side_sends,
    side_gets,
    out_sems,
):
    line = size // 4
    total_blocks = full.shape[0]
    chunks = total_blocks // BLOCKS
    tokens, width = normed.shape[0] - 2 * RANK, normed.shape[1]
    count = tokens // SEQ
    sides = {"tensor": 1 - lax.axis_index("tensor")}
    sems = (right_sends, left_sends, right_gets, left_gets, pair_sems, core_sems, early_sems)
    greet, send_own, stages, early_start, early_wait, finish = gather_parts(
        size, shard, full, sems
    )
    me = lax.axis_index("dp")
    core, column, spot = lax.rem(me, 2), lax.rem(lax.div(me, 2), 2), lax.div(me, 4)

    slow, fast = stages(1), stages(1)
    lag = (line - 1) + 3

    def tick(now, sends=True):
        for phase, stage in slow.items():
            chunk = now - phase
            if phase == 0 and not sends:
                continue
            start = 1 + BLOCKS * chunk
            if isinstance(now, int):
                if 1 <= chunk < chunks:
                    stage(chunk, start, BLOCKS)
            else:

                @pl.when((chunk >= 1) & (chunk < chunks))
                def _(stage=stage, chunk=chunk, start=start):
                    stage(chunk, start, BLOCKS)

    def first_ticks(now):
        if now in fast:
            fast[now](chunks, 0, 1)
            fast[now](0, 1, BLOCKS)

    for copy in copies:
        copy.start()
    own = pltpu.make_async_copy(shard, full.at[:, spot, column, core], local_sems.at[0])
    loads = [
        pltpu.make_async_copy(rows_ref, floats, local_sems.at[1]),
        pltpu.make_async_copy(back_ref, back, local_sems.at[2]),
    ]
    for load in loads:
        load.start()
    greet()
    copies[0].wait()
    early_start()
    send_own((0,), chunks, 0, 1)
    send_own((0,), 0, 1, BLOCKS)
    own.start()
    own.wait()
    early_wait(0)
    send_own((1,), chunks, 0, 1)
    send_own((1,), 0, 1, BLOCKS)
    early_wait(1)
    for load in loads + copies[1:]:
        load.wait()
    tile = 32

    def norm_rows(index, carry):
        place = pl.ds(pl.multiple_of(index * tile, tile), tile)
        value = floats[place].astype(jnp.float32)
        root = lax.rsqrt(jnp.mean(value * value, axis=1, keepdims=True) + NORM_EPS)
        normed[place] = (value * root * gain_ref[0:1]).astype(jnp.bfloat16)
        return carry

    def prepare():
        first_row = lax.broadcasted_iota(jnp.int32, (RANK, tokens), 0) == 0
        places = jnp.where(first_row, positions_ref[...].astype(jnp.float32), 0.0)
        angles = lax.dot_general(
            places,
            jnp.broadcast_to(frequency_ref[...], (RANK, HEAD_DIM)),
            (((0,), (0,)), ((), ())),
            precision=HIGH_PRECISION,
            preferred_element_type=jnp.float32,
        )
        lane = lax.broadcasted_iota(jnp.int32, angles.shape, 1)
        cosine_ref[...] = jnp.cos(angles)
        sine_ref[...] = jnp.where(lane < HEAD_DIM // 2, -1.0, 1.0) * jnp.sin(angles)
        lax.fori_loop(0, tokens // tile, norm_rows, 0)
        norms = jnp.sqrt(squares_ref[...] + COLUMN_EPS)
        ratios = magnitudes_ref[...] / norms
        pulls = 1.0 / (norms * magnitudes_ref[...])
        wide = funnel_down_ref.shape[1]
        lines = -(-wide // LANES)
        for i in range(2):
            ratio = long_row(ratios, 7 + lines * i, wide)
            pull = long_row(pulls, 7 + lines * i, wide)
            ratio_ref[i : i + 1] = ratio
            pull_ref[i : i + 1] = pull
            low_lift_ref[i] = (lift_ref[i] * ratio).astype(jnp.bfloat16)
            pull_lift_ref[i] = lift_ref[i] * pull
        funnel_down_ref[...] = funnel_ref[...].astype(jnp.bfloat16)
        low_output = (output_ref[1] * long_row(ratios, 2, width)).astype(jnp.bfloat16)
        funnel_lowered[...] = dot_nt(low_output, back[...]).astype(jnp.bfloat16)
        for i in range(2):
            normed[pl.ds(tokens + RANK * i, RANK)] = entry_ref[3 + i].astype(jnp.bfloat16)

    head_ticks = max(fast) + 1
    for now in range(1, head_ticks):
        first_ticks(now)
        tick(now)
        if now == 1:
            prepare()
    normed_copy = pltpu.make_async_copy(
        normed.at[pl.ds(0, tokens)], normed_out, local_sems.at[3]
    )
    normed_copy.start()
    ready = HEAD_CHUNKS - 2 + lag
    lax.fori_loop(head_ticks, ready + 1, lambda now, carry: (tick(now), carry)[1], 0)

    def head_load(block, slot):
        return pltpu.make_async_copy(
            full.at[block], heads_weight.at[slot], weight_sems.at[slot]
        )

    def head_weight(slot):
        return heads_weight[slot].reshape(width, CHUNK)

    cut_blocks = turned.shape[0] // 3
    head_load(0, 0).start()

    def project(block, carry):
        slot = lax.rem(block, 2)

        @pl.when(block < 3 * cut_blocks - 1)
        def _():
            head_load(block + 1, 1 - slot).start()

        head_load(block, slot).wait()
        for part in range(count):
            place = pl.ds(part * SEQ, SEQ)
            result = dot_nn(normed[place], head_weight(slot))
            plain[block, place] = result.astype(jnp.bfloat16)

            @pl.when(block < 2 * cut_blocks)
            def _(result=result, place=place):
                for half in range(CHUNK // HEAD_DIM):
                    lanes = slice(half * HEAD_DIM, (half + 1) * HEAD_DIM)
                    head = result[:, lanes]
                    turned[block, place, lanes] = (
                        head * cosine_ref[place]
                        + pltpu.roll(head, HEAD_DIM // 2, 1) * sine_ref[place]
                    ).astype(jnp.bfloat16)

            @pl.when(block >= 2 * cut_blocks)
            def _(result=result, place=place):
                turned[block, place] = result.astype(jnp.bfloat16)

        return carry

    lax.fori_loop(0, 3 * cut_blocks, project, 0)
    outs = [
        pltpu.make_async_copy(cosine_ref, cosine_out, out_sems.at[6]),
        pltpu.make_async_copy(sine_ref, sine_out, out_sems.at[7]),
        pltpu.make_async_copy(turned, turned_out, out_sems.at[0]),
        pltpu.make_async_copy(plain.at[pl.ds(0, 2 * cut_blocks)], plain_out, out_sems.at[1]),
    ]
    for out in outs:
        out.start()
    tick(ready + 1)

    mixer_loads = [
        pltpu.make_async_copy(
            full.at[3 * cut_blocks + b],
            feed_weight.at[0, :, :, :, :, pl.ds(b * CHUNK, CHUNK)],
            weight_sems.at[b],
        )
        for b in range(cut_blocks)
    ]
    for load in mixer_loads:
        load.start()
    line_up = lax.broadcasted_iota(jnp.int32, (SEQ, SEQ), 0)
    line_on = lax.broadcasted_iota(jnp.int32, (SEQ, SEQ), 1)

    def attend(block, carry):
        for part in range(count):
            place = pl.ds(part * SEQ, SEQ)
            allowed = ((line_up >= line_on) & (keep_ref[part] > 0)) | (line_up == line_on)
            for half in range(CHUNK // HEAD_DIM):
                lanes = slice(half * HEAD_DIM, (half + 1) * HEAD_DIM)
                scores = dot_nt(
                    turned[block, place, lanes], turned[cut_blocks + block, place, lanes]
                ) * (HEAD_DIM ** (-0.5))
                masked = jnp.where(allowed, scores, MASKED)
                top = jnp.max(masked, axis=1, keepdims=True)
                weight = jnp.exp(masked - top)
                attention = weight / jnp.sum(weight, axis=1, keepdims=True)
                mixed[block, place, lanes] = dot_nn(
                    attention.astype(jnp.bfloat16), turned[2 * cut_blocks + block, place, lanes]
                ).astype(jnp.bfloat16)
        return carry

    lax.fori_loop(0, cut_blocks, attend, 0)
    outs.append(pltpu.make_async_copy(mixed, mixed_out, out_sems.at[2]))
    outs[-1].start()
    tick(ready + 2)

    for load in mixer_loads:
        load.wait()

    def side_copy(part):
        place = pl.ds(part * SEQ, SEQ)
        return pltpu.make_async_remote_copy(
            src_ref=outbox.at[place],
            dst_ref=inbox.at[place],
            send_sem=side_sends.at[part],
            recv_sem=side_gets.at[part],
            device_id=sides,
            device_id_type=MESH,
        )

    for part in range(count):
        place = pl.ds(part * SEQ, SEQ)
        joined = jnp.concatenate([mixed[b, place] for b in range(cut_blocks)], axis=1)
        per = 512 // (4 * feed_weight.shape[4])
        for piece in range(width // 512):
            weight = feed_weight[0, pl.ds(piece * per, per), :, :, :, pl.ds(0, cut_blocks * CHUNK)]
            outbox[place, pl.ds(piece * 512, 512)] = dot_nt(
                joined, weight.reshape(512, cut_blocks * CHUNK)
            ).astype(jnp.bfloat16)
        side_copy(part).start()
    tick(ready + 3)

    normed_copy.wait()
    for part in range(count):
        side_copy(part).wait()

        def add_up(index, carry, part=part):
            place = pl.ds(pl.multiple_of(part * SEQ + index * tile, tile), tile)
            value = floats[place].astype(jnp.float32) + (
                outbox[place].astype(jnp.float32) + inbox[place].astype(jnp.float32)
            )
            residual[place] = value
            root = lax.rsqrt(jnp.mean(value * value, axis=1, keepdims=True) + NORM_EPS)
            normed[place] = (value * root * gain_ref[1:2]).astype(jnp.bfloat16)
            return carry

        lax.fori_loop(0, SEQ // tile, add_up, 0)
        if part == 0:
            tick(ready + 4)
            tick(ready + 5)
    outs.append(pltpu.make_async_copy(residual, residual_out, out_sems.at[3]))
    outs[-1].start()
    reduced[...] = dot_nt(normed[pl.ds(tokens, 2 * RANK)], normed[pl.ds(0, tokens)]).astype(
        jnp.bfloat16
    )
    d_normed[...] = jnp.zeros_like(d_normed)
    funneled[...] = jnp.zeros_like(funneled)
    lowered[...] = jnp.zeros_like(lowered)
    funnel_reduced[...] = jnp.zeros_like(funnel_reduced)

    def feed_load(index, slot, owner):
        return [
            pltpu.make_async_copy(
                full.at[4 * cut_blocks + BLOCKS * index + b, :, :, owner],
                feed_weight.at[slot, :, :, owner, :, pl.ds(b * CHUNK, CHUNK)],
                feed_sems.at[slot, owner, b],
            )
            for b in range(BLOCKS)
        ]

    for load in feed_load(0, 0, core):
        load.start()
    nothing = jnp.zeros((RANK, CHUNK), jnp.bfloat16)
    ahead_copy = pltpu.make_async_remote_copy(
        src_ref=outbox.at[:, pl.ds(0, 512)],
        dst_ref=d_normed_other,
        send_sem=side_sends.at[count],
        recv_sem=side_gets.at[count],
        device_id=sides,
        device_id_type=MESH,
    )

    def feed(index, carry):
        now = index + HEAD_CHUNKS + lag
        first = ready + 6
        for early_step in range(EXTRA_TICKS):

            @pl.when(index == 2 * early_step + 1)
            def _(early_step=early_step):
                tick(first + early_step)

        @pl.when(now >= first + EXTRA_TICKS)
        def _():
            tick(now)

        slot = lax.rem(index, 2)
        for load in feed_load(index, slot, 1 - core):
            load.start()

        @pl.when(index < chunks - HEAD_CHUNKS - 1)
        def _():
            for load in feed_load(index + 1, 1 - slot, core):
                load.start()

        for owner in (core, 1 - core):
            for load in feed_load(index, slot, owner):
                load.wait()
        columns = pl.ds(pl.multiple_of(index * CHUNK, CHUNK), CHUNK)
        weight = feed_weight[slot, :, :, :, :, pl.ds(0, 2 * CHUNK)].reshape(width, 2 * CHUNK)
        both = dot_nn(normed[...], weight)
        gate, lifted = both[:tokens, :CHUNK], both[:tokens, CHUNK:]
        gate_seen = both[tokens : tokens + RANK, :CHUNK]
        lifted_seen = both[tokens + RANK :, CHUNK:]
        funnel = feed_weight[slot, :, :, :, :, pl.ds(2 * CHUNK, CHUNK)].reshape(width, CHUNK)
        d_hidden = dot_nn(back[...], funnel)
        sigmoid = 1.0 / (1.0 + jnp.exp(-gate))
        silu = gate * sigmoid
        hidden = (silu * lifted).astype(jnp.bfloat16)
        d_gate = (d_hidden * lifted * (sigmoid * (1.0 + gate * (1.0 - sigmoid)))).astype(
            jnp.bfloat16
        )
        d_lifted = (d_hidden * silu).astype(jnp.bfloat16)
        gate_dots = jnp.sum(d_gate.astype(jnp.float32) * gate, axis=0, keepdims=True)
        lifted_dots = jnp.sum(d_lifted.astype(jnp.float32) * lifted, axis=0, keepdims=True)
        dots_out[0:1, columns] = gate_dots
        dots_out[1:2, columns] = lifted_dots
        gate_pull = (pull_lift_ref[0, :, columns] * gate_dots).astype(jnp.bfloat16)
        lifted_pull = (pull_lift_ref[1, :, columns] * lifted_dots).astype(jnp.bfloat16)
        up_out[0, :, columns] = ADAPTER_SCALE * (
            dot_nn(reduced[pl.ds(0, RANK)], d_gate) * ratio_ref[0:1, columns]
            - gate_seen * (pull_ref[0:1, columns] * gate_dots)
        )
        up_out[1, :, columns] = ADAPTER_SCALE * (
            dot_nn(reduced[pl.ds(RANK, RANK)], d_lifted) * ratio_ref[1:2, columns]
            - lifted_seen * (pull_ref[1:2, columns] * lifted_dots)
        )
        lowered[pl.ds(0, RANK)] += dot_nt(low_lift_ref[0, :, columns], d_gate)
        lowered[pl.ds(RANK, RANK)] += dot_nt(low_lift_ref[1, :, columns], d_lifted)
        funnel_down_out[:, columns] = ADAPTER_SCALE * dot_nn(funnel_lowered[...], hidden)
        funnel_down = funnel_down_ref[:, columns]
        funnel_reduced[...] += dot_nt(funnel_down, hidden)
        sources = jnp.concatenate([hidden, funnel_down], axis=0)
        gradients = jnp.concatenate(
            [
                jnp.concatenate([d_gate, d_lifted], axis=1),
                jnp.concatenate([gate_pull, nothing], axis=1),
                jnp.concatenate([nothing, lifted_pull], axis=1),
            ],
            axis=0,
        )
        per = 512 // (4 * feed_weight.shape[4])
        for piece in range(width // 512):
            gate_rows = feed_weight[slot, pl.ds(piece * per, per), :, :, :, pl.ds(0, 2 * CHUNK)]
            lanes = pl.ds(piece * 512, 512)
            d_normed[:, lanes] += dot_nt(
                gradients, gate_rows.reshape(512, 2 * CHUNK)
            )
            if piece == 0:

                @pl.when(index == chunks - HEAD_CHUNKS - 1)
                def _():
                    outbox[:, pl.ds(0, 512)] = d_normed[pl.ds(0, tokens), pl.ds(0, 512)].astype(
                        jnp.bfloat16
                    )
                    ahead_copy.start()

        for piece in range(width // 512):
            funnel_rows = feed_weight[
                slot, pl.ds(piece * per, per), :, :, :, pl.ds(2 * CHUNK, CHUNK)
            ]
            lanes = pl.ds(piece * 512, 512)
            funneled[:, lanes] += dot_nt(sources, funnel_rows.reshape(512, CHUNK))
        return carry

    lax.fori_loop(0, chunks - HEAD_CHUNKS, feed, 0)
    late = pl.ds(512, width - 512)
    outbox[:, late] = d_normed[pl.ds(0, tokens), late].astype(jnp.bfloat16)
    outs.append(pltpu.make_async_copy(outbox, d_normed_out, out_sems.at[4]))
    outs[-1].start()
    down_out[...] = ADAPTER_SCALE * (
        dot_nn(lowered[...].astype(jnp.bfloat16), normed[pl.ds(0, tokens)])
        - d_normed[pl.ds(tokens, 2 * RANK)]
    )
    floats[...] = funneled[pl.ds(0, tokens)].astype(jnp.bfloat16)
    outs.append(pltpu.make_async_copy(floats, funneled_out, out_sems.at[5]))
    outs[-1].start()
    funnel_up_out[...] = dot_nn(funnel_reduced[...].astype(jnp.bfloat16), back[...])
    funnel_seen_out[...] = funneled[pl.ds(tokens, RANK)]
    finish(chunks - 1, 1 + BLOCKS * (chunks - 1), BLOCKS)
    for out in outs:
        out.wait()
    ahead_copy.wait()


def run_block(shard, rows, back, small):
    size = lax.axis_size("dp")
    line = size // 4
    tokens, width = rows.shape
    blocks, height, _ = shard.shape
    chunks = blocks // BLOCKS
    cut_blocks = (BLOCKS * HEAD_CHUNKS + 1) // 4
    wide = small[6].shape[2]
    anywhere = pl.BlockSpec(memory_space=pl.ANY)
    local = pl.BlockSpec(memory_space=pltpu.VMEM)
    low = jnp.bfloat16
    full = jnp.float32
    out_shape = (
        jax.ShapeDtypeStruct((blocks, line, 2, 2, height, CHUNK), low),
        jax.ShapeDtypeStruct((tokens, HEAD_DIM), full),
        jax.ShapeDtypeStruct((tokens, HEAD_DIM), full),
        jax.ShapeDtypeStruct((tokens, width), low),
        jax.ShapeDtypeStruct((3 * cut_blocks, tokens, CHUNK), low),
        jax.ShapeDtypeStruct((2 * cut_blocks, tokens, CHUNK), low),
        jax.ShapeDtypeStruct((cut_blocks, tokens, CHUNK), low),
        jax.ShapeDtypeStruct((tokens, width), full),
        jax.ShapeDtypeStruct((tokens, width), low),
        jax.ShapeDtypeStruct((tokens, 512), low),
        jax.ShapeDtypeStruct((tokens, width), low),
        jax.ShapeDtypeStruct((2, RANK, wide), full),
        jax.ShapeDtypeStruct((2 * RANK, width), full),
        jax.ShapeDtypeStruct((RANK, wide), full),
        jax.ShapeDtypeStruct((RANK, width), full),
        jax.ShapeDtypeStruct((RANK, width), full),
        jax.ShapeDtypeStruct((2, wide), full),
    )
    scratch = [
        pltpu.VMEM((tokens + 2 * RANK, width), low),
        pltpu.VMEM((tokens, width), low),
        pltpu.VMEM((tokens, width), low),
        pltpu.VMEM((3 * cut_blocks, tokens, CHUNK), low),
        pltpu.VMEM((3 * cut_blocks, tokens, CHUNK), low),
        pltpu.VMEM((cut_blocks, tokens, CHUNK), low),
        pltpu.VMEM((2, line, 2, 2, height, CHUNK), low),
        pltpu.VMEM((2, line, 2, 2, height, 4 * CHUNK), low),
        pltpu.VMEM((tokens, width), full),
        pltpu.VMEM((tokens + 2 * RANK, width), full),
        pltpu.VMEM((tokens + RANK, width), full),
        pltpu.VMEM((tokens, width), low),
        pltpu.VMEM((tokens, width), low),
        pltpu.VMEM((2 * RANK, tokens), full),
        pltpu.VMEM((2 * RANK, tokens), low),
        pltpu.VMEM((RANK, tokens), low),
        pltpu.VMEM((RANK, tokens), full),
        pltpu.VMEM((2, RANK, wide), low),
        pltpu.VMEM((2, RANK, wide), full),
        pltpu.VMEM((2, wide), full),
        pltpu.VMEM((2, wide), full),
        pltpu.VMEM((RANK, wide), low),
        pltpu.VMEM((tokens, HEAD_DIM), full),
        pltpu.VMEM((tokens, HEAD_DIM), full),
        pltpu.SemaphoreType.DMA((chunks + 1, 2 * (line - 1))),
        pltpu.SemaphoreType.DMA((chunks + 1, 2 * (line - 1))),
        pltpu.SemaphoreType.DMA((chunks + 1, 2 * (line - 1))),
        pltpu.SemaphoreType.DMA((chunks + 1, 2 * (line - 1))),
        pltpu.SemaphoreType.DMA((chunks + 1, 2)),
        pltpu.SemaphoreType.DMA((chunks + 1, 2)),
        pltpu.SemaphoreType.DMA((2, 2)),
        pltpu.SemaphoreType.DMA((4,)),
        pltpu.SemaphoreType.DMA((4,)),
        pltpu.SemaphoreType.DMA((2, 2, BLOCKS)),
        pltpu.SemaphoreType.DMA((tokens // SEQ + 1,)),
        pltpu.SemaphoreType.DMA((tokens // SEQ + 1,)),
        pltpu.SemaphoreType.DMA((8,)),
        *stage_of((shard, *small)),
    ]
    return pl.pallas_call(
        staged(functools.partial(block_kernel, size), 2, 1 + len(small)),
        name="block",
        out_shape=out_shape,
        in_specs=[anywhere] * (3 + len(small)),
        out_specs=[anywhere] * 11 + [local] * 6,
        scratch_shapes=scratch,
        compiler_params=pltpu.CompilerParams(
            collective_id=1, has_side_effects=True, vmem_limit_bytes=VMEM
        ),
    )(rows, back, shard, *small)


def tail_kernel(
    size,
    sides,
    widths,
    copies,
    full,
    turned_ref,
    plain_ref,
    mixed_ref,
    residual_ref,
    d_normed_ref,
    d_normed_other,
    funneled_ref,
    back_ref,
    rows_ref,
    normed_ref,
    cosine_ref,
    sine_ref,
    keep_ref,
    gain_ref,
    entry_ref,
    attend_ref,
    mixer_ref,
    output_ref,
    squares_ref,
    magnitudes_ref,
    funnel_down_ref,
    funnel_up_ref,
    funnel_seen_ref,
    feed_dots_ref,
    feed_down_ref,
    feed_up_ref,
    gradient_out,
    block_out,
    funneled_out,
    total,
    norm_out,
    weights,
    residual,
    floats,
    back,
    normed,
    turned,
    plain,
    mixed,
    own,
    inbox,
    last_inbox,
    funneled,
    attention,
    d_low,
    d_heads,
    funnel_weight,
    dots_box,
    mixer_dots,
    entry_down_ref,
    funnel_down,
    gathered,
    dots_out,
    side_box,
    norm_box,
    kept_rows,
    other_rows,
    load_sems,
    weight_sems,
    funnel_sems,
    side_sends,
    side_gets,
    out_sems,
    kept_sems,
    *sum_refs,
):
    tokens, width = back.shape
    count = tokens // SEQ
    cut = d_heads.shape[2]
    near = cut // CHUNK
    wide = funnel_down_ref.shape[1]
    scale = HEAD_DIM ** (-0.5)
    other = {"tensor": lax.rem(lax.axis_index("tensor") + 1, sides)}
    halves = CHUNK // HEAD_DIM
    half_rows = gathered.shape[0] // 2

    loads = [
        pltpu.make_async_copy(source, target, load_sems.at[i])
        for i, (source, target) in enumerate(
            (
                (funneled_ref, funneled),
                (back_ref, back),
                (turned_ref, turned),
                (normed_ref, normed),
                (d_normed_ref, own),
                (residual_ref, residual),
                (rows_ref, floats),
                (mixed_ref, mixed),
                (plain_ref, plain),
                (d_normed_other, inbox.at[:, pl.ds(0, 512)]),
            )
        )
    ]
    weight_loads = [
        pltpu.make_async_copy(
            full.at[near * i + b],
            weights.at[i, :, :, :, :, pl.ds(b * CHUNK, CHUNK)],
            weight_sems.at[near * i + b],
        )
        for i in range(4)
        for b in range(near)
    ]
    for load in loads[:3] + copies:
        load.start()
    greet_sum(size, sides)

    def remote(source, target, index):
        return pltpu.make_async_remote_copy(
            src_ref=source,
            dst_ref=target,
            send_sem=side_sends.at[index],
            recv_sem=side_gets.at[index],
            device_id=other,
            device_id_type=MESH,
        )

    def rows_of(part):
        return pl.ds(part * SEQ, SEQ)

    part_copies = [
        remote(
            d_normed_ref.at[rows_of(part), pl.ds(512, width - 512)],
            inbox.at[rows_of(part), pl.ds(512, width - 512)],
            part,
        )
        for part in range(count)
    ]
    part_copies[0].start()
    for load in loads[3:] + weight_loads:
        load.start()
    dots_copy = remote(dots_box.at[0], dots_box.at[1], count)
    funneled_copies = [
        remote(funneled_ref.at[rows], funneled_out.at[rows], count + 1 + piece)
        for piece in range(2 * count)
        for rows in (pl.ds(piece * (SEQ // 2), SEQ // 2),)
    ]
    last_copies = [
        remote(own.at[rows_of(part)], last_inbox.at[rows_of(part)], 3 * count + 1 + part)
        for part in range(count)
    ]
    for copy in copies:
        copy.wait()
    norms = jnp.sqrt(squares_ref[...] + COLUMN_EPS)
    ratios = magnitudes_ref[...] / norms
    pulls = 1.0 / (norms * magnitudes_ref[...])
    for i in range(3):
        entry_down_ref[pl.ds(RANK * i, RANK)] = entry_ref[i].astype(jnp.bfloat16)
    mixer_low = mixer_ref[...].astype(jnp.bfloat16)
    output_ratio = [long_row(ratios, 2 * i, width) for i in range(2)]
    output_pull = [long_row(pulls, 2 * i, width) for i in range(2)]

    def weight_of(i):
        return weights[i].reshape(width, cut)

    loads[0].wait()
    loads[1].wait()
    tile = 64

    def count_dots(index, total):
        place = pl.ds(pl.multiple_of(index * tile, tile), tile)
        return total + jnp.sum(
            back[place].astype(jnp.float32) * funneled[place].astype(jnp.float32),
            axis=0,
            keepdims=True,
        )

    funnel_dots = lax.fori_loop(
        0, tokens // tile, count_dots, jnp.zeros((1, width), jnp.float32)
    )
    dots_box[0] = jnp.broadcast_to(funnel_dots, dots_box.shape[1:])
    dots_copy.start()
    loads[2].wait()
    line_up = lax.broadcasted_iota(jnp.int32, (SEQ, SEQ), 0)
    line_on = lax.broadcasted_iota(jnp.int32, (SEQ, SEQ), 1)

    def attend(block, carry):
        for part in range(count):
            place = rows_of(part)
            allowed = ((line_up >= line_on) & (keep_ref[part] > 0)) | (line_up == line_on)
            for half in range(halves):
                lanes = slice(half * HEAD_DIM, (half + 1) * HEAD_DIM)
                scores = dot_nt(
                    turned[block, place, lanes], turned[near + block, place, lanes]
                ) * scale
                masked = jnp.where(allowed, scores, MASKED)
                top = jnp.max(masked, axis=1, keepdims=True)
                weight = jnp.exp(masked - top)
                attention[part, halves * block + half] = weight / jnp.sum(
                    weight, axis=1, keepdims=True
                )
        return carry

    lax.fori_loop(0, near, attend, 0)
    for copy in part_copies[1:]:
        copy.start()

    def funnel_lanes(block):
        half = 0 if isinstance(block, int) else lax.rem(block, 2) * (CHUNK // 2)
        return pl.ds(pl.multiple_of(half, CHUNK // 2), CHUNK // 2)

    def funnel_load(block, slot):
        return pltpu.make_async_copy(
            full.at[4 * near + BLOCKS * lax.div(block, 2) + 2, :, :, :, :, funnel_lanes(block)],
            funnel_weight.at[slot],
            funnel_sems.at[slot],
        )

    funnel_load(0, 0).start()
    for load in loads[3:] + weight_loads:
        load.wait()
    head_seen = [
        dot_nn(entry_down_ref[pl.ds(RANK * i, RANK)], weight_of(i)) for i in range(3)
    ]
    mixer_seen = dot_nt(mixer_low, weight_of(3))
    reduced = dot_nt(entry_down_ref[...], normed[...]).astype(jnp.bfloat16)
    dots_copy.wait()
    funnel_dots = dots_box[0, 0:1] + dots_box[1, 0:1]
    funnel_pull = (output_ref[1] * (output_pull[1] * funnel_dots)).astype(jnp.bfloat16)

    def correct(block, carry):
        slot = lax.rem(block, 2)

        @pl.when(block < 2 * wide // CHUNK - 1)
        def _():
            funnel_load(block + 1, 1 - slot).start()

        funnel_load(block, slot).wait()
        columns = pl.ds(pl.multiple_of(block * (CHUNK // 2), CHUNK // 2), CHUNK // 2)
        funnel_down[:, columns] = funnel_down_ref[:, columns] - ADAPTER_SCALE * dot_nn(
            funnel_pull, funnel_weight[slot].reshape(width, CHUNK // 2)
        )
        return carry

    lax.fori_loop(0, 2 * wide // CHUNK, correct, 0)
    gathered[pl.ds(6 * RANK, RANK)] = ADAPTER_SCALE * (
        funnel_up_ref[...] * output_ratio[1]
        - funnel_seen_ref[...] * (output_pull[1] * funnel_dots)
    )
    gathered[pl.ds(3 * RANK, 2 * RANK)] = feed_down_ref[...]
    mixer_dots[...] = jnp.zeros_like(mixer_dots)
    small = 32
    for part in range(count):
        part_copies[part].wait()
        if part == count - 1:
            for copy in funneled_copies[: 2 * count - 2]:
                copy.start()

        def pull_back(index, carry, part=part):
            place = pl.ds(pl.multiple_of(part * SEQ + index * small, small), small)
            value = residual[place]
            weighted = gain_ref[1:2] * (
                own[place].astype(jnp.float32) + inbox[place].astype(jnp.float32)
            )
            root = lax.rsqrt(jnp.mean(value * value, axis=1, keepdims=True) + NORM_EPS)
            along = jnp.mean(value * weighted, axis=1, keepdims=True)
            gradient = back[place].astype(jnp.float32) + (
                root * weighted - value * (root * root * root * along)
            )
            rounded = gradient.astype(jnp.bfloat16)
            d_low[place] = rounded
            attended = value - floats[place].astype(jnp.float32)
            mixer_dots[...] += jnp.sum(
                (rounded.astype(jnp.float32) * attended).reshape(small // 8, 8, width), axis=0
            )
            residual[place] = gradient
            return carry

        lax.fori_loop(0, SEQ // small, pull_back, 0)
        place = rows_of(part)

        def attend_back(block, carry, part=part, place=place):
            columns = pl.ds(pl.multiple_of(block * CHUNK, CHUNK), CHUNK)
            mixer = weights[3, :, :, :, :, columns].reshape(width, CHUNK)
            d_mixed = dot_nn(d_low[place], mixer).astype(jnp.bfloat16)
            for half in range(halves):
                lanes = slice(half * HEAD_DIM, (half + 1) * HEAD_DIM)
                spot = pl.ds(
                    pl.multiple_of(block * CHUNK + half * HEAD_DIM, HEAD_DIM), HEAD_DIM
                )
                weight = attention[part, halves * block + half]
                d_head = d_mixed[:, lanes]
                d_attention = dot_nt(d_head, turned[2 * near + block, place, lanes])
                d_heads[2, place, spot] = dot_nn(
                    weight.astype(jnp.bfloat16).T, d_head
                ).astype(jnp.bfloat16)
                inner = jnp.sum(weight * d_attention, axis=1, keepdims=True)
                d_scores = (weight * (d_attention - inner)).astype(jnp.bfloat16)
                d_query = dot_nn(d_scores, turned[near + block, place, lanes]) * scale
                d_key = dot_nn(d_scores.T, turned[block, place, lanes]) * scale
                for i, value in ((0, d_query), (1, d_key)):
                    d_heads[i, place, spot] = (
                        value * cosine_ref[place]
                        - pltpu.roll(value, HEAD_DIM // 2, 1) * sine_ref[place]
                    ).astype(jnp.bfloat16)
            return carry

        lax.fori_loop(0, near, attend_back, 0)
        if part == count - 1:
            funneled_copies[2 * count - 2].start()
    per = 512 // (4 * weights.shape[4])
    for i in range(3):
        dots = []
        for block in range(near):
            lanes = slice(block * CHUNK, (block + 1) * CHUNK)
            source = plain if i < 2 else turned
            dots.append(
                jnp.sum(
                    d_heads[i, :tokens, lanes].astype(jnp.float32)
                    * source[near * i + block].astype(jnp.float32),
                    axis=0,
                    keepdims=True,
                )
            )
        dots = jnp.concatenate(dots, axis=1)
        dots_out[4 + i : 5 + i] = dots
        pulled = (attend_ref[i] * (pulls[4 + i : 5 + i] * dots)).astype(jnp.bfloat16)
        d_heads[i, tokens:] = pulled
    for piece in range(width // 512):
        lanes = slice(piece * 512, (piece + 1) * 512)
        results = [
            dot_nt(d_heads[i], weights[i, pl.ds(piece * per, per)].reshape(512, cut))
            for i in range(3)
        ]
        own[:, lanes] = (
            results[0][:tokens] + results[1][:tokens] + results[2][:tokens]
        ).astype(jnp.bfloat16)
        for i in range(3):
            gathered[pl.ds(RANK * i, RANK), lanes] = -ADAPTER_SCALE * results[i][tokens:]
    last_copies[0].start()
    for i in range(3):
        head_ratio = ratios[4 + i : 5 + i]
        place_in(
            gathered,
            half_rows,
            cut * i,
            ADAPTER_SCALE
            * (
                dot_nn(reduced[RANK * i : RANK * (i + 1)], d_heads[i, :tokens]) * head_ratio
                - head_seen[i] * (pulls[4 + i : 5 + i] * dots_out[4 + i : 5 + i])
            ),
        )
        low_lift = (attend_ref[i] * head_ratio).astype(jnp.bfloat16)
        lowered = dot_nt(low_lift, d_heads[i, :tokens]).astype(jnp.bfloat16)
        gathered[pl.ds(RANK * i, RANK)] += ADAPTER_SCALE * dot_nn(lowered, normed[...])
    mixer_total = jnp.sum(mixer_dots[...], axis=0, keepdims=True)
    joined = jnp.concatenate([mixed[b] for b in range(near)], axis=1)
    low_output = (output_ref[0] * output_ratio[0]).astype(jnp.bfloat16)
    lowered = dot_nt(low_output, d_low[...]).astype(jnp.bfloat16)
    pulled = (output_ref[0] * (output_pull[0] * mixer_total)).astype(jnp.bfloat16)
    mixer_down = ADAPTER_SCALE * (dot_nn(lowered, joined) - dot_nn(pulled, weight_of(3)))
    reduced_mixed = dot_nt(mixer_low, joined).astype(jnp.bfloat16)
    gathered[pl.ds(5 * RANK, RANK)] = ADAPTER_SCALE * (
        dot_nn(reduced_mixed, d_low[...]) * output_ratio[0]
        - mixer_seen * (output_pull[0] * mixer_total)
    )
    for i, value in enumerate((mixer_total, funnel_dots)):
        for r in range(2):
            dots_out[2 * i + r : 2 * i + r + 1] = value[:, r * LANES : (r + 1) * LANES]
    row = 7
    for i in range(2):
        for start in range(0, wide, LANES):
            size = min(LANES, wide - start)
            dots_out[row : row + 1, pl.ds(0, size)] = feed_dots_ref[
                i : i + 1, pl.ds(start, size)
            ]
            if size < LANES:
                dots_out[row : row + 1, pl.ds(size, LANES - size)] = jnp.zeros(
                    (1, LANES - size), jnp.float32
                )
            row += 1
    if row < dots_out.shape[0]:
        dots_out[row:] = jnp.zeros((dots_out.shape[0] - row, LANES), jnp.float32)
    offset = 3 * cut
    scales = dots_out[...] / magnitudes_ref[...]
    for value in (feed_up_ref[0], feed_up_ref[1], mixer_down, funnel_down[...], scales):
        place_in(gathered, half_rows, offset, value)
        offset += value.shape[1]
    rest_columns = half_rows // RANK * width - offset
    place_in(gathered, half_rows, offset, jnp.zeros((RANK, rest_columns), jnp.float32))
    def meanwhile():
        for copy in last_copies[1:] + funneled_copies[2 * count - 1 :]:
            copy.start()

    sum_up(
        size, sides, widths, offset - LANES, total, norm_out, gathered, side_box, norm_box,
        meanwhile, *sum_refs,
    )
    tile = kept_rows.shape[1]
    steps = SEQ // tile

    def kept_loads(part, index, slot):
        place = pl.ds(pl.multiple_of(part * SEQ + index * tile, tile), tile)
        return [
            pltpu.make_async_copy(residual_ref.at[place], kept_rows.at[slot], kept_sems.at[0, slot]),
            pltpu.make_async_copy(funneled_out.at[place], other_rows.at[slot], kept_sems.at[1, slot]),
        ]

    gradient_copies = []
    for part in range(count):
        last_copies[part].wait()

        def pull_rows(index, carry, part=part):
            place = pl.ds(pl.multiple_of(part * SEQ + index * small, small), small)
            value = floats[place].astype(jnp.float32)
            weighted = gain_ref[0:1] * (
                own[place].astype(jnp.float32) + last_inbox[place].astype(jnp.float32)
            )
            root = lax.rsqrt(jnp.mean(value * value, axis=1, keepdims=True) + NORM_EPS)
            along = jnp.mean(value * weighted, axis=1, keepdims=True)
            residual[place] += root * weighted - value * (root * root * root * along)
            return carry

        lax.fori_loop(0, SEQ // small, pull_rows, 0)
        gradient_copies.append(
            pltpu.make_async_copy(
                residual.at[rows_of(part)], gradient_out.at[rows_of(part)], out_sems.at[part]
            )
        )
        gradient_copies[-1].start()
    for part in range(count):
        funneled_copies[2 * part].wait()
        funneled_copies[2 * part + 1].wait()
        for load in kept_loads(part, 0, 0):
            load.start()

        def end_rows(index, carry, part=part):
            slot = lax.rem(index, 2)

            @pl.when(index < steps - 1)
            def _():
                for load in kept_loads(part, index + 1, 1 - slot):
                    load.start()

            for load in kept_loads(part, index, slot):
                load.wait()
            place = pl.ds(pl.multiple_of(part * SEQ + index * tile, tile), tile)
            d_low[place] = (
                kept_rows[slot]
                + (funneled[place].astype(jnp.float32) + other_rows[slot].astype(jnp.float32))
            ).astype(jnp.bfloat16)
            return carry

        lax.fori_loop(0, steps, end_rows, 0)
        gradient_copies.append(
            pltpu.make_async_copy(
                d_low.at[rows_of(part)], block_out.at[rows_of(part)], out_sems.at[count + part]
            )
        )
        gradient_copies[-1].start()
    for copy in gradient_copies:
        copy.wait()


def run_tail(big, small):
    size = lax.axis_size("dp")
    sides = lax.axis_size("tensor")
    full, turned, plain, mixed, residual = big[:5]
    tokens, width = residual.shape
    line, height = full.shape[1], full.shape[4]
    near = mixed.shape[0]
    cut = near * CHUNK
    wide = small[10].shape[1]
    lines = small[8].shape[0]
    count = tokens // SEQ
    anywhere = pl.BlockSpec(memory_space=pl.ANY)
    local = pl.BlockSpec(memory_space=pltpu.VMEM)
    low, full_type = jnp.bfloat16, jnp.float32
    heads = cut // HEAD_DIM
    rows = 7 * RANK
    bits = len(bin(size)) - 3
    widths = [max(width >> (step + 1), 128) for step in range(bits)]
    halvings = sum(1 for step in range(bits) if width >> (step + 1) >= 128)
    boxes = [pltpu.VMEM((2 * rows, w), low) for w in widths]
    copies = bits + halvings + 2 * (sides - 1)
    return pl.pallas_call(
        staged(functools.partial(tail_kernel, size, sides, widths), len(big), len(small)),
        name="tail",
        out_shape=(
            jax.ShapeDtypeStruct((tokens, width), full_type),
            jax.ShapeDtypeStruct((tokens, width), low),
            jax.ShapeDtypeStruct((tokens, width), low),
            jax.ShapeDtypeStruct((2 * rows + RANK, width), low),
            jax.ShapeDtypeStruct((8, 128), full_type),
        ),
        in_specs=[anywhere] * (len(big) + len(small)),
        out_specs=[anywhere] * 3 + [local] * 2,
        scratch_shapes=[
            pltpu.VMEM((4, line, 2, 2, height, cut), low),
            pltpu.VMEM((tokens, width), full_type),
            pltpu.VMEM((tokens, width), low),
            pltpu.VMEM((tokens, width), low),
            pltpu.VMEM((tokens, width), low),
            pltpu.VMEM(turned.shape, low),
            pltpu.VMEM(plain.shape, low),
            pltpu.VMEM(mixed.shape, low),
            pltpu.VMEM((tokens, width), low),
            pltpu.VMEM((tokens, width), low),
            pltpu.VMEM((tokens, width), low),
            pltpu.VMEM((tokens, width), low),
            pltpu.VMEM((count, heads, SEQ, SEQ), full_type),
            pltpu.VMEM((tokens, width), low),
            pltpu.VMEM((3, tokens + RANK, cut), low),
            pltpu.VMEM((2, line, 2, 2, height, CHUNK // 2), low),
            pltpu.VMEM((2, 8, width), full_type),
            pltpu.VMEM((8, width), full_type),
            pltpu.VMEM((3 * RANK, width), low),
            pltpu.VMEM((RANK, wide), full_type),
            pltpu.VMEM((2 * rows, width), full_type),
            pltpu.VMEM((lines, LANES), full_type),
            pltpu.VMEM((sides, rows, widths[-1]), low),
            pltpu.VMEM((sides, 8, 128), full_type),
            pltpu.VMEM((2, 32, width), full_type),
            pltpu.VMEM((2, 32, width), low),
            pltpu.SemaphoreType.DMA((10,)),
            pltpu.SemaphoreType.DMA((4 * near,)),
            pltpu.SemaphoreType.DMA((2,)),
            pltpu.SemaphoreType.DMA((4 * count + 1,)),
            pltpu.SemaphoreType.DMA((4 * count + 1,)),
            pltpu.SemaphoreType.DMA((2 * count,)),
            pltpu.SemaphoreType.DMA((2, 2)),
            *boxes,
            *boxes,
            pltpu.SemaphoreType.DMA((copies,)),
            pltpu.SemaphoreType.DMA((copies,)),
            *stage_of(small),
        ],
        compiler_params=pltpu.CompilerParams(
            collective_id=2, has_side_effects=True, vmem_limit_bytes=VMEM
        ),
    )(*big, *small)


def place_in(target, base, offset, value):
    width = target.shape[1]
    start = 0
    while start < value.shape[1]:
        group, lane = divmod(offset + start, width)
        size = min(value.shape[1] - start, width - lane)
        target[pl.ds(base + RANK * group, RANK), pl.ds(lane, size)] = value[
            :, start : start + size
        ].astype(target.dtype)
        start += size


def take_from(source, base, offset, size):
    width = source.shape[1]
    pieces = []
    start = 0
    while start < size:
        group, lane = divmod(offset + start, width)
        count = min(size - start, width - lane)
        pieces.append(
            source[pl.ds(base + RANK * group, RANK), pl.ds(lane, count)].astype(jnp.float32)
        )
        start += count
    return pieces[0] if len(pieces) == 1 else jnp.concatenate(pieces, axis=1)


def sum_up(
    size,
    sides,
    widths,
    scales_offset,
    total,
    norm_out,
    gathered,
    side_box,
    norm_box,
    meanwhile,
    *rest,
):
    bits = len(widths)
    outboxes, inboxes = rest[:bits], rest[bits : 2 * bits]
    sends, receives = rest[2 * bits :]
    half = gathered.shape[0] // 2
    me = lax.axis_index("dp")
    side = lax.axis_index("tensor")
    partners = partners_of(size)

    def remote(source, target, index, where):
        return pltpu.make_async_remote_copy(
            src_ref=source,
            dst_ref=target,
            send_sem=sends.at[index],
            recv_sem=receives.at[index],
            device_id=where,
            device_id_type=MESH,
        )

    start = 0
    width = gathered.shape[1]
    marks = []
    for step in range(bits):
        bit = lax.rem(lax.div(me, 2**step), 2)
        where = {"dp": partners[step]}
        if widths[step] < width:
            width = widths[step]
            marks.append((step, bit, width))
            mine = pl.ds(pl.multiple_of(start + bit * width, 128), width)
            theirs = pl.ds(pl.multiple_of(start + (1 - bit) * width, 128), width)
            outboxes[step][...] = gathered[:, theirs].astype(jnp.bfloat16)
            copy = remote(outboxes[step], inboxes[step], step, where)
            copy.start()
            copy.wait()
            gathered[:, mine] += inboxes[step][...].astype(jnp.float32)
            start = start + bit * width
        else:
            mine = pl.ds(pl.multiple_of(start, 128), width)
            outboxes[step][...] = gathered[:, mine].astype(jnp.bfloat16)
            copy = remote(outboxes[step], inboxes[step], step, where)
            copy.start()
            copy.wait()
            gathered[:, mine] = outboxes[step][...].astype(jnp.float32) + inboxes[step][
                ...
            ].astype(jnp.float32)
    mine = pl.ds(pl.multiple_of(start, 128), width)
    side_box[0] = gathered[pl.ds(0, half), mine].astype(jnp.bfloat16)
    split = gathered[pl.ds(half, half), mine].astype(jnp.bfloat16)
    value = split.astype(jnp.float32)
    group, lane = divmod(scales_offset, gathered.shape[1])
    row = lax.broadcasted_iota(jnp.int32, value.shape, 0) - RANK * group
    column = lax.broadcasted_iota(jnp.int32, value.shape, 1) + start - lane
    both_hold = (row >= 0) & (row < 4) & (column >= 0) & (column < LANES)
    norm_box[0] = jnp.full(
        norm_box.shape[1:],
        jnp.sum(jnp.where(both_hold, value * value / sides, value * value)),
        jnp.float32,
    )
    copies = []
    for step in range(1, sides):
        where = {"tensor": lax.rem(side + step, sides)}
        copies.append(remote(side_box.at[0], side_box.at[step], bits + 2 * step - 2, where))
        copies.append(remote(norm_box.at[0], norm_box.at[step], bits + 2 * step - 1, where))
    for copy in copies:
        copy.start()
    meanwhile()
    for copy in copies:
        copy.wait()
    shared = side_box[0].astype(jnp.float32)
    squares = norm_box[0]
    for step in range(1, sides):
        shared += side_box[step].astype(jnp.float32)
        squares += norm_box[step]
    shared = shared.astype(jnp.bfloat16)
    total[pl.ds(0, half), mine] = shared
    total[pl.ds(half, half), mine] = split
    value = shared.astype(jnp.float32)
    rest_of = jnp.full((1, width), jnp.sum(value * value)) + squares[0:1, 0:1]
    pieces = []
    for _ in range(3):
        pieces.append(rest_of.astype(jnp.bfloat16))
        rest_of = rest_of - pieces[-1].astype(jnp.float32)
    pieces.append(jnp.zeros((RANK - 3, width), jnp.bfloat16))
    total[pl.ds(2 * half, RANK), mine] = jnp.concatenate(pieces, axis=0)
    index = bits + 2 * (sides - 1)
    for step, bit, width in reversed(marks):
        mine = pl.ds(pl.multiple_of(start, 128), width)
        copy = remote(
            total.at[:, mine], total.at[:, mine], index, {"dp": partners[step]}
        )
        copy.start()
        copy.wait()
        index += 1
        start = start - bit * width
    pieces = total[pl.ds(2 * half, RANK)].astype(jnp.float32)
    norm = jnp.sqrt(jnp.sum(pieces) / widths[-1])
    norm_out[...] = jnp.full(norm_out.shape, norm, jnp.float32)


def update_kernel(*refs):
    total, norm_ref = refs[:2]
    values, firsts, seconds = refs[2:11], refs[11:20], refs[20:29]
    fresh, momenta, variances = refs[31:40], refs[40:49], refs[49:58]
    norm_out, boxes, sems = refs[60], refs[61:63], refs[63]
    ins = [pltpu.make_async_copy(refs[29 + i], boxes[i], sems.at[i]) for i in range(2)]
    outs = [pltpu.make_async_copy(boxes[i], refs[58 + i], sems.at[2 + i]) for i in range(2)]
    for copy in ins:
        copy.start()
    norm_out[...] = norm_ref[0:1, 0:1]
    factor = jnp.minimum(1.0, CLIP / (norm_ref[0:1, 0:1] + 1e-06))
    half = total.shape[0] // 2 - RANK // 2
    cut, wide = values[1].shape[2], values[2].shape[2]

    def update(index, rate, piece, gradient):
        value, momentum, variance = decoupled_update(
            values[index][piece], gradient * factor, firsts[index][piece], seconds[index][piece], rate
        )
        fresh[index][piece] = value
        momenta[index][piece] = momentum
        variances[index][piece] = variance

    def shared(group):
        return total[pl.ds(RANK * group, RANK)].astype(jnp.float32)

    for i in range(5):
        update(0, RATE_FACTOR, i, shared(i))
    for i in range(2):
        ins[i].wait()
        outs[i].start()
    for i in range(2):
        update(5, RATE_LIFT, i, shared(5 + i))
    offset = 0
    for i in range(3):
        update(1, RATE_LIFT, i, take_from(total, half, offset, cut))
        offset += cut
    for i in range(2):
        update(2, RATE_LIFT, i, take_from(total, half, offset, wide))
        offset += wide
    update(3, RATE_FACTOR, Ellipsis, take_from(total, half, offset, cut))
    offset += cut
    update(4, RATE_FACTOR, Ellipsis, take_from(total, half, offset, wide))
    offset += wide
    dots = take_from(total, half, offset, LANES)

    def long(row, size):
        count = -(-size // LANES)
        return jnp.concatenate([dots[row + r : row + r + 1] for r in range(count)], axis=1)[
            :, :size
        ]

    width = total.shape[1]
    for i in range(2):
        piece = slice(i, i + 1)
        update(8, RATE_LOUD, piece, long(2 * i, width))
    for i in range(3):
        piece = slice(i, i + 1)
        update(6, RATE_SCALE, piece, long(4 + i, cut))
    lines = -(-wide // LANES)
    for i in range(2):
        piece = slice(i, i + 1)
        update(7, RATE_SCALE, piece, long(7 + lines * i, wide))
    for copy in outs:
        copy.wait()


def update_all(total, norm, params, firsts, seconds, large):
    shapes = tuple(jax.ShapeDtypeStruct(p.shape, p.dtype) for p in params)
    large_shapes = tuple(jax.ShapeDtypeStruct(p.shape, p.dtype) for p in large)
    anywhere = pl.BlockSpec(memory_space=pl.ANY)
    local = pl.BlockSpec(memory_space=pltpu.VMEM)
    return pl.pallas_call(
        update_kernel,
        name="update",
        out_shape=shapes * 3 + large_shapes + (jax.ShapeDtypeStruct((1, 1), jnp.float32),),
        in_specs=[local] * 29 + [anywhere] * 2,
        out_specs=[local] * 27 + [anywhere] * 2 + [local],
        scratch_shapes=[
            *(pltpu.VMEM(p.shape, p.dtype) for p in large),
            pltpu.SemaphoreType.DMA((4,)),
        ],
        compiler_params=pltpu.CompilerParams(vmem_limit_bytes=VMEM),
    )(total, norm, *params, *firsts, *seconds, *large)


def body(
    activations,
    cotangent,
    padding_mask,
    positions,
    norm_gains,
    base_query,
    base_key,
    base_value,
    base_gate,
    base_widen,
    base_mixer,
    base_funnel,
    entry_value,
    attend_value,
    widen_value,
    mixer_value,
    funnel_value,
    output_value,
    stature_value,
    amplitude_value,
    loudness_value,
    entry_first,
    attend_first,
    widen_first,
    mixer_first,
    funnel_first,
    output_first,
    stature_first,
    amplitude_first,
    loudness_first,
    entry_second,
    attend_second,
    widen_second,
    mixer_second,
    funnel_second,
    output_second,
    stature_second,
    amplitude_second,
    loudness_second,
):
    params = (
        entry_value,
        attend_value,
        widen_value,
        mixer_value,
        funnel_value,
        output_value,
        stature_value,
        amplitude_value,
        loudness_value,
    )
    firsts = (
        entry_first,
        attend_first,
        widen_first,
        mixer_first,
        funnel_first,
        output_first,
        stature_first,
        amplitude_first,
        loudness_first,
    )
    seconds = (
        entry_second,
        attend_second,
        widen_second,
        mixer_second,
        funnel_second,
        output_second,
        stature_second,
        amplitude_second,
        loudness_second,
    )
    entry_down = jnp.swapaxes(entry_value, 1, 2)
    shard, squares, magnitudes = merge(
        (base_query, base_key, base_value, base_gate, base_widen, base_mixer, base_funnel),
        entry_down,
        attend_value,
        widen_value,
        mixer_value.T,
        funnel_value.T,
        output_value,
        (stature_value, amplitude_value, loudness_value),
    )
    count = activations.shape[0] // SEQ
    half = jnp.arange(HEAD_DIM) % (HEAD_DIM // 2)
    frequency = (ROPE_BASE ** (-2.0 * half.astype(jnp.float32) / HEAD_DIM))[None]
    keep = padding_mask.reshape(count, 1, SEQ)
    (
        full,
        cosine,
        sine,
        normed_one,
        turned,
        plain,
        mixed,
        residual,
        d_normed_two,
        d_normed_other,
        funneled,
        feed_ups,
        feed_downs,
        funnel_down,
        funnel_up,
        funnel_seen,
        feed_dots,
    ) = run_block(
        shard,
        activations,
        cotangent,
        (
            positions.reshape(1, -1),
            frequency,
            keep,
            norm_gains,
            entry_down,
            funnel_value.T,
            widen_value,
            output_value,
            squares,
            magnitudes,
        ),
    )
    input_gradient, block_output, _, total, norm = run_tail(
        (
            full,
            turned,
            plain,
            mixed,
            residual,
            d_normed_two,
            d_normed_other,
            funneled,
            cotangent,
            activations,
            normed_one,
        ),
        (
            cosine,
            sine,
            keep,
            norm_gains,
            entry_down,
            attend_value,
            mixer_value.T,
            output_value,
            squares,
            magnitudes,
            funnel_down,
            funnel_up,
            funnel_seen,
            feed_dots,
            feed_downs,
            feed_ups,
        ),
    )

    def turned_over(items):
        return [
            jnp.swapaxes(item, -1, -2) if i in (0, 3, 4) else item for i, item in enumerate(items)
        ]

    results = update_all(
        total,
        norm,
        turned_over(params),
        turned_over(firsts),
        turned_over(seconds),
        (input_gradient, block_output),
    )
    input_gradient, block_output, gradient_norm = results[27:]
    updated, momenta, variances = (turned_over(results[i : i + 9]) for i in (0, 9, 18))
    gradient_norm = gradient_norm.reshape(())
    return (
        block_output,
        input_gradient,
        gradient_norm,
        updated[0],
        updated[1],
        updated[2],
        updated[3],
        updated[4],
        updated[5],
        updated[6],
        updated[7],
        updated[8],
        momenta[0],
        momenta[1],
        momenta[2],
        momenta[3],
        momenta[4],
        momenta[5],
        momenta[6],
        momenta[7],
        momenta[8],
        variances[0],
        variances[1],
        variances[2],
        variances[3],
        variances[4],
        variances[5],
        variances[6],
        variances[7],
        variances[8],
    )


def solution(mesh):
    return jax.shard_map(
        body,
        mesh=mesh,
        in_specs=(
            P("dp", None),
            P("dp", None),
            P("dp"),
            P("dp"),
            P(),
            P("dp", "tensor"),
            P("dp", "tensor"),
            P("dp", "tensor"),
            P("dp", "tensor"),
            P("dp", "tensor"),
            P("tensor", "dp"),
            P("tensor", "dp"),
            P(),
            P(None, None, "tensor"),
            P(None, None, "tensor"),
            P("tensor", None),
            P("tensor", None),
            P(),
            P(None, "tensor"),
            P(None, "tensor"),
            P(),
            P(),
            P(None, None, "tensor"),
            P(None, None, "tensor"),
            P("tensor", None),
            P("tensor", None),
            P(),
            P(None, "tensor"),
            P(None, "tensor"),
            P(),
            P(),
            P(None, None, "tensor"),
            P(None, None, "tensor"),
            P("tensor", None),
            P("tensor", None),
            P(),
            P(None, "tensor"),
            P(None, "tensor"),
            P(),
        ),
        out_specs=(
            P("dp", None),
            P("dp", None),
            P(),
            P(),
            P(None, None, "tensor"),
            P(None, None, "tensor"),
            P("tensor", None),
            P("tensor", None),
            P(),
            P(None, "tensor"),
            P(None, "tensor"),
            P(),
            P(),
            P(None, None, "tensor"),
            P(None, None, "tensor"),
            P("tensor", None),
            P("tensor", None),
            P(),
            P(None, "tensor"),
            P(None, "tensor"),
            P(),
            P(),
            P(None, None, "tensor"),
            P(None, None, "tensor"),
            P("tensor", None),
            P("tensor", None),
            P(),
            P(None, "tensor"),
            P(None, "tensor"),
            P(),
        ),
        check_vma=False,
    )
```
